32 devices in a mesh: wide: 8 (over y, x, core), narrow: 4 (over z).
Axes of the slice: x: 2, y: 2, z: 4, core: 2. Of those that a mesh axis runs over, the one named last changes fastest.
Arguments:
- tokens: bfloat16 [18432, 1024], P(('wide', 'narrow')), may hold values from -6 to 6
- clip_cond: bfloat16 [2, 1024], replicated, may hold values from -6 to 6
- image_cond: bfloat16 [8, 1024], P('wide'), may hold values from -6 to 6
- image_count: int32 [8], P('wide'), may hold values from 0 to 1, as said below
- space_modulate: bfloat16 [1024, 6144], P('wide', 'narrow'), may hold values from -0.1875 to 0.1875
- space_project: bfloat16 [1024, 3072], P('wide', 'narrow'), may hold values from -0.1875 to 0.1875
- space_output: bfloat16 [1024, 1024], P('wide', 'narrow'), may hold values from -0.75 to 0.75
- space_expand: bfloat16 [1024, 4096], P('wide', 'narrow'), may hold values from -0.1875 to 0.1875
- space_reduce: bfloat16 [4096, 1024], P('wide', 'narrow'), may hold values from -0.09375 to 0.09375
- space_bias: float32 [16, 961], replicated, may hold values from -4 to 4
- joint_modulate: bfloat16 [1024, 6144], P('wide', 'narrow'), may hold values from -0.1875 to 0.1875
- joint_project: bfloat16 [1024, 3072], P('wide', 'narrow'), may hold values from -0.1875 to 0.1875
- joint_output: bfloat16 [1024, 1024], P('wide', 'narrow'), may hold values from -0.75 to 0.75
- joint_expand: bfloat16 [1024, 4096], P('wide', 'narrow'), may hold values from -0.1875 to 0.1875
- joint_reduce: bfloat16 [4096, 1024], P('wide', 'narrow'), may hold values from -0.09375 to 0.09375
- joint_bias: float32 [16, 2025], replicated, may hold values from -4 to 4
- cotangent: bfloat16 [18432, 1024], P(('wide', 'narrow')), may hold values from -6 to 6
Outputs:
- output_tokens: bfloat16 [18432, 1024], P(('wide', 'narrow'))
- grad_tokens: float32 [18432, 1024], P(('wide', 'narrow'))
- grad_space_modulate: float32 [1024, 6144], P('wide', 'narrow')
- grad_space_project: float32 [1024, 3072], P('wide', 'narrow')
- grad_space_output: float32 [1024, 1024], P('wide', 'narrow')
- grad_space_expand: float32 [1024, 4096], P('wide', 'narrow')
- grad_space_reduce: float32 [4096, 1024], P('wide', 'narrow')
- grad_space_bias: float32 [16, 961], replicated
- grad_joint_modulate: float32 [1024, 6144], P('wide', 'narrow')
- grad_joint_project: float32 [1024, 3072], P('wide', 'narrow')
- grad_joint_output: float32 [1024, 1024], P('wide', 'narrow')
- grad_joint_expand: float32 [1024, 4096], P('wide', 'narrow')
- grad_joint_reduce: float32 [4096, 1024], P('wide', 'narrow')
- grad_joint_bias: float32 [16, 2025], replicated
The draws below stay inside these ranges and needn't reach their ends.
Inputs may be any that keep to these rules, and one draw needn't show every extreme that they name: Image slots 0 to image_count[w] - 1 of group w hold images, the others are ignored; some group has all 1 slots live.
All inputs are finite; a program needn't handle non-finite values.
Results may differ from the reference program's by a relative error of at most 0.03.
The reference program's roundings to bfloat16 on the way count: a program that leaves them out, or rounds other values in their place, can miss the bound.
Values may be sent and summed in bfloat16 or wider, within the bound.
A program may use at most 448 MiB of HBM per device.

```python
import jax
import jax.numpy as jnp
import numpy as np
from jax import lax

D = 1024
HEADS = 16
FF = 4096
COND = 1024
HEAD_DIM = 64
SW = 8
TW = 5
CLIP_DEV = 1
IMG_DEV = 1
GROUPS = 8
CLIPS = 2
IMAGES = 8
ROWS_DEV = 576
ROWS = 18432
NREL_S = 961
NREL_T = 2025
N_NARROW = 4


def draw_image_count(key, part):
    key = jax.random.fold_in(key, 11)
    count_key, pick_key = jax.random.split(key)
    counts = jax.random.randint(count_key, (GROUPS,), 0, IMG_DEV + 1)
    chosen = jax.random.randint(pick_key, (), 0, GROUPS)
    return jnp.where(jnp.arange(GROUPS) == chosen, IMG_DEV, counts).astype(jnp.int32)


def with_spikes(values, key, source, target, parts, factor):
    def block_of(position):
        return (jnp.arange(values.shape[position]) // (values.shape[position] // parts)).reshape((-1,) + (1,) * (values.ndim - 1 - position))

    one_side = jax.random.permutation(key, parts)[block_of(target)]
    other_side = (block_of(target) + parts // 2) % parts
    return jnp.where((block_of(source) == one_side) | (block_of(source) == other_side), factor * values, values)


def block_levels(own_key, shape, cuts, smallest, top_value):
    level = 1.0
    for axis_at, parts in cuts:
        heights = jax.random.uniform(jax.random.fold_in(jax.random.fold_in(own_key, 6), axis_at), (parts,), jnp.float32, smallest / len(cuts), top_value / len(cuts))
        level = level * jnp.repeat(jnp.exp(heights), shape[axis_at] // parts).reshape((-1,) + (1,) * (len(shape) - 1 - axis_at))
    return level


def scatter_about(rng, dims, width, reach, cuts=(), dtype=jnp.bfloat16):
    values = jax.random.normal(rng, dims, jnp.float32) * width
    if len(cuts) > 0:
        values = block_levels(rng, dims, cuts, -0.22, 0.18) * values
    return jnp.clip(values, min=-reach, max=reach).astype(dtype)


def noise_with(stream_key, dims, scale, bound, cuts, heavy, kind=jnp.bfloat16):
    drawn = scale * jax.random.normal(stream_key, dims, jnp.float32)
    if cuts:
        drawn = drawn * block_levels(stream_key, dims, cuts, -0.22, 0.18)
    return jnp.clip(with_spikes(drawn, jax.random.fold_in(stream_key, 3), *heavy), -bound, bound).astype(kind)


def setup_inputs(seed: int = 0) -> dict:
    seeds = jax.random.split(jax.random.key(seed), 18)
    tokens = scatter_about(seeds[0], (ROWS, D), 1.0, 6.0, ((0, 32),))
    clip_cond = scatter_about(seeds[1], (CLIPS, COND), 1.0, 6.0)
    image_cond = scatter_about(seeds[2], (IMAGES, COND), 1.0, 6.0, ((0, 8),))
    image_count = draw_image_count(jax.random.fold_in(seeds[17], 71), 0)
    space_modulate = scatter_about(seeds[4], (COND, 6 * D), COND ** -0.5, 0.1875, ((0, 8), (1, 4)))
    space_project = scatter_about(seeds[5], (D, 3 * D), D ** -0.5, 0.1875, ((0, 8), (1, 4)))
    space_output = scatter_about(seeds[6], (D, D), (D // 16) ** -0.5, 0.75, ((0, 8), (1, 4)))
    space_expand = scatter_about(seeds[7], (D, FF), D ** -0.5, 0.1875, ((0, 8), (1, 4)))
    space_reduce = scatter_about(seeds[8], (FF, D), FF ** -0.5, 0.09375, ((0, 8), (1, 4)))
    space_bias = scatter_about(seeds[9], (HEADS, NREL_S), 1.0, 4.0, (), jnp.float32)
    joint_modulate = scatter_about(seeds[10], (COND, 6 * D), COND ** -0.5, 0.1875, ((0, 8), (1, 4)))
    joint_project = scatter_about(seeds[11], (D, 3 * D), D ** -0.5, 0.1875, ((0, 8), (1, 4)))
    joint_output = scatter_about(seeds[12], (D, D), (D // 16) ** -0.5, 0.75, ((0, 8), (1, 4)))
    joint_expand = scatter_about(seeds[13], (D, FF), D ** -0.5, 0.1875, ((0, 8), (1, 4)))
    joint_reduce = scatter_about(seeds[14], (FF, D), FF ** -0.5, 0.09375, ((0, 8), (1, 4)))
    joint_bias = scatter_about(seeds[15], (HEADS, NREL_T), 1.0, 4.0, (), jnp.float32)
    cotangent = noise_with(seeds[16], (ROWS, D), 1.0, 6.0, ((0, 32),), (0, 1, 32, 2.75))
    return {"tokens": tokens, "clip_cond": clip_cond, "image_cond": image_cond, "image_count": image_count, "space_modulate": space_modulate, "space_project": space_project, "space_output": space_output, "space_expand": space_expand, "space_reduce": space_reduce, "space_bias": space_bias, "joint_modulate": joint_modulate, "joint_project": joint_project, "joint_output": joint_output, "joint_expand": joint_expand, "joint_reduce": joint_reduce, "joint_bias": joint_bias, "cotangent": cotangent}


epsilon = 1e-06

@jax.custom_vjp
def low(v):
    return lax.optimization_barrier(v.astype(jnp.bfloat16)).astype(jnp.float32)

@jax.custom_vjp
def low_back(v):
    return v

def low_keep(v):
    return (low(v), None)

def low_pass(kept, grad):
    return (grad,)

def back_keep(v):
    return (v, None)

def back_low(kept, grad):
    return (low(grad),)
low.defvjp(low_keep, low_pass)
low_back.defvjp(back_keep, back_low)

def layer_norm(values):
    centred = values - lax.optimization_barrier(jnp.mean(values, axis=-1, keepdims=True))
    spread = lax.optimization_barrier(jnp.mean(centred * centred, axis=-1, keepdims=True))
    return centred * lax.rsqrt(spread + epsilon)

def product(left, right):
    return jnp.matmul(left, right, precision=lax.Precision.HIGHEST)

def space_index(query_quarter, query_cells):
    key_quarter = jnp.repeat(jnp.arange(4), SW * SW)
    key_cells = jnp.tile(jnp.arange(SW * SW), 4)
    span_side = 4 * SW - 1
    row_gap = (query_quarter // 2 * SW + query_cells // SW)[:, None] - (key_quarter // 2 * SW + key_cells // SW)[None, :]
    col_gap = (query_quarter % 2 * SW + query_cells % SW)[:, None] - (key_quarter % 2 * SW + key_cells % SW)[None, :]
    return ((row_gap + 2 * SW - 1) * span_side + col_gap + 2 * SW - 1).astype(jnp.int32)

def joint_index(frames):
    cell_ids = jnp.arange(frames * SW * SW)
    frame_pos = cell_ids // (SW * SW)
    row_pos = cell_ids // SW % SW
    col_pos = cell_ids % SW
    span_side = 2 * SW - 1
    frame_gap = frame_pos[:, None] - frame_pos[None, :] + TW - 1
    row_gap = row_pos[:, None] - row_pos[None, :] + SW - 1
    col_gap = col_pos[:, None] - col_pos[None, :] + SW - 1
    return ((frame_gap * span_side + row_gap) * span_side + col_gap).astype(jnp.int32)

def spread_rows(per_sequence):
    repeats = np.array([TW * SW * SW] * CLIP_DEV + [4 * SW * SW] * IMG_DEV)
    return jnp.repeat(per_sequence, repeats, axis=0, total_repeat_length=CLIP_DEV * TW * SW * SW + 4 * IMG_DEV * SW * SW)

def live_rows(live_count):
    slot_live = (jnp.arange(IMG_DEV) < live_count).astype(jnp.float32)
    return jnp.concatenate([jnp.ones((CLIP_DEV * TW * SW * SW,), jnp.float32), jnp.repeat(slot_live, 4 * SW * SW)])

def premix(residual, mod_rows, offset):
    return layer_norm(residual) * (1.0 + mod_rows[:, (offset + 1) * D:(offset + 2) * D]) + mod_rows[:, offset * D:(offset + 1) * D]

def attend(queries, key_rows, values, rel_bias):
    win_count, query_len, key_len = (queries.shape[0], queries.shape[1], key_rows.shape[1])
    query_heads = queries.reshape(win_count, query_len, HEADS, HEAD_DIM)
    key_heads = key_rows.reshape(win_count, key_len, HEADS, HEAD_DIM)
    value_heads = values.reshape(win_count, key_len, HEADS, HEAD_DIM)
    scores = jnp.einsum('wqhd,wkhd->whqk', query_heads, key_heads, precision=lax.Precision.HIGHEST) * HEAD_DIM ** (-0.5) + rel_bias[None]
    scores = low_back(scores)
    row_top = lax.optimization_barrier(jnp.max(scores, axis=-1, keepdims=True))
    powered = jnp.exp(scores - row_top)
    softmaxed = powered / lax.optimization_barrier(jnp.sum(powered, axis=-1, keepdims=True))
    attended = jnp.einsum('whqk,wkhd->wqhd', low(softmaxed), value_heads, precision=lax.Precision.HIGHEST)
    return attended.reshape(win_count, query_len, D)

def space_attention(triple, lookup):
    win_count = triple.shape[1] // (SW * SW)
    grouped = triple.reshape(4, win_count, SW * SW, 3 * D).transpose(1, 0, 2, 3).reshape(win_count, 4 * SW * SW, 3 * D)
    all_quarters = jnp.repeat(jnp.arange(4), SW * SW)
    all_cells = jnp.tile(jnp.arange(SW * SW), 4)
    rel_bias = lookup[:, space_index(all_quarters, all_cells)]
    attended = attend(grouped[..., :D], grouped[..., D:2 * D], grouped[..., 2 * D:], rel_bias)
    return attended.reshape(win_count, 4, SW * SW, D).transpose(1, 0, 2, 3).reshape(4, win_count * SW * SW, D)

def joint_attention(triple, lookup):
    clip_rows = CLIP_DEV * TW * SW * SW
    clip_triple = triple[:, :clip_rows].reshape(4 * CLIP_DEV, TW * SW * SW, 3 * D)
    image_triple = triple[:, clip_rows:].reshape(16 * IMG_DEV, SW * SW, 3 * D)
    clip_out = attend(clip_triple[..., :D], clip_triple[..., D:2 * D], clip_triple[..., 2 * D:], lookup[:, joint_index(TW)])
    image_out = attend(image_triple[..., :D], image_triple[..., D:2 * D], image_triple[..., 2 * D:], lookup[:, joint_index(1)])
    return jnp.concatenate([clip_out.reshape(4, clip_rows, D), image_out.reshape(4, 4 * IMG_DEV * SW * SW, D)], axis=1)

def one_block(residual, cond_low, weights, attention):
    modulate, project, output, expand, shrink, lookup = weights
    mod_rows = spread_rows(product(cond_low, modulate))
    normed = low(premix(residual, mod_rows, 0))
    triple = low_back(low(product(normed, project)))
    attended = low_back(low(attention(triple, lookup)))
    branch = low_back(product(attended, output))
    middle = residual + mod_rows[:, 2 * D:3 * D] * branch
    normed_two = low(premix(middle, mod_rows, 3))
    before = low_back(product(normed_two, expand))
    active = low(jax.nn.gelu(before, approximate=False))
    reduced = low_back(product(active, shrink))
    return middle + mod_rows[:, 5 * D:] * reduced

def group_pass(residual, clip_rows, image_rows, live_count, space_weights, joint_weights):
    cond_low = low(jax.nn.silu(jnp.concatenate([clip_rows, image_rows], axis=0)))
    middle = one_block(residual, cond_low, space_weights, space_attention)
    result = one_block(middle, cond_low, joint_weights, joint_attention)
    return result * live_rows(live_count)[None, :, None]

def reference(tokens, clip_cond, image_cond, image_count, space_modulate, space_project, space_output, space_expand, space_reduce, space_bias, joint_modulate, joint_project, joint_output, joint_expand, joint_reduce, joint_bias, cotangent):
    residual = tokens.astype(jnp.float32).reshape(GROUPS, N_NARROW, ROWS_DEV, D)
    clip_shared = clip_cond.astype(jnp.float32).reshape(GROUPS // 4, 1, CLIP_DEV, COND)
    clip_rows = jnp.broadcast_to(clip_shared, (GROUPS // 4, 4, CLIP_DEV, COND)).reshape(GROUPS, CLIP_DEV, COND)
    image_rows = image_cond.astype(jnp.float32).reshape(GROUPS, IMG_DEV, COND)
    space_weights = (space_modulate.astype(jnp.float32), space_project.astype(jnp.float32), space_output.astype(jnp.float32), space_expand.astype(jnp.float32), space_reduce.astype(jnp.float32), space_bias.astype(jnp.float32))
    joint_weights = (joint_modulate.astype(jnp.float32), joint_project.astype(jnp.float32), joint_output.astype(jnp.float32), joint_expand.astype(jnp.float32), joint_reduce.astype(jnp.float32), joint_bias.astype(jnp.float32))
    checked = jax.checkpoint(group_pass)

    def whole_pass(residual_in, space_in, joint_in):

        def scan_step(nothing, pieces):
            return (nothing, checked(pieces[0], pieces[1], pieces[2], pieces[3], space_in, joint_in))
        return lax.scan(scan_step, None, (residual_in, clip_rows, image_rows, image_count))[1]
    result, pullback = jax.vjp(whole_pass, residual, space_weights, joint_weights)
    grad_residual, grad_space, grad_joint = pullback(cotangent.astype(jnp.float32).reshape(result.shape))
    return (result.reshape(ROWS, D).astype(jnp.bfloat16), grad_residual.reshape(ROWS, D), grad_space[0], grad_space[1], grad_space[2], grad_space[3], grad_space[4], grad_space[5], grad_joint[0], grad_joint[1], grad_joint[2], grad_joint[3], grad_joint[4], grad_joint[5])
```

```python
import functools
import math

import jax
import jax.numpy as jnp
import numpy as np
from jax import lax
from jax.experimental import pallas as pl
from jax.experimental.pallas import tpu as pltpu
from jax.sharding import PartitionSpec as P

D = 1024
HEADS = 16
HEAD_DIM = 64
FF = 4096
SW = 8
TW = 5
CHUNK = SW * SW
CLIP_ROWS = TW * CHUNK
ROWS_DEV = CLIP_ROWS + 4 * CHUNK
SPAN_S = 4 * SW - 1
SPAN_T = 2 * SW - 1
MESH = pl.DeviceIdType.MESH


epsilon = 1e-06


def normalise(values):
    centred = values - jnp.mean(values, axis=-1, keepdims=True)
    spread = jnp.mean(centred * centred, axis=-1, keepdims=True)
    scale = lax.rsqrt(spread + epsilon)
    return centred * scale, scale


def norm_back(unit, scale, grad):
    return scale * (
        grad
        - jnp.mean(grad, axis=-1, keepdims=True)
        - unit * jnp.mean(grad * unit, axis=-1, keepdims=True)
    )


def nn(left, right):
    return lax.dot_general(left, right, (((1,), (0,)), ((), ())), preferred_element_type=jnp.float32)


def nt(left, right):
    return lax.dot_general(left, right, (((1,), (1,)), ((), ())), preferred_element_type=jnp.float32)


def tn(left, right):
    return lax.dot_general(left, right, (((0,), (0,)), ((), ())), preferred_element_type=jnp.float32)


def each_chunk(body, count=ROWS_DEV // CHUNK):
    @pl.loop(0, count)
    def _(i):
        inner = lax.rem(i, ROWS_DEV // CHUNK)
        seq = jnp.where(inner >= CLIP_ROWS // CHUNK, 1, 0)
        body(pl.ds(pl.multiple_of(i * CHUNK, CHUNK), CHUNK), pl.ds(seq, 1))


def part(index):
    return slice(index * D, (index + 1) * D)


def whole(shape):
    return pl.BlockSpec(shape, lambda *_: (0,) * len(shape), pipeline_mode=pl.Buffered(1))


def spec(shape, index):
    return pl.BlockSpec(shape, index)


def params(limit=56):
    return pltpu.CompilerParams(vmem_limit_bytes=limit * 2**20)


def shape(dims, kind):
    return jax.ShapeDtypeStruct(dims, kind)


LOW = jnp.bfloat16
FULL = jnp.float32


def space_triple_kernel(quarter, rows, mods, weight, normed, queries, pairs):
    step = pl.program_id(0)

    @pl.when(step == 0)
    def _():
        def chunk(at, seq):
            unit, _ = normalise(rows[at, :].astype(FULL))
            normed[at, :] = (unit * (1.0 + mods[seq, part(1)]) + mods[seq, part(0)]).astype(LOW)

        each_chunk(chunk, 4 * ROWS_DEV // CHUNK)

    @pl.when(step < 2)
    def _():
        own = pl.ds(pl.multiple_of(quarter[0] * ROWS_DEV, ROWS_DEV), ROWS_DEV)
        queries[...] = nn(normed[own, :], weight[...]).astype(LOW)

    @pl.when(step >= 2)
    def _():
        for q in range(4):
            pairs[q] = nn(normed[q * ROWS_DEV : (q + 1) * ROWS_DEV, :], weight[...]).astype(LOW)


def space_triple(quarter, rows, mods, weight):
    tile = 512
    return pl.pallas_call(
        space_triple_kernel,
        grid=(3 * D // tile,),
        in_specs=[
            pl.BlockSpec(memory_space=pltpu.SMEM),
            whole((4 * ROWS_DEV, D)),
            whole((2, 6 * D)),
            spec((D, tile), lambda t: (0, t)),
        ],
        out_specs=[
            whole((4 * ROWS_DEV, D)),
            spec((ROWS_DEV, tile), lambda t: (0, jnp.minimum(t, 1))),
            spec((4, ROWS_DEV, tile), lambda t: (0, 0, jnp.maximum(t - 2, 0))),
        ],
        out_shape=[
            shape((4 * ROWS_DEV, D), LOW),
            shape((ROWS_DEV, D), LOW),
            shape((4, ROWS_DEV, 2 * D), LOW),
        ],
        compiler_params=params(),
        name="space_triple",
    )(quarter, rows, mods, weight)


def joint_triple_kernel(rows, mods, weight, normed, triple):
    @pl.when(pl.program_id(0) == 0)
    def _():
        def chunk(at, seq):
            unit, _ = normalise(rows[at, :])
            normed[at, :] = (unit * (1.0 + mods[seq, part(1)]) + mods[seq, part(0)]).astype(LOW)

        each_chunk(chunk)

    triple[...] = nn(normed[...], weight[...]).astype(LOW)


def joint_triple(rows, mods, weight):
    tile = 512
    return pl.pallas_call(
        joint_triple_kernel,
        grid=(3 * D // tile,),
        in_specs=[whole((ROWS_DEV, D)), whole((2, 6 * D)), spec((D, tile), lambda t: (0, t))],
        out_specs=[whole((ROWS_DEV, D)), spec((ROWS_DEV, tile), lambda t: (0, t))],
        out_shape=[shape((ROWS_DEV, D), LOW), shape((ROWS_DEV, 3 * D), LOW)],
        compiler_params=params(),
        name="joint_triple",
    )(rows, mods, weight)


def half_mask():
    return lax.broadcasted_iota(jnp.int32, (1, 2 * HEAD_DIM), 1) < HEAD_DIM


def split_heads(rows):
    first = half_mask()
    zero = jnp.zeros_like(rows)
    return jnp.concatenate([jnp.where(first, rows, zero), jnp.where(first, zero, rows)], axis=0)


def join_heads(stacked):
    return jnp.where(half_mask(), stacked[:CHUNK], stacked[CHUNK:])


def softmax_keys(keys, queries, bias):
    scores = nt(keys, queries) * HEAD_DIM**-0.5 + bias
    powered = jnp.exp(scores - jnp.max(scores, axis=0, keepdims=True))
    return powered / jnp.sum(powered, axis=0, keepdims=True)


def attend(queries, keys, values, bias):
    probs = softmax_keys(keys, split_heads(queries), bias)
    return join_heads(tn(values, probs.astype(LOW)).T).astype(LOW)


def attend_back(queries, keys, values, bias, grad):
    queries, grad = split_heads(queries), split_heads(grad)
    probs = softmax_keys(keys, queries, bias)
    grad_values = nn(probs.astype(LOW), grad)
    grad_probs = nt(values, grad)
    centre = jnp.sum(probs * grad_probs, axis=0, keepdims=True)
    grad_scores = (probs * (grad_probs - centre)).astype(LOW)
    grad_queries = join_heads(tn(keys, grad_scores).T) * HEAD_DIM**-0.5
    grad_keys = nn(grad_scores, queries) * HEAD_DIM**-0.5
    return grad_queries, grad_keys, grad_values, grad_scores.astype(FULL)


def space_attend_kernel(queries, keys, values, bias, out):
    table = bias[0]
    for i in range(ROWS_DEV // CHUNK):
        at = slice(i * CHUNK, (i + 1) * CHUNK)
        key_rows = keys[:, at, :].reshape(4 * CHUNK, 2 * HEAD_DIM)
        value_rows = values[:, at, :].reshape(4 * CHUNK, 2 * HEAD_DIM)
        out[at, :] = attend(queries[at, :], key_rows, value_rows, table)


def space_attend(queries, pairs, bias):
    wide = 2 * HEAD_DIM
    return pl.pallas_call(
        space_attend_kernel,
        grid=(HEADS // 2,),
        in_specs=[
            spec((ROWS_DEV, wide), lambda h: (0, h)),
            spec((4, ROWS_DEV, wide), lambda h: (0, 0, h)),
            spec((4, ROWS_DEV, wide), lambda h: (0, 0, h + HEADS // 2)),
            spec((1, 4 * CHUNK, wide), lambda h: (h, 0, 0)),
        ],
        out_specs=spec((ROWS_DEV, wide), lambda h: (0, h)),
        out_shape=shape((ROWS_DEV, D), LOW),
        compiler_params=params(),
        name="space_attend",
    )(queries, pairs, pairs, bias)


def space_attend_back_kernel(queries, keys, values, bias, grad, grad_q, grad_pairs, grad_bias):
    table = bias[0]
    for i in range(ROWS_DEV // CHUNK):
        at = slice(i * CHUNK, (i + 1) * CHUNK)
        key_rows = keys[:, at, :].reshape(4 * CHUNK, 2 * HEAD_DIM)
        value_rows = values[:, at, :].reshape(4 * CHUNK, 2 * HEAD_DIM)
        to_q, to_k, to_v, to_bias = attend_back(
            queries[at, :], key_rows, value_rows, table, grad[at, :]
        )
        grad_q[at, :] = to_q.astype(LOW)
        grad_pairs[0, :, at, :] = to_k.astype(LOW).reshape(4, CHUNK, 2 * HEAD_DIM)
        grad_pairs[1, :, at, :] = to_v.astype(LOW).reshape(4, CHUNK, 2 * HEAD_DIM)
        if i == 0:
            grad_bias[0] = to_bias
        else:
            grad_bias[0] += to_bias


def space_attend_back(queries, pairs, bias, grad):
    wide = 2 * HEAD_DIM
    head = spec((ROWS_DEV, wide), lambda h: (0, h))
    four = spec((4, ROWS_DEV, wide), lambda h: (0, 0, h))
    table = spec((1, 4 * CHUNK, wide), lambda h: (h, 0, 0))
    return pl.pallas_call(
        space_attend_back_kernel,
        grid=(HEADS // 2,),
        in_specs=[
            head,
            four,
            spec((4, ROWS_DEV, wide), lambda h: (0, 0, h + HEADS // 2)),
            table,
            head,
        ],
        out_specs=[head, spec((2, 4, ROWS_DEV, wide), lambda h: (0, 0, 0, h)), table],
        out_shape=[
            shape((ROWS_DEV, D), LOW),
            shape((2, 4, ROWS_DEV, D), LOW),
            shape((HEADS // 2, 4 * CHUNK, wide), FULL),
        ],
        compiler_params=params(),
        name="space_attend_back",
    )(queries, pairs, pairs, bias, grad)


def clip_table(bias, frame):
    return jnp.concatenate([bias[0, frame - t + TW - 1] for t in range(TW)], axis=0)


def joint_attend_kernel(queries, keys, values, bias, out):
    for i in range(ROWS_DEV // CHUNK):
        at = slice(i * CHUNK, (i + 1) * CHUNK)
        seen = slice(0, CLIP_ROWS) if i < TW else at
        table = clip_table(bias, i) if i < TW else bias[0, TW - 1]
        out[at, :] = attend(queries[at, :], keys[seen, :], values[seen, :], table)


def joint_specs():
    wide = 2 * HEAD_DIM
    return [
        spec((ROWS_DEV, wide), lambda h: (0, h)),
        spec((ROWS_DEV, wide), lambda h: (0, h + HEADS // 2)),
        spec((ROWS_DEV, wide), lambda h: (0, h + HEADS)),
        spec((1, 2 * TW - 1, CHUNK, wide), lambda h: (h, 0, 0, 0)),
    ]


def joint_attend(triple, bias):
    return pl.pallas_call(
        joint_attend_kernel,
        grid=(HEADS // 2,),
        in_specs=joint_specs(),
        out_specs=spec((ROWS_DEV, 2 * HEAD_DIM), lambda h: (0, h)),
        out_shape=shape((ROWS_DEV, D), LOW),
        compiler_params=params(),
        name="joint_attend",
    )(triple, triple, triple, bias)


def joint_attend_back_kernel(
    queries, keys, values, bias, grad, grads, grad_bias, sum_k, sum_v
):
    grad_bias[...] = jnp.zeros_like(grad_bias)
    for i in range(ROWS_DEV // CHUNK):
        at = slice(i * CHUNK, (i + 1) * CHUNK)
        seen = slice(0, CLIP_ROWS) if i < TW else at
        table = clip_table(bias, i) if i < TW else bias[0, TW - 1]
        to_q, to_k, to_v, to_bias = attend_back(
            queries[at, :], keys[seen, :], values[seen, :], table, grad[at, :]
        )
        grads[0, at, :] = to_q.astype(LOW)
        if i >= TW:
            grad_bias[0, TW - 1] += to_bias
            grads[1, at, :] = to_k.astype(LOW)
            grads[2, at, :] = to_v.astype(LOW)
            continue
        for t in range(TW):
            grad_bias[0, i - t + TW - 1] += to_bias[t * CHUNK : (t + 1) * CHUNK]
        if i == 0:
            sum_k[...] = to_k
            sum_v[...] = to_v
        elif i < TW - 1:
            sum_k[...] += to_k
            sum_v[...] += to_v
        else:
            grads[1, seen, :] = (sum_k[...] + to_k).astype(LOW)
            grads[2, seen, :] = (sum_v[...] + to_v).astype(LOW)


def joint_attend_back(triple, bias, grad):
    wide = 2 * HEAD_DIM
    head = spec((ROWS_DEV, wide), lambda h: (0, h))
    return pl.pallas_call(
        joint_attend_back_kernel,
        grid=(HEADS // 2,),
        in_specs=joint_specs() + [head],
        out_specs=[spec((3, ROWS_DEV, wide), lambda h: (0, 0, h)), joint_specs()[3]],
        out_shape=[
            shape((3, ROWS_DEV, D), LOW),
            shape((HEADS // 2, 2 * TW - 1, CHUNK, wide), FULL),
        ],
        scratch_shapes=[pltpu.VMEM((CLIP_ROWS, wide), FULL)] * 2,
        compiler_params=params(),
        name="joint_attend_back",
    )(triple, triple, triple, bias, grad)


def mlp_kernel(last_block, live, rows, attended, mods, output, expand, shrink, *refs):
    branch, middle, normed, active, slope, reduced, result, total = refs
    step = pl.program_id(0)

    @pl.when(step == 0)
    def _():
        def chunk(at, seq):
            grown = nn(attended[at, :], output[...])
            branch[at, :] = grown.astype(LOW)
            mixed = rows[at, :].astype(FULL) + mods[seq, part(2)] * grown
            middle[at, :] = mixed
            unit, _ = normalise(mixed)
            normed[at, :] = (unit * (1.0 + mods[seq, part(4)]) + mods[seq, part(3)]).astype(LOW)

        each_chunk(chunk)
        total[...] = jnp.zeros_like(total)

    before = nn(normed[...], expand[...])
    inner = 0.5 * (1.0 + lax.erf(before * 0.5**0.5))
    low_active = (before * inner).astype(LOW)
    active[...] = low_active
    slope[...] = (inner + before * jnp.exp(-0.5 * before * before) * (2.0 * math.pi) ** -0.5).astype(LOW)
    total[...] += nn(low_active, shrink[...])

    @pl.when(step == pl.num_programs(0) - 1)
    def _():
        def chunk(at, seq):
            reduced[at, :] = total[at, :].astype(LOW)
            value = middle[at, :] + mods[seq, part(5)] * total[at, :]
            if last_block:
                value = value * jnp.where(seq.start > 0, live[0], 1.0)
            result[at, :] = value.astype(result.dtype)

        each_chunk(chunk)


def mlp(last_block, live, rows, attended, mods, output, expand, shrink):
    tile = 512
    square = whole((ROWS_DEV, D))
    strip = spec((ROWS_DEV, tile), lambda f: (0, f))
    return pl.pallas_call(
        functools.partial(mlp_kernel, last_block),
        grid=(FF // tile,),
        in_specs=[
            pl.BlockSpec(memory_space=pltpu.SMEM),
            square,
            square,
            whole((2, 6 * D)),
            whole((D, D)),
            spec((D, tile), lambda f: (0, f)),
            spec((tile, D), lambda f: (f, 0)),
        ],
        out_specs=[square, square, square, strip, strip, square, square],
        out_shape=[
            shape((ROWS_DEV, D), LOW),
            shape((ROWS_DEV, D), FULL),
            shape((ROWS_DEV, D), LOW),
            shape((ROWS_DEV, FF), LOW),
            shape((ROWS_DEV, FF), LOW),
            shape((ROWS_DEV, D), LOW),
            shape((ROWS_DEV, D), LOW if last_block else FULL),
        ],
        scratch_shapes=[pltpu.VMEM((ROWS_DEV, D), FULL)],
        compiler_params=params(),
        name="mlp",
    )(live, rows, attended, mods, output, expand, shrink)


def mlp_back_kernel(first_block, live, *refs):
    (grad_result, attended, mods, branch, middle, normed, reduced, output, active, slope) = refs[:10]
    expand, shrink = refs[10:12]
    grad_shrink, grad_expand, grad_output, grad_middle, grad_attended, grad_mods = refs[12:18]
    grad_reduced, normed_t, total, grad_branch = refs[18:]
    step = pl.program_id(0)

    def incoming(at, seq):
        value = grad_result[at, :].astype(FULL)
        if first_block:
            value = value * jnp.where(seq.start > 0, live[0], 1.0)
        return value

    @pl.when(step == 0)
    def _():
        grad_mods[...] = jnp.zeros_like(grad_mods)

        def chunk(at, seq):
            value = incoming(at, seq)
            grad_reduced[at, :] = (mods[seq, part(5)] * value).astype(LOW)
            grad_mods[seq, part(5)] += jnp.sum(
                reduced[at, :].astype(FULL) * value, axis=0, keepdims=True
            )

        each_chunk(chunk)
        total[...] = jnp.zeros_like(total)
        normed_t[...] = normed[...].T

    grad_active = nt(grad_reduced[...], shrink[...])
    grad_before = (grad_active * slope[...].astype(FULL)).astype(LOW)
    grad_shrink[...] = tn(active[...], grad_reduced[...]).astype(LOW)
    grad_expand[...] = nn(normed_t[...], grad_before).astype(LOW)
    total[...] += nt(grad_before, expand[...])

    @pl.when(step == pl.num_programs(0) - 1)
    def _():
        def chunk(at, seq):
            grad = total[at, :]
            unit, scale = normalise(middle[at, :])
            grad_mods[seq, part(3)] += jnp.sum(grad, axis=0, keepdims=True)
            grad_mods[seq, part(4)] += jnp.sum(unit * grad, axis=0, keepdims=True)
            value = incoming(at, seq) + norm_back(unit, scale, (1.0 + mods[seq, part(4)]) * grad)
            grad_middle[at, :] = value
            grad_mods[seq, part(2)] += jnp.sum(
                branch[at, :].astype(FULL) * value, axis=0, keepdims=True
            )
            grad_branch[at, :] = (mods[seq, part(2)] * value).astype(LOW)

        each_chunk(chunk)
        grad_attended[...] = nt(grad_branch[...], output[...]).astype(LOW)
        grad_output[...] = tn(attended[...], grad_branch[...]).astype(LOW)


def mlp_back(first_block, live, grad_result, attended, mods, saved, output, expand, shrink):
    branch, middle, normed, active, slope, reduced = saved
    tile = 512
    square = whole((ROWS_DEV, D))
    strip = spec((ROWS_DEV, tile), lambda f: (0, f))
    across = spec((D, tile), lambda f: (0, f))
    down = spec((tile, D), lambda f: (f, 0))
    return pl.pallas_call(
        functools.partial(mlp_back_kernel, first_block),
        grid=(FF // tile,),
        in_specs=[
            pl.BlockSpec(memory_space=pltpu.SMEM),
            square,
            square,
            whole((2, 6 * D)),
            square,
            square,
            square,
            square,
            whole((D, D)),
            strip,
            strip,
            across,
            down,
        ],
        out_specs=[down, across, whole((D, D)), square, square, whole((2, 6 * D))],
        out_shape=[
            shape((FF, D), LOW),
            shape((D, FF), LOW),
            shape((D, D), LOW),
            shape((ROWS_DEV, D), FULL),
            shape((ROWS_DEV, D), LOW),
            shape((2, 6 * D), FULL),
        ],
        scratch_shapes=[
            pltpu.VMEM((ROWS_DEV, D), LOW),
            pltpu.VMEM((D, ROWS_DEV), LOW),
            pltpu.VMEM((ROWS_DEV, D), FULL),
            pltpu.VMEM((ROWS_DEV, D), LOW),
        ],
        compiler_params=params(),
        name="mlp_back",
    )(live, grad_result, attended, mods, branch, middle, normed, reduced, output, active, slope, expand, shrink)


def finish_rows(rows, grad_normed, grad_middle, mods, grad_rows, grad_mods):
    grad_mods[...] = jnp.zeros_like(grad_mods)

    def chunk(at, seq):
        grad = grad_normed[at, :].astype(FULL)
        unit, scale = normalise(rows[at, :].astype(FULL))
        grad_mods[seq, part(0)] += jnp.sum(grad, axis=0, keepdims=True)
        grad_mods[seq, part(1)] += jnp.sum(unit * grad, axis=0, keepdims=True)
        grad_rows[at, :] = grad_middle[at, :] + norm_back(
            unit, scale, (1.0 + mods[seq, part(1)]) * grad
        )

    each_chunk(chunk)


def joint_project_back_kernel(
    rows, mods, normed, grad_middle, weight, grad, grad_weight, grad_rows, grad_mods, total, normed_t
):
    step = pl.program_id(0)

    @pl.when(step == 0)
    def _():
        total[...] = jnp.zeros_like(total)
        normed_t[...] = normed[...].T

    grad_weight[...] = nn(normed_t[...], grad[0]).astype(LOW)
    total[...] += nt(grad[0], weight[...])

    @pl.when(step == pl.num_programs(0) - 1)
    def _():
        finish_rows(rows, total, grad_middle, mods, grad_rows, grad_mods)


def joint_project_back(rows, mods, normed, grad_middle, weight, grads):
    tile = 1024
    square = whole((ROWS_DEV, D))
    across = spec((D, tile), lambda t: (0, t))
    return pl.pallas_call(
        joint_project_back_kernel,
        grid=(3 * D // tile,),
        in_specs=[square, whole((2, 6 * D)), square, square, across, spec((1, ROWS_DEV, tile), lambda t: (t, 0, 0))],
        out_specs=[across, square, whole((2, 2 * D))],
        out_shape=[shape((D, 3 * D), LOW), shape((ROWS_DEV, D), FULL), shape((2, 2 * D), FULL)],
        scratch_shapes=[pltpu.VMEM((ROWS_DEV, D), FULL), pltpu.VMEM((D, ROWS_DEV), LOW)],
        compiler_params=params(),
        name="joint_project_back",
    )(rows, mods, normed, grad_middle, weight, grads)


def space_project_back_kernel(quarter, normed, weight, grad_q, grad_pairs, grad_weight, grad_normed, total):
    step = pl.program_id(0)

    @pl.when(step == 0)
    def _():
        own = pl.ds(pl.multiple_of(quarter[0] * ROWS_DEV, ROWS_DEV), ROWS_DEV)
        total[...] = jnp.zeros_like(total)
        grad_weight[...] = tn(normed[own, :], grad_q[...]).astype(LOW)
        total[own, :] = nt(grad_q[...], weight[...])

    @pl.when(step > 0)
    def _():
        flat = grad_pairs[0].reshape(4 * ROWS_DEV, D)
        grad_weight[...] = tn(normed[...], flat).astype(LOW)
        for q in range(4):
            at = slice(q * ROWS_DEV, (q + 1) * ROWS_DEV)
            value = total[at, :] + nt(grad_pairs[0, q], weight[...])
            total[at, :] = value

    @pl.when(step == pl.num_programs(0) - 1)
    def _():
        grad_normed[...] = total[...].astype(LOW)


def space_project_back(quarter, normed, weight, grad_q, grad_pairs):
    across = spec((D, D), lambda t: (0, t))
    return pl.pallas_call(
        space_project_back_kernel,
        grid=(3,),
        in_specs=[
            pl.BlockSpec(memory_space=pltpu.SMEM),
            whole((4 * ROWS_DEV, D)),
            across,
            whole((ROWS_DEV, D)),
            spec((1, 4, ROWS_DEV, D), lambda t: (jnp.maximum(t - 1, 0), 0, 0, 0)),
        ],
        out_specs=[across, whole((4 * ROWS_DEV, D))],
        out_shape=[shape((D, 3 * D), LOW), shape((4 * ROWS_DEV, D), LOW)],
        scratch_shapes=[pltpu.VMEM((4 * ROWS_DEV, D), FULL)],
        compiler_params=params(),
        name="space_project_back",
    )(quarter, normed, weight, grad_q, grad_pairs)


def finish_kernel(rows, mods, grad_normed, grad_middle, grad_rows, grad_mods):
    finish_rows(rows, grad_normed, grad_middle, mods, grad_rows, grad_mods)


def finish(rows, mods, grad_normed, grad_middle):
    return pl.pallas_call(
        finish_kernel,
        out_shape=[shape((ROWS_DEV, D), FULL), shape((2, 2 * D), FULL)],
        compiler_params=params(),
        name="finish",
    )(rows, mods, grad_normed, grad_middle)


def near_order(n):
    return (
        n,
        lax.bitwise_xor(n, 1),
        jnp.where(n < 2, 2, 1),
        jnp.where(n < 2, 3, 0),
    )


def enter(w, n, peers):
    barrier = pltpu.get_barrier_semaphore()
    for peer in peers:
        pl.semaphore_signal(barrier, inc=1, device_id=(peer, n), device_id_type=MESH)

    @pl.when(n > 0)
    def _():
        pl.semaphore_signal(barrier, inc=1, device_id=(w, n - 1), device_id_type=MESH)

    @pl.when(n < 3)
    def _():
        pl.semaphore_signal(barrier, inc=1, device_id=(w, n + 1), device_id_type=MESH)

    ends = jnp.where(n > 0, 1, 0) + jnp.where(n < 3, 1, 0)
    pl.semaphore_wait(barrier, len(peers) + ends)


PIECES = 4
PIECE = ROWS_DEV // PIECES


def gather_kernel(shapes, line, *refs):
    count = len(shapes)
    extra = 1 if line else 0
    shards, refs = refs[:count], refs[count:]
    line_in, refs = refs[:extra], refs[extra:]
    fulls, refs = refs[:count], refs[count:]
    line_out, refs = refs[:extra], refs[extra:]
    z_send, z_recv, x_send, x_recv, y_send, y_recv, c_send, c_recv, own_sem = refs[:9]
    if line:
        rows, all_rows = line_in[0], line_out[0]
        t_send, t_recv, t_own = refs[9:]
    w = lax.axis_index("wide")
    n = lax.axis_index("narrow")
    x_peer = lax.bitwise_xor(w, 2)
    y_peer = lax.bitwise_xor(w, 4)
    c_peer = lax.bitwise_xor(w, 1)
    d_peer = lax.bitwise_xor(w, 6)
    order = near_order(n)
    enter(w, n, (x_peer, y_peer, c_peer))

    def block(k, row, col):
        rows, cols = shapes[k]
        return fulls[k].at[
            pl.ds(pl.multiple_of(row * rows, rows), rows), pl.ds(pl.multiple_of(col * cols, cols), cols)
        ]

    def copy(k, src, row, col, send, recv, to):
        return pltpu.make_async_remote_copy(
            src_ref=src,
            dst_ref=block(k, row, col),
            send_sem=send,
            recv_sem=recv,
            device_id=to,
            device_id_type=MESH,
        )

    def z_copy(k, src, col, to):
        return copy(k, src, w, col, z_send.at[k, col], z_recv.at[k, col], (w, to))

    def x_copy(k, src, row, far, col):
        return copy(k, src, row, col, x_send.at[k, far, col], x_recv.at[k, far, col], (x_peer, n))

    def y_copy(k, src, row, far, col):
        return copy(k, src, row, col, y_send.at[k, far, col], y_recv.at[k, far, col], (y_peer, n))

    def c_copy(k, src, row, chip, col):
        return copy(k, src, row, col, c_send.at[k, chip, col], c_recv.at[k, chip, col], (c_peer, n))

    up = jnp.minimum(n + 1, 3)
    down = jnp.maximum(n - 1, 0)

    def own_copy(k):
        return pltpu.make_async_copy(shards[k], block(k, w, n), own_sem.at[k])

    for k in range(count):
        own_copy(k).start()
        x_copy(k, shards[k], w, 0, n).start()
        y_copy(k, shards[k], w, 0, n).start()

        @pl.when(n < 3)
        def _():
            copy(k, shards[k], w, n, z_send.at[k, n], z_recv.at[k, n], (w, up)).start()

        @pl.when(n > 0)
        def _():
            copy(k, shards[k], w, n, z_send.at[k, 4], z_recv.at[k, n], (w, down)).start()

        c_copy(k, shards[k], w, 0, n).start()

    def z_stage(k, j):
        col = order[j]
        here = block(k, w, col)
        z_copy(k, here, col, up).wait_recv()
        x_copy(k, here, w, 0, col).start()
        y_copy(k, here, w, 0, col).start()

        @pl.when(jnp.logical_and(col < n, n < 3))
        def _():
            z_copy(k, here, col, up).start()

        @pl.when(jnp.logical_and(col > n, n > 0))
        def _():
            z_copy(k, here, col, down).start()

        c_copy(k, here, w, 0, col).start()

    def xy_stage(k, j):
        col = order[j]
        from_x = block(k, x_peer, col)
        from_y = block(k, y_peer, col)
        x_copy(k, from_x, x_peer, 0, col).wait_recv()
        if j < 2:
            y_copy(k, from_x, x_peer, 1, col).start()
        c_copy(k, from_x, x_peer, 1, col).start()
        y_copy(k, from_y, y_peer, 0, col).wait_recv()
        if j >= 2:
            x_copy(k, from_y, y_peer, 1, col).start()
        c_copy(k, from_y, y_peer, 2, col).start()

    def far_stage(k, j):
        col = order[j]
        far = block(k, d_peer, col)
        if j < 2:
            y_copy(k, far, d_peer, 1, col).wait_recv()
        else:
            x_copy(k, far, d_peer, 1, col).wait_recv()
        c_copy(k, far, d_peer, 3, col).start()

    def t_copy(p, src, col, slot, to):
        return pltpu.make_async_remote_copy(
            src_ref=src,
            dst_ref=all_rows.at[col, pl.ds(p * PIECE, PIECE)],
            send_sem=t_send.at[p, slot],
            recv_sem=t_recv.at[p, col],
            device_id=(w, to),
            device_id_type=MESH,
        )

    def t_own_copy(p):
        here = pl.ds(p * PIECE, PIECE)
        return pltpu.make_async_copy(rows.at[here], all_rows.at[n, here], t_own.at[p])

    def t_start(p):
        src = rows.at[pl.ds(p * PIECE, PIECE)]
        t_own_copy(p).start()

        @pl.when(n < 3)
        def _():
            t_copy(p, src, n, n, up).start()

        @pl.when(n > 0)
        def _():
            t_copy(p, src, n, 4, down).start()

    def t_stage(p):
        for j in range(1, 4):
            col = order[j]
            here = all_rows.at[col, pl.ds(p * PIECE, PIECE)]
            t_copy(p, here, col, col, up).wait_recv()

            @pl.when(jnp.logical_and(col < n, n < 3))
            def _():
                t_copy(p, here, col, col, up).start()

            @pl.when(jnp.logical_and(col > n, n > 0))
            def _():
                t_copy(p, here, col, col, down).start()

    def t_drain(p):
        for col in range(4):
            here = all_rows.at[col, pl.ds(p * PIECE, PIECE)]

            @pl.when(jnp.logical_or(jnp.logical_and(col <= n, n < 3), jnp.logical_and(col > n, n > 0)))
            def _():
                t_copy(p, here, col, col, up).wait_send()

        @pl.when(n > 0)
        def _():
            t_copy(p, all_rows.at[n, pl.ds(p * PIECE, PIECE)], n, 4, down).wait_send()

        t_own_copy(p).wait()

    def z_all(k):
        for j in range(1, 4):
            z_stage(k, j)

    def xy_all(k):
        for j in range(4):
            xy_stage(k, j)

    def far_all(k):
        for j in range(4):
            far_stage(k, j)

    def t_all(start, stage):
        if line:
            if start >= 0:
                t_start(start)
            if stage >= 0:
                t_stage(stage)

    z_all(0)
    t_all(0, -1)
    z_all(1)
    t_all(1, -1)
    xy_all(0)
    z_all(2)
    t_all(2, 0)
    xy_all(1)
    far_all(0)
    z_all(3)
    t_all(3, 1)
    xy_all(2)
    far_all(1)
    t_all(-1, 2)
    xy_all(3)
    far_all(2)
    t_all(-1, 3)
    far_all(3)

    if line:
        for p in range(PIECES):
            t_drain(p)
    for k in range(count):
        own_copy(k).wait()
        for col in range(4):
            here = block(k, w, col)

            @pl.when(jnp.logical_or(jnp.logical_and(col <= n, n < 3), jnp.logical_and(col > n, n > 0)))
            def _():
                z_copy(k, here, col, up).wait_send()

            x_copy(k, here, w, 0, col).wait_send()
            y_copy(k, here, w, 0, col).wait_send()

            for chip in range(4):
                c_copy(k, here, w, chip, col).wait()

        @pl.when(n > 0)
        def _():
            copy(k, shards[k], w, n, z_send.at[k, 4], z_recv.at[k, n], (w, down)).wait_send()

        for j in range(4):
            col = order[j]
            here = block(k, w, col)
            if j < 2:
                y_copy(k, here, w, 1, col).wait_send()
            else:
                x_copy(k, here, w, 1, col).wait_send()


def gather_weights(shards, line, collective_id, name):
    count = len(shards)
    shapes = tuple(s.shape for s in shards)
    lines = [] if line is None else [line]
    dma = pltpu.SemaphoreType.DMA
    line_scratch = [dma((PIECES, 5)), dma((PIECES, 4)), dma((PIECES,))]
    return pl.pallas_call(
        functools.partial(gather_kernel, shapes, bool(lines)),
        out_shape=[shape((8 * r, 4 * c), LOW) for r, c in shapes]
        + [shape((4,) + rows.shape, LOW) for rows in lines],
        in_specs=[pl.BlockSpec(memory_space=pl.ANY)] * (count + len(lines)),
        out_specs=[pl.BlockSpec(memory_space=pl.ANY)] * (count + len(lines)),
        scratch_shapes=[
            dma((count, 5)),
            dma((count, 4)),
            dma((count, 2, 4)),
            dma((count, 2, 4)),
            dma((count, 2, 4)),
            dma((count, 2, 4)),
            dma((count, 4, 4)),
            dma((count, 4, 4)),
            dma((count,)),
        ]
        + line_scratch * len(lines),
        compiler_params=pltpu.CompilerParams(collective_id=collective_id, has_side_effects=True),
        cost_estimate=pl.CostEstimate(flops=100_000_000_000, bytes_accessed=0, transcendentals=0),
        name=name,
    )(*shards, *lines)


def scatter_kernel(shapes, line, *refs):
    count = len(shapes)
    extra = 1 if line else 0
    parts, refs = refs[:count], refs[count:]
    line_part, refs = refs[:extra], refs[extra:]
    outs, refs = refs[:count], refs[count:]
    line_out, scratch = refs[:extra], refs[extra:]
    held, core_in = scratch[:count], scratch[count : 2 * count]
    far_in, near_in, z_in = (
        scratch[2 * count : 3 * count],
        scratch[3 * count : 4 * count],
        scratch[4 * count : 5 * count],
    )
    load, c_send, c_recv, d_send, d_recv, n_send, n_recv, z_send, z_recv = scratch[
        5 * count : 5 * count + 9
    ]
    if line:
        line_held, line_in, line_load, line_send, line_recv = scratch[5 * count + 9 :]
    w = lax.axis_index("wide")
    n = lax.axis_index("narrow")
    x_peer = lax.bitwise_xor(w, 2)
    y_peer = lax.bitwise_xor(w, 4)
    c_peer = lax.bitwise_xor(w, 1)
    d_peer = lax.bitwise_xor(w, 6)
    chips = (w, x_peer, y_peer, d_peer)
    order = near_order(n)
    up = jnp.minimum(n + 1, 3)
    down = jnp.maximum(n - 1, 0)
    enter(w, n, (x_peer, y_peer, c_peer))

    def source(k, row, col):
        rows, cols = shapes[k]
        return parts[k].at[
            pl.ds(pl.multiple_of(row * rows, rows), rows), pl.ds(pl.multiple_of(col * cols, cols), cols)
        ]

    def load_copy(k, chip, col):
        return pltpu.make_async_copy(
            source(k, chips[chip], col), held[k].at[chip, col], load.at[k, chip, col]
        )

    def c_copy(k, chip, col):
        row = lax.bitwise_xor(chips[chip], 1)
        return pltpu.make_async_remote_copy(
            src_ref=source(k, row, col),
            dst_ref=core_in[k].at[chip, col],
            send_sem=c_send.at[k, chip, col],
            recv_sem=c_recv.at[k, chip, col],
            device_id=(c_peer, n),
            device_id_type=MESH,
        )

    def d_copy(k, j):
        return pltpu.make_async_remote_copy(
            src_ref=held[k].at[3, order[j]],
            dst_ref=far_in[k].at[j],
            send_sem=d_send.at[k, j],
            recv_sem=d_recv.at[k, j],
            device_id=(x_peer if j < 2 else y_peer, n),
            device_id_type=MESH,
        )

    def n_copy(k, chip, col):
        return pltpu.make_async_remote_copy(
            src_ref=held[k].at[chip, col],
            dst_ref=near_in[k].at[chip - 1, col],
            send_sem=n_send.at[k, chip - 1, col],
            recv_sem=n_recv.at[k, chip - 1, col],
            device_id=(chips[chip], n),
            device_id_type=MESH,
        )

    def z_copy(k, col, slot, to):
        return pltpu.make_async_remote_copy(
            src_ref=held[k].at[0, col],
            dst_ref=z_in[k].at[slot],
            send_sem=z_send.at[k, col],
            recv_sem=z_recv.at[k, slot],
            device_id=(w, to),
            device_id_type=MESH,
        )

    def add(k, chip, col, *others):
        rows = shapes[k][0]
        step = 32

        @pl.loop(0, rows // step)
        def _(i):
            at = pl.ds(pl.multiple_of(i * step, step), step)
            total = held[k][chip, col, at, :].astype(jnp.float32)
            for ref, index in others:
                total += ref[*index, at, :].astype(jnp.float32)
            held[k][chip, col, at, :] = total.astype(jnp.bfloat16)

    def fold_core(k, chip, col):
        load_copy(k, chip, col).wait()
        c_copy(k, chip, col).wait_recv()
        add(k, chip, col, (core_in[k], (chip, col)))

    def first(k):
        for j in range(4):
            fold_core(k, 3, order[j])
            d_copy(k, j).start()
        for j in range(2):
            fold_core(k, 1, order[j])
            n_copy(k, 1, order[j]).start()
            fold_core(k, 2, order[j + 2])
            n_copy(k, 2, order[j + 2]).start()

    def second(k):
        for j in range(2):
            load_copy(k, 2, order[j]).wait()
            c_copy(k, 2, order[j]).wait_recv()
            d_copy(k, j).wait_recv()
            add(k, 2, order[j], (core_in[k], (2, order[j])), (far_in[k], (j,)))
            n_copy(k, 2, order[j]).start()
            load_copy(k, 1, order[j + 2]).wait()
            c_copy(k, 1, order[j + 2]).wait_recv()
            d_copy(k, j + 2).wait_recv()
            add(k, 1, order[j + 2], (core_in[k], (1, order[j + 2])), (far_in[k], (j + 2,)))
            n_copy(k, 1, order[j + 2]).start()

    def fold_near(k, j):
        col = order[j]
        load_copy(k, 0, col).wait()
        c_copy(k, 0, col).wait_recv()
        n_copy(k, 1, col).wait_recv()
        n_copy(k, 2, col).wait_recv()
        add(k, 0, col, (core_in[k], (0, col)), (near_in[k], (0, col)), (near_in[k], (1, col)))

    def third(k):
        for j in (3, 2, 1):
            col = order[j]
            fold_near(k, j)
            upward = col > n
            carried = jnp.logical_or(
                jnp.logical_and(upward, n > 0), jnp.logical_and(col < n, n < 3)
            )

            @pl.when(carried)
            def _():
                z_copy(k, col, col, up).wait_recv()
                add(k, 0, col, (z_in[k], (col,)))

            to = jnp.where(upward, up, down)
            slot = jnp.where(jnp.logical_and(jnp.logical_not(upward), to == col), 4, col)
            z_copy(k, col, slot, to).start()

    def last(k):
        fold_near(k, 0)
        outs[k][...] = held[k][0, n].astype(FULL)

        @pl.when(n > 0)
        def _():
            z_copy(k, n, n, up).wait_recv()
            outs[k][...] += z_in[k][n].astype(FULL)

        @pl.when(n < 3)
        def _():
            z_copy(k, n, 4, up).wait_recv()
            outs[k][...] += z_in[k][4].astype(FULL)

    def line_loads(p, col):
        return pltpu.make_async_copy(
            line_part[0].at[pl.ds(pl.multiple_of(col * ROWS_DEV + p * PIECE, 16), PIECE)],
            line_held.at[p, col],
            line_load.at[p, col],
        )

    def line_copy(p, col, slot, to):
        return pltpu.make_async_remote_copy(
            src_ref=line_held.at[p, col],
            dst_ref=line_in.at[p, slot],
            send_sem=line_send.at[p, col],
            recv_sem=line_recv.at[p, slot],
            device_id=(w, to),
            device_id_type=MESH,
        )

    def line_stage(p, j):
        col = order[j]
        line_loads(p, col).wait()
        upward = col > n
        carried = jnp.logical_or(jnp.logical_and(upward, n > 0), jnp.logical_and(col < n, n < 3))

        @pl.when(carried)
        def _():
            line_copy(p, col, col, up).wait_recv()

            @pl.loop(0, PIECE // 16)
            def _(i):
                at = pl.ds(pl.multiple_of(i * 16, 16), 16)
                total = line_held[p, col, at, :].astype(FULL) + line_in[p, col, at, :].astype(FULL)
                line_held[p, col, at, :] = total.astype(LOW)

        to = jnp.where(upward, up, down)
        slot = jnp.where(jnp.logical_and(jnp.logical_not(upward), to == col), 4, col)
        line_copy(p, col, slot, to).start()

    def line_last(p):
        here = pl.ds(p * PIECE, PIECE)
        line_loads(p, n).wait()
        line_out[0][here, :] = line_held[p, n].astype(FULL)

        @pl.when(n > 0)
        def _():
            line_copy(p, n, n, up).wait_recv()
            line_out[0][here, :] += line_in[p, n].astype(FULL)

        @pl.when(n < 3)
        def _():
            line_copy(p, n, 4, up).wait_recv()
            line_out[0][here, :] += line_in[p, 4].astype(FULL)

    def line_all(j):
        if not line:
            return
        for p in range(PIECES):
            if j:
                line_stage(p, j)
            else:
                line_last(p)

    if line:
        for j in (3, 2, 1, 0):
            for p in range(PIECES):
                line_loads(p, order[j]).start()
    for k in range(count):
        for chip in (3, 1, 2, 0):
            for j in range(4):
                c_copy(k, chip, order[j]).start()
                load_copy(k, chip, order[j]).start()
    line_all(3)
    first(0)
    line_all(2)
    second(0)
    first(1)
    line_all(1)
    second(1)
    third(0)
    for t in range(2, count + 2):
        if t < count:
            first(t)
            second(t)
        if t - 1 < count:
            third(t - 1)
        last(t - 2)
        if t == 2:
            line_all(0)
    for k in range(count):
        for chip in range(4):
            for col in range(4):
                c_copy(k, chip, col).wait_send()
        for j in range(4):
            d_copy(k, j).wait_send()
            n_copy(k, 1, j).wait_send()
            n_copy(k, 2, j).wait_send()
        for j in range(1, 4):
            z_copy(k, order[j], order[j], up).wait_send()
    if line:
        for p in range(PIECES):
            for j in range(1, 4):
                line_copy(p, order[j], order[j], up).wait_send()


def scatter_grads(partials, line, collective_id, name):
    count = len(partials)
    shapes = tuple((g.shape[0] // 8, g.shape[1] // 4) for g in partials)
    dma = pltpu.SemaphoreType.DMA
    lines = [] if line is None else [line]
    line_scratch = [
        pltpu.VMEM((PIECES, 4, PIECE, D), LOW),
        pltpu.VMEM((PIECES, 5, PIECE, D), LOW),
        dma((PIECES, 4)),
        dma((PIECES, 4)),
        dma((PIECES, 5)),
    ]
    return pl.pallas_call(
        functools.partial(scatter_kernel, shapes, bool(lines)),
        out_shape=[shape(s, FULL) for s in shapes] + [shape((ROWS_DEV, D), FULL)] * len(lines),
        in_specs=[pl.BlockSpec(memory_space=pl.ANY)] * (count + len(lines)),
        out_specs=[pl.BlockSpec(memory_space=pltpu.VMEM)] * (count + len(lines)),
        scratch_shapes=[pltpu.VMEM((4, 4) + s, LOW) for s in shapes]
        + [pltpu.VMEM((4, 4) + s, LOW) for s in shapes]
        + [pltpu.VMEM((4,) + s, LOW) for s in shapes]
        + [pltpu.VMEM((2, 4) + s, LOW) for s in shapes]
        + [pltpu.VMEM((5,) + s, LOW) for s in shapes]
        + [
            dma((count, 4, 4)),
            dma((count, 4, 4)),
            dma((count, 4, 4)),
            dma((count, 4)),
            dma((count, 4)),
            dma((count, 2, 4)),
            dma((count, 2, 4)),
            dma((count, 4)),
            dma((count, 5)),
        ]
        + line_scratch * len(lines),
        compiler_params=pltpu.CompilerParams(
            collective_id=collective_id, has_side_effects=True, vmem_limit_bytes=56 * 2**20
        ),
        cost_estimate=pl.CostEstimate(flops=100_000_000_000, bytes_accessed=0, transcendentals=0),
        name=name,
    )(*partials, *lines)


def exact(left, right, dims):
    return lax.dot_general(
        left, right, (dims, ((), ())), precision=lax.Precision.HIGHEST, preferred_element_type=FULL
    )


def joint_pattern():
    keys, queries = np.meshgrid(np.arange(CHUNK), np.arange(CHUNK), indexing="ij")
    at = (queries // SW - keys // SW + SW - 1) * SPAN_T + queries % SW - keys % SW + SW - 1
    return (jnp.arange(SPAN_T**2)[:, None] == jnp.asarray(at.reshape(-1), jnp.int32)[None, :]).astype(FULL)


def joint_table(lookup):
    flat = lookup.reshape(HEADS * (2 * TW - 1), SPAN_T**2)
    grid = exact(flat, joint_pattern(), ((1,), (0,)))
    grid = grid.reshape(HEADS // 2, 2, 2 * TW - 1, CHUNK, CHUNK)
    return jnp.concatenate([grid[:, 0], grid[:, 1]], axis=-1)


def joint_table_back(grad):
    pairs = jnp.stack([grad[..., :CHUNK], grad[..., CHUNK:]], axis=1)
    flat = pairs.reshape(HEADS * (2 * TW - 1), CHUNK * CHUNK)
    return exact(flat, joint_pattern(), ((1,), (1,))).reshape(HEADS, -1)


def space_pattern(quarter):
    query = jnp.arange(CHUNK)
    key_col = jnp.arange(2 * SW)
    gap = quarter % 2 * SW + (query % SW)[None, :] - key_col[:, None] + 2 * SW - 1
    row = jnp.broadcast_to((query // SW)[None, :], gap.shape)
    at = (row * SPAN_S + gap).reshape(-1)
    return (jnp.arange(SW * SPAN_S)[:, None] == at[None, :]).astype(FULL)


def space_table(lookup, quarter):
    grid = lookup.reshape(HEADS, SPAN_S, SPAN_S)
    seen = lax.dynamic_slice_in_dim(grid, quarter // 2 * SW, 3 * SW - 1, 1)
    rows = jnp.stack([seen[:, 2 * SW - 1 - k : 3 * SW - 1 - k] for k in range(2 * SW)])
    made = exact(rows.reshape(2 * SW * HEADS, SW * SPAN_S), space_pattern(quarter), ((1,), (0,)))
    made = made.reshape(2, SW, HEADS // 2, 2, 2, SW, CHUNK)
    made = made.transpose(2, 0, 4, 1, 5, 3, 6)
    return made.reshape(HEADS // 2, 4 * CHUNK, 2 * CHUNK)


def space_table_back(grad, quarter):
    made = grad.reshape(HEADS // 2, 2, 2, SW, SW, 2, CHUNK).transpose(1, 3, 0, 5, 2, 4, 6)
    flat = made.reshape(2 * SW * HEADS, 2 * SW * CHUNK)
    rows = exact(flat, space_pattern(quarter), ((1,), (1,))).reshape(2 * SW, HEADS, SW, SPAN_S)
    seen = sum(
        jnp.pad(rows[k], ((0, 0), (2 * SW - 1 - k, k), (0, 0))) for k in range(2 * SW)
    )
    grid = jnp.zeros((HEADS, SPAN_S, SPAN_S), FULL)
    return lax.dynamic_update_slice_in_dim(grid, seen, quarter // 2 * SW, 1).reshape(HEADS, -1)


def modulations(cond, shards):
    groups = cond.shape[0]
    rows = shards[0].shape[0]
    own = lax.dynamic_slice_in_dim(cond, lax.axis_index("wide") * rows, rows, 2)
    flat = own.reshape(groups * 2, rows)
    terms = jnp.stack([nn(flat, s).reshape(groups, 2, -1) for s in shards], axis=1)
    summed = lax.psum_scatter(terms, "wide", scatter_dimension=0, tiled=False)
    gathered = lax.all_gather(summed, "narrow", axis=0, tiled=False)
    return gathered.transpose(1, 2, 0, 3).reshape(2, 2, 6 * D)


def modulation_grads(cond, grads, rows):
    groups = cond.shape[0]
    own = lax.dynamic_slice_in_dim(cond, lax.axis_index("wide") * rows, rows, 2)
    flat = own.reshape(groups * 2, rows).astype(FULL)
    summed = lax.psum_scatter(
        grads.reshape(2, 2, 4, -1), "narrow", scatter_dimension=2, tiled=False
    )
    gathered = lax.all_gather(summed, "wide", axis=0, tiled=False)
    return [exact(flat, gathered[:, b].reshape(groups * 2, -1), ((0,), (0,))) for b in range(2)]


def gather_flat(shards):
    wide, narrow = lax.axis_size("wide"), lax.axis_size("narrow")
    project, output, expand, shrink = shards
    rows = project.shape[0]

    def settle(blocks):
        rows, cols = blocks.shape[-2:]
        blocks = blocks.reshape(wide, narrow, rows, cols).transpose(0, 2, 1, 3)
        return blocks.reshape(wide * rows, narrow * cols)

    first = lax.all_gather(
        jnp.concatenate([project, output, expand], axis=1), ("wide", "narrow"), axis=0, tiled=False
    )
    second = lax.all_gather(shrink, ("wide", "narrow"), axis=0, tiled=False)
    a, b = project.shape[1], project.shape[1] + output.shape[1]
    return settle(first[..., :a]), settle(first[..., a:b]), settle(first[..., b:]), settle(second)


def scatter_plain(partials):
    outs = []
    for g in partials:
        summed = lax.psum_scatter(g, "wide", scatter_dimension=0, tiled=True)
        outs.append(lax.psum_scatter(summed, "narrow", scatter_dimension=1, tiled=True).astype(FULL))
    return outs


def body(
    tokens,
    clip_cond,
    image_cond,
    image_count,
    space_modulate,
    space_project,
    space_output,
    space_expand,
    space_reduce,
    space_bias,
    joint_modulate,
    joint_project,
    joint_output,
    joint_expand,
    joint_reduce,
    joint_bias,
    cotangent,
):
    groups = lax.axis_size("wide")
    small = groups == 8
    narrow = lax.axis_index("narrow")
    quarter = narrow.reshape(1).astype(jnp.int32)
    live = (image_count > 0).astype(FULL)

    image_all = lax.all_gather(image_cond, "wide", axis=0, tiled=True)
    cond = jax.nn.silu(
        jnp.stack([jnp.repeat(clip_cond, 4, axis=0), image_all], axis=1).astype(FULL)
    ).astype(LOW)
    mods = modulations(cond, (space_modulate, joint_modulate))
    space_shards = (space_project, space_output, space_expand, space_reduce)
    joint_shards = (joint_project, joint_output, joint_expand, joint_reduce)
    if small:
        *space_weights, all_tokens = gather_weights(space_shards, tokens, 0, "space_gather")
        joint_weights = gather_weights(joint_shards, None, 3, "joint_gather")
    else:
        joint_weights = gather_flat(joint_shards)
        space_weights = gather_flat(space_shards)
        all_tokens = lax.all_gather(tokens, "narrow", axis=0, tiled=False)
    all_tokens = all_tokens.reshape(4 * ROWS_DEV, D)
    space_bias_table = space_table(space_bias, narrow)
    joint_bias_table = joint_table(joint_bias)

    project, output, expand, shrink = space_weights
    space_normed, space_queries, space_pairs = space_triple(quarter, all_tokens, mods[0], project)
    space_attended = space_attend(space_queries, space_pairs, space_bias_table)
    *space_saved, middle_rows = mlp(
        False, live, tokens, space_attended, mods[0], output, expand, shrink
    )

    project, output, expand, shrink = joint_weights
    joint_normed, joint_three = joint_triple(middle_rows, mods[1], project)
    joint_attended = joint_attend(joint_three, joint_bias_table)
    *joint_saved, output_tokens = mlp(
        True, live, middle_rows, joint_attended, mods[1], output, expand, shrink
    )

    grad_shrink, grad_expand, grad_output, grad_middle, grad_attended, late_mods = mlp_back(
        True, live, cotangent, joint_attended, mods[1], joint_saved, output, expand, shrink
    )
    grad_three, grad_table = joint_attend_back(joint_three, joint_bias_table, grad_attended)
    grad_project, grad_rows, early_mods = joint_project_back(
        middle_rows, mods[1], joint_normed, grad_middle, project, grad_three
    )
    joint_partials = (grad_shrink, grad_expand, grad_project, grad_output)
    joint_mods = jnp.concatenate([early_mods, late_mods[:, 2 * D :]], axis=1)
    joint_bias_grad = joint_table_back(grad_table)

    project, output, expand, shrink = space_weights
    grad_shrink, grad_expand, grad_output, grad_middle, grad_attended, late_mods = mlp_back(
        False, live, grad_rows, space_attended, mods[0], space_saved, output, expand, shrink
    )
    grad_q, grad_pairs, grad_table = space_attend_back(
        space_queries, space_pairs, space_bias_table, grad_attended
    )
    grad_project, grad_normed = space_project_back(quarter, space_normed, project, grad_q, grad_pairs)
    space_partials = (grad_shrink, grad_expand, grad_project, grad_output)
    space_bias_grad = space_table_back(grad_table, narrow)

    if small:
        joint_local = scatter_grads(joint_partials, None, 1, "joint_scatter")
        *space_local, own_normed = scatter_grads(space_partials, grad_normed, 2, "space_scatter")
    else:
        joint_local = scatter_plain(joint_partials)
        space_local = scatter_plain(space_partials)
        own_normed = lax.psum_scatter(grad_normed, "narrow", scatter_dimension=0, tiled=True)
    grad_tokens, early_mods = finish(tokens, mods[0], own_normed, grad_middle)
    space_mods = jnp.concatenate([early_mods, late_mods[:, 2 * D :]], axis=1)
    grad_space_modulate, grad_joint_modulate = modulation_grads(
        cond, jnp.stack([space_mods, joint_mods]), space_modulate.shape[0]
    )
    bias_grads = lax.psum(
        jnp.concatenate([space_bias_grad, joint_bias_grad], axis=1), ("wide", "narrow")
    )
    split = space_bias.shape[1]
    return (
        output_tokens,
        grad_tokens,
        grad_space_modulate,
        space_local[2],
        space_local[3],
        space_local[1],
        space_local[0],
        bias_grads[:, :split],
        grad_joint_modulate,
        joint_local[2],
        joint_local[3],
        joint_local[1],
        joint_local[0],
        bias_grads[:, split:],
    )


def solution(mesh):
    rows = P(("wide", "narrow"), None)
    block = P("wide", "narrow")
    in_specs = (
        (rows, P(), P("wide", None), P("wide"))
        + (block,) * 5
        + (P(),)
        + (block,) * 5
        + (P(), rows)
    )
    out_specs = (rows, rows) + ((block,) * 5 + (P(),)) * 2
    return jax.shard_map(body, mesh=mesh, in_specs=in_specs, out_specs=out_specs, check_vma=False)
```

```python
import functools
import math

import jax
import jax.numpy as jnp
import numpy as np
from jax import lax
from jax.experimental import pallas as pl
from jax.experimental.pallas import tpu as pltpu
from jax.sharding import PartitionSpec as P

D = 1024
HEADS = 16
HEAD_DIM = 64
FF = 4096
SW = 8
TW = 5
CHUNK = SW * SW
CLIP_ROWS = TW * CHUNK
ROWS_DEV = CLIP_ROWS + 4 * CHUNK
SPAN_S = 4 * SW - 1
SPAN_T = 2 * SW - 1
MESH = pl.DeviceIdType.MESH


epsilon = 1e-06


def normalise(values):
    centred = values - jnp.mean(values, axis=-1, keepdims=True)
    spread = jnp.mean(centred * centred, axis=-1, keepdims=True)
    scale = lax.rsqrt(spread + epsilon)
    return centred * scale, scale


def norm_back(unit, scale, grad):
    return scale * (
        grad
        - jnp.mean(grad, axis=-1, keepdims=True)
        - unit * jnp.mean(grad * unit, axis=-1, keepdims=True)
    )


def nn(left, right):
    return lax.dot_general(left, right, (((1,), (0,)), ((), ())), preferred_element_type=jnp.float32)


def nt(left, right):
    return lax.dot_general(left, right, (((1,), (1,)), ((), ())), preferred_element_type=jnp.float32)


def tn(left, right):
    return lax.dot_general(left, right, (((0,), (0,)), ((), ())), preferred_element_type=jnp.float32)


def each_chunk(body, count=ROWS_DEV // CHUNK):
    @pl.loop(0, count)
    def _(i):
        inner = lax.rem(i, ROWS_DEV // CHUNK)
        seq = jnp.where(inner >= CLIP_ROWS // CHUNK, 1, 0)
        body(pl.ds(pl.multiple_of(i * CHUNK, CHUNK), CHUNK), pl.ds(seq, 1))


def part(index):
    return slice(index * D, (index + 1) * D)


class Tiled:
    def __init__(self, block, index):
        self.block, self.index = block, index

    def spec(self):
        return pl.BlockSpec(self.block, self.index)


class Whole:
    def __init__(self, block):
        self.block = block

    def spec(self):
        rank = len(self.block)
        return pl.BlockSpec(self.block, lambda *_: (0,) * rank, pipeline_mode=pl.Buffered(1))


class Scalars:
    def spec(self):
        return pl.BlockSpec(memory_space=pltpu.SMEM)


SCALARS = Scalars()
whole, spec = Whole, Tiled


def params(limit=56):
    return pltpu.CompilerParams(vmem_limit_bytes=limit * 2**20)


def shape(dims, kind):
    return jax.ShapeDtypeStruct(dims, kind)


LOW = jnp.bfloat16
FULL = jnp.float32


class Phase:
    def __init__(self, kernel, *, grid, in_specs, out_specs, out_shape, name, ticks=1, scratch_shapes=()):
        self.kernel, self.grid, self.name, self.ticks = kernel, grid, name, ticks
        self.in_specs, self.out_specs, self.out_shape = in_specs, out_specs, out_shape
        self.scratch = list(scratch_shapes)

    def __call__(self, *args):
        return pl.pallas_call(
            functools.partial(self.kernel, lambda t: None),
            grid=self.grid,
            in_specs=[s.spec() for s in self.in_specs],
            out_specs=[s.spec() for s in self.out_specs],
            out_shape=self.out_shape,
            scratch_shapes=self.scratch,
            compiler_params=params(),
            name=self.name,
        )(*args)

    def inside(self, tick, ins, outs):
        specs = list(self.in_specs) + list(self.out_specs)
        refs = list(ins) + list(outs)
        first_out = len(ins)
        held = [i for i, s in enumerate(specs) if isinstance(s, Whole)]
        tiled = [i for i, s in enumerate(specs) if isinstance(s, Tiled)]

        def scoped(buffers, scratch, sems):
            place = dict(zip(held, buffers))
            loads = [
                pltpu.make_async_copy(refs[i], place[i], sems.at[at])
                for at, i in enumerate(held)
                if i < first_out
            ]
            for load in loads:
                load.start()
            for load in loads:
                load.wait()

            def body(*blocks):
                now = dict(zip(tiled, blocks))
                now.update(place)
                operands = [now.get(i, refs[i]) for i in range(len(refs))]
                self.kernel(tick, *operands, *scratch)

            pltpu.emit_pipeline(
                body,
                grid=self.grid,
                in_specs=[specs[i].spec() for i in tiled if i < first_out],
                out_specs=[specs[i].spec() for i in tiled if i >= first_out],
            )(*[refs[i] for i in tiled])
            stores = [
                pltpu.make_async_copy(place[i], refs[i], sems.at[at])
                for at, i in enumerate(held)
                if i >= first_out
            ]
            for store in stores:
                store.start()
            for store in stores:
                store.wait()

        kinds = [refs[i].dtype for i in held]
        pl.run_scoped(
            scoped,
            [pltpu.VMEM(specs[i].block, kind) for i, kind in zip(held, kinds)],
            self.scratch,
            pltpu.SemaphoreType.DMA((len(held),)),
        )


def space_triple_kernel(tick, rows, mods, weight, normed, queries, pairs):
    step = pl.program_id(0)

    @pl.when(step == 0)
    def _():
        def chunk(at, seq):
            unit, _ = normalise(rows[at, :].astype(FULL))
            normed[at, :] = (unit * (1.0 + mods[seq, part(1)]) + mods[seq, part(0)]).astype(LOW)

        each_chunk(chunk, 4 * ROWS_DEV // CHUNK)

    tick(0)

    @pl.when(step < 2)
    def _():
        own = span(lax.axis_index("narrow"), ROWS_DEV)
        queries[...] = nn(normed[own, :], weight[...]).astype(LOW)

    for q in range(4):
        if q:
            tick(q)

        @pl.when(step >= 2)
        def _():
            pairs[q] = nn(normed[q * ROWS_DEV : (q + 1) * ROWS_DEV, :], weight[...]).astype(LOW)


def space_triple():
    tile = 512
    return Phase(
        space_triple_kernel,
        grid=(3 * D // tile,),
        in_specs=[
            whole((4 * ROWS_DEV, D)),
            whole((2, 6 * D)),
            spec((D, tile), lambda t: (0, t)),
        ],
        out_specs=[
            whole((4 * ROWS_DEV, D)),
            spec((ROWS_DEV, tile), lambda t: (0, jnp.minimum(t, 1))),
            spec((4, ROWS_DEV, tile), lambda t: (0, 0, jnp.maximum(t - 2, 0))),
        ],
        out_shape=[
            shape((4 * ROWS_DEV, D), LOW),
            shape((ROWS_DEV, D), LOW),
            shape((4, ROWS_DEV, 2 * D), LOW),
        ],
        name="space_triple",
        ticks=4,
    )


def joint_triple_kernel(tick, rows, mods, weight, normed, triple):
    @pl.when(pl.program_id(0) == 0)
    def _():
        def chunk(at, seq):
            unit, _ = normalise(rows[at, :])
            normed[at, :] = (unit * (1.0 + mods[seq, part(1)]) + mods[seq, part(0)]).astype(LOW)

        each_chunk(chunk)

    tick(0)
    triple[...] = nn(normed[...], weight[...]).astype(LOW)


def joint_triple():
    tile = 512
    return Phase(
        joint_triple_kernel,
        grid=(3 * D // tile,),
        in_specs=[whole((ROWS_DEV, D)), whole((2, 6 * D)), spec((D, tile), lambda t: (0, t))],
        out_specs=[whole((ROWS_DEV, D)), spec((ROWS_DEV, tile), lambda t: (0, t))],
        out_shape=[shape((ROWS_DEV, D), LOW), shape((ROWS_DEV, 3 * D), LOW)],
        name="joint_triple",
        ticks=1,
    )


def half_mask():
    return lax.broadcasted_iota(jnp.int32, (1, 2 * HEAD_DIM), 1) < HEAD_DIM


def split_heads(rows):
    first = half_mask()
    zero = jnp.zeros_like(rows)
    return jnp.concatenate([jnp.where(first, rows, zero), jnp.where(first, zero, rows)], axis=0)


def join_heads(stacked):
    return jnp.where(half_mask(), stacked[:CHUNK], stacked[CHUNK:])


def softmax_keys(keys, queries, bias):
    scores = nt(keys, queries) * HEAD_DIM**-0.5 + bias
    powered = jnp.exp(scores - jnp.max(scores, axis=0, keepdims=True))
    return powered / jnp.sum(powered, axis=0, keepdims=True)


def attend(queries, keys, values, bias):
    probs = softmax_keys(keys, split_heads(queries), bias)
    return join_heads(tn(values, probs.astype(LOW)).T).astype(LOW)


def attend_back(queries, keys, values, bias, grad):
    queries, grad = split_heads(queries), split_heads(grad)
    probs = softmax_keys(keys, queries, bias)
    grad_values = nn(probs.astype(LOW), grad)
    grad_probs = nt(values, grad)
    centre = jnp.sum(probs * grad_probs, axis=0, keepdims=True)
    grad_scores = (probs * (grad_probs - centre)).astype(LOW)
    grad_queries = join_heads(tn(keys, grad_scores).T) * HEAD_DIM**-0.5
    grad_keys = nn(grad_scores, queries) * HEAD_DIM**-0.5
    return grad_queries, grad_keys, grad_values, grad_scores.astype(FULL)


def space_attend_kernel(tick, queries, keys, values, bias, out):
    table = bias[0]
    for i in range(ROWS_DEV // CHUNK):
        if i % 3 == 0:
            tick(i // 3)
        at = slice(i * CHUNK, (i + 1) * CHUNK)
        key_rows = keys[:, at, :].reshape(4 * CHUNK, 2 * HEAD_DIM)
        value_rows = values[:, at, :].reshape(4 * CHUNK, 2 * HEAD_DIM)
        out[at, :] = attend(queries[at, :], key_rows, value_rows, table)


def space_attend():
    wide = 2 * HEAD_DIM
    return Phase(
        space_attend_kernel,
        grid=(HEADS // 2,),
        in_specs=[
            spec((ROWS_DEV, wide), lambda h: (0, h)),
            spec((4, ROWS_DEV, wide), lambda h: (0, 0, h)),
            spec((4, ROWS_DEV, wide), lambda h: (0, 0, h + HEADS // 2)),
            spec((1, 4 * CHUNK, wide), lambda h: (h, 0, 0)),
        ],
        out_specs=[spec((ROWS_DEV, wide), lambda h: (0, h))],
        out_shape=[shape((ROWS_DEV, D), LOW)],
        name="space_attend",
        ticks=3,
    )


def space_attend_back_kernel(tick, queries, keys, values, bias, grad, grad_q, grad_pairs, grad_bias):
    table = bias[0]
    for i in range(ROWS_DEV // CHUNK):
        if i % 3 == 0:
            tick(i // 3)
        at = slice(i * CHUNK, (i + 1) * CHUNK)
        key_rows = keys[:, at, :].reshape(4 * CHUNK, 2 * HEAD_DIM)
        value_rows = values[:, at, :].reshape(4 * CHUNK, 2 * HEAD_DIM)
        to_q, to_k, to_v, to_bias = attend_back(
            queries[at, :], key_rows, value_rows, table, grad[at, :]
        )
        grad_q[at, :] = to_q.astype(LOW)
        grad_pairs[0, :, at, :] = to_k.astype(LOW).reshape(4, CHUNK, 2 * HEAD_DIM)
        grad_pairs[1, :, at, :] = to_v.astype(LOW).reshape(4, CHUNK, 2 * HEAD_DIM)
        if i == 0:
            grad_bias[0] = to_bias
        else:
            grad_bias[0] += to_bias


def space_attend_back():
    wide = 2 * HEAD_DIM
    head = spec((ROWS_DEV, wide), lambda h: (0, h))
    four = spec((4, ROWS_DEV, wide), lambda h: (0, 0, h))
    table = spec((1, 4 * CHUNK, wide), lambda h: (h, 0, 0))
    return Phase(
        space_attend_back_kernel,
        grid=(HEADS // 2,),
        in_specs=[
            head,
            four,
            spec((4, ROWS_DEV, wide), lambda h: (0, 0, h + HEADS // 2)),
            table,
            head,
        ],
        out_specs=[head, spec((2, 4, ROWS_DEV, wide), lambda h: (0, 0, 0, h)), table],
        out_shape=[
            shape((ROWS_DEV, D), LOW),
            shape((2, 4, ROWS_DEV, D), LOW),
            shape((HEADS // 2, 4 * CHUNK, wide), FULL),
        ],
        name="space_attend_back",
        ticks=3,
    )


def clip_table(bias, frame):
    return jnp.concatenate([bias[0, frame - t + TW - 1] for t in range(TW)], axis=0)


def joint_attend_kernel(tick, queries, keys, values, bias, out):
    for i in range(ROWS_DEV // CHUNK):
        if i % 3 == 0:
            tick(i // 3)
        at = slice(i * CHUNK, (i + 1) * CHUNK)
        seen = slice(0, CLIP_ROWS) if i < TW else at
        table = clip_table(bias, i) if i < TW else bias[0, TW - 1]
        out[at, :] = attend(queries[at, :], keys[seen, :], values[seen, :], table)


def joint_specs():
    wide = 2 * HEAD_DIM
    return [
        spec((ROWS_DEV, wide), lambda h: (0, h)),
        spec((ROWS_DEV, wide), lambda h: (0, h + HEADS // 2)),
        spec((ROWS_DEV, wide), lambda h: (0, h + HEADS)),
        spec((1, 2 * TW - 1, CHUNK, wide), lambda h: (h, 0, 0, 0)),
    ]


def joint_attend():
    return Phase(
        joint_attend_kernel,
        grid=(HEADS // 2,),
        in_specs=joint_specs(),
        out_specs=[spec((ROWS_DEV, 2 * HEAD_DIM), lambda h: (0, h))],
        out_shape=[shape((ROWS_DEV, D), LOW)],
        name="joint_attend",
        ticks=3,
    )


def joint_attend_back_kernel(
    tick, queries, keys, values, bias, grad, grads, grad_bias, sum_k, sum_v
):
    grad_bias[...] = jnp.zeros_like(grad_bias)
    for i in range(ROWS_DEV // CHUNK):
        if i % 3 == 0:
            tick(i // 3)
        at = slice(i * CHUNK, (i + 1) * CHUNK)
        seen = slice(0, CLIP_ROWS) if i < TW else at
        table = clip_table(bias, i) if i < TW else bias[0, TW - 1]
        to_q, to_k, to_v, to_bias = attend_back(
            queries[at, :], keys[seen, :], values[seen, :], table, grad[at, :]
        )
        grads[0, at, :] = to_q.astype(LOW)
        if i >= TW:
            grad_bias[0, TW - 1] += to_bias
            grads[1, at, :] = to_k.astype(LOW)
            grads[2, at, :] = to_v.astype(LOW)
            continue
        for t in range(TW):
            grad_bias[0, i - t + TW - 1] += to_bias[t * CHUNK : (t + 1) * CHUNK]
        if i == 0:
            sum_k[...] = to_k
            sum_v[...] = to_v
        elif i < TW - 1:
            sum_k[...] += to_k
            sum_v[...] += to_v
        else:
            grads[1, seen, :] = (sum_k[...] + to_k).astype(LOW)
            grads[2, seen, :] = (sum_v[...] + to_v).astype(LOW)


def joint_attend_back():
    wide = 2 * HEAD_DIM
    head = spec((ROWS_DEV, wide), lambda h: (0, h))
    return Phase(
        joint_attend_back_kernel,
        grid=(HEADS // 2,),
        in_specs=joint_specs() + [head],
        out_specs=[spec((3, ROWS_DEV, wide), lambda h: (0, 0, h)), joint_specs()[3]],
        out_shape=[
            shape((3, ROWS_DEV, D), LOW),
            shape((HEADS // 2, 2 * TW - 1, CHUNK, wide), FULL),
        ],
        scratch_shapes=[pltpu.VMEM((CLIP_ROWS, wide), FULL)] * 2,
        name="joint_attend_back",
        ticks=3,
    )


def mlp_kernel(last_block, tick, live, rows, attended, mods, output, expand, shrink, *refs):
    branch, middle, normed, active, slope, reduced, result, total = refs
    step = pl.program_id(0)

    @pl.when(step == 0)
    def _():
        def chunk(at, seq):
            grown = nn(attended[at, :], output[...])
            branch[at, :] = grown.astype(LOW)
            mixed = rows[at, :].astype(FULL) + mods[seq, part(2)] * grown
            middle[at, :] = mixed
            unit, _ = normalise(mixed)
            normed[at, :] = (unit * (1.0 + mods[seq, part(4)]) + mods[seq, part(3)]).astype(LOW)

        each_chunk(chunk)
        total[...] = jnp.zeros_like(total)

    tick(0)
    before = nn(normed[...], expand[...])
    inner = 0.5 * (1.0 + lax.erf(before * 0.5**0.5))
    low_active = (before * inner).astype(LOW)
    tick(1)
    active[...] = low_active
    slope[...] = (inner + before * jnp.exp(-0.5 * before * before) * (2.0 * math.pi) ** -0.5).astype(LOW)
    total[...] += nn(low_active, shrink[...])

    @pl.when(step == pl.num_programs(0) - 1)
    def _():
        def chunk(at, seq):
            reduced[at, :] = total[at, :].astype(LOW)
            value = middle[at, :] + mods[seq, part(5)] * total[at, :]
            if last_block:
                value = value * jnp.where(seq.start > 0, live[0], 1.0)
            result[at, :] = value.astype(result.dtype)

        each_chunk(chunk)


def mlp(last_block):
    tile = 512
    square = whole((ROWS_DEV, D))
    strip = spec((ROWS_DEV, tile), lambda f: (0, f))
    return Phase(
        functools.partial(mlp_kernel, last_block),
        grid=(FF // tile,),
        in_specs=[
            SCALARS,
            square,
            square,
            whole((2, 6 * D)),
            whole((D, D)),
            spec((D, tile), lambda f: (0, f)),
            spec((tile, D), lambda f: (f, 0)),
        ],
        out_specs=[square, square, square, strip, strip, square, square],
        out_shape=[
            shape((ROWS_DEV, D), LOW),
            shape((ROWS_DEV, D), FULL),
            shape((ROWS_DEV, D), LOW),
            shape((ROWS_DEV, FF), LOW),
            shape((ROWS_DEV, FF), LOW),
            shape((ROWS_DEV, D), LOW),
            shape((ROWS_DEV, D), LOW if last_block else FULL),
        ],
        scratch_shapes=[pltpu.VMEM((ROWS_DEV, D), FULL)],
        name="mlp",
        ticks=2,
    )


def mlp_back_kernel(first_block, tick, live, *refs):
    (grad_result, attended, mods, branch, middle, normed, reduced, output, active, slope) = refs[:10]
    expand, shrink = refs[10:12]
    grad_shrink, grad_expand, grad_output, grad_middle, grad_attended, grad_mods = refs[12:18]
    grad_reduced, normed_t, total = refs[18:]
    grad_branch = grad_reduced
    step = pl.program_id(0)

    def incoming(at, seq):
        value = grad_result[at, :].astype(FULL)
        if first_block:
            value = value * jnp.where(seq.start > 0, live[0], 1.0)
        return value

    @pl.when(step == 0)
    def _():
        grad_mods[...] = jnp.zeros_like(grad_mods)

        def chunk(at, seq):
            value = incoming(at, seq)
            grad_reduced[at, :] = (mods[seq, part(5)] * value).astype(LOW)
            grad_mods[seq, part(5)] += jnp.sum(
                reduced[at, :].astype(FULL) * value, axis=0, keepdims=True
            )

        each_chunk(chunk)
        total[...] = jnp.zeros_like(total)
        normed_t[...] = normed[...].T

    tick(0)
    grad_active = nt(grad_reduced[...], shrink[...])
    grad_before = (grad_active * slope[...].astype(FULL)).astype(LOW)
    tick(1)
    grad_shrink[...] = tn(active[...], grad_reduced[...]).astype(LOW)
    tick(2)
    grad_expand[...] = nn(normed_t[...], grad_before).astype(LOW)
    tick(3)
    total[...] += nt(grad_before, expand[...])

    @pl.when(step == pl.num_programs(0) - 1)
    def _():
        def chunk(at, seq):
            grad = total[at, :]
            unit, scale = normalise(middle[at, :])
            grad_mods[seq, part(3)] += jnp.sum(grad, axis=0, keepdims=True)
            grad_mods[seq, part(4)] += jnp.sum(unit * grad, axis=0, keepdims=True)
            value = incoming(at, seq) + norm_back(unit, scale, (1.0 + mods[seq, part(4)]) * grad)
            grad_middle[at, :] = value
            grad_mods[seq, part(2)] += jnp.sum(
                branch[at, :].astype(FULL) * value, axis=0, keepdims=True
            )
            grad_branch[at, :] = (mods[seq, part(2)] * value).astype(LOW)

        each_chunk(chunk)
        grad_attended[...] = nt(grad_branch[...], output[...]).astype(LOW)
        grad_output[...] = tn(attended[...], grad_branch[...]).astype(LOW)


def mlp_back(first_block):
    tile = 512
    square = whole((ROWS_DEV, D))
    strip = spec((ROWS_DEV, tile), lambda f: (0, f))
    across = spec((D, tile), lambda f: (0, f))
    down = spec((tile, D), lambda f: (f, 0))
    return Phase(
        functools.partial(mlp_back_kernel, first_block),
        grid=(FF // tile,),
        in_specs=[
            SCALARS,
            square,
            square,
            whole((2, 6 * D)),
            square,
            square,
            square,
            square,
            whole((D, D)),
            strip,
            strip,
            across,
            down,
        ],
        out_specs=[down, across, whole((D, D)), square, square, whole((2, 6 * D))],
        out_shape=[
            shape((FF, D), LOW),
            shape((D, FF), LOW),
            shape((D, D), LOW),
            shape((ROWS_DEV, D), FULL),
            shape((ROWS_DEV, D), LOW),
            shape((2, 6 * D), FULL),
        ],
        scratch_shapes=[
            pltpu.VMEM((ROWS_DEV, D), LOW),
            pltpu.VMEM((D, ROWS_DEV), LOW),
            pltpu.VMEM((ROWS_DEV, D), FULL),
        ],
        name="mlp_back",
        ticks=4,
    )


def finish_rows(rows, grad_normed, grad_middle, mods, grad_rows, grad_mods):
    grad_mods[...] = jnp.zeros_like(grad_mods)

    def chunk(at, seq):
        grad = grad_normed[at, :].astype(FULL)
        unit, scale = normalise(rows[at, :].astype(FULL))
        grad_mods[seq, part(0)] += jnp.sum(grad, axis=0, keepdims=True)
        grad_mods[seq, part(1)] += jnp.sum(unit * grad, axis=0, keepdims=True)
        grad_rows[at, :] = grad_middle[at, :] + norm_back(
            unit, scale, (1.0 + mods[seq, part(1)]) * grad
        )

    each_chunk(chunk)


def joint_project_back_kernel(
    tick, rows, mods, normed, grad_middle, weight, grad, grad_weight, grad_rows, grad_mods, total, normed_t
):
    step = pl.program_id(0)

    @pl.when(step == 0)
    def _():
        total[...] = jnp.zeros_like(total)
        normed_t[...] = normed[...].T

    tick(0)
    grad_weight[...] = nn(normed_t[...], grad[0]).astype(LOW)
    tick(1)
    total[...] += nt(grad[0], weight[...])

    @pl.when(step == pl.num_programs(0) - 1)
    def _():
        finish_rows(rows, total, grad_middle, mods, grad_rows, grad_mods)


def joint_project_back():
    tile = 512
    square = whole((ROWS_DEV, D))
    across = spec((D, tile), lambda t: (0, t))
    return Phase(
        joint_project_back_kernel,
        grid=(3 * D // tile,),
        in_specs=[square, whole((2, 6 * D)), square, square, across, spec((1, ROWS_DEV, tile), lambda t: (t // 2, 0, t % 2))],
        out_specs=[across, square, whole((2, 2 * D))],
        out_shape=[shape((D, 3 * D), LOW), shape((ROWS_DEV, D), FULL), shape((2, 2 * D), FULL)],
        scratch_shapes=[pltpu.VMEM((ROWS_DEV, D), FULL), pltpu.VMEM((D, ROWS_DEV), LOW)],
        name="joint_project_back",
        ticks=2,
    )


def space_project_back_kernel(tick, normed, weight, grad_q, grad_pairs, grad_weight, grad_normed, total):
    step = pl.program_id(0)
    own = span(lax.axis_index("narrow"), ROWS_DEV)

    @pl.when(step == 0)
    def _():
        total[...] = jnp.zeros_like(total)

    tick(0)

    @pl.when(step < 2)
    def _():
        grad_weight[...] = tn(normed[own, :], grad_q[...]).astype(LOW)
        total[own, :] += nt(grad_q[...], weight[...])

    @pl.when(step >= 2)
    def _():
        flat = grad_pairs[0].reshape(4 * ROWS_DEV, grad_pairs.shape[-1])
        grad_weight[...] = tn(normed[...], flat).astype(LOW)

    for q in range(4):
        tick(q + 1)

        @pl.when(step >= 2)
        def _():
            at = slice(q * ROWS_DEV, (q + 1) * ROWS_DEV)
            total[at, :] += nt(grad_pairs[0, q], weight[...])

    @pl.when(step == pl.num_programs(0) - 1)
    def _():
        grad_normed[...] = total[...].astype(LOW)


def space_project_back():
    tile = 512
    across = spec((D, tile), lambda t: (0, t))

    def pair(t):
        late = jnp.maximum(t - 2, 0)
        return (late // 2, 0, 0, late % 2)

    return Phase(
        space_project_back_kernel,
        grid=(3 * D // tile,),
        in_specs=[
            whole((4 * ROWS_DEV, D)),
            across,
            spec((ROWS_DEV, tile), lambda t: (0, jnp.minimum(t, 1))),
            spec((1, 4, ROWS_DEV, tile), pair),
        ],
        out_specs=[across, whole((4 * ROWS_DEV, D))],
        out_shape=[shape((D, 3 * D), LOW), shape((4 * ROWS_DEV, D), LOW)],
        scratch_shapes=[pltpu.VMEM((4 * ROWS_DEV, D), FULL)],
        name="space_project_back",
        ticks=5,
    )


def finish_kernel(tick, rows, mods, grad_normed, grad_middle, grad_rows, grad_mods):
    tick(0)
    finish_rows(rows, grad_normed, grad_middle, mods, grad_rows, grad_mods)


def finish():
    square = whole((ROWS_DEV, D))
    return Phase(
        finish_kernel,
        grid=(1,),
        in_specs=[square, whole((2, 6 * D)), square, square],
        out_specs=[square, whole((2, 2 * D))],
        out_shape=[shape((ROWS_DEV, D), FULL), shape((2, 2 * D), FULL)],
        name="finish",
    )


class Place:
    def __init__(self):
        self.w = lax.axis_index("wide")
        self.n = lax.axis_index("narrow")
        self.c = lax.bitwise_xor(self.w, 1)
        self.x = lax.bitwise_xor(self.w, 2)
        self.y = lax.bitwise_xor(self.w, 4)
        self.d = lax.bitwise_xor(self.w, 6)
        self.up = jnp.minimum(self.n + 1, 3)
        self.down = jnp.maximum(self.n - 1, 0)
        self.order = (
            self.n,
            lax.bitwise_xor(self.n, 1),
            jnp.where(self.n < 2, 2, 1),
            jnp.where(self.n < 2, 3, 0),
        )

    def enter(self):
        barrier = pltpu.get_barrier_semaphore()
        for peer in (self.x, self.y, self.c):
            pl.semaphore_signal(barrier, inc=1, device_id=(peer, self.n), device_id_type=MESH)

        @pl.when(self.n > 0)
        def _():
            pl.semaphore_signal(barrier, inc=1, device_id=(self.w, self.n - 1), device_id_type=MESH)

        @pl.when(self.n < 3)
        def _():
            pl.semaphore_signal(barrier, inc=1, device_id=(self.w, self.n + 1), device_id_type=MESH)

        ends = jnp.where(self.n > 0, 1, 0) + jnp.where(self.n < 3, 1, 0)
        pl.semaphore_wait(barrier, 3 + ends)

    def enter_all(self):
        barrier = pltpu.get_barrier_semaphore()
        for step in range(1, 8):
            peer = (lax.bitwise_xor(self.w, step), self.n)
            pl.semaphore_signal(barrier, inc=1, device_id=peer, device_id_type=MESH)
        for step in range(1, 4):
            peer = (self.w, lax.bitwise_xor(self.n, step))
            pl.semaphore_signal(barrier, inc=1, device_id=peer, device_id_type=MESH)
        pl.semaphore_wait(barrier, 10)

    def passes_on(self, col):
        return jnp.logical_or(
            jnp.logical_and(col < self.n, self.n < 3), jnp.logical_and(col > self.n, self.n > 0)
        )

    def carried(self, col):
        return jnp.logical_or(
            jnp.logical_and(col > self.n, self.n > 0), jnp.logical_and(col < self.n, self.n < 3)
        )


def remote(src, dst, send, recv, to):
    return pltpu.make_async_remote_copy(
        src_ref=src, dst_ref=dst, send_sem=send, recv_sem=recv, device_id=to, device_id_type=MESH
    )


def span(index, size):
    return pl.ds(pl.multiple_of(index * size, size), size)


DMA = pltpu.SemaphoreType.DMA
FOLDS = [(3, 1), (3, 3), (3, 0), (3, 2)]
FOLDS += [(2, 3), (1, 3), (2, 2), (1, 2), (1, 1), (2, 1), (1, 0), (2, 0)]
FOLDS += [(0, 3), (0, 2), (0, 1), (0, 0)]
LOADS = 2
PIECES = 4
PIECE = ROWS_DEV // PIECES


class Names:
    def __init__(self, owner):
        self.owner = owner

    def __getattr__(self, name):
        return self.owner, name


A, S, J = Names(0), Names(1), Names(2)


class Feed:
    def __init__(self, enter):
        self.enter, self.steps, self.drains = enter, [], []
        self.late_enter = lambda: None

    def add(self, function, *args):
        self.steps.append(functools.partial(function, *args))

    def drain(self, function, *args):
        self.drains.append(functools.partial(function, *args))

    def follow(self, tables):
        self.lists = []
        for table in tables:
            parts = [[]]
            for number in table:
                if number < 0:
                    parts.append([])
                else:
                    parts[-1].append(self.steps[number])
            self.lists.append(parts)
        self.slot = 0
        self.at_end = jnp.logical_or(Place().n == 0, Place().n == 3)

    def do(self, slot):
        ends, middles = (parts[slot] for parts in self.lists)

        @pl.when(self.at_end)
        def _():
            for step in ends:
                step()

        @pl.when(jnp.logical_not(self.at_end))
        def _():
            for step in middles:
                step()

    def over(self, phase):
        first, total = self.slot, phase.grid[0]
        self.do(first)
        self.slot += total * phase.ticks

        def tick(t):
            for i in range(total):
                slot = first + i * phase.ticks + t
                if slot > first and any(parts[slot] for parts in self.lists):

                    @pl.when(pl.program_id(0) == i)
                    def _():
                        self.do(slot)

        return tick

    def rest(self):
        self.do(self.slot)
        for step in self.drains:
            step()


class Gather:
    def __init__(self, shapes, line, collective_id):
        self.shapes, self.line, self.collective_id = shapes, line, collective_id
        count, lines = len(shapes), 1 if line else 0
        self.in_specs = [pl.BlockSpec(memory_space=pl.ANY)] * (count + lines)
        self.out_specs = self.in_specs
        self.out_shape = [shape((8 * r, 4 * c), LOW) for r, c in shapes]
        self.out_shape += [shape((4 * ROWS_DEV, D), LOW)] * lines
        self.scratch = [
            DMA((count, 5)),
            DMA((count, 4)),
            DMA((count, 2, 4)),
            DMA((count, 2, 4)),
            DMA((count, 2, 4)),
            DMA((count, 2, 4)),
            DMA((count, 4, 4)),
            DMA((count, 4, 4)),
            DMA((count,)),
        ]
        self.scratch += [DMA((PIECES, 5)), DMA((PIECES, 4)), DMA((PIECES,))] * lines

    def steps(self, ins, outs, scratch):
        at = Place()
        shapes, count = self.shapes, len(self.shapes)
        w, n = at.w, at.n
        shards, fulls = ins[:count], outs[:count]
        z_send, z_recv, x_send, x_recv, y_send, y_recv, c_send, c_recv, own_sem = scratch[:9]

        def block(k, row, col):
            rows, cols = shapes[k]
            return fulls[k].at[span(row, rows), span(col, cols)]

        def z_copy(k, src, col, slot, to):
            return remote(src, block(k, w, col), z_send.at[k, slot], z_recv.at[k, col], (w, to))

        def x_copy(k, src, row, far, col):
            sems = x_send.at[k, far, col], x_recv.at[k, far, col]
            return remote(src, block(k, row, col), *sems, (at.x, n))

        def y_copy(k, src, row, far, col):
            sems = y_send.at[k, far, col], y_recv.at[k, far, col]
            return remote(src, block(k, row, col), *sems, (at.y, n))

        def c_copy(k, src, row, chip, col):
            sems = c_send.at[k, chip, col], c_recv.at[k, chip, col]
            return remote(src, block(k, row, col), *sems, (at.c, n))

        def own_copy(k):
            return pltpu.make_async_copy(shards[k], block(k, w, n), own_sem.at[k])

        def own(k):
            @pl.when(n < 3)
            def _():
                z_copy(k, shards[k], n, n, at.up).start()

            @pl.when(n > 0)
            def _():
                z_copy(k, shards[k], n, 4, at.down).start()

            x_copy(k, shards[k], w, 0, n).start()
            y_copy(k, shards[k], w, 0, n).start()
            c_copy(k, shards[k], w, 0, n).start()
            own_copy(k).start()

        def z_stage(k, j):
            col = at.order[j]
            here = block(k, w, col)
            z_copy(k, here, col, col, at.up).wait_recv()

            @pl.when(at.passes_on(col))
            def _():
                z_copy(k, here, col, col, jnp.where(col < n, at.up, at.down)).start()

            x_copy(k, here, w, 0, col).start()
            y_copy(k, here, w, 0, col).start()
            c_copy(k, here, w, 0, col).start()

        def near_stage(k, j):
            col = at.order[j]
            from_x = block(k, at.x, col)
            from_y = block(k, at.y, col)
            x_copy(k, from_x, at.x, 0, col).wait_recv()
            if j < 2:
                y_copy(k, from_x, at.x, 1, col).start()
            c_copy(k, from_x, at.x, 1, col).start()
            y_copy(k, from_y, at.y, 0, col).wait_recv()
            if j >= 2:
                x_copy(k, from_y, at.y, 1, col).start()
            c_copy(k, from_y, at.y, 2, col).start()

        def far_stage(k, j):
            col = at.order[j]
            far = block(k, at.d, col)
            (y_copy if j < 2 else x_copy)(k, far, at.d, 1, col).wait_recv()
            c_copy(k, far, at.d, 3, col).start()

        def ready(k):
            own_copy(k).wait()
            for col in range(4):
                for chip in range(4):
                    c_copy(k, block(k, w, col), w, chip, col).wait_recv()

        def drain(k):
            for j in range(4):
                col = at.order[j]
                here = block(k, w, col)

                @pl.when(at.passes_on(col) if j else n < 3)
                def _():
                    z_copy(k, here, col, col, at.up).wait_send()

                x_copy(k, here, w, 0, col).wait_send()
                y_copy(k, here, w, 0, col).wait_send()
                (y_copy if j < 2 else x_copy)(k, here, w, 1, col).wait_send()
                for chip in range(4):
                    c_copy(k, here, w, chip, col).wait_send()

            @pl.when(n > 0)
            def _():
                z_copy(k, shards[k], n, 4, at.down).wait_send()

        if self.line:
            rows, all_rows = ins[count], outs[count]
            t_send, t_recv, t_own = scratch[9:]

            def piece(p, col):
                return all_rows.at[pl.ds(pl.multiple_of(col * ROWS_DEV + p * PIECE, 16), PIECE)]

            def t_copy(p, src, col, slot, to):
                dst = piece(p, col)
                return remote(src, dst, t_send.at[p, slot], t_recv.at[p, col], (w, to))

            def t_own_copy(p):
                here = pl.ds(p * PIECE, PIECE)
                return pltpu.make_async_copy(rows.at[here], piece(p, n), t_own.at[p])

            def t_start(p, late):
                src = rows.at[pl.ds(p * PIECE, PIECE)]
                if not late:
                    t_own_copy(p).start()

                @pl.when(n == 2 if late else n < 2)
                def _():
                    t_copy(p, src, n, n, at.up).start()

                @pl.when(n == 1 if late else n >= 2)
                def _():
                    t_copy(p, src, n, 4, at.down).start()

            def t_stage(p, j):
                col = at.order[j]
                here = piece(p, col)
                t_copy(p, here, col, col, at.up).wait_recv()

                @pl.when(at.passes_on(col))
                def _():
                    t_copy(p, here, col, col, jnp.where(col < n, at.up, at.down)).start()

            def t_drain(p):
                for j in range(4):
                    col = at.order[j]
                    here = piece(p, col)

                    @pl.when(at.passes_on(col) if j else n < 3)
                    def _():
                        t_copy(p, here, col, col, at.up).wait_send()

                @pl.when(n > 0)
                def _():
                    t_copy(p, piece(p, n), n, 4, at.down).wait_send()

            def t_ready():
                for p in range(PIECES):
                    t_own_copy(p).wait()

        items = Feed(at.enter)
        for k in range(count):
            items.add(own, k)
            for j in range(1, 4):
                items.add(z_stage, k, j)
            for j in range(4):
                items.add(near_stage, k, j)
            for j in range(4):
                items.add(far_stage, k, j)
            items.add(ready, k)
            items.drain(drain, k)
        if self.line:
            for p in range(PIECES):
                items.add(t_start, p, False)
                items.add(t_start, p, True)
                for j in range(1, 4):
                    items.add(t_stage, p, j)
                items.drain(t_drain, p)
            items.add(t_ready)
        return items


class Scatter:
    def __init__(self, shapes, line, collective_id):
        self.shapes, self.line, self.collective_id = shapes, line, collective_id
        count, lines = len(shapes), 1 if line else 0
        self.in_specs = [pl.BlockSpec(memory_space=pl.ANY)] * (count + lines)
        self.out_shape = [shape(s, FULL) for s in shapes] + [shape((ROWS_DEV, D), FULL)] * lines
        self.out_specs = [pl.BlockSpec(memory_space=pltpu.VMEM)] * len(self.out_shape)
        self.scratch = []
        for s in shapes:
            self.scratch += [
                pltpu.VMEM((4, 4) + s, LOW),
                pltpu.VMEM((4,) + s, LOW),
                pltpu.VMEM((2, 4) + s, LOW),
                pltpu.VMEM((5,) + s, LOW),
                pltpu.VMEM((LOADS,) + s, LOW),
            ]
        self.scratch += [
            DMA((count, 4, 4)),
            DMA((count, 4, 4)),
            DMA((count, 4, 4)),
            DMA((count, 4)),
            DMA((count, 4)),
            DMA((count, 2, 4)),
            DMA((count, 2, 4)),
            DMA((count, 4)),
            DMA((count, 5)),
        ]
        self.scratch += [
            pltpu.VMEM((PIECES, 4, PIECE, D), LOW),
            pltpu.VMEM((PIECES, 5, PIECE, D), LOW),
            DMA((PIECES, 4)),
            DMA((PIECES, 4)),
            DMA((PIECES, 5)),
        ] * lines

    def steps(self, ins, outs, scratch):
        at = Place()
        shapes, count = self.shapes, len(self.shapes)
        w, n, order = at.w, at.n, at.order
        chips = (w, at.x, at.y, at.d)
        held, far_in, near_in, z_in, staged = (scratch[i : 5 * count : 5] for i in range(5))
        load, c_send, c_recv, d_send, d_recv, n_send, n_recv, z_send, z_recv = scratch[
            5 * count : 5 * count + 9
        ]

        def source(k, row, col):
            rows, cols = shapes[k]
            return ins[k].at[span(row, rows), span(col, cols)]

        def load_copy(k, chip, j):
            slot = FOLDS.index((chip, j)) % LOADS
            return pltpu.make_async_copy(
                source(k, chips[chip], order[j]), staged[k].at[slot], load.at[k, chip, j]
            )

        def c_copy(k, chip, col):
            src = source(k, lax.bitwise_xor(chips[chip], 1), col)
            sems = c_send.at[k, chip, col], c_recv.at[k, chip, col]
            return remote(src, held[k].at[chip, col], *sems, (at.c, n))

        def d_copy(k, j):
            sems = d_send.at[k, j], d_recv.at[k, j]
            to = (at.x if j < 2 else at.y, n)
            return remote(held[k].at[3, order[j]], far_in[k].at[j], *sems, to)

        def n_copy(k, chip, col):
            sems = n_send.at[k, chip - 1, col], n_recv.at[k, chip - 1, col]
            dst = near_in[k].at[chip - 1, col]
            return remote(held[k].at[chip, col], dst, *sems, (chips[chip], n))

        def z_copy(k, col, slot, to):
            sems = z_send.at[k, col], z_recv.at[k, slot]
            return remote(held[k].at[0, col], z_in[k].at[slot], *sems, (w, to))

        def add(target, rows, *others):
            step = 64 if rows % 64 == 0 else 48

            @pl.loop(0, rows // step)
            def _(i):
                here = span(i, step)
                total = target[here, :]
                for other in others:
                    total = total + other[here, :]
                target[here, :] = total

        def fold(k, chip, j, *others):
            number = FOLDS.index((chip, j))
            load_copy(k, chip, j).wait()
            c_copy(k, chip, order[j]).wait_recv()
            add(held[k].at[chip, order[j]], shapes[k][0], staged[k].at[number % LOADS], *others)
            if number + LOADS < len(FOLDS):
                load_copy(k, *FOLDS[number + LOADS]).start()

        def begin(k):
            for chip, j in FOLDS:
                c_copy(k, chip, order[j]).start()
            for chip, j in FOLDS[:LOADS]:
                load_copy(k, chip, j).start()

        def far(k, j):
            fold(k, 3, j)
            d_copy(k, j).start()

        def near(k, j):
            chip = 2 if j >= 2 else 1
            fold(k, chip, j)
            n_copy(k, chip, order[j]).start()

        def near_far(k, j):
            chip = 1 if j >= 2 else 2
            d_copy(k, j).wait_recv()
            fold(k, chip, j, far_in[k].at[j])
            n_copy(k, chip, order[j]).start()

        def line_slot(col):
            to = jnp.where(col > n, at.up, at.down)
            return jnp.where(jnp.logical_and(col < n, to == col), 4, col), to

        def fold_near(k, j):
            col = order[j]
            n_copy(k, 1, col).wait_recv()
            n_copy(k, 2, col).wait_recv()
            fold(k, 0, j, near_in[k].at[0, col], near_in[k].at[1, col])

        def along(k, j):
            col = order[j]
            fold_near(k, j)

            @pl.when(at.carried(col))
            def _():
                z_copy(k, col, col, at.up).wait_recv()
                add(held[k].at[0, col], shapes[k][0], z_in[k].at[col])

            slot, to = line_slot(col)
            z_copy(k, col, slot, to).start()

        def last(k):
            fold_near(k, 0)
            outs[k][...] = held[k][0, n].astype(FULL)

            @pl.when(n > 0)
            def _():
                z_copy(k, n, n, at.up).wait_recv()
                outs[k][...] += z_in[k][n].astype(FULL)

            @pl.when(n < 3)
            def _():
                z_copy(k, n, 4, at.up).wait_recv()
                outs[k][...] += z_in[k][4].astype(FULL)

        def drain(k):
            for chip in range(4):
                for col in range(4):
                    c_copy(k, chip, col).wait_send()
            for j in range(4):
                d_copy(k, j).wait_send()
                n_copy(k, 1, j).wait_send()
                n_copy(k, 2, j).wait_send()
            for j in range(1, 4):
                z_copy(k, order[j], order[j], at.up).wait_send()

        if self.line:
            line_held, line_in, line_load, line_send, line_recv = scratch[5 * count + 9 :]

            def line_loads(p, col):
                here = pl.ds(pl.multiple_of(col * ROWS_DEV + p * PIECE, 16), PIECE)
                return pltpu.make_async_copy(
                    ins[count].at[here], line_held.at[p, col], line_load.at[p, col]
                )

            def line_copy(p, col, slot, to):
                sems = line_send.at[p, col], line_recv.at[p, slot]
                return remote(line_held.at[p, col], line_in.at[p, slot], *sems, (w, to))

            def line_begin():
                for j in (3, 2, 1, 0):
                    for p in range(PIECES):
                        line_loads(p, order[j]).start()

            def line_stage(j, p):
                col = order[j]
                line_loads(p, col).wait()

                @pl.when(at.carried(col))
                def _():
                    line_copy(p, col, col, at.up).wait_recv()
                    add(line_held.at[p, col], PIECE, line_in.at[p, col])

                slot, to = line_slot(col)
                line_copy(p, col, slot, to).start()

            def line_last(p):
                here = pl.ds(p * PIECE, PIECE)
                line_loads(p, n).wait()
                outs[count][here, :] = line_held[p, n].astype(FULL)

                @pl.when(n > 0)
                def _():
                    line_copy(p, n, n, at.up).wait_recv()
                    outs[count][here, :] += line_in[p, n].astype(FULL)

                @pl.when(n < 3)
                def _():
                    line_copy(p, n, 4, at.up).wait_recv()
                    outs[count][here, :] += line_in[p, 4].astype(FULL)

            def line_drain():
                for p in range(PIECES):
                    for j in range(1, 4):
                        line_copy(p, order[j], order[j], at.up).wait_send()

        items = Feed(at.enter)
        for k in range(count):
            items.add(begin, k)
            for j in (1, 3, 0, 2):
                items.add(far, k, j)
            for j in (3, 2, 1, 0):
                items.add(near, k, j)
                items.add(near_far, k, j)
            for j in (3, 2, 1):
                items.add(along, k, j)
            items.add(last, k)
            items.drain(drain, k)
        if self.line:
            for j in (3, 2, 1):
                for p in range(PIECES):
                    items.add(line_stage, j, p)
            for p in range(PIECES):
                items.add(line_last, p)
            items.add(lambda: None)
            items.drain(line_drain)
            items.enter = lambda: (at.enter(), line_begin())
            items.late_enter = line_begin
        return items


def fused(script, args, outs, engine, moved, name):
    in_specs = [SCALARS.spec() if k == A.live else pl.BlockSpec(memory_space=pl.ANY) for k in args]
    counts = [len(args), len(outs), len(engine.out_specs)]

    def kernel(*refs):
        groups = []
        for count in counts:
            groups.append(refs[:count])
            refs = refs[count:]
        named = dict(zip(list(args) + list(outs), groups[0] + groups[1]))
        feed = engine.steps([named[k] for k in moved], groups[2], refs)
        script(named, groups[2], feed)

    results = pl.pallas_call(
        kernel,
        in_specs=in_specs,
        out_specs=[pl.BlockSpec(memory_space=pl.ANY)] * len(outs) + engine.out_specs,
        out_shape=list(outs.values()) + engine.out_shape,
        scratch_shapes=engine.scratch,
        compiler_params=pltpu.CompilerParams(
            collective_id=engine.collective_id, has_side_effects=True, vmem_limit_bytes=62 * 2**20
        ),
        cost_estimate=pl.CostEstimate(flops=100_000_000_000, bytes_accessed=0, transcendentals=0),
        name=name,
    )(*args.values())
    return dict(zip(outs, results)), list(results[len(outs) :])


class Joined:
    def __init__(self, engine, other):
        self.engine, self.other = engine, other
        self.collective_id = engine.collective_id
        self.out_specs = engine.out_specs + other.out_specs
        self.out_shape = engine.out_shape + other.out_shape
        self.scratch = engine.scratch + other.scratch

    def steps(self, ins, outs, scratch):
        cuts = len(ins) - self.other.takes, len(self.engine.out_specs), len(self.engine.scratch)
        feed = self.engine.steps(ins[: cuts[0]], outs[: cuts[1]], scratch[: cuts[2]])
        for step in self.other.steps(ins[cuts[0] :], outs[cuts[1] :], scratch[cuts[2] :]):
            feed.add(step)
        begin = feed.late_enter

        def enter():
            Place().enter_all()
            begin()

        feed.enter = enter
        return feed


STRIP = 768


def strips(b, q):
    return b * 2 + q


class Modulation:
    takes = 4

    def __init__(self):
        self.out_shape = [shape((2, 6 * D), FULL)] * 2 + [shape((16, 128), FULL)]
        self.out_specs = [pl.BlockSpec(memory_space=pl.ANY)] * 2
        self.out_specs += [pl.BlockSpec(memory_space=pltpu.VMEM)]
        self.scratch = [
            pltpu.VMEM((8, 8, 128), FULL),
            pltpu.VMEM((8, 128), FULL),
            pltpu.VMEM((2, 128, 2 * STRIP), LOW),
            pltpu.VMEM((8, 8, STRIP), FULL),
            pltpu.VMEM((8, 8, STRIP), FULL),
            pltpu.VMEM((4, 8, STRIP), FULL),
            pltpu.VMEM((2, 2, 6 * D), FULL),
            DMA((3, 8)),
            DMA((3, 8)),
            DMA((6,)),
        ]

    def steps(self, ins, outs, scratch):
        at = Place()
        w, n = at.w, at.n
        images, clips, *shards = ins
        cond, clip, held, terms, arrived, got, made, send, recv, local = scratch

        def across(stage, step, src, dst):
            to = (lax.bitwise_xor(w, step), n)
            return remote(src, dst, send.at[stage, step], recv.at[stage, step], to)

        def first(step):
            return across(0, step, images.at[lax.bitwise_xor(w, step)], cond.at[w])

        def second(step):
            return across(1, step, terms.at[lax.bitwise_xor(w, step)], arrived.at[w])

        def third(step):
            to = (w, lax.bitwise_xor(n, step))
            return remote(got.at[n], got.at[n], send.at[2, step], recv.at[2, step], to)

        def loads():
            return [
                pltpu.make_async_copy(images.at[w], cond.at[w], local.at[0]),
                pltpu.make_async_copy(clips, clip, local.at[1]),
                pltpu.make_async_copy(shards[0], held.at[0], local.at[2]),
                pltpu.make_async_copy(shards[1], held.at[1], local.at[3]),
            ]

        def stores():
            return [
                pltpu.make_async_copy(made.at[b], outs[b], local.at[4 + b]) for b in range(2)
            ]

        def start():
            for copy in loads():
                copy.start()
            for step in range(1, 8):
                first(step).start()

        def project():
            for copy in loads():
                copy.wait()
            for step in range(1, 8):
                first(step).wait_recv()
            flat = jnp.concatenate([cond[:, 0, :], clip[...]], axis=0).astype(LOW)
            outs[2][8:16, :] = cond[:, 0, :]
            for g in range(8):
                outs[2][g : g + 1, :] = clip[g // 4 : g // 4 + 1, :]
            for b in range(2):
                product = nn(flat, held[b])
                for g in range(8):
                    for r, row in enumerate((8 + g // 4, g)):
                        for q in range(2):
                            to = r * 4 + strips(b, q)
                            terms[g, to : to + 1, :] = product[row : row + 1, q * STRIP : (q + 1) * STRIP]
            for step in range(1, 8):
                second(step).start()

        def total():
            value = terms[w]
            for step in range(1, 8):
                second(step).wait_recv()
                value = value + arrived[lax.bitwise_xor(w, step)]
            got[n] = value
            for step in range(1, 4):
                third(step).start()

        def spread():
            for step in range(1, 4):
                third(step).wait_recv()
            for col in range(4):
                for b in range(2):
                    for r in range(2):
                        for q in range(2):
                            here = r * 4 + strips(b, q)
                            to = col * 2 * STRIP + q * STRIP
                            made[b, r : r + 1, to : to + STRIP] = got[col, here : here + 1, :]
            for copy in stores():
                copy.start()

        def settle():
            for copy in stores():
                copy.wait()
            for step in range(1, 8):
                first(step).wait_send()
                second(step).wait_send()
            for step in range(1, 4):
                third(step).wait_send()

        return start, project, total, spread, settle


class ModulationBack:
    takes = 0

    def __init__(self):
        self.out_shape = [shape((128, 2 * STRIP), FULL)] * 2
        self.out_specs = [pl.BlockSpec(memory_space=pltpu.VMEM)] * 2
        self.scratch = [
            pltpu.VMEM((4, 8, STRIP), FULL),
            pltpu.VMEM((4, 8, STRIP), FULL),
            pltpu.VMEM((8, 8, STRIP), FULL),
            pltpu.VMEM((2, 2, 6 * D), FULL),
            pltpu.VMEM((16, 128), FULL),
            DMA((2, 8)),
            DMA((2, 8)),
            DMA((5,)),
        ]

    def steps(self, ins, outs, scratch):
        at = Place()
        w, n = at.w, at.n
        pieces, arrived, every, grads, cond, send, recv, local = scratch

        def along(step):
            to = (w, lax.bitwise_xor(n, step))
            src = pieces.at[lax.bitwise_xor(n, step)]
            return remote(src, arrived.at[n], send.at[0, step], recv.at[0, step], to)

        def across(step):
            to = (lax.bitwise_xor(w, step), n)
            return remote(every.at[w], every.at[w], send.at[1, step], recv.at[1, step], to)

        def finish(cond_ref, early, late):
            copies = [pltpu.make_async_copy(cond_ref, cond, local.at[4])]
            for b in range(2):
                cut = pl.ds(2 * D, 4 * D)
                here = grads.at[b, :, pl.ds(0, 2 * D)]
                copies.append(pltpu.make_async_copy(early[b], here, local.at[2 * b]))
                here = grads.at[b, :, cut]
                copies.append(pltpu.make_async_copy(late[b].at[:, cut], here, local.at[2 * b + 1]))
            for copy in copies:
                copy.start()
            for copy in copies:
                copy.wait()
            for col in range(4):
                for b in range(2):
                    for r in range(2):
                        for q in range(2):
                            to = r * 4 + strips(b, q)
                            here = col * 2 * STRIP + q * STRIP
                            pieces[col, to : to + 1, :] = grads[b, r : r + 1, here : here + STRIP]
            for step in range(1, 4):
                along(step).start()
            value = pieces[n]
            for step in range(1, 4):
                along(step).wait_recv()
                value = value + arrived[lax.bitwise_xor(n, step)]
            every[w] = value
            for step in range(1, 8):
                across(step).start()
            for step in range(1, 8):
                across(step).wait_recv()
            for b in range(2):
                for q in range(2):
                    rows = [every[:, r * 4 + strips(b, q), :] for r in range(2)]
                    outs[b][:, q * STRIP : (q + 1) * STRIP] = lax.dot_general(
                        cond[...],
                        jnp.concatenate(rows, axis=0),
                        (((0,), (0,)), ((), ())),
                        precision=lax.Precision.HIGHEST,
                        preferred_element_type=FULL,
                    )
            for step in range(1, 4):
                along(step).wait_send()
            for step in range(1, 8):
                across(step).wait_send()

        self.finish = finish
        return ()


FORWARD_ENDS = (
    0, 13, 125, 1, 4, 104, 109, 114, 119, 14, 17, 5, 2, 26, 126, 8, 18, 27, 21, 15, 39, 127, 9, 3,
    6, 40, 30, 22, 107, 31, 28, 19, 16, 128, 10, 43, 112, 7, 108, 44, 23, 41, 65, 66, 34, 11, 12,
    35, 117, 32, 122, 52, 20, 53, 36, 47, 113, 24, 48, 25, 118, 45, 69, 70, 123, 49, 56, 57, 29,
    105, 110, 115, 120, 129, 73, 74, 106, 60, 61, 111, 33, 116, 37, 121, 124, -1, 38, 67, 91, -1,
    -1, 71, 92, -1, -1, -1, -1, -1, 95, 42, 75, -1, -1, -1, 54, 78, -1, 96, -1, -1, -1, 79, -1, 99,
    68, -1, -1, -1, 55, -1, 46, -1, -1, -1, 58, 93, -1, -1, -1, -1, -1, -1, -1, -1, 82, 80, -1, -1,
    -1, -1, -1, -1, -1, -1, -1, -1, 100, 94, -1, -1, -1, -1, -1, -1, -1, 83, 81, 50, 72, 51, -1,
    62, 59, -1, -1, 97, -1, -1, -1, 86, -1, -1, -1, 84, -1, -1, -1, 98, -1, 76, -1, 77, -1, 63, 87,
    -1, 64, -1, 101, 85, -1, -1, 88, -1, -1, -1, 102, -1, -1, 103, -1, -1, -1, -1, 89, -1, -1, -1,
    90, -1, -1, -1, -1, -1, -1, -1, -1, -1, -1, -1, -1, -1, -1, -1, -1, -1, -1, -1, -1, -1, -1, -1,
    -1, -1, -1, -1, -1, -1, -1, -1,
)
FORWARD_MIDDLES = (
    0, 13, 125, 1, 2, 4, 104, 26, 126, 14, 15, 109, 17, 3, 5, 106, 39, 127, 6, 114, 107, 119, 8,
    111, 28, 16, 128, 30, 116, 18, 19, 21, 112, 121, 7, 108, 10, 9, 27, 41, 65, 43, 40, 23, 117,
    32, 11, 20, 12, 122, 52, 34, 22, 113, 66, 31, 118, 45, 69, 123, 36, 124, 24, 47, 25, 53, 29,
    105, 129, 110, 115, 120, 67, 44, 91, -1, 56, -1, 42, 49, 70, -1, -1, -1, 54, 78, 68, 35, -1,
    73, -1, -1, 55, -1, 57, -1, -1, -1, -1, 93, -1, 33, -1, 71, -1, -1, 80, -1, -1, 48, -1, -1, -1,
    -1, -1, 95, -1, -1, -1, -1, -1, -1, 60, -1, -1, -1, -1, -1, -1, -1, -1, -1, -1, -1, 46, -1, -1,
    74, -1, -1, -1, -1, -1, 58, 37, 75, 82, 38, 92, 72, 59, 94, 61, 50, 51, -1, 79, 62, 97, -1, -1,
    84, -1, 76, 81, -1, 77, 63, 99, -1, 64, -1, -1, 86, -1, -1, -1, 96, -1, -1, -1, 101, 98, -1,
    -1, -1, 88, 83, -1, -1, 85, -1, -1, 102, 100, -1, 103, -1, -1, -1, -1, 89, 87, -1, -1, -1, 90,
    -1, -1, -1, -1, -1, -1, -1, -1, -1, -1, -1, -1, -1, -1, -1, -1, -1, -1, -1, -1, -1, -1, -1, -1,
    -1, -1, -1, -1, -1, -1, -1, -1, -1,
)
BACK_JOINT_ENDS = (
    -1, -1, -1, -1, -1, -1, -1, -1, -1, -1, -1, -1, -1, -1, -1, -1, -1, -1, -1, -1, -1, -1, -1, -1,
    -1, -1, -1, -1, -1, -1, -1, -1, 0, -1, 1, 2, 3, 4, 5, 17, -1, 18, -1, 19, 6, 20, 7, 21, 22, 34,
    8, 35, 9, 36, 10, 37, 11, 38, 12, 39, -1, -1, -1, -1, -1, -1, -1, 13, 23, 24, -1, -1, -1, -1,
    -1, -1, -1, -1, -1, 14, 25, 26, 27, 28, 29, -1, -1, -1, -1, -1, 40, 41, -1, -1, 15, -1, 42, 43,
    44, 45, 46, -1, -1, 30, -1, 16, -1, -1, -1, 31, -1, -1, -1, 51, 32, 52, 53, 54, 55, -1, 56, 47,
    48, 49, -1, 33, -1, -1, -1, 57, 58, -1, -1, -1, 50, 59, 60, 61, 62, 63, -1, -1, 64, -1, -1, -1,
    65, -1, -1, -1, 66, -1, -1, -1, -1, -1, -1, -1, -1, 67, -1, -1, -1, -1, -1, -1, -1, -1,
)
BACK_JOINT_MIDDLES = (
    -1, -1, -1, -1, -1, -1, -1, -1, -1, -1, -1, -1, -1, -1, -1, -1, -1, -1, -1, -1, -1, -1, -1, -1,
    -1, -1, -1, -1, -1, -1, -1, -1, 0, -1, 1, 2, 3, 4, 5, 17, -1, 18, -1, 19, 6, 20, 7, 21, 22, 34,
    8, 35, 9, 36, 10, 37, 11, 38, 12, 39, -1, -1, -1, -1, -1, -1, -1, 23, 24, -1, -1, -1, -1, -1,
    -1, 13, -1, -1, -1, 25, 26, 27, 28, 29, -1, -1, -1, -1, -1, 40, 14, 41, -1, -1, 15, 42, 43, 44,
    45, 46, -1, -1, -1, -1, 16, -1, -1, -1, -1, 30, -1, -1, 51, 31, 52, 32, 53, 54, 55, 56, -1, -1,
    -1, 33, 47, -1, 48, -1, 57, 49, 58, 50, -1, -1, 59, 60, 61, 62, 63, -1, -1, -1, -1, -1, -1, -1,
    -1, 64, -1, -1, -1, 65, -1, 66, -1, -1, -1, 67, -1, -1, -1, -1, -1, -1, -1, -1, -1, -1,
)
BACK_SPACE_ENDS = (
    0, -1, 1, 2, 3, 4, 5, -1, -1, -1, -1, -1, 6, 7, 17, -1, 18, 8, 19, 9, 20, 10, 21, 11, 22, 12,
    -1, -1, 13, -1, -1, -1, -1, -1, -1, -1, -1, -1, 14, 23, 24, 34, 35, 36, 15, 37, 38, 39, -1, -1,
    -1, -1, 25, 26, 27, 28, 29, -1, -1, -1, -1, -1, -1, 30, 16, -1, -1, -1, -1, -1, -1, -1, 40, 31,
    41, 42, 43, 44, 45, 46, -1, -1, -1, -1, -1, 32, -1, -1, -1, -1, -1, 47, -1, 48, -1, 33, 49, -1,
    -1, -1, -1, -1, -1, 50, -1,
)
BACK_SPACE_MIDDLES = (
    0, -1, 1, 2, 3, 4, 5, -1, -1, -1, -1, -1, 6, 7, 17, -1, 18, 8, 19, 9, 20, 10, 21, 11, 22, 12,
    -1, -1, -1, -1, -1, -1, -1, -1, 13, -1, -1, -1, 23, 24, 34, 35, 36, 37, 38, 39, -1, -1, 14, 15,
    -1, -1, 25, 26, 27, 28, 29, -1, -1, -1, -1, -1, -1, 16, -1, -1, -1, -1, -1, -1, -1, 30, 40, 41,
    42, 43, 44, 45, 46, -1, -1, -1, -1, -1, 31, 32, -1, -1, -1, -1, -1, -1, -1, 33, -1, 47, -1, 48,
    -1, 49, -1, 50, -1, -1, -1,
)
LAST_ENDS = (
    0, 17, 18, 19, 20, 21, 22, 23, 24, 25, 26, 27, 28, 1, 2, 3, 4, 5, 6, 7, 8, 9, 10, 11, 12, 13,
    29, 14, 30, 15, 31, 32, 33, -1, -1, 16,
)
LAST_MIDDLES = (
    0, 1, 2, 3, 4, 5, 6, 7, 17, 8, 9, 10, 11, 12, 18, 25, 19, 26, 20, 27, 21, 28, 22, 23, 24, 29,
    30, 31, 32, 33, -1, 13, -1, 14, 15, 16,
)


def exact(left, right, dims):
    return lax.dot_general(
        left, right, (dims, ((), ())), precision=lax.Precision.HIGHEST, preferred_element_type=FULL
    )


def joint_pattern():
    keys, queries = np.meshgrid(np.arange(CHUNK), np.arange(CHUNK), indexing="ij")
    at = (queries // SW - keys // SW + SW - 1) * SPAN_T + queries % SW - keys % SW + SW - 1
    return (jnp.arange(SPAN_T**2)[:, None] == jnp.asarray(at.reshape(-1), jnp.int32)[None, :]).astype(FULL)


def joint_table(lookup):
    flat = lookup.reshape(HEADS * (2 * TW - 1), SPAN_T**2)
    grid = exact(flat, joint_pattern(), ((1,), (0,)))
    grid = grid.reshape(HEADS // 2, 2, 2 * TW - 1, CHUNK, CHUNK)
    return jnp.concatenate([grid[:, 0], grid[:, 1]], axis=-1)


def joint_table_back(grad):
    pairs = jnp.stack([grad[..., :CHUNK], grad[..., CHUNK:]], axis=1)
    flat = pairs.reshape(HEADS * (2 * TW - 1), CHUNK * CHUNK)
    return exact(flat, joint_pattern(), ((1,), (1,))).reshape(HEADS, -1)


def space_pattern(quarter):
    query = jnp.arange(CHUNK)
    key_col = jnp.arange(2 * SW)
    gap = quarter % 2 * SW + (query % SW)[None, :] - key_col[:, None] + 2 * SW - 1
    row = jnp.broadcast_to((query // SW)[None, :], gap.shape)
    at = (row * SPAN_S + gap).reshape(-1)
    return (jnp.arange(SW * SPAN_S)[:, None] == at[None, :]).astype(FULL)


def space_table(lookup, quarter):
    grid = lookup.reshape(HEADS, SPAN_S, SPAN_S)
    seen = lax.dynamic_slice_in_dim(grid, quarter // 2 * SW, 3 * SW - 1, 1)
    rows = jnp.stack([seen[:, 2 * SW - 1 - k : 3 * SW - 1 - k] for k in range(2 * SW)])
    made = exact(rows.reshape(2 * SW * HEADS, SW * SPAN_S), space_pattern(quarter), ((1,), (0,)))
    made = made.reshape(2, SW, HEADS // 2, 2, 2, SW, CHUNK)
    made = made.transpose(2, 0, 4, 1, 5, 3, 6)
    return made.reshape(HEADS // 2, 4 * CHUNK, 2 * CHUNK)


def space_table_back(grad, quarter):
    made = grad.reshape(HEADS // 2, 2, 2, SW, SW, 2, CHUNK).transpose(1, 3, 0, 5, 2, 4, 6)
    flat = made.reshape(2 * SW * HEADS, 2 * SW * CHUNK)
    rows = exact(flat, space_pattern(quarter), ((1,), (1,))).reshape(2 * SW, HEADS, SW, SPAN_S)
    seen = sum(
        jnp.pad(rows[k], ((0, 0), (2 * SW - 1 - k, k), (0, 0))) for k in range(2 * SW)
    )
    grid = jnp.zeros((HEADS, SPAN_S, SPAN_S), FULL)
    return lax.dynamic_update_slice_in_dim(grid, seen, quarter // 2 * SW, 1).reshape(HEADS, -1)


def modulations(cond, shards):
    groups = cond.shape[0]
    rows = shards[0].shape[0]
    own = lax.dynamic_slice_in_dim(cond, lax.axis_index("wide") * rows, rows, 2)
    flat = own.reshape(groups * 2, rows)
    terms = jnp.stack([nn(flat, s).reshape(groups, 2, -1) for s in shards], axis=1)
    summed = lax.psum_scatter(terms, "wide", scatter_dimension=0, tiled=False)
    gathered = lax.all_gather(summed, "narrow", axis=0, tiled=False)
    return gathered.transpose(1, 2, 0, 3).reshape(2, 2, 6 * D)


def modulation_grads(cond, grads, rows):
    groups = cond.shape[0]
    own = lax.dynamic_slice_in_dim(cond, lax.axis_index("wide") * rows, rows, 2)
    flat = own.reshape(groups * 2, rows).astype(FULL)
    summed = lax.psum_scatter(
        grads.reshape(2, 2, 4, -1), "narrow", scatter_dimension=2, tiled=False
    )
    gathered = lax.all_gather(summed, "wide", axis=0, tiled=False)
    return [exact(flat, gathered[:, b].reshape(groups * 2, -1), ((0,), (0,))) for b in range(2)]


def gather_flat(shards):
    wide, narrow = lax.axis_size("wide"), lax.axis_size("narrow")
    project, output, expand, shrink = shards
    rows = project.shape[0]

    def settle(blocks):
        rows, cols = blocks.shape[-2:]
        blocks = blocks.reshape(wide, narrow, rows, cols).transpose(0, 2, 1, 3)
        return blocks.reshape(wide * rows, narrow * cols)

    first = lax.all_gather(
        jnp.concatenate([project, output, expand], axis=1), ("wide", "narrow"), axis=0, tiled=False
    )
    second = lax.all_gather(shrink, ("wide", "narrow"), axis=0, tiled=False)
    a, b = project.shape[1], project.shape[1] + output.shape[1]
    return settle(first[..., :a]), settle(first[..., a:b]), settle(first[..., b:]), settle(second)


def scatter_plain(partials):
    outs = []
    for g in partials:
        summed = lax.psum_scatter(g, "wide", scatter_dimension=0, tiled=True)
        outs.append(lax.psum_scatter(summed, "narrow", scatter_dimension=1, tiled=True).astype(FULL))
    return outs


def saved(b):
    return b.branch, b.middle, b.normed, b.active, b.slope, b.reduced


def mlp_takes(b):
    return A.live, b.rows, b.attended, b.mods, b.output, b.expand, b.shrink


def back_takes(b, grad):
    early = A.live, grad, b.attended, b.mods, b.branch, b.middle, b.normed, b.reduced
    return early + (b.output, b.active, b.slope, b.expand, b.shrink)


def back_gives(b):
    return b.to_shrink, b.to_expand, b.to_output, b.to_middle, b.to_attended, b.late


def weights_of(b):
    return b.project, b.output, b.expand, b.shrink


def shards_of(b):
    return b.own_project, b.own_output, b.own_expand, b.own_shrink


def partials_of(b):
    return b.to_shrink, b.to_expand, b.to_output, b.to_project


def grads_of(b):
    return b.grad_shrink, b.grad_expand, b.grad_output, b.grad_project


def stages():
    return {
        S.triple: (
            space_triple(),
            (A.all_rows, S.mods, S.project),
            (S.first, S.queries, S.pairs),
        ),
        S.attend: (
            space_attend(),
            (S.queries, S.pairs, S.pairs, S.table),
            (S.attended,),
        ),
        S.mlp: (
            mlp(False),
            mlp_takes(S),
            saved(S) + (J.rows,),
        ),
        J.triple: (
            joint_triple(),
            (J.rows, J.mods, J.project),
            (J.first, J.three),
        ),
        J.attend: (
            joint_attend(),
            (J.three,) * 3 + (J.table,),
            (J.attended,),
        ),
        J.mlp: (
            mlp(True),
            mlp_takes(J),
            saved(J) + (A.output_tokens,),
        ),
        J.mlp_back: (
            mlp_back(True),
            back_takes(J, A.cotangent),
            back_gives(J),
        ),
        J.attend_back: (
            joint_attend_back(),
            (J.three,) * 3 + (J.table, J.to_attended),
            (J.to_three, J.to_table),
        ),
        J.project_back: (
            joint_project_back(),
            (J.rows, J.mods, J.first, J.to_middle, J.project, J.to_three),
            (J.to_project, J.to_rows, J.early),
        ),
        S.mlp_back: (
            mlp_back(False),
            back_takes(S, J.to_rows),
            back_gives(S),
        ),
        S.attend_back: (
            space_attend_back(),
            (S.queries, S.pairs, S.pairs, S.table, S.to_attended),
            (S.to_queries, S.to_pairs, S.to_table),
        ),
        S.project_back: (
            space_project_back(),
            (S.first, S.project, S.to_queries, S.to_pairs),
            (S.to_project, A.to_first),
        ),
        A.finish: (
            finish(),
            (S.rows, S.mods, A.own_first, S.to_middle),
            (A.grad_tokens, S.early),
        ),
    }


def apart(values, names):
    for name in names:
        phase, takes, gives = stages()[name]
        values.update(zip(gives, phase(*[values[k] for k in takes])))


def together(values, plan, tables, engine, moved, brought, name, more=(), final=None):
    table = stages()
    outs, args = {}, {}
    for phase_name in plan:
        phase, takes, gives = table[phase_name]
        outs.update(zip(gives, phase.out_shape))
    for phase_name in plan:
        for k in table[phase_name][1]:
            if k not in outs and k not in brought:
                args[k] = values[k]
    for k in tuple(moved) + tuple(more):
        if k not in outs:
            args[k] = values[k]

    def script(refs, engine_outs, feed):
        refs.update(zip(brought, engine_outs))
        feed.follow(tables)
        feed.enter()
        for phase_name in plan:
            phase, takes, gives = table[phase_name]
            phase.inside(feed.over(phase), [refs[k] for k in takes], [refs[k] for k in gives])
        if final is not None:
            feed.do(feed.slot)
            feed.slot += 1
            final(refs)
        feed.rest()

    made, arrived = fused(script, args, outs, engine, moved, name)
    values.update(made)
    values.update(zip(brought, arrived))


def body(
    tokens,
    clip_cond,
    image_cond,
    image_count,
    space_modulate,
    space_project,
    space_output,
    space_expand,
    space_reduce,
    space_bias,
    joint_modulate,
    joint_project,
    joint_output,
    joint_expand,
    joint_reduce,
    joint_bias,
    cotangent,
):
    small = lax.axis_size("wide") == 8
    narrow = lax.axis_index("narrow")
    wide = lax.axis_index("wide")
    rows = space_modulate.shape[0]
    low_clips = jax.nn.silu(clip_cond.astype(FULL)).astype(LOW)
    low_images = jax.nn.silu(image_cond.astype(FULL)).astype(LOW)
    values = {
        A.live: (image_count > 0).astype(FULL),
        S.rows: tokens,
        A.cotangent: cotangent,
        S.table: space_table(space_bias, narrow),
        J.table: joint_table(joint_bias),
    }
    weights = weights_of(S) + weights_of(J)
    space_shards = space_project, space_output, space_expand, space_reduce
    joint_shards = joint_project, joint_output, joint_expand, joint_reduce

    if small:
        moved = shards_of(S) + shards_of(J)
        shapes = [v.shape for v in space_shards + joint_shards]
        values.update(zip(moved, space_shards + joint_shards))
        values[A.images] = jnp.broadcast_to(low_images.astype(FULL).reshape(8, 1, rows), (8, 8, rows))
        own_clips = lax.dynamic_slice_in_dim(low_clips, wide * rows, rows, 1).astype(FULL)
        values[A.clips] = jnp.pad(own_clips, ((0, 6), (0, 0)))
        values[S.own_modulate] = space_modulate
        values[J.own_modulate] = joint_modulate
        gather = Gather(shapes, True, 0)
        together(
            values,
            FORWARD,
            (FORWARD_ENDS, FORWARD_MIDDLES),
            Joined(gather, Modulation()),
            moved + (S.rows, A.images, A.clips, S.own_modulate, J.own_modulate),
            weights + (A.all_rows, S.mods, J.mods, A.cond),
            "forward",
        )
        project_shape, output_shape, expand_shape, shrink_shape = shapes[:4]
        shapes = [shrink_shape, expand_shape, output_shape, project_shape]
        engine = Scatter(shapes, False, 1)
        tables = BACK_JOINT_ENDS, BACK_JOINT_MIDDLES
        together(values, BACK_JOINT, tables, engine, partials_of(J), grads_of(J), "back_joint")
        engine = Scatter(shapes[:3], False, 2)
        tables = BACK_SPACE_ENDS, BACK_SPACE_MIDDLES
        takes, gives = partials_of(S)[:3], grads_of(S)[:3]
        together(values, BACK_SPACE, tables, engine, takes, gives, "back_space")
        back = ModulationBack()
        late = (A.cond, S.late, J.early, J.late)

        def final(refs):
            early = refs[S.early], refs[J.early]
            back.finish(refs[A.cond], early, (refs[S.late], refs[J.late]))

        together(
            values,
            LAST,
            (LAST_ENDS, LAST_MIDDLES),
            Joined(Scatter(shapes[3:], True, 3), back),
            (S.to_project, A.to_first),
            (S.grad_project, A.own_first, S.modulate, J.modulate),
            "last_sums",
            late,
            final,
        )
        modulate = values[S.modulate], values[J.modulate]
    else:
        image_all = lax.all_gather(low_images, "wide", axis=0, tiled=True)
        cond = jnp.stack([jnp.repeat(low_clips, 4, axis=0), image_all], axis=1)
        values[S.mods], values[J.mods] = modulations(
            cond, (space_modulate, joint_modulate)
        )
        values.update(zip(weights[:4], gather_flat(space_shards)))
        values.update(zip(weights[4:], gather_flat(joint_shards)))
        values[A.all_rows] = lax.all_gather(tokens, "narrow", axis=0, tiled=True)
        apart(values, FORWARD + BACK_JOINT + BACK_SPACE)
        for b in (J, S):
            values.update(zip(grads_of(b), scatter_plain([values[k] for k in partials_of(b)])))
        values[A.own_first] = lax.psum_scatter(
            values[A.to_first].astype(FULL), "narrow", scatter_dimension=0, tiled=True
        )
        apart(values, [A.finish])
        both = [
            jnp.concatenate([values[b.early], values[b.late][:, 2 * D :]], axis=1) for b in (S, J)
        ]
        modulate = modulation_grads(cond, jnp.stack(both), rows)
    bias = lax.psum(
        jnp.concatenate(
            [
                space_table_back(values[S.to_table], narrow),
                joint_table_back(values[J.to_table]),
            ],
            axis=1,
        ),
        ("wide", "narrow"),
    )
    split = space_bias.shape[1]
    bias = (bias[:, :split], bias[:, split:])
    outs = [values[A.output_tokens], values[A.grad_tokens]]
    for i, b in enumerate((S, J)):
        outs += [modulate[i]] + [values[k] for k in reversed(grads_of(b))] + [bias[i]]
    return tuple(outs)


FORWARD = S.triple, S.attend, S.mlp, J.triple, J.attend, J.mlp
BACK_JOINT = J.mlp_back, J.attend_back, J.project_back, S.mlp_back
BACK_SPACE = S.attend_back, S.project_back
LAST = (A.finish,)


def solution(mesh):
    rows = P(("wide", "narrow"), None)
    block = P("wide", "narrow")
    in_specs = (
        (rows, P(), P("wide", None), P("wide"))
        + (block,) * 5
        + (P(),)
        + (block,) * 5
        + (P(), rows)
    )
    out_specs = (rows, rows) + ((block,) * 5 + (P(),)) * 2
    return jax.shard_map(body, mesh=mesh, in_specs=in_specs, out_specs=out_specs, check_vma=False)
```

```python
import functools
import math

import jax
import jax.numpy as jnp
import numpy as np
from jax import lax
from jax.experimental import pallas as pl
from jax.experimental.pallas import tpu as pltpu
from jax.sharding import PartitionSpec as P

D = 1024
HEADS = 16
HEAD_DIM = 64
FF = 4096
SW = 8
TW = 5
CHUNK = SW * SW
CLIP_ROWS = TW * CHUNK
ROWS_DEV = CLIP_ROWS + 4 * CHUNK
SPAN_S = 4 * SW - 1
SPAN_T = 2 * SW - 1
MESH = pl.DeviceIdType.MESH


epsilon = 1e-06


def normalise(values):
    centred = values - jnp.mean(values, axis=-1, keepdims=True)
    spread = jnp.mean(centred * centred, axis=-1, keepdims=True)
    scale = lax.rsqrt(spread + epsilon)
    return centred * scale, scale


def norm_back(unit, scale, grad):
    return scale * (
        grad
        - jnp.mean(grad, axis=-1, keepdims=True)
        - unit * jnp.mean(grad * unit, axis=-1, keepdims=True)
    )


def nn(left, right):
    return lax.dot_general(left, right, (((1,), (0,)), ((), ())), preferred_element_type=jnp.float32)


def nt(left, right):
    return lax.dot_general(left, right, (((1,), (1,)), ((), ())), preferred_element_type=jnp.float32)


def tn(left, right):
    return lax.dot_general(left, right, (((0,), (0,)), ((), ())), preferred_element_type=jnp.float32)


def each_chunk(body, count=ROWS_DEV // CHUNK):
    @pl.loop(0, count)
    def _(i):
        inner = lax.rem(i, ROWS_DEV // CHUNK)
        seq = jnp.where(inner >= CLIP_ROWS // CHUNK, 1, 0)
        body(pl.ds(pl.multiple_of(i * CHUNK, CHUNK), CHUNK), pl.ds(seq, 1))


def part(index):
    return slice(index * D, (index + 1) * D)


class Tiled:
    def __init__(self, block, index):
        self.block, self.index = block, index

    def spec(self):
        return pl.BlockSpec(self.block, self.index)


class Whole:
    def __init__(self, block):
        self.block = block

    def spec(self):
        rank = len(self.block)
        return pl.BlockSpec(self.block, lambda *_: (0,) * rank, pipeline_mode=pl.Buffered(1))


class Scalars:
    def spec(self):
        return pl.BlockSpec(memory_space=pltpu.SMEM)


SCALARS = Scalars()
whole, spec = Whole, Tiled


def params(limit=56):
    return pltpu.CompilerParams(vmem_limit_bytes=limit * 2**20)


def shape(dims, kind):
    return jax.ShapeDtypeStruct(dims, kind)


LOW = jnp.bfloat16
FULL = jnp.float32


class Phase:
    def __init__(self, kernel, *, grid, in_specs, out_specs, out_shape, name, ticks=1, scratch_shapes=()):
        self.kernel, self.grid, self.name, self.ticks = kernel, grid, name, ticks
        self.in_specs, self.out_specs, self.out_shape = in_specs, out_specs, out_shape
        self.scratch = list(scratch_shapes)

    def __call__(self, *args):
        return pl.pallas_call(
            functools.partial(self.kernel, lambda t: None),
            grid=self.grid,
            in_specs=[s.spec() for s in self.in_specs],
            out_specs=[s.spec() for s in self.out_specs],
            out_shape=self.out_shape,
            scratch_shapes=self.scratch,
            compiler_params=params(),
            name=self.name,
        )(*args)

    def inside(self, tick, ins, outs):
        specs = list(self.in_specs) + list(self.out_specs)
        refs = list(ins) + list(outs)
        first_out = len(ins)
        held = [i for i, s in enumerate(specs) if isinstance(s, Whole)]
        tiled = [i for i, s in enumerate(specs) if isinstance(s, Tiled)]

        def scoped(buffers, scratch, sems):
            place = dict(zip(held, buffers))
            loads = [
                pltpu.make_async_copy(refs[i], place[i], sems.at[at])
                for at, i in enumerate(held)
                if i < first_out
            ]
            for load in loads:
                load.start()
            for load in loads:
                load.wait()

            def body(*blocks):
                now = dict(zip(tiled, blocks))
                now.update(place)
                operands = [now.get(i, refs[i]) for i in range(len(refs))]
                self.kernel(tick, *operands, *scratch)

            pltpu.emit_pipeline(
                body,
                grid=self.grid,
                in_specs=[specs[i].spec() for i in tiled if i < first_out],
                out_specs=[specs[i].spec() for i in tiled if i >= first_out],
            )(*[refs[i] for i in tiled])
            stores = [
                pltpu.make_async_copy(place[i], refs[i], sems.at[at])
                for at, i in enumerate(held)
                if i >= first_out
            ]
            for store in stores:
                store.start()
            for store in stores:
                store.wait()

        kinds = [refs[i].dtype for i in held]
        pl.run_scoped(
            scoped,
            [pltpu.VMEM(specs[i].block, kind) for i, kind in zip(held, kinds)],
            self.scratch,
            pltpu.SemaphoreType.DMA((len(held),)),
        )


def space_triple_kernel(tick, rows, mods, weight, normed, queries, pairs):
    step = pl.program_id(0)

    @pl.when(step == 0)
    def _():
        def chunk(at, seq):
            unit, _ = normalise(rows[at, :].astype(FULL))
            normed[at, :] = (unit * (1.0 + mods[seq, part(1)]) + mods[seq, part(0)]).astype(LOW)

        each_chunk(chunk, 4 * ROWS_DEV // CHUNK)

    tick(0)

    @pl.when(step < 2)
    def _():
        own = span(lax.axis_index("narrow"), ROWS_DEV)
        queries[...] = nn(normed[own, :], weight[...]).astype(LOW)

    for q in range(4):
        if q:
            tick(q)

        @pl.when(step >= 2)
        def _():
            pairs[q] = nn(normed[q * ROWS_DEV : (q + 1) * ROWS_DEV, :], weight[...]).astype(LOW)


def space_triple():
    tile = 512
    return Phase(
        space_triple_kernel,
        grid=(3 * D // tile,),
        in_specs=[
            whole((4 * ROWS_DEV, D)),
            whole((2, 6 * D)),
            spec((D, tile), lambda t: (0, t)),
        ],
        out_specs=[
            whole((4 * ROWS_DEV, D)),
            spec((ROWS_DEV, tile), lambda t: (0, jnp.minimum(t, 1))),
            spec((4, ROWS_DEV, tile), lambda t: (0, 0, jnp.maximum(t - 2, 0))),
        ],
        out_shape=[
            shape((4 * ROWS_DEV, D), LOW),
            shape((ROWS_DEV, D), LOW),
            shape((4, ROWS_DEV, 2 * D), LOW),
        ],
        name="space_triple",
        ticks=4,
    )


def joint_triple_kernel(tick, rows, mods, weight, normed, triple):
    @pl.when(pl.program_id(0) == 0)
    def _():
        def chunk(at, seq):
            unit, _ = normalise(rows[at, :])
            normed[at, :] = (unit * (1.0 + mods[seq, part(1)]) + mods[seq, part(0)]).astype(LOW)

        each_chunk(chunk)

    tick(0)
    triple[...] = nn(normed[...], weight[...]).astype(LOW)


def joint_triple():
    tile = 512
    return Phase(
        joint_triple_kernel,
        grid=(3 * D // tile,),
        in_specs=[whole((ROWS_DEV, D)), whole((2, 6 * D)), spec((D, tile), lambda t: (0, t))],
        out_specs=[whole((ROWS_DEV, D)), spec((ROWS_DEV, tile), lambda t: (0, t))],
        out_shape=[shape((ROWS_DEV, D), LOW), shape((ROWS_DEV, 3 * D), LOW)],
        name="joint_triple",
        ticks=1,
    )


def half_mask():
    return lax.broadcasted_iota(jnp.int32, (1, 2 * HEAD_DIM), 1) < HEAD_DIM


def split_heads(rows):
    first = half_mask()
    zero = jnp.zeros_like(rows)
    return jnp.concatenate([jnp.where(first, rows, zero), jnp.where(first, zero, rows)], axis=0)


def join_heads(stacked):
    return jnp.where(half_mask(), stacked[:CHUNK], stacked[CHUNK:])


def softmax_keys(keys, queries, bias):
    scores = nt(keys, queries) * HEAD_DIM**-0.5 + bias
    powered = jnp.exp(scores - jnp.max(scores, axis=0, keepdims=True))
    return powered / jnp.sum(powered, axis=0, keepdims=True)


def attend(queries, keys, values, bias):
    probs = softmax_keys(keys, split_heads(queries), bias)
    return join_heads(tn(values, probs.astype(LOW)).T).astype(LOW)


def attend_back(queries, keys, values, bias, grad):
    queries, grad = split_heads(queries), split_heads(grad)
    probs = softmax_keys(keys, queries, bias)
    grad_values = nn(probs.astype(LOW), grad)
    grad_probs = nt(values, grad)
    centre = jnp.sum(probs * grad_probs, axis=0, keepdims=True)
    grad_scores = (probs * (grad_probs - centre)).astype(LOW)
    grad_queries = join_heads(tn(keys, grad_scores).T) * HEAD_DIM**-0.5
    grad_keys = nn(grad_scores, queries) * HEAD_DIM**-0.5
    return grad_queries, grad_keys, grad_values, grad_scores.astype(FULL)


def space_attend_kernel(tick, queries, keys, values, bias, out):
    table = bias[0]
    for i in range(ROWS_DEV // CHUNK):
        if i % 3 == 0:
            tick(i // 3)
        at = slice(i * CHUNK, (i + 1) * CHUNK)
        key_rows = keys[:, at, :].reshape(4 * CHUNK, 2 * HEAD_DIM)
        value_rows = values[:, at, :].reshape(4 * CHUNK, 2 * HEAD_DIM)
        out[at, :] = attend(queries[at, :], key_rows, value_rows, table)


def space_attend():
    wide = 2 * HEAD_DIM
    return Phase(
        space_attend_kernel,
        grid=(HEADS // 2,),
        in_specs=[
            spec((ROWS_DEV, wide), lambda h: (0, h)),
            spec((4, ROWS_DEV, wide), lambda h: (0, 0, h)),
            spec((4, ROWS_DEV, wide), lambda h: (0, 0, h + HEADS // 2)),
            spec((1, 4 * CHUNK, wide), lambda h: (h, 0, 0)),
        ],
        out_specs=[spec((ROWS_DEV, wide), lambda h: (0, h))],
        out_shape=[shape((ROWS_DEV, D), LOW)],
        name="space_attend",
        ticks=3,
    )


def space_attend_back_kernel(tick, queries, keys, values, bias, grad, grad_q, grad_pairs, grad_bias):
    table = bias[0]
    for i in range(ROWS_DEV // CHUNK):
        if i % 3 == 0:
            tick(i // 3)
        at = slice(i * CHUNK, (i + 1) * CHUNK)
        key_rows = keys[:, at, :].reshape(4 * CHUNK, 2 * HEAD_DIM)
        value_rows = values[:, at, :].reshape(4 * CHUNK, 2 * HEAD_DIM)
        to_q, to_k, to_v, to_bias = attend_back(
            queries[at, :], key_rows, value_rows, table, grad[at, :]
        )
        grad_q[at, :] = to_q.astype(LOW)
        grad_pairs[0, :, at, :] = to_k.astype(LOW).reshape(4, CHUNK, 2 * HEAD_DIM)
        grad_pairs[1, :, at, :] = to_v.astype(LOW).reshape(4, CHUNK, 2 * HEAD_DIM)
        to_bias = to_bias.reshape(2, 2, SW, SW, 2 * HEAD_DIM)
        if i == 0:
            grad_bias[0] = to_bias
        else:
            grad_bias[0] += to_bias


def space_attend_back():
    wide = 2 * HEAD_DIM
    head = spec((ROWS_DEV, wide), lambda h: (0, h))
    four = spec((4, ROWS_DEV, wide), lambda h: (0, 0, h))
    table = spec((1, 4 * CHUNK, wide), lambda h: (h, 0, 0))
    return Phase(
        space_attend_back_kernel,
        grid=(HEADS // 2,),
        in_specs=[
            head,
            four,
            spec((4, ROWS_DEV, wide), lambda h: (0, 0, h + HEADS // 2)),
            table,
            head,
        ],
        out_specs=[
            head,
            spec((2, 4, ROWS_DEV, wide), lambda h: (0, 0, 0, h)),
            spec((1, 2, 2, SW, SW, wide), lambda h: (h, 0, 0, 0, 0, 0)),
        ],
        out_shape=[
            shape((ROWS_DEV, D), LOW),
            shape((2, 4, ROWS_DEV, D), LOW),
            shape((HEADS // 2, 2, 2, SW, SW, wide), FULL),
        ],
        name="space_attend_back",
        ticks=3,
    )


def clip_table(bias, frame):
    return jnp.concatenate([bias[0, frame - t + TW - 1] for t in range(TW)], axis=0)


def joint_attend_kernel(tick, queries, keys, values, bias, out):
    for i in range(ROWS_DEV // CHUNK):
        if i % 3 == 0:
            tick(i // 3)
        at = slice(i * CHUNK, (i + 1) * CHUNK)
        seen = slice(0, CLIP_ROWS) if i < TW else at
        table = clip_table(bias, i) if i < TW else bias[0, TW - 1]
        out[at, :] = attend(queries[at, :], keys[seen, :], values[seen, :], table)


def joint_specs():
    wide = 2 * HEAD_DIM
    return [
        spec((ROWS_DEV, wide), lambda h: (0, h)),
        spec((ROWS_DEV, wide), lambda h: (0, h + HEADS // 2)),
        spec((ROWS_DEV, wide), lambda h: (0, h + HEADS)),
        spec((1, 2 * TW - 1, CHUNK, wide), lambda h: (h, 0, 0, 0)),
    ]


def joint_attend():
    return Phase(
        joint_attend_kernel,
        grid=(HEADS // 2,),
        in_specs=joint_specs(),
        out_specs=[spec((ROWS_DEV, 2 * HEAD_DIM), lambda h: (0, h))],
        out_shape=[shape((ROWS_DEV, D), LOW)],
        name="joint_attend",
        ticks=3,
    )


def joint_attend_back_kernel(
    tick, queries, keys, values, bias, grad, grads, grad_bias, sum_k, sum_v
):
    grad_bias[...] = jnp.zeros_like(grad_bias)
    for i in range(ROWS_DEV // CHUNK):
        if i % 3 == 0:
            tick(i // 3)
        at = slice(i * CHUNK, (i + 1) * CHUNK)
        seen = slice(0, CLIP_ROWS) if i < TW else at
        table = clip_table(bias, i) if i < TW else bias[0, TW - 1]
        to_q, to_k, to_v, to_bias = attend_back(
            queries[at, :], keys[seen, :], values[seen, :], table, grad[at, :]
        )
        grads[0, at, :] = to_q.astype(LOW)
        if i >= TW:
            grad_bias[TW - 1] += to_bias
            grads[1, at, :] = to_k.astype(LOW)
            grads[2, at, :] = to_v.astype(LOW)
            continue
        for t in range(TW):
            grad_bias[i - t + TW - 1] += to_bias[t * CHUNK : (t + 1) * CHUNK]
        if i == 0:
            sum_k[...] = to_k
            sum_v[...] = to_v
        elif i < TW - 1:
            sum_k[...] += to_k
            sum_v[...] += to_v
        else:
            grads[1, seen, :] = (sum_k[...] + to_k).astype(LOW)
            grads[2, seen, :] = (sum_v[...] + to_v).astype(LOW)


def joint_attend_back():
    wide = 2 * HEAD_DIM
    head = spec((ROWS_DEV, wide), lambda h: (0, h))
    return Phase(
        joint_attend_back_kernel,
        grid=(HEADS // 2,),
        in_specs=joint_specs() + [head],
        out_specs=[
            spec((3, ROWS_DEV, wide), lambda h: (0, 0, h)),
            spec((2 * TW - 1, CHUNK, wide), lambda h: (h, 0, 0)),
        ],
        out_shape=[
            shape((3, ROWS_DEV, D), LOW),
            shape((HEADS // 2 * (2 * TW - 1), CHUNK, wide), FULL),
        ],
        scratch_shapes=[pltpu.VMEM((CLIP_ROWS, wide), FULL)] * 2,
        name="joint_attend_back",
        ticks=3,
    )


def mlp_kernel(last_block, tick, live, rows, attended, mods, output, expand, shrink, *refs):
    branch, middle, normed, active, slope, reduced, result, total = refs
    step = pl.program_id(0)

    @pl.when(step == 0)
    def _():
        def chunk(at, seq):
            grown = nn(attended[at, :], output[...])
            branch[at, :] = grown.astype(LOW)
            mixed = rows[at, :].astype(FULL) + mods[seq, part(2)] * grown
            middle[at, :] = mixed
            unit, _ = normalise(mixed)
            normed[at, :] = (unit * (1.0 + mods[seq, part(4)]) + mods[seq, part(3)]).astype(LOW)

        each_chunk(chunk)
        total[...] = jnp.zeros_like(total)

    tick(0)
    before = nn(normed[...], expand[...])
    inner = 0.5 * (1.0 + lax.erf(before * 0.5**0.5))
    low_active = (before * inner).astype(LOW)
    tick(1)
    active[...] = low_active
    slope[...] = (inner + before * jnp.exp(-0.5 * before * before) * (2.0 * math.pi) ** -0.5).astype(LOW)
    total[...] += nn(low_active, shrink[...])

    @pl.when(step == pl.num_programs(0) - 1)
    def _():
        def chunk(at, seq):
            reduced[at, :] = total[at, :].astype(LOW)
            value = middle[at, :] + mods[seq, part(5)] * total[at, :]
            if last_block:
                value = value * jnp.where(seq.start > 0, live[0], 1.0)
            result[at, :] = value.astype(result.dtype)

        each_chunk(chunk)


def mlp(last_block):
    tile = 512
    square = whole((ROWS_DEV, D))
    strip = spec((ROWS_DEV, tile), lambda f: (0, f))
    return Phase(
        functools.partial(mlp_kernel, last_block),
        grid=(FF // tile,),
        in_specs=[
            SCALARS,
            square,
            square,
            whole((2, 6 * D)),
            whole((D, D)),
            spec((D, tile), lambda f: (0, f)),
            spec((tile, D), lambda f: (f, 0)),
        ],
        out_specs=[square, square, square, strip, strip, square, square],
        out_shape=[
            shape((ROWS_DEV, D), LOW),
            shape((ROWS_DEV, D), FULL),
            shape((ROWS_DEV, D), LOW),
            shape((ROWS_DEV, FF), LOW),
            shape((ROWS_DEV, FF), LOW),
            shape((ROWS_DEV, D), LOW),
            shape((ROWS_DEV, D), LOW if last_block else FULL),
        ],
        scratch_shapes=[pltpu.VMEM((ROWS_DEV, D), FULL)],
        name="mlp",
        ticks=2,
    )


def mlp_back_kernel(first_block, tick, live, *refs):
    (grad_result, attended, mods, branch, middle, normed, reduced, output, active, slope) = refs[:10]
    expand, shrink = refs[10:12]
    grad_shrink, grad_expand, grad_output, grad_middle, grad_attended, grad_mods = refs[12:18]
    grad_reduced, normed_t, total = refs[18:]
    grad_branch = grad_reduced
    step = pl.program_id(0)

    def incoming(at, seq):
        value = grad_result[at, :].astype(FULL)
        if first_block:
            value = value * jnp.where(seq.start > 0, live[0], 1.0)
        return value

    @pl.when(step == 0)
    def _():
        grad_mods[...] = jnp.zeros_like(grad_mods)

        def chunk(at, seq):
            value = incoming(at, seq)
            grad_reduced[at, :] = (mods[seq, part(5)] * value).astype(LOW)
            grad_mods[seq, part(5)] += jnp.sum(
                reduced[at, :].astype(FULL) * value, axis=0, keepdims=True
            )

        each_chunk(chunk)
        total[...] = jnp.zeros_like(total)
        normed_t[...] = normed[...].T

    tick(0)
    grad_active = nt(grad_reduced[...], shrink[...])
    grad_before = (grad_active * slope[...].astype(FULL)).astype(LOW)
    tick(1)
    grad_shrink[...] = tn(active[...], grad_reduced[...]).astype(LOW)
    tick(2)
    grad_expand[...] = nn(normed_t[...], grad_before).astype(LOW)
    tick(3)
    total[...] += nt(grad_before, expand[...])

    @pl.when(step == pl.num_programs(0) - 1)
    def _():
        def chunk(at, seq):
            grad = total[at, :]
            unit, scale = normalise(middle[at, :])
            grad_mods[seq, part(3)] += jnp.sum(grad, axis=0, keepdims=True)
            grad_mods[seq, part(4)] += jnp.sum(unit * grad, axis=0, keepdims=True)
            value = incoming(at, seq) + norm_back(unit, scale, (1.0 + mods[seq, part(4)]) * grad)
            grad_middle[at, :] = value
            grad_mods[seq, part(2)] += jnp.sum(
                branch[at, :].astype(FULL) * value, axis=0, keepdims=True
            )
            grad_branch[at, :] = (mods[seq, part(2)] * value).astype(LOW)

        each_chunk(chunk)
        grad_attended[...] = nt(grad_branch[...], output[...]).astype(LOW)
        grad_output[...] = tn(attended[...], grad_branch[...]).astype(LOW)


def mlp_back(first_block):
    tile = 512
    square = whole((ROWS_DEV, D))
    strip = spec((ROWS_DEV, tile), lambda f: (0, f))
    across = spec((D, tile), lambda f: (0, f))
    down = spec((tile, D), lambda f: (f, 0))
    return Phase(
        functools.partial(mlp_back_kernel, first_block),
        grid=(FF // tile,),
        in_specs=[
            SCALARS,
            square,
            square,
            whole((2, 6 * D)),
            square,
            square,
            square,
            square,
            whole((D, D)),
            strip,
            strip,
            across,
            down,
        ],
        out_specs=[down, across, whole((D, D)), square, square, whole((2, 6 * D))],
        out_shape=[
            shape((FF, D), LOW),
            shape((D, FF), LOW),
            shape((D, D), LOW),
            shape((ROWS_DEV, D), FULL),
            shape((ROWS_DEV, D), LOW),
            shape((2, 6 * D), FULL),
        ],
        scratch_shapes=[
            pltpu.VMEM((ROWS_DEV, D), LOW),
            pltpu.VMEM((D, ROWS_DEV), LOW),
            pltpu.VMEM((ROWS_DEV, D), FULL),
        ],
        name="mlp_back",
        ticks=4,
    )


def finish_rows(rows, grad_normed, grad_middle, mods, grad_rows, grad_mods):
    grad_mods[...] = jnp.zeros_like(grad_mods)

    def chunk(at, seq):
        grad = grad_normed[at, :].astype(FULL)
        unit, scale = normalise(rows[at, :].astype(FULL))
        grad_mods[seq, part(0)] += jnp.sum(grad, axis=0, keepdims=True)
        grad_mods[seq, part(1)] += jnp.sum(unit * grad, axis=0, keepdims=True)
        grad_rows[at, :] = grad_middle[at, :] + norm_back(
            unit, scale, (1.0 + mods[seq, part(1)]) * grad
        )

    each_chunk(chunk)


def joint_project_back_kernel(
    tick, rows, mods, normed, grad_middle, weight, grad, grad_weight, grad_rows, grad_mods, total, normed_t
):
    step = pl.program_id(0)

    @pl.when(step == 0)
    def _():
        total[...] = jnp.zeros_like(total)
        normed_t[...] = normed[...].T

    tick(0)
    grad_weight[...] = nn(normed_t[...], grad[0]).astype(LOW)
    tick(1)
    total[...] += nt(grad[0], weight[...])

    @pl.when(step == pl.num_programs(0) - 1)
    def _():
        finish_rows(rows, total, grad_middle, mods, grad_rows, grad_mods)


def joint_project_back():
    tile = 512
    square = whole((ROWS_DEV, D))
    across = spec((D, tile), lambda t: (0, t))
    return Phase(
        joint_project_back_kernel,
        grid=(3 * D // tile,),
        in_specs=[square, whole((2, 6 * D)), square, square, across, spec((1, ROWS_DEV, tile), lambda t: (t // 2, 0, t % 2))],
        out_specs=[across, square, whole((2, 2 * D))],
        out_shape=[shape((D, 3 * D), LOW), shape((ROWS_DEV, D), FULL), shape((2, 2 * D), FULL)],
        scratch_shapes=[pltpu.VMEM((ROWS_DEV, D), FULL), pltpu.VMEM((D, ROWS_DEV), LOW)],
        name="joint_project_back",
        ticks=2,
    )


def space_project_back_kernel(tick, normed, weight, grad_q, grad_pairs, grad_weight, grad_normed, total):
    step = pl.program_id(0)
    own = span(lax.axis_index("narrow"), ROWS_DEV)

    @pl.when(step == 0)
    def _():
        total[...] = jnp.zeros_like(total)

    tick(0)

    @pl.when(step < 2)
    def _():
        grad_weight[...] = tn(normed[own, :], grad_q[...]).astype(LOW)
        total[own, :] += nt(grad_q[...], weight[...])

    @pl.when(step >= 2)
    def _():
        flat = grad_pairs[0].reshape(4 * ROWS_DEV, grad_pairs.shape[-1])
        grad_weight[...] = tn(normed[...], flat).astype(LOW)

    for q in range(4):
        tick(q + 1)

        @pl.when(step >= 2)
        def _():
            at = slice(q * ROWS_DEV, (q + 1) * ROWS_DEV)
            total[at, :] += nt(grad_pairs[0, q], weight[...])

    @pl.when(step == pl.num_programs(0) - 1)
    def _():
        grad_normed[...] = total[...].astype(LOW)


def space_project_back():
    tile = 512
    across = spec((D, tile), lambda t: (0, t))

    def pair(t):
        late = jnp.maximum(t - 2, 0)
        return (late // 2, 0, 0, late % 2)

    return Phase(
        space_project_back_kernel,
        grid=(3 * D // tile,),
        in_specs=[
            whole((4 * ROWS_DEV, D)),
            across,
            spec((ROWS_DEV, tile), lambda t: (0, jnp.minimum(t, 1))),
            spec((1, 4, ROWS_DEV, tile), pair),
        ],
        out_specs=[across, whole((4 * ROWS_DEV, D))],
        out_shape=[shape((D, 3 * D), LOW), shape((4 * ROWS_DEV, D), LOW)],
        scratch_shapes=[pltpu.VMEM((4 * ROWS_DEV, D), FULL)],
        name="space_project_back",
        ticks=5,
    )


def space_first_back(feed, ticks, order, weight, grad_q, grad_pairs, out):
    half = ROWS_DEV // 2
    first = feed.slot
    feed.slot += ticks

    def scoped(weights, queries, pairs, sems):
        def pair_load(j):
            return pltpu.make_async_copy(
                grad_pairs.at[:, order[j]], pairs.at[(3 - j) % 2], sems.at[(3 - j) % 2]
            )

        loads = [
            pltpu.make_async_copy(weight, weights, sems.at[2]),
            pltpu.make_async_copy(grad_q, queries, sems.at[3]),
        ]
        for load in loads:
            load.start()
        pair_load(3).start()
        for load in loads:
            load.wait()
        for step in range(4):
            j = 3 - step
            if j:
                pair_load(j - 1).start()
            pair_load(j).wait()
            for side in range(2):
                feed.do(first + 2 * step + side)
                rows = slice(side * half, (side + 1) * half)
                value = nt(pairs[step % 2, 0, rows, :], weights[:, part(1)])
                value += nt(pairs[step % 2, 1, rows, :], weights[:, part(2)])
                if j == 0:
                    value += nt(queries[rows, :], weights[:, part(0)])
                for p in range(2):
                    piece = value[p * (half // 2) : (p + 1) * (half // 2)]
                    out[2 * side + p, order[j]] = piece.astype(LOW)

    pl.run_scoped(
        scoped,
        pltpu.VMEM((D, 3 * D), LOW),
        pltpu.VMEM((ROWS_DEV, D), LOW),
        pltpu.VMEM((2, 2, ROWS_DEV, D), LOW),
        pltpu.SemaphoreType.DMA((4,)),
    )


def space_weight_back_kernel(tick, normed, grad_q, grad_pairs, grad_weight):
    step = pl.program_id(0)
    own = span(lax.axis_index("narrow"), ROWS_DEV)
    tick(0)

    @pl.when(step < 2)
    def _():
        grad_weight[...] = tn(normed[own, :], grad_q[...]).astype(LOW)

    for side in range(2):
        if side:
            tick(1)

        @pl.when(step >= 2)
        def _():
            columns = slice(side * 256, (side + 1) * 256)
            flat = grad_pairs[0, :, :, columns].reshape(4 * ROWS_DEV, 256)
            grad_weight[:, columns] = tn(normed[...], flat).astype(LOW)


def space_weight_back():
    tile = 512

    def pair(t):
        late = jnp.maximum(t - 2, 0)
        return (late // 2, 0, 0, late % 2)

    return Phase(
        space_weight_back_kernel,
        grid=(3 * D // tile,),
        in_specs=[
            whole((4 * ROWS_DEV, D)),
            spec((ROWS_DEV, tile), lambda t: (0, jnp.minimum(t, 1))),
            spec((1, 4, ROWS_DEV, tile), pair),
        ],
        out_specs=[spec((D, tile), lambda t: (0, t))],
        out_shape=[shape((D, 3 * D), LOW)],
        name="space_weight_back",
        ticks=2,
    )


def finish_kernel(tick, rows, mods, grad_normed, grad_middle, grad_rows, grad_mods):
    tick(0)
    finish_rows(rows, grad_normed, grad_middle, mods, grad_rows, grad_mods)


def finish():
    square = whole((ROWS_DEV, D))
    return Phase(
        finish_kernel,
        grid=(1,),
        in_specs=[square, whole((2, 6 * D)), square, square],
        out_specs=[square, whole((2, 2 * D))],
        out_shape=[shape((ROWS_DEV, D), FULL), shape((2, 2 * D), FULL)],
        name="finish",
    )


class Place:
    def __init__(self):
        self.w = lax.axis_index("wide")
        self.n = lax.axis_index("narrow")
        self.c = lax.bitwise_xor(self.w, 1)
        self.x = lax.bitwise_xor(self.w, 2)
        self.y = lax.bitwise_xor(self.w, 4)
        self.d = lax.bitwise_xor(self.w, 6)
        self.up = jnp.minimum(self.n + 1, 3)
        self.down = jnp.maximum(self.n - 1, 0)
        self.order = (
            self.n,
            lax.bitwise_xor(self.n, 1),
            jnp.where(self.n < 2, 2, 1),
            jnp.where(self.n < 2, 3, 0),
        )

    def enter(self):
        barrier = pltpu.get_barrier_semaphore()
        for peer in (self.x, self.y, self.c):
            pl.semaphore_signal(barrier, inc=1, device_id=(peer, self.n), device_id_type=MESH)

        @pl.when(self.n > 0)
        def _():
            pl.semaphore_signal(barrier, inc=1, device_id=(self.w, self.n - 1), device_id_type=MESH)

        @pl.when(self.n < 3)
        def _():
            pl.semaphore_signal(barrier, inc=1, device_id=(self.w, self.n + 1), device_id_type=MESH)

        ends = jnp.where(self.n > 0, 1, 0) + jnp.where(self.n < 3, 1, 0)
        pl.semaphore_wait(barrier, 3 + ends)

    def enter_all(self):
        barrier = pltpu.get_barrier_semaphore()
        for step in range(1, 8):
            peer = (lax.bitwise_xor(self.w, step), self.n)
            pl.semaphore_signal(barrier, inc=1, device_id=peer, device_id_type=MESH)
        for step in range(1, 4):
            peer = (self.w, lax.bitwise_xor(self.n, step))
            pl.semaphore_signal(barrier, inc=1, device_id=peer, device_id_type=MESH)
        pl.semaphore_wait(barrier, 10)

    def passes_on(self, col):
        return jnp.logical_or(
            jnp.logical_and(col < self.n, self.n < 3), jnp.logical_and(col > self.n, self.n > 0)
        )

    def carried(self, col):
        return jnp.logical_or(
            jnp.logical_and(col > self.n, self.n > 0), jnp.logical_and(col < self.n, self.n < 3)
        )


def remote(src, dst, send, recv, to):
    return pltpu.make_async_remote_copy(
        src_ref=src, dst_ref=dst, send_sem=send, recv_sem=recv, device_id=to, device_id_type=MESH
    )


def span(index, size):
    return pl.ds(pl.multiple_of(index * size, size), size)


DMA = pltpu.SemaphoreType.DMA
FOLDS = [(3, 1), (3, 3), (3, 0), (3, 2)]
FOLDS += [(2, 3), (1, 3), (2, 2), (1, 2), (1, 1), (2, 1), (1, 0), (2, 0)]
FOLDS += [(0, 3), (0, 2), (0, 1), (0, 0)]
LOADS = 2
PIECES = 4
PIECE = ROWS_DEV // PIECES


class Names:
    def __init__(self, owner):
        self.owner = owner

    def __getattr__(self, name):
        return self.owner, name


A, S, J = Names(0), Names(1), Names(2)


class Feed:
    def __init__(self, enter):
        self.enter, self.steps, self.drains = enter, [], []

    def add(self, function, *args):
        self.steps.append(functools.partial(function, *args))

    def drain(self, function, *args):
        self.drains.append(functools.partial(function, *args))

    def follow(self, tables):
        self.lists = []
        for table in tables:
            parts = [[]]
            for number in table:
                if number < 0:
                    parts.append([])
                else:
                    parts[-1].append(self.steps[number])
            self.lists.append(parts)
        self.slot = 0
        self.at_end = jnp.logical_or(Place().n == 0, Place().n == 3)

    def do(self, slot):
        ends, middles = (parts[slot] for parts in self.lists)

        @pl.when(self.at_end)
        def _():
            for step in ends:
                step()

        @pl.when(jnp.logical_not(self.at_end))
        def _():
            for step in middles:
                step()

    def over(self, phase):
        first, total = self.slot, phase.grid[0]
        self.do(first)
        self.slot += total * phase.ticks

        def tick(t):
            for i in range(total):
                slot = first + i * phase.ticks + t
                if slot > first and any(parts[slot] for parts in self.lists):

                    @pl.when(pl.program_id(0) == i)
                    def _():
                        self.do(slot)

        return tick

    def rest(self):
        self.do(self.slot)
        for step in self.drains:
            step()


class Gather:
    def __init__(self, shapes, line, collective_id):
        self.shapes, self.line, self.collective_id = shapes, line, collective_id
        count, lines = len(shapes), 1 if line else 0
        self.in_specs = [pl.BlockSpec(memory_space=pl.ANY)] * (count + lines)
        self.out_specs = self.in_specs
        self.out_shape = [shape((8 * r, 4 * c), LOW) for r, c in shapes]
        self.out_shape += [shape((4 * ROWS_DEV, D), LOW)] * lines
        self.scratch = [
            DMA((count, 5)),
            DMA((count, 4)),
            DMA((count, 2, 4)),
            DMA((count, 2, 4)),
            DMA((count, 2, 4)),
            DMA((count, 2, 4)),
            DMA((count, 4, 4)),
            DMA((count, 4, 4)),
            DMA((count,)),
        ]
        self.scratch += [DMA((PIECES, 5)), DMA((PIECES, 4)), DMA((PIECES,))] * lines

    def steps(self, ins, outs, scratch):
        at = Place()
        shapes, count = self.shapes, len(self.shapes)
        w, n = at.w, at.n
        shards, fulls = ins[:count], outs[:count]
        z_send, z_recv, x_send, x_recv, y_send, y_recv, c_send, c_recv, own_sem = scratch[:9]

        def block(k, row, col):
            rows, cols = shapes[k]
            return fulls[k].at[span(row, rows), span(col, cols)]

        def z_copy(k, src, col, slot, to):
            return remote(src, block(k, w, col), z_send.at[k, slot], z_recv.at[k, col], (w, to))

        def x_copy(k, src, row, far, col):
            sems = x_send.at[k, far, col], x_recv.at[k, far, col]
            return remote(src, block(k, row, col), *sems, (at.x, n))

        def y_copy(k, src, row, far, col):
            sems = y_send.at[k, far, col], y_recv.at[k, far, col]
            return remote(src, block(k, row, col), *sems, (at.y, n))

        def c_copy(k, src, row, chip, col):
            sems = c_send.at[k, chip, col], c_recv.at[k, chip, col]
            return remote(src, block(k, row, col), *sems, (at.c, n))

        def own_copy(k):
            return pltpu.make_async_copy(shards[k], block(k, w, n), own_sem.at[k])

        def own(k):
            @pl.when(n < 3)
            def _():
                z_copy(k, shards[k], n, n, at.up).start()

            @pl.when(n > 0)
            def _():
                z_copy(k, shards[k], n, 4, at.down).start()

            x_copy(k, shards[k], w, 0, n).start()
            y_copy(k, shards[k], w, 0, n).start()
            c_copy(k, shards[k], w, 0, n).start()
            own_copy(k).start()

        def z_stage(k, j):
            col = at.order[j]
            here = block(k, w, col)
            z_copy(k, here, col, col, at.up).wait_recv()

            @pl.when(at.passes_on(col))
            def _():
                z_copy(k, here, col, col, jnp.where(col < n, at.up, at.down)).start()

            x_copy(k, here, w, 0, col).start()
            y_copy(k, here, w, 0, col).start()
            c_copy(k, here, w, 0, col).start()

        def near_stage(k, j):
            col = at.order[j]
            from_x = block(k, at.x, col)
            from_y = block(k, at.y, col)
            x_copy(k, from_x, at.x, 0, col).wait_recv()
            if j < 2:
                y_copy(k, from_x, at.x, 1, col).start()
            c_copy(k, from_x, at.x, 1, col).start()
            y_copy(k, from_y, at.y, 0, col).wait_recv()
            if j >= 2:
                x_copy(k, from_y, at.y, 1, col).start()
            c_copy(k, from_y, at.y, 2, col).start()

        def far_stage(k, j):
            col = at.order[j]
            far = block(k, at.d, col)
            (y_copy if j < 2 else x_copy)(k, far, at.d, 1, col).wait_recv()
            c_copy(k, far, at.d, 3, col).start()

        def ready(k):
            own_copy(k).wait()
            for col in range(4):
                for chip in range(4):
                    c_copy(k, block(k, w, col), w, chip, col).wait_recv()

        def drain(k):
            for j in range(4):
                col = at.order[j]
                here = block(k, w, col)

                @pl.when(at.passes_on(col) if j else n < 3)
                def _():
                    z_copy(k, here, col, col, at.up).wait_send()

                x_copy(k, here, w, 0, col).wait_send()
                y_copy(k, here, w, 0, col).wait_send()
                (y_copy if j < 2 else x_copy)(k, here, w, 1, col).wait_send()
                for chip in range(4):
                    c_copy(k, here, w, chip, col).wait_send()

            @pl.when(n > 0)
            def _():
                z_copy(k, shards[k], n, 4, at.down).wait_send()

        if self.line:
            rows, all_rows = ins[count], outs[count]
            t_send, t_recv, t_own = scratch[9:]

            def piece(p, col):
                return all_rows.at[pl.ds(pl.multiple_of(col * ROWS_DEV + p * PIECE, 16), PIECE)]

            def t_copy(p, src, col, slot, to):
                dst = piece(p, col)
                return remote(src, dst, t_send.at[p, slot], t_recv.at[p, col], (w, to))

            def t_own_copy(p):
                here = pl.ds(p * PIECE, PIECE)
                return pltpu.make_async_copy(rows.at[here], piece(p, n), t_own.at[p])

            def t_start(p, late):
                src = rows.at[pl.ds(p * PIECE, PIECE)]
                if not late:
                    t_own_copy(p).start()

                @pl.when(n == 2 if late else n < 2)
                def _():
                    t_copy(p, src, n, n, at.up).start()

                @pl.when(n == 1 if late else n >= 2)
                def _():
                    t_copy(p, src, n, 4, at.down).start()

            def t_stage(p, j):
                col = at.order[j]
                here = piece(p, col)
                t_copy(p, here, col, col, at.up).wait_recv()

                @pl.when(at.passes_on(col))
                def _():
                    t_copy(p, here, col, col, jnp.where(col < n, at.up, at.down)).start()

            def t_drain(p):
                for j in range(4):
                    col = at.order[j]
                    here = piece(p, col)

                    @pl.when(at.passes_on(col) if j else n < 3)
                    def _():
                        t_copy(p, here, col, col, at.up).wait_send()

                @pl.when(n > 0)
                def _():
                    t_copy(p, piece(p, n), n, 4, at.down).wait_send()

            def t_ready():
                for p in range(PIECES):
                    t_own_copy(p).wait()

        items = Feed(at.enter)
        for k in range(count):
            items.add(own, k)
            for j in range(1, 4):
                items.add(z_stage, k, j)
            for j in range(4):
                items.add(near_stage, k, j)
            for j in range(4):
                items.add(far_stage, k, j)
            items.add(ready, k)
            items.drain(drain, k)
        if self.line:
            for p in range(PIECES):
                items.add(t_start, p, False)
                items.add(t_start, p, True)
                for j in range(1, 4):
                    items.add(t_stage, p, j)
                items.drain(t_drain, p)
            items.add(t_ready)
        return items


class Scatter:
    def __init__(self, shapes, line, collective_id):
        self.shapes, self.line, self.collective_id = shapes, line, collective_id
        count, lines = len(shapes), 1 if line else 0
        self.out_shape = [shape(s, FULL) for s in shapes] + [shape((ROWS_DEV, D), FULL)] * lines
        self.out_specs = [pl.BlockSpec(memory_space=pltpu.VMEM)] * len(self.out_shape)
        self.scratch = []
        for s in shapes:
            self.scratch += [
                pltpu.VMEM((4, 4) + s, LOW),
                pltpu.VMEM((4,) + s, LOW),
                pltpu.VMEM((2, 4) + s, LOW),
                pltpu.VMEM((5,) + s, LOW),
                pltpu.VMEM((LOADS,) + s, LOW),
            ]
        self.scratch += [
            DMA((count, 4, 4)),
            DMA((count, 4, 4)),
            DMA((count, 4, 4)),
            DMA((count, 4)),
            DMA((count, 4)),
            DMA((count, 2, 4)),
            DMA((count, 2, 4)),
            DMA((count, 4)),
            DMA((count, 5)),
        ]
        self.scratch += [
            pltpu.VMEM((PIECES, 4, PIECE, D), LOW),
            pltpu.VMEM((PIECES, 5, PIECE, D), LOW),
            DMA((PIECES, 4)),
            DMA((PIECES, 5)),
        ] * lines

    def steps(self, ins, outs, scratch):
        at = Place()
        shapes, count = self.shapes, len(self.shapes)
        w, n, order = at.w, at.n, at.order
        chips = (w, at.x, at.y, at.d)
        held, far_in, near_in, z_in, staged = (scratch[i : 5 * count : 5] for i in range(5))
        load, c_send, c_recv, d_send, d_recv, n_send, n_recv, z_send, z_recv = scratch[
            5 * count : 5 * count + 9
        ]

        def source(k, row, col):
            rows, cols = shapes[k]
            return ins[k].at[span(row, rows), span(col, cols)]

        def load_copy(k, chip, j):
            slot = FOLDS.index((chip, j)) % LOADS
            return pltpu.make_async_copy(
                source(k, chips[chip], order[j]), staged[k].at[slot], load.at[k, chip, j]
            )

        def c_copy(k, chip, col):
            src = source(k, lax.bitwise_xor(chips[chip], 1), col)
            sems = c_send.at[k, chip, col], c_recv.at[k, chip, col]
            return remote(src, held[k].at[chip, col], *sems, (at.c, n))

        def d_copy(k, j):
            sems = d_send.at[k, j], d_recv.at[k, j]
            to = (at.x if j < 2 else at.y, n)
            return remote(held[k].at[3, order[j]], far_in[k].at[j], *sems, to)

        def n_copy(k, chip, col):
            sems = n_send.at[k, chip - 1, col], n_recv.at[k, chip - 1, col]
            dst = near_in[k].at[chip - 1, col]
            return remote(held[k].at[chip, col], dst, *sems, (chips[chip], n))

        def z_copy(k, col, slot, to):
            sems = z_send.at[k, col], z_recv.at[k, slot]
            return remote(held[k].at[0, col], z_in[k].at[slot], *sems, (w, to))

        def add(target, rows, *others):
            step = 64 if rows % 64 == 0 else 48

            @pl.loop(0, rows // step)
            def _(i):
                here = span(i, step)
                total = target[here, :]
                for other in others:
                    total = total + other[here, :]
                target[here, :] = total

        def fold(k, chip, j, *others):
            number = FOLDS.index((chip, j))
            load_copy(k, chip, j).wait()
            c_copy(k, chip, order[j]).wait_recv()
            add(held[k].at[chip, order[j]], shapes[k][0], staged[k].at[number % LOADS], *others)
            if number + LOADS < len(FOLDS):
                load_copy(k, *FOLDS[number + LOADS]).start()

        def begin(k):
            for chip, j in FOLDS:
                c_copy(k, chip, order[j]).start()
            for chip, j in FOLDS[:LOADS]:
                load_copy(k, chip, j).start()

        def far(k, j):
            fold(k, 3, j)
            d_copy(k, j).start()

        def near(k, j):
            chip = 2 if j >= 2 else 1
            fold(k, chip, j)
            n_copy(k, chip, order[j]).start()

        def near_far(k, j):
            chip = 1 if j >= 2 else 2
            d_copy(k, j).wait_recv()
            fold(k, chip, j, far_in[k].at[j])
            n_copy(k, chip, order[j]).start()

        def line_slot(col):
            to = jnp.where(col > n, at.up, at.down)
            return jnp.where(jnp.logical_and(col < n, to == col), 4, col), to

        def fold_near(k, j):
            col = order[j]
            n_copy(k, 1, col).wait_recv()
            n_copy(k, 2, col).wait_recv()
            fold(k, 0, j, near_in[k].at[0, col], near_in[k].at[1, col])

        def along(k, j):
            col = order[j]
            fold_near(k, j)

            @pl.when(at.carried(col))
            def _():
                z_copy(k, col, col, at.up).wait_recv()
                add(held[k].at[0, col], shapes[k][0], z_in[k].at[col])

            slot, to = line_slot(col)
            z_copy(k, col, slot, to).start()

        def last(k):
            fold_near(k, 0)
            outs[k][...] = held[k][0, n].astype(FULL)

            @pl.when(n > 0)
            def _():
                z_copy(k, n, n, at.up).wait_recv()
                outs[k][...] += z_in[k][n].astype(FULL)

            @pl.when(n < 3)
            def _():
                z_copy(k, n, 4, at.up).wait_recv()
                outs[k][...] += z_in[k][4].astype(FULL)

        def drain(k):
            for chip in range(4):
                for col in range(4):
                    c_copy(k, chip, col).wait_send()
            for j in range(4):
                d_copy(k, j).wait_send()
                n_copy(k, 1, j).wait_send()
                n_copy(k, 2, j).wait_send()
            for j in range(1, 4):
                z_copy(k, order[j], order[j], at.up).wait_send()

        if self.line:
            line_held, line_in, line_send, line_recv = scratch[5 * count + 9 :]
            self.line_held = line_held

            def line_copy(p, col, slot, to):
                sems = line_send.at[p, col], line_recv.at[p, slot]
                return remote(line_held.at[p, col], line_in.at[p, slot], *sems, (w, to))

            def line_stage(j, p):
                col = order[j]

                @pl.when(at.carried(col))
                def _():
                    line_copy(p, col, col, at.up).wait_recv()
                    add(line_held.at[p, col], PIECE, line_in.at[p, col])

                slot, to = line_slot(col)
                line_copy(p, col, slot, to).start()

            def line_last(p):
                here = pl.ds(p * PIECE, PIECE)
                outs[count][here, :] = line_held[p, n].astype(FULL)

                @pl.when(n > 0)
                def _():
                    line_copy(p, n, n, at.up).wait_recv()
                    outs[count][here, :] += line_in[p, n].astype(FULL)

                @pl.when(n < 3)
                def _():
                    line_copy(p, n, 4, at.up).wait_recv()
                    outs[count][here, :] += line_in[p, 4].astype(FULL)

            def line_drain():
                for p in range(PIECES):
                    for j in range(1, 4):
                        line_copy(p, order[j], order[j], at.up).wait_send()

        items = Feed(at.enter)
        for k in range(count):
            items.add(begin, k)
            for j in (1, 3, 0, 2):
                items.add(far, k, j)
            for j in (3, 2, 1, 0):
                items.add(near, k, j)
                items.add(near_far, k, j)
            for j in (3, 2, 1):
                items.add(along, k, j)
            items.add(last, k)
            items.drain(drain, k)
        if self.line:
            for j in (3, 2, 1):
                for p in range(PIECES):
                    items.add(line_stage, j, p)
            for p in range(PIECES):
                items.add(line_last, p)
            items.add(lambda: None)
            items.drain(line_drain)
        return items


def fused(script, args, outs, engine, moved, name):
    in_specs = [SCALARS.spec() if k == A.live else pl.BlockSpec(memory_space=pl.ANY) for k in args]
    counts = [len(args), len(outs), len(engine.out_specs)]

    def kernel(*refs):
        groups = []
        for count in counts:
            groups.append(refs[:count])
            refs = refs[count:]
        named = dict(zip(list(args) + list(outs), groups[0] + groups[1]))
        feed = engine.steps([named[k] for k in moved], groups[2], refs)
        script(named, groups[2], feed)

    results = pl.pallas_call(
        kernel,
        in_specs=in_specs,
        out_specs=[pl.BlockSpec(memory_space=pl.ANY)] * len(outs) + engine.out_specs,
        out_shape=list(outs.values()) + engine.out_shape,
        scratch_shapes=engine.scratch,
        compiler_params=pltpu.CompilerParams(
            collective_id=engine.collective_id, has_side_effects=True, vmem_limit_bytes=62 * 2**20
        ),
        cost_estimate=pl.CostEstimate(flops=100_000_000_000, bytes_accessed=0, transcendentals=0),
        name=name,
    )(*args.values())
    return dict(zip(outs, results)), list(results[len(outs) :])


class Joined:
    def __init__(self, engine, other):
        self.engine, self.other = engine, other
        self.collective_id = engine.collective_id
        self.out_specs = engine.out_specs + other.out_specs
        self.out_shape = engine.out_shape + other.out_shape
        self.scratch = engine.scratch + other.scratch

    def steps(self, ins, outs, scratch):
        cuts = len(ins) - self.other.takes, len(self.engine.out_specs), len(self.engine.scratch)
        feed = self.engine.steps(ins[: cuts[0]], outs[: cuts[1]], scratch[: cuts[2]])
        for step in self.other.steps(ins[cuts[0] :], outs[cuts[1] :], scratch[cuts[2] :]):
            feed.add(step)
        feed.enter = Place().enter_all
        return feed


STRIP = 768


def strips(b, q):
    return b * 2 + q


class Modulation:
    takes = 4

    def __init__(self):
        self.out_shape = [shape((2, 6 * D), FULL)] * 2 + [shape((16, 128), FULL)]
        self.out_specs = [pl.BlockSpec(memory_space=pl.ANY)] * 2
        self.out_specs += [pl.BlockSpec(memory_space=pltpu.VMEM)]
        self.scratch = [
            pltpu.VMEM((8, 8, 128), FULL),
            pltpu.VMEM((8, 128), FULL),
            pltpu.VMEM((2, 128, 2 * STRIP), LOW),
            pltpu.VMEM((8, 8, STRIP), FULL),
            pltpu.VMEM((8, 8, STRIP), FULL),
            pltpu.VMEM((4, 8, STRIP), FULL),
            pltpu.VMEM((2, 2, 6 * D), FULL),
            DMA((3, 8)),
            DMA((3, 8)),
            DMA((6,)),
        ]

    def steps(self, ins, outs, scratch):
        at = Place()
        w, n = at.w, at.n
        images, clips, *shards = ins
        cond, clip, held, terms, arrived, got, made, send, recv, local = scratch

        def across(stage, step, src, dst):
            to = (lax.bitwise_xor(w, step), n)
            return remote(src, dst, send.at[stage, step], recv.at[stage, step], to)

        def first(step):
            return across(0, step, images.at[lax.bitwise_xor(w, step)], cond.at[w])

        def second(step):
            return across(1, step, terms.at[lax.bitwise_xor(w, step)], arrived.at[w])

        def third(step):
            to = (w, lax.bitwise_xor(n, step))
            return remote(got.at[n], got.at[n], send.at[2, step], recv.at[2, step], to)

        def loads():
            return [
                pltpu.make_async_copy(images.at[w], cond.at[w], local.at[0]),
                pltpu.make_async_copy(clips, clip, local.at[1]),
                pltpu.make_async_copy(shards[0], held.at[0], local.at[2]),
                pltpu.make_async_copy(shards[1], held.at[1], local.at[3]),
            ]

        def stores():
            return [
                pltpu.make_async_copy(made.at[b], outs[b], local.at[4 + b]) for b in range(2)
            ]

        def start():
            for copy in loads():
                copy.start()
            for step in range(1, 8):
                first(step).start()

        def project():
            for copy in loads():
                copy.wait()
            for step in range(1, 8):
                first(step).wait_recv()
            flat = jnp.concatenate([cond[:, 0, :], clip[...]], axis=0).astype(LOW)
            outs[2][8:16, :] = cond[:, 0, :]
            for g in range(8):
                outs[2][g : g + 1, :] = clip[g // 4 : g // 4 + 1, :]
            for b in range(2):
                product = nn(flat, held[b])
                for g in range(8):
                    for r, row in enumerate((8 + g // 4, g)):
                        for q in range(2):
                            to = r * 4 + strips(b, q)
                            terms[g, to : to + 1, :] = product[row : row + 1, q * STRIP : (q + 1) * STRIP]
            for step in range(1, 8):
                second(step).start()

        def total():
            value = terms[w]
            for step in range(1, 8):
                second(step).wait_recv()
                value = value + arrived[lax.bitwise_xor(w, step)]
            got[n] = value
            for step in range(1, 4):
                third(step).start()

        def spread():
            for step in range(1, 4):
                third(step).wait_recv()
            for col in range(4):
                for b in range(2):
                    for r in range(2):
                        for q in range(2):
                            here = r * 4 + strips(b, q)
                            to = col * 2 * STRIP + q * STRIP
                            made[b, r : r + 1, to : to + STRIP] = got[col, here : here + 1, :]
            for copy in stores():
                copy.start()

        def settle():
            for copy in stores():
                copy.wait()
            for step in range(1, 8):
                first(step).wait_send()
                second(step).wait_send()
            for step in range(1, 4):
                third(step).wait_send()

        return start, project, total, spread, settle


class ModulationBack:
    takes = 0

    def __init__(self):
        self.out_shape = [shape((128, 2 * STRIP), FULL)] * 2
        self.out_specs = [pl.BlockSpec(memory_space=pltpu.VMEM)] * 2
        self.scratch = [
            pltpu.VMEM((4, 8, STRIP), FULL),
            pltpu.VMEM((4, 8, STRIP), FULL),
            pltpu.VMEM((8, 8, STRIP), FULL),
            pltpu.VMEM((2, 2, 6 * D), FULL),
            pltpu.VMEM((16, 128), FULL),
            DMA((2, 8)),
            DMA((2, 8)),
            DMA((5,)),
        ]

    def steps(self, ins, outs, scratch):
        at = Place()
        w, n = at.w, at.n
        pieces, arrived, every, grads, cond, send, recv, local = scratch

        def along(step):
            to = (w, lax.bitwise_xor(n, step))
            src = pieces.at[lax.bitwise_xor(n, step)]
            return remote(src, arrived.at[n], send.at[0, step], recv.at[0, step], to)

        def across(step):
            to = (lax.bitwise_xor(w, step), n)
            return remote(every.at[w], every.at[w], send.at[1, step], recv.at[1, step], to)

        def begin():
            cond_ref, early, late = self.sources
            copies = [pltpu.make_async_copy(cond_ref, cond, local.at[4])]
            for b in range(2):
                cut = pl.ds(2 * D, 4 * D)
                here = grads.at[b, :, pl.ds(0, 2 * D)]
                copies.append(pltpu.make_async_copy(early[b], here, local.at[2 * b]))
                here = grads.at[b, :, cut]
                copies.append(pltpu.make_async_copy(late[b].at[:, cut], here, local.at[2 * b + 1]))
            for copy in copies:
                copy.start()
            for copy in copies:
                copy.wait()
            for col in range(4):
                for b in range(2):
                    for r in range(2):
                        for q in range(2):
                            to = r * 4 + strips(b, q)
                            here = col * 2 * STRIP + q * STRIP
                            pieces[col, to : to + 1, :] = grads[b, r : r + 1, here : here + STRIP]
            for step in range(1, 4):
                along(step).start()

        def finish():
            value = pieces[n]
            for step in range(1, 4):
                along(step).wait_recv()
                value = value + arrived[lax.bitwise_xor(n, step)]
            every[w] = value
            for step in range(1, 8):
                across(step).start()
            for step in range(1, 8):
                across(step).wait_recv()
            for b in range(2):
                for q in range(2):
                    rows = [every[:, r * 4 + strips(b, q), :] for r in range(2)]
                    outs[b][:, q * STRIP : (q + 1) * STRIP] = lax.dot_general(
                        cond[...],
                        jnp.concatenate(rows, axis=0),
                        (((0,), (0,)), ((), ())),
                        precision=lax.Precision.HIGHEST,
                        preferred_element_type=FULL,
                    )
            for step in range(1, 4):
                along(step).wait_send()
            for step in range(1, 8):
                across(step).wait_send()

        return begin, finish


TILES = 32
JOINT_TILES = 18


def thirds(value):
    high = value.astype(LOW)
    rest = value - high.astype(FULL)
    middle = rest.astype(LOW)
    return high, middle, (rest - middle.astype(FULL)).astype(LOW)


def gathered_by(value, pattern):
    first = half_mask()
    zero = jnp.zeros_like(value)
    both = jnp.concatenate([jnp.where(first, value, zero), jnp.where(first, zero, value)], axis=0)
    parts = [nn(part, pattern) for part in thirds(both)]
    return parts[0] + (parts[1] + parts[2])


class BiasBack:
    takes = 2

    def __init__(self):
        self.out_shape = [shape((TILES, 8, 256), FULL)]
        self.out_specs = [pl.BlockSpec(memory_space=pltpu.VMEM)]
        gaps = HEADS // 2 * (2 * TW - 1)
        self.scratch = [
            pltpu.VMEM((CHUNK, gaps, 128), FULL),
            pltpu.VMEM((2 * SW, 8, 2, SW, 128), FULL),
            pltpu.VMEM((2 * gaps, 256), FULL),
            pltpu.VMEM((2, 8, 2 * SW, 256), FULL),
            pltpu.VMEM((TILES, 8, 256), FULL),
            pltpu.VMEM((8, 4, 8, 256), FULL),
            pltpu.VMEM((4, 4, 8, 256), FULL),
            DMA((CHUNK + 2 * SW,)),
            DMA((3, 8)),
            DMA((3, 8)),
        ]

    def steps(self, ins, outs, scratch):
        at = Place()
        w, n = at.w, at.n
        joint_grad, space_grad = ins
        (result,) = outs
        joint_rows, space_rows, joint_sum, space_sum, tiles, groups, line, local, send, recv = scratch
        query = lax.broadcasted_iota(jnp.int32, (128, 256), 0) % CHUNK
        column = lax.broadcasted_iota(jnp.int32, (128, 256), 1)

        def load(k):
            if k < CHUNK:
                return pltpu.make_async_copy(joint_grad.at[:, k, :], joint_rows.at[k], local.at[k])
            k -= CHUNK
            src = space_grad.at[:, :, k // SW, :, k % SW, :]
            return pltpu.make_async_copy(src, space_rows.at[k], local.at[CHUNK + k])

        def start():
            joint_sum[...] = jnp.zeros_like(joint_sum)
            space_sum[...] = jnp.zeros_like(space_sum)
            tiles[...] = jnp.zeros_like(tiles)
            for k in range(CHUNK + 2 * SW):
                load(k).start()

        def joint_part(part):
            for k in range(part * SW, (part + 1) * SW):
                load(k).wait()

            @pl.loop(0, SW)
            def _(col):
                to = (query // SW - part + SW - 1) * SPAN_T + query % SW - col + SW - 1
                pattern = jnp.where(column == to, 1.0, 0.0).astype(LOW)
                joint_sum[...] += gathered_by(joint_rows[part * SW + col], pattern)

        def space_part(part):
            for k in range(CHUNK + part * 4, CHUNK + part * 4 + 4):
                load(k).wait()

            @pl.loop(0, 4)
            def _(i):
                col = part * 4 + i
                to = query // SW * SPAN_S + lax.rem(n, 2) * SW + query % SW - col + 2 * SW - 1
                pattern = jnp.where(column == to, 1.0, 0.0).astype(LOW)
                value = gathered_by(space_rows[col].reshape(128, 128), pattern)
                space_sum[...] += value.reshape(2, 8, 2 * SW, 256)

        def across(stage, step, src, dst):
            to = (lax.bitwise_xor(w, step), n)
            return remote(src, dst, send.at[stage, step], recv.at[stage, step], to)

        def first(step):
            src = tiles.at[span(lax.bitwise_xor(w, step), 4)]
            return across(0, step, src, groups.at[w])

        def second(step):
            to = (w, lax.bitwise_xor(n, step))
            return remote(line.at[n], line.at[n], send.at[1, step], recv.at[1, step], to)

        def third(step):
            here = result.at[span(w, 4)]
            return across(2, step, here, here)

        def settle():
            for t in range(JOINT_TILES):
                tiles[t] = joint_sum[t * 8 : (t + 1) * 8, :]
            for half in range(2):
                total = jnp.zeros((8, 1024), FULL)
                for row in range(2 * SW):
                    here = space_sum[half, :, row, :]
                    here = jnp.concatenate([here, jnp.zeros((8, 768), FULL)], axis=1)
                    total = total + pltpu.roll(here, (2 * SW - 1 - row) * SPAN_S, 1)
                moved = pltpu.roll(total, SW * SPAN_S, 1)
                total = jnp.where(n >= 2, moved, total)
                for q in range(4):
                    tiles[JOINT_TILES + half * 4 + q] = total[:, q * 256 : (q + 1) * 256]
            for step in range(1, 8):
                first(step).start()

        def sum_groups():
            value = tiles[span(w, 4)]
            for step in range(1, 8):
                first(step).wait_recv()
                value = value + groups[lax.bitwise_xor(w, step)]
            line[n] = value
            for step in range(1, 4):
                second(step).start()

        def sum_line():
            for step in range(1, 4):
                second(step).wait_recv()
            result[span(w, 4)] = (line[0] + line[1]) + (line[2] + line[3])
            for step in range(1, 8):
                third(step).start()

        def done():
            for step in range(1, 8):
                third(step).wait_recv()
            for step in range(1, 8):
                first(step).wait_send()
                third(step).wait_send()
            for step in range(1, 4):
                second(step).wait_send()

        made = [start] + [functools.partial(joint_part, p) for p in range(SW)]
        made += [functools.partial(space_part, p) for p in range(4)]
        return made + [settle, sum_groups, sum_line, done]


def bias_tables(tiles):
    gaps = 2 * TW - 1
    joint = tiles[:JOINT_TILES].reshape(2, HEADS // 2, gaps, 256)[..., : SPAN_T**2]
    space = tiles[JOINT_TILES : JOINT_TILES + 8].reshape(2, 4, 8, 256)
    space = space.transpose(2, 0, 1, 3).reshape(HEADS, 1024)[:, : SPAN_S**2]
    return space, joint.transpose(1, 0, 2, 3).reshape(HEADS, -1)


FORWARD_ENDS = (
    0, 13, 125, 1, 4, 104, 109, 114, 119, 14, 17, 5, 2, 26, 126, 8, 18, 27, 21, 15, 39, 127, 9, 3,
    6, 40, 30, 22, 107, 31, 28, 19, 16, 128, 10, 43, 112, 7, 108, 44, 23, 41, 65, 66, 34, 11, 12,
    35, 117, 32, 122, 52, 20, 53, 36, 47, 113, 24, 48, 25, 118, 45, 69, 70, 123, 49, 56, 57, 29,
    105, 110, 115, 120, 129, 73, 74, 106, 60, 61, 111, 33, 116, 37, 121, 124, -1, 38, 67, 91, -1,
    -1, 71, 92, -1, -1, -1, -1, -1, 95, 42, 75, -1, -1, -1, 54, 78, -1, 96, -1, -1, -1, 79, -1, 99,
    68, -1, -1, -1, 55, -1, 46, -1, -1, -1, 58, 93, -1, -1, -1, -1, -1, -1, -1, -1, 82, 80, -1, -1,
    -1, -1, -1, -1, -1, -1, -1, -1, 100, 94, -1, -1, -1, -1, -1, -1, -1, 83, 81, 50, 72, 51, -1,
    62, 59, -1, -1, 97, -1, -1, -1, 86, -1, -1, -1, 84, -1, -1, -1, 98, -1, 76, -1, 77, -1, 63, 87,
    -1, 64, -1, 101, 85, -1, -1, 88, -1, -1, -1, 102, -1, -1, 103, -1, -1, -1, -1, 89, -1, -1, -1,
    90, -1, -1, -1, -1, -1, -1, -1, -1, -1, -1, -1, -1, -1, -1, -1, -1, -1, -1, -1, -1, -1, -1, -1,
    -1, -1, -1, -1, -1, -1, -1, -1,
)
FORWARD_MIDDLES = (
    0, 13, 125, 1, 2, 4, 104, 26, 126, 14, 15, 109, 17, 3, 5, 106, 39, 127, 6, 114, 107, 119, 8,
    111, 28, 16, 30, 128, 116, 18, 19, 21, 112, 121, 7, 108, 10, 9, 27, 41, 65, 43, 40, 23, 117,
    32, 11, 20, 12, 122, 52, 34, 22, 113, 66, 31, 118, 45, 69, 123, 36, 124, 24, 47, 25, 53, 29,
    105, 129, 110, 115, 120, 67, 44, 91, -1, 56, -1, 42, 49, 70, -1, -1, -1, 54, 78, 68, 35, -1,
    73, -1, -1, 55, -1, 57, -1, -1, -1, -1, 93, -1, 33, -1, 71, -1, -1, 80, -1, -1, 48, -1, -1, -1,
    -1, -1, 95, -1, -1, -1, -1, -1, -1, 60, -1, -1, -1, -1, -1, -1, -1, -1, -1, -1, -1, 46, -1, -1,
    74, -1, -1, -1, -1, -1, 58, 37, 75, 82, 38, 92, 72, 59, 94, 61, 50, 51, -1, 79, 62, 97, -1, -1,
    84, -1, 76, 81, -1, 77, 63, 99, -1, 64, -1, -1, 86, -1, -1, -1, 96, -1, -1, -1, 101, 98, -1,
    -1, -1, 88, 83, -1, -1, 85, -1, -1, 102, 100, -1, 103, -1, -1, -1, -1, 89, 87, -1, -1, -1, 90,
    -1, -1, -1, -1, -1, -1, -1, -1, -1, -1, -1, -1, -1, -1, -1, -1, -1, -1, -1, -1, -1, -1, -1, -1,
    -1, -1, -1, -1, -1, -1, -1, -1, -1,
)
BACK_JOINT_ENDS = (
    -1, -1, -1, -1, -1, -1, -1, -1, -1, -1, -1, -1, -1, -1, -1, -1, -1, -1, -1, -1, -1, -1, -1, -1,
    -1, -1, -1, -1, -1, -1, -1, -1, 0, -1, 1, 2, 3, 4, 5, 17, -1, 18, -1, 19, 6, 20, 7, 21, 22, 34,
    8, 35, 9, 36, 10, 37, 11, 38, 12, 39, -1, -1, -1, -1, -1, -1, -1, 13, 23, 24, -1, -1, -1, -1,
    -1, -1, -1, -1, -1, 14, 25, 26, 27, 28, 29, -1, -1, -1, -1, -1, 40, 41, -1, -1, 15, -1, 42, 43,
    44, 45, 46, -1, -1, 30, -1, 16, -1, -1, -1, 31, -1, -1, -1, 51, 32, 52, 53, 54, 55, -1, 56, 47,
    48, 49, -1, 33, -1, -1, -1, 57, 58, -1, -1, -1, 50, 59, 60, 61, 62, 63, -1, -1, 64, -1, -1, -1,
    65, -1, -1, -1, 66, -1, -1, -1, -1, -1, -1, -1, -1, 67, -1, -1, -1, -1, -1, -1, -1, -1,
)
BACK_JOINT_MIDDLES = (
    -1, -1, -1, -1, -1, -1, -1, -1, -1, -1, -1, -1, -1, -1, -1, -1, -1, -1, -1, -1, -1, -1, -1, -1,
    -1, -1, -1, -1, -1, -1, -1, -1, 0, -1, 1, 2, 3, 4, 5, 17, -1, 18, -1, 19, 6, 20, 7, 21, 22, 34,
    8, 35, 9, 36, 10, 37, 11, 38, 12, 39, -1, -1, -1, -1, -1, -1, -1, 23, 24, -1, -1, -1, -1, -1,
    -1, 13, -1, -1, -1, 25, 26, 27, 28, 29, -1, -1, -1, -1, -1, 40, 14, 41, -1, -1, 15, 42, 43, 44,
    45, 46, -1, -1, -1, -1, 16, -1, -1, -1, -1, 30, -1, -1, 51, 31, 52, 32, 53, 54, 55, 56, -1, -1,
    -1, 33, 47, -1, 48, -1, 57, 49, 58, 50, -1, -1, 59, 60, 61, 62, 63, -1, -1, -1, -1, -1, -1, -1,
    -1, 64, -1, -1, -1, 65, -1, 66, -1, -1, -1, 67, -1, -1, -1, -1, -1, -1, -1, -1, -1, -1,
)
BACK_SPACE_ENDS = (
    0, -1, 1, 2, 3, 4, 5, -1, -1, -1, -1, -1, 6, 7, -1, -1, -1, -1, 8, 9, 10, 11, 17, 12, 18, 13,
    19, 20, 21, -1, 22, -1, -1, 14, -1, -1, -1, -1, -1, 15, -1, -1, -1, -1, -1, -1, -1, 23, 16, 24,
    -1, 68, 69, 70, 71, 25, 26, 27, 28, 34, 29, 35, 30, 36, 37, 38, 39, -1, 31, -1, 72, 73, 74, 75,
    32, -1, -1, 76, 77, 78, 79, 40, 41, 42, 43, 44, 45, 46, -1, 47, 48, 49, -1, 80, 81, -1, -1, -1,
    82, -1, -1, -1, -1, -1, 83, 84, -1, -1, -1, 33, -1, 51, 87, 52, 88, 53, 89, 54, 90, 55, 91, 56,
    92, 57, 93, 58, 94, 59, 95, 60, 96, 61, 97, 62, 98, 63, 99, 64, 100, 65, 101, 66, -1, 50, 102,
    85, 103, 86, 67,
)
BACK_SPACE_MIDDLES = (
    0, -1, 1, 2, 3, 4, 5, -1, -1, -1, -1, -1, 6, 7, -1, -1, -1, -1, 8, 9, 10, 11, 17, 12, 18, -1,
    19, 20, 21, 22, -1, -1, -1, -1, 13, -1, -1, -1, -1, 14, -1, -1, 15, -1, -1, -1, -1, 16, 23, 24,
    -1, 25, 26, 27, 28, 34, 29, 35, 36, 37, 38, 39, -1, 68, -1, -1, -1, 69, -1, 76, 70, -1, 40, 77,
    41, 42, 43, 44, 45, 46, 71, -1, 78, -1, 30, -1, -1, -1, -1, 79, 31, -1, -1, -1, 32, -1, 72, -1,
    -1, 51, 87, 73, 52, 74, 88, 53, 75, 89, 54, 90, 55, 33, 91, 56, 92, 57, 80, 93, 58, 94, 59, 81,
    95, 60, 96, 61, 82, 97, 62, 98, 63, 83, 99, 47, 84, 100, 48, 101, 49, -1, 50, 64, 102, 85, 65,
    103, 66, 86, 67,
)


def exact(left, right, dims):
    return lax.dot_general(
        left, right, (dims, ((), ())), precision=lax.Precision.HIGHEST, preferred_element_type=FULL
    )


def joint_pattern():
    keys, queries = np.meshgrid(np.arange(CHUNK), np.arange(CHUNK), indexing="ij")
    at = (queries // SW - keys // SW + SW - 1) * SPAN_T + queries % SW - keys % SW + SW - 1
    return (jnp.arange(SPAN_T**2)[:, None] == jnp.asarray(at.reshape(-1), jnp.int32)[None, :]).astype(FULL)


def joint_table(lookup):
    flat = lookup.reshape(HEADS * (2 * TW - 1), SPAN_T**2)
    grid = exact(flat, joint_pattern(), ((1,), (0,)))
    grid = grid.reshape(HEADS // 2, 2, 2 * TW - 1, CHUNK, CHUNK)
    return jnp.concatenate([grid[:, 0], grid[:, 1]], axis=-1)


def joint_table_back(grad):
    grad = grad.reshape(HEADS // 2, 2 * TW - 1, CHUNK, 2 * CHUNK)
    pairs = jnp.stack([grad[..., :CHUNK], grad[..., CHUNK:]], axis=1)
    flat = pairs.reshape(HEADS * (2 * TW - 1), CHUNK * CHUNK)
    return exact(flat, joint_pattern(), ((1,), (1,))).reshape(HEADS, -1)


def space_pattern(quarter):
    query = jnp.arange(CHUNK)
    key_col = jnp.arange(2 * SW)
    gap = quarter % 2 * SW + (query % SW)[None, :] - key_col[:, None] + 2 * SW - 1
    row = jnp.broadcast_to((query // SW)[None, :], gap.shape)
    at = (row * SPAN_S + gap).reshape(-1)
    return (jnp.arange(SW * SPAN_S)[:, None] == at[None, :]).astype(FULL)


def space_table(lookup, quarter):
    grid = lookup.reshape(HEADS, SPAN_S, SPAN_S)
    seen = lax.dynamic_slice_in_dim(grid, quarter // 2 * SW, 3 * SW - 1, 1)
    rows = jnp.stack([seen[:, 2 * SW - 1 - k : 3 * SW - 1 - k] for k in range(2 * SW)])
    made = exact(rows.reshape(2 * SW * HEADS, SW * SPAN_S), space_pattern(quarter), ((1,), (0,)))
    made = made.reshape(2, SW, HEADS // 2, 2, 2, SW, CHUNK)
    made = made.transpose(2, 0, 4, 1, 5, 3, 6)
    return made.reshape(HEADS // 2, 4 * CHUNK, 2 * CHUNK)


def space_table_back(grad, quarter):
    made = grad.reshape(HEADS // 2, 2, 2, SW, SW, 2, CHUNK).transpose(1, 3, 0, 5, 2, 4, 6)
    flat = made.reshape(2 * SW * HEADS, 2 * SW * CHUNK)
    rows = exact(flat, space_pattern(quarter), ((1,), (1,))).reshape(2 * SW, HEADS, SW, SPAN_S)
    seen = sum(
        jnp.pad(rows[k], ((0, 0), (2 * SW - 1 - k, k), (0, 0))) for k in range(2 * SW)
    )
    grid = jnp.zeros((HEADS, SPAN_S, SPAN_S), FULL)
    return lax.dynamic_update_slice_in_dim(grid, seen, quarter // 2 * SW, 1).reshape(HEADS, -1)


def modulations(cond, shards):
    groups = cond.shape[0]
    rows = shards[0].shape[0]
    own = lax.dynamic_slice_in_dim(cond, lax.axis_index("wide") * rows, rows, 2)
    flat = own.reshape(groups * 2, rows)
    terms = jnp.stack([nn(flat, s).reshape(groups, 2, -1) for s in shards], axis=1)
    summed = lax.psum_scatter(terms, "wide", scatter_dimension=0, tiled=False)
    gathered = lax.all_gather(summed, "narrow", axis=0, tiled=False)
    return gathered.transpose(1, 2, 0, 3).reshape(2, 2, 6 * D)


def modulation_grads(cond, grads, rows):
    groups = cond.shape[0]
    own = lax.dynamic_slice_in_dim(cond, lax.axis_index("wide") * rows, rows, 2)
    flat = own.reshape(groups * 2, rows).astype(FULL)
    summed = lax.psum_scatter(
        grads.reshape(2, 2, 4, -1), "narrow", scatter_dimension=2, tiled=False
    )
    gathered = lax.all_gather(summed, "wide", axis=0, tiled=False)
    return [exact(flat, gathered[:, b].reshape(groups * 2, -1), ((0,), (0,))) for b in range(2)]


def gather_flat(shards):
    wide, narrow = lax.axis_size("wide"), lax.axis_size("narrow")
    project, output, expand, shrink = shards
    rows = project.shape[0]

    def settle(blocks):
        rows, cols = blocks.shape[-2:]
        blocks = blocks.reshape(wide, narrow, rows, cols).transpose(0, 2, 1, 3)
        return blocks.reshape(wide * rows, narrow * cols)

    first = lax.all_gather(
        jnp.concatenate([project, output, expand], axis=1), ("wide", "narrow"), axis=0, tiled=False
    )
    second = lax.all_gather(shrink, ("wide", "narrow"), axis=0, tiled=False)
    a, b = project.shape[1], project.shape[1] + output.shape[1]
    return settle(first[..., :a]), settle(first[..., a:b]), settle(first[..., b:]), settle(second)


def scatter_plain(partials):
    outs = []
    for g in partials:
        summed = lax.psum_scatter(g, "wide", scatter_dimension=0, tiled=True)
        outs.append(lax.psum_scatter(summed, "narrow", scatter_dimension=1, tiled=True).astype(FULL))
    return outs


def saved(b):
    return b.branch, b.middle, b.normed, b.active, b.slope, b.reduced


def mlp_takes(b):
    return A.live, b.rows, b.attended, b.mods, b.output, b.expand, b.shrink


def back_takes(b, grad):
    early = A.live, grad, b.attended, b.mods, b.branch, b.middle, b.normed, b.reduced
    return early + (b.output, b.active, b.slope, b.expand, b.shrink)


def back_gives(b):
    return b.to_shrink, b.to_expand, b.to_output, b.to_middle, b.to_attended, b.late


def weights_of(b):
    return b.project, b.output, b.expand, b.shrink


def shards_of(b):
    return b.own_project, b.own_output, b.own_expand, b.own_shrink


def partials_of(b):
    return b.to_shrink, b.to_expand, b.to_output, b.to_project


def grads_of(b):
    return b.grad_shrink, b.grad_expand, b.grad_output, b.grad_project


def stages():
    return {
        S.triple: (
            space_triple(),
            (A.all_rows, S.mods, S.project),
            (S.first, S.queries, S.pairs),
        ),
        S.attend: (
            space_attend(),
            (S.queries, S.pairs, S.pairs, S.table),
            (S.attended,),
        ),
        S.mlp: (
            mlp(False),
            mlp_takes(S),
            saved(S) + (J.rows,),
        ),
        J.triple: (
            joint_triple(),
            (J.rows, J.mods, J.project),
            (J.first, J.three),
        ),
        J.attend: (
            joint_attend(),
            (J.three,) * 3 + (J.table,),
            (J.attended,),
        ),
        J.mlp: (
            mlp(True),
            mlp_takes(J),
            saved(J) + (A.output_tokens,),
        ),
        J.mlp_back: (
            mlp_back(True),
            back_takes(J, A.cotangent),
            back_gives(J),
        ),
        J.attend_back: (
            joint_attend_back(),
            (J.three,) * 3 + (J.table, J.to_attended),
            (J.to_three, J.to_table),
        ),
        J.project_back: (
            joint_project_back(),
            (J.rows, J.mods, J.first, J.to_middle, J.project, J.to_three),
            (J.to_project, J.to_rows, J.early),
        ),
        S.mlp_back: (
            mlp_back(False),
            back_takes(S, J.to_rows),
            back_gives(S),
        ),
        S.attend_back: (
            space_attend_back(),
            (S.queries, S.pairs, S.pairs, S.table, S.to_attended),
            (S.to_queries, S.to_pairs, S.to_table),
        ),
        S.project_back: (
            space_project_back(),
            (S.first, S.project, S.to_queries, S.to_pairs),
            (S.to_project, A.to_first),
        ),
        S.weight_back: (
            space_weight_back(),
            (S.first, S.to_queries, S.to_pairs),
            (S.to_project,),
        ),
        A.finish: (
            finish(),
            (S.rows, S.mods, A.own_first, S.to_middle),
            (A.grad_tokens, S.early),
        ),
    }


def apart(values, names):
    for name in names:
        phase, takes, gives = stages()[name]
        values.update(zip(gives, phase(*[values[k] for k in takes])))


def together(values, plan, tables, engine, moved, brought, name, more=(), prepare=None, inline={}):
    table = stages()
    outs, args = {}, {}
    steps = [k for k in plan if k not in inline]
    for phase_name in steps:
        phase, takes, gives = table[phase_name]
        outs.update(zip(gives, phase.out_shape))
    for phase_name in steps:
        for k in table[phase_name][1]:
            if k not in outs and k not in brought:
                args[k] = values[k]
    for k in tuple(moved) + tuple(more):
        if k not in outs:
            args[k] = values[k]

    def script(refs, engine_outs, feed):
        refs.update(zip(brought, engine_outs))
        if prepare is not None:
            prepare(refs)
        feed.follow(tables)
        feed.enter()
        for phase_name in plan:
            if phase_name in inline:
                feed.do(feed.slot)
                inline[phase_name](refs, feed)
                continue
            phase, takes, gives = table[phase_name]
            phase.inside(feed.over(phase), [refs[k] for k in takes], [refs[k] for k in gives])
        feed.rest()

    made, arrived = fused(script, args, outs, engine, moved, name)
    values.update(made)
    values.update(zip(brought, arrived))


def body(
    tokens,
    clip_cond,
    image_cond,
    image_count,
    space_modulate,
    space_project,
    space_output,
    space_expand,
    space_reduce,
    space_bias,
    joint_modulate,
    joint_project,
    joint_output,
    joint_expand,
    joint_reduce,
    joint_bias,
    cotangent,
):
    small = lax.axis_size("wide") == 8
    narrow = lax.axis_index("narrow")
    wide = lax.axis_index("wide")
    rows = space_modulate.shape[0]
    low_clips = jax.nn.silu(clip_cond.astype(FULL)).astype(LOW)
    low_images = jax.nn.silu(image_cond.astype(FULL)).astype(LOW)
    values = {
        A.live: (image_count > 0).astype(FULL),
        S.rows: tokens,
        A.cotangent: cotangent,
        S.table: space_table(space_bias, narrow),
        J.table: joint_table(joint_bias),
    }
    weights = weights_of(S) + weights_of(J)
    space_shards = space_project, space_output, space_expand, space_reduce
    joint_shards = joint_project, joint_output, joint_expand, joint_reduce

    if small:
        moved = shards_of(S) + shards_of(J)
        shapes = [v.shape for v in space_shards + joint_shards]
        values.update(zip(moved, space_shards + joint_shards))
        values[A.images] = jnp.broadcast_to(low_images.astype(FULL).reshape(8, 1, rows), (8, 8, rows))
        own_clips = lax.dynamic_slice_in_dim(low_clips, wide * rows, rows, 1).astype(FULL)
        values[A.clips] = jnp.pad(own_clips, ((0, 6), (0, 0)))
        values[S.own_modulate] = space_modulate
        values[J.own_modulate] = joint_modulate
        gather = Gather(shapes, True, 0)
        together(
            values,
            FORWARD,
            (FORWARD_ENDS, FORWARD_MIDDLES),
            Joined(gather, Modulation()),
            moved + (S.rows, A.images, A.clips, S.own_modulate, J.own_modulate),
            weights + (A.all_rows, S.mods, J.mods, A.cond),
            "forward",
        )
        project_shape, output_shape, expand_shape, shrink_shape = shapes[:4]
        shapes = [shrink_shape, expand_shape, output_shape, project_shape]
        engine = Scatter(shapes, False, 1)
        tables = BACK_JOINT_ENDS, BACK_JOINT_MIDDLES
        together(values, BACK_JOINT, tables, engine, partials_of(J), grads_of(J), "back_joint")
        back = ModulationBack()
        engine = Scatter(shapes, True, 2)

        def first_back(refs, feed):
            takes = refs[S.project], refs[S.to_queries], refs[S.to_pairs]
            space_first_back(feed, 8, Place().order, *takes, engine.line_held)

        def prepare(refs):
            early = refs[S.early], refs[J.early]
            back.sources = refs[A.cond], early, (refs[S.late], refs[J.late])

        together(
            values,
            BACK_SPACE,
            (BACK_SPACE_ENDS, BACK_SPACE_MIDDLES),
            Joined(Joined(engine, back), BiasBack()),
            partials_of(S) + (J.to_table, S.to_table),
            grads_of(S) + (A.own_first, S.modulate, J.modulate, A.bias),
            "back_space",
            (A.cond, S.late, J.early, J.late, S.project),
            prepare,
            {A.first_back: first_back},
        )
        modulate = values[S.modulate], values[J.modulate]
        bias = bias_tables(values[A.bias])
    else:
        image_all = lax.all_gather(low_images, "wide", axis=0, tiled=True)
        cond = jnp.stack([jnp.repeat(low_clips, 4, axis=0), image_all], axis=1)
        values[S.mods], values[J.mods] = modulations(
            cond, (space_modulate, joint_modulate)
        )
        values.update(zip(weights[:4], gather_flat(space_shards)))
        values.update(zip(weights[4:], gather_flat(joint_shards)))
        values[A.all_rows] = lax.all_gather(tokens, "narrow", axis=0, tiled=True)
        apart(values, FORWARD + BACK_JOINT + (S.attend_back, S.project_back))
        for b in (J, S):
            values.update(zip(grads_of(b), scatter_plain([values[k] for k in partials_of(b)])))
        values[A.own_first] = lax.psum_scatter(
            values[A.to_first].astype(FULL), "narrow", scatter_dimension=0, tiled=True
        )
        apart(values, [A.finish])
        both = [
            jnp.concatenate([values[b.early], values[b.late][:, 2 * D :]], axis=1) for b in (S, J)
        ]
        modulate = modulation_grads(cond, jnp.stack(both), rows)
        space_grad = space_table_back(values[S.to_table], narrow)
        grads = jnp.concatenate([space_grad, joint_table_back(values[J.to_table])], axis=1)
        bias = lax.psum(grads, ("wide", "narrow"))
        split = space_bias.shape[1]
        bias = bias[:, :split], bias[:, split:]
    outs = [values[A.output_tokens], values[A.grad_tokens]]
    for i, b in enumerate((S, J)):
        outs += [modulate[i]] + [values[k] for k in reversed(grads_of(b))] + [bias[i]]
    return tuple(outs)


FORWARD = S.triple, S.attend, S.mlp, J.triple, J.attend, J.mlp
BACK_JOINT = J.mlp_back, J.attend_back, J.project_back, S.mlp_back
BACK_SPACE = S.attend_back, A.first_back, S.weight_back, A.finish


def solution(mesh):
    rows = P(("wide", "narrow"), None)
    block = P("wide", "narrow")
    in_specs = (
        (rows, P(), P("wide", None), P("wide"))
        + (block,) * 5
        + (P(),)
        + (block,) * 5
        + (P(), rows)
    )
    out_specs = (rows, rows) + ((block,) * 5 + (P(),)) * 2
    return jax.shard_map(body, mesh=mesh, in_specs=in_specs, out_specs=out_specs, check_vma=False)
```

```python
import functools
import math

import jax
import jax.numpy as jnp
import numpy as np
from jax import lax
from jax.experimental import pallas as pl
from jax.experimental.pallas import tpu as pltpu
from jax.sharding import PartitionSpec as P

D = 1024
HEADS = 16
HEAD_DIM = 64
FF = 4096
SW = 8
TW = 5
CHUNK = SW * SW
CLIP_ROWS = TW * CHUNK
ROWS_DEV = CLIP_ROWS + 4 * CHUNK
SPAN_S = 4 * SW - 1
SPAN_T = 2 * SW - 1
MESH = pl.DeviceIdType.MESH


epsilon = 1e-06


def normalise(values):
    centred = values - jnp.mean(values, axis=-1, keepdims=True)
    spread = jnp.mean(centred * centred, axis=-1, keepdims=True)
    scale = lax.rsqrt(spread + epsilon)
    return centred * scale, scale


def norm_back(unit, scale, grad):
    return scale * (
        grad
        - jnp.mean(grad, axis=-1, keepdims=True)
        - unit * jnp.mean(grad * unit, axis=-1, keepdims=True)
    )


def nn(left, right):
    return lax.dot_general(left, right, (((1,), (0,)), ((), ())), preferred_element_type=jnp.float32)


def nt(left, right):
    return lax.dot_general(left, right, (((1,), (1,)), ((), ())), preferred_element_type=jnp.float32)


def tn(left, right):
    return lax.dot_general(left, right, (((0,), (0,)), ((), ())), preferred_element_type=jnp.float32)


def each_chunk(body, count=ROWS_DEV // CHUNK):
    @pl.loop(0, count)
    def _(i):
        inner = lax.rem(i, ROWS_DEV // CHUNK)
        seq = jnp.where(inner >= CLIP_ROWS // CHUNK, 1, 0)
        body(pl.ds(pl.multiple_of(i * CHUNK, CHUNK), CHUNK), pl.ds(seq, 1))


def part(index):
    return slice(index * D, (index + 1) * D)


class Tiled:
    def __init__(self, block, index):
        self.block, self.index = block, index

    def spec(self):
        return pl.BlockSpec(self.block, self.index)


class Whole:
    def __init__(self, block):
        self.block = block

    def spec(self):
        rank = len(self.block)
        return pl.BlockSpec(self.block, lambda *_: (0,) * rank, pipeline_mode=pl.Buffered(1))


class Scalars:
    def spec(self):
        return pl.BlockSpec(memory_space=pltpu.SMEM)


SCALARS = Scalars()
whole, spec = Whole, Tiled


def params(limit=56):
    return pltpu.CompilerParams(vmem_limit_bytes=limit * 2**20)


def shape(dims, kind):
    return jax.ShapeDtypeStruct(dims, kind)


LOW = jnp.bfloat16
FULL = jnp.float32


class Phase:
    def __init__(self, kernel, *, grid, in_specs, out_specs, out_shape, name, ticks=1, scratch_shapes=()):
        self.kernel, self.grid, self.name, self.ticks = kernel, grid, name, ticks
        self.in_specs, self.out_specs, self.out_shape = in_specs, out_specs, out_shape
        self.scratch = list(scratch_shapes)

    def __call__(self, *args):
        return pl.pallas_call(
            functools.partial(self.kernel, lambda t: None),
            grid=self.grid,
            in_specs=[s.spec() for s in self.in_specs],
            out_specs=[s.spec() for s in self.out_specs],
            out_shape=self.out_shape,
            scratch_shapes=self.scratch,
            compiler_params=params(),
            name=self.name,
        )(*args)

    def inside(self, tick, ins, outs):
        specs = list(self.in_specs) + list(self.out_specs)
        refs = list(ins) + list(outs)
        first_out = len(ins)
        held = [i for i, s in enumerate(specs) if isinstance(s, Whole)]
        tiled = [i for i, s in enumerate(specs) if isinstance(s, Tiled)]

        def scoped(buffers, scratch, sems):
            place = dict(zip(held, buffers))
            loads = [
                pltpu.make_async_copy(refs[i], place[i], sems.at[at])
                for at, i in enumerate(held)
                if i < first_out
            ]
            for load in loads:
                load.start()
            for load in loads:
                load.wait()

            def body(*blocks):
                now = dict(zip(tiled, blocks))
                now.update(place)
                operands = [now.get(i, refs[i]) for i in range(len(refs))]
                self.kernel(tick, *operands, *scratch)

            pltpu.emit_pipeline(
                body,
                grid=self.grid,
                in_specs=[specs[i].spec() for i in tiled if i < first_out],
                out_specs=[specs[i].spec() for i in tiled if i >= first_out],
            )(*[refs[i] for i in tiled])
            stores = [
                pltpu.make_async_copy(place[i], refs[i], sems.at[at])
                for at, i in enumerate(held)
                if i >= first_out
            ]
            for store in stores:
                store.start()
            for store in stores:
                store.wait()

        kinds = [refs[i].dtype for i in held]
        pl.run_scoped(
            scoped,
            [pltpu.VMEM(specs[i].block, kind) for i, kind in zip(held, kinds)],
            self.scratch,
            pltpu.SemaphoreType.DMA((len(held),)),
        )


def space_triple_kernel(tick, rows, mods, weight, normed, queries, pairs):
    step = pl.program_id(0)

    @pl.when(step == 0)
    def _():
        def chunk(at, seq):
            unit, _ = normalise(rows[at, :].astype(FULL))
            normed[at, :] = (unit * (1.0 + mods[seq, part(1)]) + mods[seq, part(0)]).astype(LOW)

        each_chunk(chunk, 4 * ROWS_DEV // CHUNK)

    tick(0)

    @pl.when(step < 2)
    def _():
        own = span(lax.axis_index("narrow"), ROWS_DEV)
        queries[...] = nn(normed[own, :], weight[...]).astype(LOW)

    for q in range(4):
        if q:
            tick(q)

        @pl.when(step >= 2)
        def _():
            pairs[q] = nn(normed[q * ROWS_DEV : (q + 1) * ROWS_DEV, :], weight[...]).astype(LOW)


def space_triple():
    tile = 512
    return Phase(
        space_triple_kernel,
        grid=(3 * D // tile,),
        in_specs=[
            whole((4 * ROWS_DEV, D)),
            whole((2, 6 * D)),
            spec((D, tile), lambda t: (0, t)),
        ],
        out_specs=[
            whole((4 * ROWS_DEV, D)),
            spec((ROWS_DEV, tile), lambda t: (0, jnp.minimum(t, 1))),
            spec((4, ROWS_DEV, tile), lambda t: (0, 0, jnp.maximum(t - 2, 0))),
        ],
        out_shape=[
            shape((4 * ROWS_DEV, D), LOW),
            shape((ROWS_DEV, D), LOW),
            shape((4, ROWS_DEV, 2 * D), LOW),
        ],
        name="space_triple",
        ticks=4,
    )


def space_triple_parts(feed, ticks, order, own_rows, all_rows, mods, weight, first, queries, pairs):
    tile = 512
    slot = feed.slot
    feed.slot += ticks

    def scoped(weights, modulation, rows, normed, made, sems):
        loads = [
            pltpu.make_async_copy(weight, weights, sems.at[0]),
            pltpu.make_async_copy(mods, modulation, sems.at[1]),
        ]
        for load in loads:
            load.start()
        stores = []
        at_slot = slot
        for j in range(4):
            side = j % 2
            here = span(order[j], ROWS_DEV)
            if j:
                feed.do(at_slot)
            source = all_rows.at[here] if j else own_rows
            fetch = pltpu.make_async_copy(source, rows.at[side], sems.at[2 + j])
            fetch.start()
            if j == 0:
                for load in loads:
                    load.wait()
            if j >= 2:
                for store in stores[j - 2]:
                    store.wait()
            fetch.wait()

            def chunk(at, seq):
                unit, _ = normalise(rows[side, at, :].astype(FULL))
                value = unit * (1.0 + modulation[seq, part(1)]) + modulation[seq, part(0)]
                normed[side, at, :] = value.astype(LOW)

            each_chunk(chunk)
            stores.append([pltpu.make_async_copy(normed.at[side], first.at[here], sems.at[6 + j])])
            stores[j][0].start()
            for t in range(2 if j else 0, 3 * D // tile):
                if t > (2 if j else 0):
                    feed.do(at_slot)
                at_slot += 1
                columns = slice(t * tile, (t + 1) * tile)
                made[side, :, columns] = nn(normed[side], weights[:, columns]).astype(LOW)
            out = made.at[side, :, pl.ds(D, 2 * D)]
            stores[j].append(pltpu.make_async_copy(out, pairs.at[order[j]], sems.at[10 + j]))
            if j == 0:
                out = made.at[0, :, pl.ds(0, D)]
                stores[j].append(pltpu.make_async_copy(out, queries, sems.at[14]))
            for store in stores[j][1:]:
                store.start()
        for store in stores[2] + stores[3]:
            store.wait()

    pl.run_scoped(
        scoped,
        pltpu.VMEM((D, 3 * D), LOW),
        pltpu.VMEM((2, 6 * D), FULL),
        pltpu.VMEM((2, ROWS_DEV, D), LOW),
        pltpu.VMEM((2, ROWS_DEV, D), LOW),
        pltpu.VMEM((2, ROWS_DEV, 3 * D), LOW),
        pltpu.SemaphoreType.DMA((15,)),
    )


def joint_triple_kernel(tick, rows, mods, weight, normed, triple):
    @pl.when(pl.program_id(0) == 0)
    def _():
        def chunk(at, seq):
            unit, _ = normalise(rows[at, :])
            normed[at, :] = (unit * (1.0 + mods[seq, part(1)]) + mods[seq, part(0)]).astype(LOW)

        each_chunk(chunk)

    tick(0)
    triple[...] = nn(normed[...], weight[...]).astype(LOW)


def joint_triple():
    tile = 512
    return Phase(
        joint_triple_kernel,
        grid=(3 * D // tile,),
        in_specs=[whole((ROWS_DEV, D)), whole((2, 6 * D)), spec((D, tile), lambda t: (0, t))],
        out_specs=[whole((ROWS_DEV, D)), spec((ROWS_DEV, tile), lambda t: (0, t))],
        out_shape=[shape((ROWS_DEV, D), LOW), shape((ROWS_DEV, 3 * D), LOW)],
        name="joint_triple",
        ticks=1,
    )


def half_mask():
    return lax.broadcasted_iota(jnp.int32, (1, 2 * HEAD_DIM), 1) < HEAD_DIM


def split_heads(rows):
    first = half_mask()
    zero = jnp.zeros_like(rows)
    return jnp.concatenate([jnp.where(first, rows, zero), jnp.where(first, zero, rows)], axis=0)


def join_heads(stacked):
    return jnp.where(half_mask(), stacked[:CHUNK], stacked[CHUNK:])


def softmax_keys(keys, queries, bias):
    scores = nt(keys, queries) * HEAD_DIM**-0.5 + bias
    powered = jnp.exp(scores - jnp.max(scores, axis=0, keepdims=True))
    return powered / jnp.sum(powered, axis=0, keepdims=True)


def attend(queries, keys, values, bias):
    probs = softmax_keys(keys, split_heads(queries), bias)
    return join_heads(tn(values, probs.astype(LOW)).T).astype(LOW)


def attend_back(queries, keys, values, bias, grad):
    queries, grad = split_heads(queries), split_heads(grad)
    probs = softmax_keys(keys, queries, bias)
    grad_values = nn(probs.astype(LOW), grad)
    grad_probs = nt(values, grad)
    centre = jnp.sum(probs * grad_probs, axis=0, keepdims=True)
    grad_scores = (probs * (grad_probs - centre)).astype(LOW)
    grad_queries = join_heads(tn(keys, grad_scores).T) * HEAD_DIM**-0.5
    grad_keys = nn(grad_scores, queries) * HEAD_DIM**-0.5
    return grad_queries, grad_keys, grad_values, grad_scores.astype(FULL)


def space_attend_kernel(tick, queries, keys, values, bias, out):
    table = bias[0]
    for i in range(ROWS_DEV // CHUNK):
        if i % 3 == 0:
            tick(i // 3)
        at = slice(i * CHUNK, (i + 1) * CHUNK)
        key_rows = keys[:, at, :].reshape(4 * CHUNK, 2 * HEAD_DIM)
        value_rows = values[:, at, :].reshape(4 * CHUNK, 2 * HEAD_DIM)
        out[at, :] = attend(queries[at, :], key_rows, value_rows, table)


def space_attend():
    wide = 2 * HEAD_DIM
    return Phase(
        space_attend_kernel,
        grid=(HEADS // 2,),
        in_specs=[
            spec((ROWS_DEV, wide), lambda h: (0, h)),
            spec((4, ROWS_DEV, wide), lambda h: (0, 0, h)),
            spec((4, ROWS_DEV, wide), lambda h: (0, 0, h + HEADS // 2)),
            spec((1, 4 * CHUNK, wide), lambda h: (h, 0, 0)),
        ],
        out_specs=[spec((ROWS_DEV, wide), lambda h: (0, h))],
        out_shape=[shape((ROWS_DEV, D), LOW)],
        name="space_attend",
        ticks=3,
    )


def space_attend_back_kernel(tick, queries, keys, values, bias, grad, grad_q, grad_pairs, grad_bias):
    table = bias[0]
    for i in range(ROWS_DEV // CHUNK):
        if i % 3 == 0:
            tick(i // 3)
        at = slice(i * CHUNK, (i + 1) * CHUNK)
        key_rows = keys[:, at, :].reshape(4 * CHUNK, 2 * HEAD_DIM)
        value_rows = values[:, at, :].reshape(4 * CHUNK, 2 * HEAD_DIM)
        to_q, to_k, to_v, to_bias = attend_back(
            queries[at, :], key_rows, value_rows, table, grad[at, :]
        )
        grad_q[at, :] = to_q.astype(LOW)
        grad_pairs[0, :, at, :] = to_k.astype(LOW).reshape(4, CHUNK, 2 * HEAD_DIM)
        grad_pairs[1, :, at, :] = to_v.astype(LOW).reshape(4, CHUNK, 2 * HEAD_DIM)
        to_bias = to_bias.reshape(2, 2, SW, SW, 2 * HEAD_DIM)
        if i == 0:
            grad_bias[0] = to_bias
        else:
            grad_bias[0] += to_bias


def space_attend_back():
    wide = 2 * HEAD_DIM
    head = spec((ROWS_DEV, wide), lambda h: (0, h))
    four = spec((4, ROWS_DEV, wide), lambda h: (0, 0, h))
    table = spec((1, 4 * CHUNK, wide), lambda h: (h, 0, 0))
    return Phase(
        space_attend_back_kernel,
        grid=(HEADS // 2,),
        in_specs=[
            head,
            four,
            spec((4, ROWS_DEV, wide), lambda h: (0, 0, h + HEADS // 2)),
            table,
            head,
        ],
        out_specs=[
            head,
            spec((2, 4, ROWS_DEV, wide), lambda h: (0, 0, 0, h)),
            spec((1, 2, 2, SW, SW, wide), lambda h: (h, 0, 0, 0, 0, 0)),
        ],
        out_shape=[
            shape((ROWS_DEV, D), LOW),
            shape((2, 4, ROWS_DEV, D), LOW),
            shape((HEADS // 2, 2, 2, SW, SW, wide), FULL),
        ],
        name="space_attend_back",
        ticks=3,
    )


def clip_table(bias, frame):
    return jnp.concatenate([bias[0, frame - t + TW - 1] for t in range(TW)], axis=0)


def joint_attend_kernel(tick, queries, keys, values, bias, out):
    for i in range(ROWS_DEV // CHUNK):
        if i % 3 == 0:
            tick(i // 3)
        at = slice(i * CHUNK, (i + 1) * CHUNK)
        seen = slice(0, CLIP_ROWS) if i < TW else at
        table = clip_table(bias, i) if i < TW else bias[0, TW - 1]
        out[at, :] = attend(queries[at, :], keys[seen, :], values[seen, :], table)


def joint_specs():
    wide = 2 * HEAD_DIM
    return [
        spec((ROWS_DEV, wide), lambda h: (0, h)),
        spec((ROWS_DEV, wide), lambda h: (0, h + HEADS // 2)),
        spec((ROWS_DEV, wide), lambda h: (0, h + HEADS)),
        spec((1, 2 * TW - 1, CHUNK, wide), lambda h: (h, 0, 0, 0)),
    ]


def joint_attend():
    return Phase(
        joint_attend_kernel,
        grid=(HEADS // 2,),
        in_specs=joint_specs(),
        out_specs=[spec((ROWS_DEV, 2 * HEAD_DIM), lambda h: (0, h))],
        out_shape=[shape((ROWS_DEV, D), LOW)],
        name="joint_attend",
        ticks=3,
    )


def joint_attend_back_kernel(
    tick, queries, keys, values, bias, grad, grads, grad_bias, sum_k, sum_v
):
    grad_bias[...] = jnp.zeros_like(grad_bias)
    for i in range(ROWS_DEV // CHUNK):
        if i % 3 == 0:
            tick(i // 3)
        at = slice(i * CHUNK, (i + 1) * CHUNK)
        seen = slice(0, CLIP_ROWS) if i < TW else at
        table = clip_table(bias, i) if i < TW else bias[0, TW - 1]
        to_q, to_k, to_v, to_bias = attend_back(
            queries[at, :], keys[seen, :], values[seen, :], table, grad[at, :]
        )
        grads[0, at, :] = to_q.astype(LOW)
        if i >= TW:
            grad_bias[TW - 1] += to_bias
            grads[1, at, :] = to_k.astype(LOW)
            grads[2, at, :] = to_v.astype(LOW)
            continue
        for t in range(TW):
            grad_bias[i - t + TW - 1] += to_bias[t * CHUNK : (t + 1) * CHUNK]
        if i == 0:
            sum_k[...] = to_k
            sum_v[...] = to_v
        elif i < TW - 1:
            sum_k[...] += to_k
            sum_v[...] += to_v
        else:
            grads[1, seen, :] = (sum_k[...] + to_k).astype(LOW)
            grads[2, seen, :] = (sum_v[...] + to_v).astype(LOW)


def joint_attend_back():
    wide = 2 * HEAD_DIM
    head = spec((ROWS_DEV, wide), lambda h: (0, h))
    return Phase(
        joint_attend_back_kernel,
        grid=(HEADS // 2,),
        in_specs=joint_specs() + [head],
        out_specs=[
            spec((3, ROWS_DEV, wide), lambda h: (0, 0, h)),
            spec((2 * TW - 1, CHUNK, wide), lambda h: (h, 0, 0)),
        ],
        out_shape=[
            shape((3, ROWS_DEV, D), LOW),
            shape((HEADS // 2 * (2 * TW - 1), CHUNK, wide), FULL),
        ],
        scratch_shapes=[pltpu.VMEM((CLIP_ROWS, wide), FULL)] * 2,
        name="joint_attend_back",
        ticks=3,
    )


def mlp_kernel(last_block, tick, live, rows, attended, mods, output, expand, shrink, *refs):
    branch, middle, normed, active, slope, reduced, result, total = refs
    step = pl.program_id(0)

    @pl.when(step == 0)
    def _():
        def chunk(at, seq):
            grown = nn(attended[at, :], output[...])
            branch[at, :] = grown.astype(LOW)
            mixed = rows[at, :].astype(FULL) + mods[seq, part(2)] * grown
            middle[at, :] = mixed
            unit, _ = normalise(mixed)
            normed[at, :] = (unit * (1.0 + mods[seq, part(4)]) + mods[seq, part(3)]).astype(LOW)

        each_chunk(chunk)
        total[...] = jnp.zeros_like(total)

    tick(0)
    before = nn(normed[...], expand[...])
    inner = 0.5 * (1.0 + lax.erf(before * 0.5**0.5))
    low_active = (before * inner).astype(LOW)
    tick(1)
    active[...] = low_active
    slope[...] = (inner + before * jnp.exp(-0.5 * before * before) * (2.0 * math.pi) ** -0.5).astype(LOW)
    total[...] += nn(low_active, shrink[...])

    @pl.when(step == pl.num_programs(0) - 1)
    def _():
        def chunk(at, seq):
            reduced[at, :] = total[at, :].astype(LOW)
            value = middle[at, :] + mods[seq, part(5)] * total[at, :]
            if last_block:
                value = value * jnp.where(seq.start > 0, live[0], 1.0)
            result[at, :] = value.astype(result.dtype)

        each_chunk(chunk)


def mlp(last_block):
    tile = 512
    square = whole((ROWS_DEV, D))
    strip = spec((ROWS_DEV, tile), lambda f: (0, f))
    return Phase(
        functools.partial(mlp_kernel, last_block),
        grid=(FF // tile,),
        in_specs=[
            SCALARS,
            square,
            square,
            whole((2, 6 * D)),
            whole((D, D)),
            spec((D, tile), lambda f: (0, f)),
            spec((tile, D), lambda f: (f, 0)),
        ],
        out_specs=[square, square, square, strip, strip, square, square],
        out_shape=[
            shape((ROWS_DEV, D), LOW),
            shape((ROWS_DEV, D), FULL),
            shape((ROWS_DEV, D), LOW),
            shape((ROWS_DEV, FF), LOW),
            shape((ROWS_DEV, FF), LOW),
            shape((ROWS_DEV, D), LOW),
            shape((ROWS_DEV, D), LOW if last_block else FULL),
        ],
        scratch_shapes=[pltpu.VMEM((ROWS_DEV, D), FULL)],
        name="mlp",
        ticks=2,
    )


def mlp_back_kernel(first_block, tick, live, *refs):
    (grad_result, attended, mods, branch, middle, normed, reduced, output, active, slope) = refs[:10]
    expand, shrink = refs[10:12]
    grad_shrink, grad_expand, grad_output, grad_middle, grad_attended, grad_mods = refs[12:18]
    grad_reduced, normed_t, total = refs[18:]
    grad_branch = grad_reduced
    step = pl.program_id(0)

    def incoming(at, seq):
        value = grad_result[at, :].astype(FULL)
        if first_block:
            value = value * jnp.where(seq.start > 0, live[0], 1.0)
        return value

    @pl.when(step == 0)
    def _():
        grad_mods[...] = jnp.zeros_like(grad_mods)

        def chunk(at, seq):
            value = incoming(at, seq)
            grad_reduced[at, :] = (mods[seq, part(5)] * value).astype(LOW)
            grad_mods[seq, part(5)] += jnp.sum(
                reduced[at, :].astype(FULL) * value, axis=0, keepdims=True
            )

        each_chunk(chunk)
        total[...] = jnp.zeros_like(total)
        normed_t[...] = normed[...].T

    tick(0)
    grad_active = nt(grad_reduced[...], shrink[...])
    grad_before = (grad_active * slope[...].astype(FULL)).astype(LOW)
    tick(1)
    grad_shrink[...] = tn(active[...], grad_reduced[...]).astype(LOW)
    tick(2)
    grad_expand[...] = nn(normed_t[...], grad_before).astype(LOW)
    tick(3)
    total[...] += nt(grad_before, expand[...])

    @pl.when(step == pl.num_programs(0) - 1)
    def _():
        def chunk(at, seq):
            grad = total[at, :]
            unit, scale = normalise(middle[at, :])
            grad_mods[seq, part(3)] += jnp.sum(grad, axis=0, keepdims=True)
            grad_mods[seq, part(4)] += jnp.sum(unit * grad, axis=0, keepdims=True)
            value = incoming(at, seq) + norm_back(unit, scale, (1.0 + mods[seq, part(4)]) * grad)
            grad_middle[at, :] = value
            grad_mods[seq, part(2)] += jnp.sum(
                branch[at, :].astype(FULL) * value, axis=0, keepdims=True
            )
            grad_branch[at, :] = (mods[seq, part(2)] * value).astype(LOW)

        each_chunk(chunk)
        grad_attended[...] = nt(grad_branch[...], output[...]).astype(LOW)
        grad_output[...] = tn(attended[...], grad_branch[...]).astype(LOW)


def mlp_back(first_block):
    tile = 512
    square = whole((ROWS_DEV, D))
    strip = spec((ROWS_DEV, tile), lambda f: (0, f))
    across = spec((D, tile), lambda f: (0, f))
    down = spec((tile, D), lambda f: (f, 0))
    return Phase(
        functools.partial(mlp_back_kernel, first_block),
        grid=(FF // tile,),
        in_specs=[
            SCALARS,
            square,
            square,
            whole((2, 6 * D)),
            square,
            square,
            square,
            square,
            whole((D, D)),
            strip,
            strip,
            across,
            down,
        ],
        out_specs=[down, across, whole((D, D)), square, square, whole((2, 6 * D))],
        out_shape=[
            shape((FF, D), LOW),
            shape((D, FF), LOW),
            shape((D, D), LOW),
            shape((ROWS_DEV, D), FULL),
            shape((ROWS_DEV, D), LOW),
            shape((2, 6 * D), FULL),
        ],
        scratch_shapes=[
            pltpu.VMEM((ROWS_DEV, D), LOW),
            pltpu.VMEM((D, ROWS_DEV), LOW),
            pltpu.VMEM((ROWS_DEV, D), FULL),
        ],
        name="mlp_back",
        ticks=4,
    )


def finish_rows(rows, grad_normed, grad_middle, mods, grad_rows, grad_mods):
    grad_mods[...] = jnp.zeros_like(grad_mods)

    def chunk(at, seq):
        grad = grad_normed[at, :].astype(FULL)
        unit, scale = normalise(rows[at, :].astype(FULL))
        grad_mods[seq, part(0)] += jnp.sum(grad, axis=0, keepdims=True)
        grad_mods[seq, part(1)] += jnp.sum(unit * grad, axis=0, keepdims=True)
        grad_rows[at, :] = grad_middle[at, :] + norm_back(
            unit, scale, (1.0 + mods[seq, part(1)]) * grad
        )

    each_chunk(chunk)


def joint_project_back_kernel(
    tick, rows, mods, normed, grad_middle, weight, grad, grad_weight, grad_rows, grad_mods, total, normed_t
):
    step = pl.program_id(0)

    @pl.when(step == 0)
    def _():
        total[...] = jnp.zeros_like(total)
        normed_t[...] = normed[...].T

    tick(0)
    grad_weight[...] = nn(normed_t[...], grad[0]).astype(LOW)
    tick(1)
    total[...] += nt(grad[0], weight[...])

    @pl.when(step == pl.num_programs(0) - 1)
    def _():
        finish_rows(rows, total, grad_middle, mods, grad_rows, grad_mods)


def joint_project_back():
    tile = 512
    square = whole((ROWS_DEV, D))
    across = spec((D, tile), lambda t: (0, t))
    return Phase(
        joint_project_back_kernel,
        grid=(3 * D // tile,),
        in_specs=[square, whole((2, 6 * D)), square, square, across, spec((1, ROWS_DEV, tile), lambda t: (t // 2, 0, t % 2))],
        out_specs=[across, square, whole((2, 2 * D))],
        out_shape=[shape((D, 3 * D), LOW), shape((ROWS_DEV, D), FULL), shape((2, 2 * D), FULL)],
        scratch_shapes=[pltpu.VMEM((ROWS_DEV, D), FULL), pltpu.VMEM((D, ROWS_DEV), LOW)],
        name="joint_project_back",
        ticks=2,
    )


def space_project_back_kernel(tick, normed, weight, grad_q, grad_pairs, grad_weight, grad_normed, total):
    step = pl.program_id(0)
    own = span(lax.axis_index("narrow"), ROWS_DEV)

    @pl.when(step == 0)
    def _():
        total[...] = jnp.zeros_like(total)

    tick(0)

    @pl.when(step < 2)
    def _():
        grad_weight[...] = tn(normed[own, :], grad_q[...]).astype(LOW)
        total[own, :] += nt(grad_q[...], weight[...])

    @pl.when(step >= 2)
    def _():
        flat = grad_pairs[0].reshape(4 * ROWS_DEV, grad_pairs.shape[-1])
        grad_weight[...] = tn(normed[...], flat).astype(LOW)

    for q in range(4):
        tick(q + 1)

        @pl.when(step >= 2)
        def _():
            at = slice(q * ROWS_DEV, (q + 1) * ROWS_DEV)
            total[at, :] += nt(grad_pairs[0, q], weight[...])

    @pl.when(step == pl.num_programs(0) - 1)
    def _():
        grad_normed[...] = total[...].astype(LOW)


def space_project_back():
    tile = 512
    across = spec((D, tile), lambda t: (0, t))

    def pair(t):
        late = jnp.maximum(t - 2, 0)
        return (late // 2, 0, 0, late % 2)

    return Phase(
        space_project_back_kernel,
        grid=(3 * D // tile,),
        in_specs=[
            whole((4 * ROWS_DEV, D)),
            across,
            spec((ROWS_DEV, tile), lambda t: (0, jnp.minimum(t, 1))),
            spec((1, 4, ROWS_DEV, tile), pair),
        ],
        out_specs=[across, whole((4 * ROWS_DEV, D))],
        out_shape=[shape((D, 3 * D), LOW), shape((4 * ROWS_DEV, D), LOW)],
        scratch_shapes=[pltpu.VMEM((4 * ROWS_DEV, D), FULL)],
        name="space_project_back",
        ticks=5,
    )


def space_first_back(feed, ticks, order, weight, grad_q, grad_pairs, out):
    half = ROWS_DEV // 2
    first = feed.slot
    feed.slot += ticks

    def scoped(weights, queries, pairs, sems):
        def pair_load(j):
            return pltpu.make_async_copy(
                grad_pairs.at[:, order[j]], pairs.at[(3 - j) % 2], sems.at[(3 - j) % 2]
            )

        loads = [
            pltpu.make_async_copy(weight, weights, sems.at[2]),
            pltpu.make_async_copy(grad_q, queries, sems.at[3]),
        ]
        for load in loads:
            load.start()
        pair_load(3).start()
        for load in loads:
            load.wait()
        for step in range(4):
            j = 3 - step
            if j:
                pair_load(j - 1).start()
            pair_load(j).wait()
            for side in range(2):
                feed.do(first + 2 * step + side)
                rows = slice(side * half, (side + 1) * half)
                value = nt(pairs[step % 2, 0, rows, :], weights[:, part(1)])
                value += nt(pairs[step % 2, 1, rows, :], weights[:, part(2)])
                if j == 0:
                    value += nt(queries[rows, :], weights[:, part(0)])
                for p in range(2):
                    piece = value[p * (half // 2) : (p + 1) * (half // 2)]
                    out[2 * side + p, order[j]] = piece.astype(LOW)

    pl.run_scoped(
        scoped,
        pltpu.VMEM((D, 3 * D), LOW),
        pltpu.VMEM((ROWS_DEV, D), LOW),
        pltpu.VMEM((2, 2, ROWS_DEV, D), LOW),
        pltpu.SemaphoreType.DMA((4,)),
    )


def space_weight_back_kernel(tick, normed, grad_q, grad_pairs, grad_weight):
    step = pl.program_id(0)
    own = span(lax.axis_index("narrow"), ROWS_DEV)
    tick(0)

    @pl.when(step < 2)
    def _():
        grad_weight[...] = tn(normed[own, :], grad_q[...]).astype(LOW)

    for side in range(2):
        if side:
            tick(1)

        @pl.when(step >= 2)
        def _():
            columns = slice(side * 256, (side + 1) * 256)
            flat = grad_pairs[0, :, :, columns].reshape(4 * ROWS_DEV, 256)
            grad_weight[:, columns] = tn(normed[...], flat).astype(LOW)


def space_weight_back():
    tile = 512

    def pair(t):
        late = jnp.maximum(t - 2, 0)
        return (late // 2, 0, 0, late % 2)

    return Phase(
        space_weight_back_kernel,
        grid=(3 * D // tile,),
        in_specs=[
            whole((4 * ROWS_DEV, D)),
            spec((ROWS_DEV, tile), lambda t: (0, jnp.minimum(t, 1))),
            spec((1, 4, ROWS_DEV, tile), pair),
        ],
        out_specs=[spec((D, tile), lambda t: (0, t))],
        out_shape=[shape((D, 3 * D), LOW)],
        name="space_weight_back",
        ticks=2,
    )


def finish_kernel(tick, rows, mods, grad_normed, grad_middle, grad_rows, grad_mods):
    tick(0)
    finish_rows(rows, grad_normed, grad_middle, mods, grad_rows, grad_mods)


def finish():
    square = whole((ROWS_DEV, D))
    return Phase(
        finish_kernel,
        grid=(1,),
        in_specs=[square, whole((2, 6 * D)), square, square],
        out_specs=[square, whole((2, 2 * D))],
        out_shape=[shape((ROWS_DEV, D), FULL), shape((2, 2 * D), FULL)],
        name="finish",
    )


class Place:
    def __init__(self):
        self.w = lax.axis_index("wide")
        self.n = lax.axis_index("narrow")
        self.c = lax.bitwise_xor(self.w, 1)
        self.x = lax.bitwise_xor(self.w, 2)
        self.y = lax.bitwise_xor(self.w, 4)
        self.d = lax.bitwise_xor(self.w, 6)
        self.up = jnp.minimum(self.n + 1, 3)
        self.down = jnp.maximum(self.n - 1, 0)
        self.order = (
            self.n,
            lax.bitwise_xor(self.n, 1),
            jnp.where(self.n < 2, 2, 1),
            jnp.where(self.n < 2, 3, 0),
        )

    def enter(self):
        barrier = pltpu.get_barrier_semaphore()
        for peer in (self.x, self.y, self.c):
            pl.semaphore_signal(barrier, inc=1, device_id=(peer, self.n), device_id_type=MESH)

        @pl.when(self.n > 0)
        def _():
            pl.semaphore_signal(barrier, inc=1, device_id=(self.w, self.n - 1), device_id_type=MESH)

        @pl.when(self.n < 3)
        def _():
            pl.semaphore_signal(barrier, inc=1, device_id=(self.w, self.n + 1), device_id_type=MESH)

        ends = jnp.where(self.n > 0, 1, 0) + jnp.where(self.n < 3, 1, 0)
        pl.semaphore_wait(barrier, 3 + ends)

    def enter_all(self):
        barrier = pltpu.get_barrier_semaphore()
        for step in range(1, 8):
            peer = (lax.bitwise_xor(self.w, step), self.n)
            pl.semaphore_signal(barrier, inc=1, device_id=peer, device_id_type=MESH)
        for step in range(1, 4):
            peer = (self.w, lax.bitwise_xor(self.n, step))
            pl.semaphore_signal(barrier, inc=1, device_id=peer, device_id_type=MESH)
        pl.semaphore_wait(barrier, 10)

    def passes_on(self, col):
        return jnp.logical_or(
            jnp.logical_and(col < self.n, self.n < 3), jnp.logical_and(col > self.n, self.n > 0)
        )

    def carried(self, col):
        return jnp.logical_or(
            jnp.logical_and(col > self.n, self.n > 0), jnp.logical_and(col < self.n, self.n < 3)
        )


def remote(src, dst, send, recv, to):
    return pltpu.make_async_remote_copy(
        src_ref=src, dst_ref=dst, send_sem=send, recv_sem=recv, device_id=to, device_id_type=MESH
    )


def span(index, size):
    return pl.ds(pl.multiple_of(index * size, size), size)


DMA = pltpu.SemaphoreType.DMA
FOLDS = [(3, 1), (3, 3), (3, 0), (3, 2)]
FOLDS += [(2, 3), (1, 3), (2, 2), (1, 2), (1, 1), (2, 1), (1, 0), (2, 0)]
FOLDS += [(0, 3), (0, 2), (0, 1), (0, 0)]
LOADS = 2
PIECES = 4
PIECE = ROWS_DEV // PIECES


class Names:
    def __init__(self, owner):
        self.owner = owner

    def __getattr__(self, name):
        return self.owner, name


A, S, J = Names(0), Names(1), Names(2)


class Feed:
    def __init__(self, enter):
        self.enter, self.steps, self.drains = enter, [], []

    def add(self, function, *args):
        self.steps.append(functools.partial(function, *args))

    def drain(self, function, *args):
        self.drains.append(functools.partial(function, *args))

    def follow(self, tables):
        self.lists = []
        for table in tables:
            parts = [[]]
            for number in table:
                if number < 0:
                    parts.append([])
                else:
                    parts[-1].append(self.steps[number])
            self.lists.append(parts)
        self.slot = 0
        self.at_end = jnp.logical_or(Place().n == 0, Place().n == 3)

    def do(self, slot):
        ends, middles = (parts[slot] for parts in self.lists)

        @pl.when(self.at_end)
        def _():
            for step in ends:
                step()

        @pl.when(jnp.logical_not(self.at_end))
        def _():
            for step in middles:
                step()

    def over(self, phase):
        first, total = self.slot, phase.grid[0]
        self.do(first)
        self.slot += total * phase.ticks

        def tick(t):
            for i in range(total):
                slot = first + i * phase.ticks + t
                if slot > first and any(parts[slot] for parts in self.lists):

                    @pl.when(pl.program_id(0) == i)
                    def _():
                        self.do(slot)

        return tick

    def rest(self):
        self.do(self.slot)
        for step in self.drains:
            step()


class Gather:
    def __init__(self, shapes, line, collective_id):
        self.shapes, self.line, self.collective_id = shapes, line, collective_id
        count, lines = len(shapes), 1 if line else 0
        self.in_specs = [pl.BlockSpec(memory_space=pl.ANY)] * (count + lines)
        self.out_specs = self.in_specs
        self.out_shape = [shape((8 * r, 4 * c), LOW) for r, c in shapes]
        self.out_shape += [shape((4 * ROWS_DEV, D), LOW)] * lines
        self.scratch = [
            DMA((count, 5)),
            DMA((count, 4)),
            DMA((count, 2, 4)),
            DMA((count, 2, 4)),
            DMA((count, 2, 4)),
            DMA((count, 2, 4)),
            DMA((count, 4)),
            DMA((count, 4)),
            DMA((count,)),
        ]
        self.scratch += [DMA((PIECES, 5)), DMA((PIECES, 4)), DMA((PIECES,))] * lines

    def steps(self, ins, outs, scratch):
        at = Place()
        shapes, count = self.shapes, len(self.shapes)
        w, n = at.w, at.n
        shards, fulls = ins[:count], outs[:count]
        z_send, z_recv, x_send, x_recv, y_send, y_recv, c_send, c_recv, own_sem = scratch[:9]

        def block(k, row, col):
            rows, cols = shapes[k]
            return fulls[k].at[span(row, rows), span(col, cols)]

        def z_copy(k, src, col, slot, to):
            return remote(src, block(k, w, col), z_send.at[k, slot], z_recv.at[k, col], (w, to))

        def x_copy(k, src, row, far, col):
            sems = x_send.at[k, far, col], x_recv.at[k, far, col]
            return remote(src, block(k, row, col), *sems, (at.x, n))

        def y_copy(k, src, row, far, col):
            sems = y_send.at[k, far, col], y_recv.at[k, far, col]
            return remote(src, block(k, row, col), *sems, (at.y, n))

        def c_copy(k, chip):
            row = (w, at.x, at.y, at.d)[chip]
            here = fulls[k].at[span(row, shapes[k][0])]
            return remote(here, here, c_send.at[k, chip], c_recv.at[k, chip], (at.c, n))

        def own_copy(k):
            return pltpu.make_async_copy(shards[k], block(k, w, n), own_sem.at[k])

        def own(k):
            @pl.when(n < 3)
            def _():
                z_copy(k, shards[k], n, n, at.up).start()

            @pl.when(n > 0)
            def _():
                z_copy(k, shards[k], n, 4, at.down).start()

            x_copy(k, shards[k], w, 0, n).start()
            y_copy(k, shards[k], w, 0, n).start()
            own_copy(k).start()

        def z_stage(k, j):
            col = at.order[j]
            here = block(k, w, col)
            z_copy(k, here, col, col, at.up).wait_recv()

            @pl.when(at.passes_on(col))
            def _():
                z_copy(k, here, col, col, jnp.where(col < n, at.up, at.down)).start()

            x_copy(k, here, w, 0, col).start()
            y_copy(k, here, w, 0, col).start()

        def near_stage(k, j):
            col = at.order[j]
            from_x = block(k, at.x, col)
            from_y = block(k, at.y, col)
            x_copy(k, from_x, at.x, 0, col).wait_recv()
            if j < 2:
                y_copy(k, from_x, at.x, 1, col).start()
            y_copy(k, from_y, at.y, 0, col).wait_recv()
            if j >= 2:
                x_copy(k, from_y, at.y, 1, col).start()

        def far_stage(k, j):
            col = at.order[j]
            far = block(k, at.d, col)
            (y_copy if j < 2 else x_copy)(k, far, at.d, 1, col).wait_recv()

        def rows_on(k):
            own_copy(k).wait()
            for chip in range(3):
                c_copy(k, chip).start()

        def far_on(k):
            c_copy(k, 3).start()

        def ready(k):
            for chip in range(4):
                c_copy(k, chip).wait_recv()

        def drain(k):
            for j in range(4):
                col = at.order[j]
                here = block(k, w, col)

                @pl.when(at.passes_on(col) if j else n < 3)
                def _():
                    z_copy(k, here, col, col, at.up).wait_send()

                x_copy(k, here, w, 0, col).wait_send()
                y_copy(k, here, w, 0, col).wait_send()
                (y_copy if j < 2 else x_copy)(k, here, w, 1, col).wait_send()
            for chip in range(4):
                c_copy(k, chip).wait_send()

            @pl.when(n > 0)
            def _():
                z_copy(k, shards[k], n, 4, at.down).wait_send()

        if self.line:
            rows, all_rows = ins[count], outs[count]
            t_send, t_recv, t_own = scratch[9:]

            def piece(p, col):
                return all_rows.at[pl.ds(pl.multiple_of(col * ROWS_DEV + p * PIECE, 16), PIECE)]

            def t_copy(p, src, col, slot, to):
                dst = piece(p, col)
                return remote(src, dst, t_send.at[p, slot], t_recv.at[p, col], (w, to))

            def t_own_copy(p):
                here = pl.ds(p * PIECE, PIECE)
                return pltpu.make_async_copy(rows.at[here], piece(p, n), t_own.at[p])

            def t_start(p, late):
                src = rows.at[pl.ds(p * PIECE, PIECE)]
                if not late:
                    t_own_copy(p).start()

                @pl.when(n == 2 if late else n < 2)
                def _():
                    t_copy(p, src, n, n, at.up).start()

                @pl.when(n == 1 if late else n >= 2)
                def _():
                    t_copy(p, src, n, 4, at.down).start()

            def t_stage(p, j):
                col = at.order[j]
                here = piece(p, col)
                t_copy(p, here, col, col, at.up).wait_recv()

                @pl.when(at.passes_on(col))
                def _():
                    t_copy(p, here, col, col, jnp.where(col < n, at.up, at.down)).start()

            def t_drain(p):
                for j in range(4):
                    col = at.order[j]
                    here = piece(p, col)

                    @pl.when(at.passes_on(col) if j else n < 3)
                    def _():
                        t_copy(p, here, col, col, at.up).wait_send()

                @pl.when(n > 0)
                def _():
                    t_copy(p, piece(p, n), n, 4, at.down).wait_send()

            def t_ready():
                for p in range(PIECES):
                    t_own_copy(p).wait()

        items = Feed(at.enter)
        for k in range(count):
            items.add(own, k)
            for j in range(1, 4):
                items.add(z_stage, k, j)
            for j in range(4):
                items.add(near_stage, k, j)
            for j in range(4):
                items.add(far_stage, k, j)
            items.add(rows_on, k)
            items.add(far_on, k)
            items.add(ready, k)
            items.drain(drain, k)
        if self.line:
            for p in range(PIECES):
                items.add(t_start, p, False)
                items.add(t_start, p, True)
                for j in range(1, 4):
                    items.add(t_stage, p, j)
                items.drain(t_drain, p)
            items.add(t_ready)
        return items


class Scatter:
    def __init__(self, shapes, line, collective_id):
        self.shapes, self.line, self.collective_id = shapes, line, collective_id
        count, lines = len(shapes), 1 if line else 0
        self.out_shape = [shape(s, FULL) for s in shapes] + [shape((ROWS_DEV, D), FULL)] * lines
        self.out_specs = [pl.BlockSpec(memory_space=pltpu.VMEM)] * len(self.out_shape)
        self.scratch = []
        for s in shapes:
            self.scratch += [
                pltpu.VMEM((4, 4) + s, LOW),
                pltpu.VMEM((4,) + s, LOW),
                pltpu.VMEM((2, 4) + s, LOW),
                pltpu.VMEM((5,) + s, LOW),
                pltpu.VMEM((LOADS,) + s, LOW),
            ]
        self.scratch += [
            DMA((count, 4, 4)),
            DMA((count, 4, 4)),
            DMA((count, 4, 4)),
            DMA((count, 4)),
            DMA((count, 4)),
            DMA((count, 2, 4)),
            DMA((count, 2, 4)),
            DMA((count, 4)),
            DMA((count, 5)),
        ]
        self.scratch += [
            pltpu.VMEM((PIECES, 4, PIECE, D), LOW),
            pltpu.VMEM((PIECES, 5, PIECE, D), LOW),
            DMA((PIECES, 4)),
            DMA((PIECES, 5)),
        ] * lines

    def steps(self, ins, outs, scratch):
        at = Place()
        shapes, count = self.shapes, len(self.shapes)
        w, n, order = at.w, at.n, at.order
        chips = (w, at.x, at.y, at.d)
        held, far_in, near_in, z_in, staged = (scratch[i : 5 * count : 5] for i in range(5))
        load, c_send, c_recv, d_send, d_recv, n_send, n_recv, z_send, z_recv = scratch[
            5 * count : 5 * count + 9
        ]

        def source(k, row, col):
            rows, cols = shapes[k]
            return ins[k].at[span(row, rows), span(col, cols)]

        def load_copy(k, chip, j):
            slot = FOLDS.index((chip, j)) % LOADS
            return pltpu.make_async_copy(
                source(k, chips[chip], order[j]), staged[k].at[slot], load.at[k, chip, j]
            )

        def c_copy(k, chip, col):
            src = source(k, lax.bitwise_xor(chips[chip], 1), col)
            sems = c_send.at[k, chip, col], c_recv.at[k, chip, col]
            return remote(src, held[k].at[chip, col], *sems, (at.c, n))

        def d_copy(k, j):
            sems = d_send.at[k, j], d_recv.at[k, j]
            to = (at.x if j < 2 else at.y, n)
            return remote(held[k].at[3, order[j]], far_in[k].at[j], *sems, to)

        def n_copy(k, chip, col):
            sems = n_send.at[k, chip - 1, col], n_recv.at[k, chip - 1, col]
            dst = near_in[k].at[chip - 1, col]
            return remote(held[k].at[chip, col], dst, *sems, (chips[chip], n))

        def z_copy(k, col, slot, to):
            sems = z_send.at[k, col], z_recv.at[k, slot]
            return remote(held[k].at[0, col], z_in[k].at[slot], *sems, (w, to))

        def add(target, rows, *others):
            step = 64 if rows % 64 == 0 else 48

            @pl.loop(0, rows // step)
            def _(i):
                here = span(i, step)
                total = target[here, :]
                for other in others:
                    total = total + other[here, :]
                target[here, :] = total

        def fold(k, chip, j, *others):
            number = FOLDS.index((chip, j))
            load_copy(k, chip, j).wait()
            c_copy(k, chip, order[j]).wait_recv()
            add(held[k].at[chip, order[j]], shapes[k][0], staged[k].at[number % LOADS], *others)
            if number + LOADS < len(FOLDS):
                load_copy(k, *FOLDS[number + LOADS]).start()

        def begin(k):
            for chip, j in FOLDS:
                c_copy(k, chip, order[j]).start()
            for chip, j in FOLDS[:LOADS]:
                load_copy(k, chip, j).start()

        def far(k, j):
            fold(k, 3, j)
            d_copy(k, j).start()

        def near(k, j):
            chip = 2 if j >= 2 else 1
            fold(k, chip, j)
            n_copy(k, chip, order[j]).start()

        def near_far(k, j):
            chip = 1 if j >= 2 else 2
            d_copy(k, j).wait_recv()
            fold(k, chip, j, far_in[k].at[j])
            n_copy(k, chip, order[j]).start()

        def line_slot(col):
            to = jnp.where(col > n, at.up, at.down)
            return jnp.where(jnp.logical_and(col < n, to == col), 4, col), to

        def fold_near(k, j):
            col = order[j]
            n_copy(k, 1, col).wait_recv()
            n_copy(k, 2, col).wait_recv()
            fold(k, 0, j, near_in[k].at[0, col], near_in[k].at[1, col])

        def along(k, j):
            col = order[j]
            fold_near(k, j)

            @pl.when(at.carried(col))
            def _():
                z_copy(k, col, col, at.up).wait_recv()
                add(held[k].at[0, col], shapes[k][0], z_in[k].at[col])

            slot, to = line_slot(col)
            z_copy(k, col, slot, to).start()

        def last(k):
            fold_near(k, 0)
            outs[k][...] = held[k][0, n].astype(FULL)

            @pl.when(n > 0)
            def _():
                z_copy(k, n, n, at.up).wait_recv()
                outs[k][...] += z_in[k][n].astype(FULL)

            @pl.when(n < 3)
            def _():
                z_copy(k, n, 4, at.up).wait_recv()
                outs[k][...] += z_in[k][4].astype(FULL)

        def drain(k):
            for chip in range(4):
                for col in range(4):
                    c_copy(k, chip, col).wait_send()
            for j in range(4):
                d_copy(k, j).wait_send()
                n_copy(k, 1, j).wait_send()
                n_copy(k, 2, j).wait_send()
            for j in range(1, 4):
                z_copy(k, order[j], order[j], at.up).wait_send()

        if self.line:
            line_held, line_in, line_send, line_recv = scratch[5 * count + 9 :]
            self.line_held = line_held

            def line_copy(p, col, slot, to):
                sems = line_send.at[p, col], line_recv.at[p, slot]
                return remote(line_held.at[p, col], line_in.at[p, slot], *sems, (w, to))

            def line_stage(j, p):
                col = order[j]

                @pl.when(at.carried(col))
                def _():
                    line_copy(p, col, col, at.up).wait_recv()
                    add(line_held.at[p, col], PIECE, line_in.at[p, col])

                slot, to = line_slot(col)
                line_copy(p, col, slot, to).start()

            def line_last(p):
                here = pl.ds(p * PIECE, PIECE)
                outs[count][here, :] = line_held[p, n].astype(FULL)

                @pl.when(n > 0)
                def _():
                    line_copy(p, n, n, at.up).wait_recv()
                    outs[count][here, :] += line_in[p, n].astype(FULL)

                @pl.when(n < 3)
                def _():
                    line_copy(p, n, 4, at.up).wait_recv()
                    outs[count][here, :] += line_in[p, 4].astype(FULL)

            def line_drain():
                for p in range(PIECES):
                    for j in range(1, 4):
                        line_copy(p, order[j], order[j], at.up).wait_send()

        items = Feed(at.enter)
        for k in range(count):
            items.add(begin, k)
            for j in (1, 3, 0, 2):
                items.add(far, k, j)
            for j in (3, 2, 1, 0):
                items.add(near, k, j)
                items.add(near_far, k, j)
            for j in (3, 2, 1):
                items.add(along, k, j)
            items.add(last, k)
            items.drain(drain, k)
        if self.line:
            for j in (3, 2, 1):
                for p in range(PIECES):
                    items.add(line_stage, j, p)
            for p in range(PIECES):
                items.add(line_last, p)
            items.add(lambda: None)
            items.drain(line_drain)
        return items


def fused(script, args, outs, engine, moved, name):
    in_specs = [SCALARS.spec() if k == A.live else pl.BlockSpec(memory_space=pl.ANY) for k in args]
    counts = [len(args), len(outs), len(engine.out_specs)]

    def kernel(*refs):
        groups = []
        for count in counts:
            groups.append(refs[:count])
            refs = refs[count:]
        named = dict(zip(list(args) + list(outs), groups[0] + groups[1]))
        feed = engine.steps([named[k] for k in moved], groups[2], refs)
        script(named, groups[2], feed)

    results = pl.pallas_call(
        kernel,
        in_specs=in_specs,
        out_specs=[pl.BlockSpec(memory_space=pl.ANY)] * len(outs) + engine.out_specs,
        out_shape=list(outs.values()) + engine.out_shape,
        scratch_shapes=engine.scratch,
        compiler_params=pltpu.CompilerParams(
            collective_id=engine.collective_id, has_side_effects=True, vmem_limit_bytes=62 * 2**20
        ),
        cost_estimate=pl.CostEstimate(flops=100_000_000_000, bytes_accessed=0, transcendentals=0),
        name=name,
    )(*args.values())
    return dict(zip(outs, results)), list(results[len(outs) :])


class Joined:
    def __init__(self, engine, other):
        self.engine, self.other = engine, other
        self.collective_id = engine.collective_id
        self.out_specs = engine.out_specs + other.out_specs
        self.out_shape = engine.out_shape + other.out_shape
        self.scratch = engine.scratch + other.scratch

    def steps(self, ins, outs, scratch):
        cuts = len(ins) - self.other.takes, len(self.engine.out_specs), len(self.engine.scratch)
        feed = self.engine.steps(ins[: cuts[0]], outs[: cuts[1]], scratch[: cuts[2]])
        for step in self.other.steps(ins[cuts[0] :], outs[cuts[1] :], scratch[cuts[2] :]):
            feed.add(step)
        feed.enter = Place().enter_all
        return feed


STRIP = 768


def strips(b, q):
    return b * 2 + q


class Modulation:
    takes = 4

    def __init__(self):
        self.out_shape = [shape((2, 6 * D), FULL)] * 2 + [shape((16, 128), FULL)]
        self.out_specs = [pl.BlockSpec(memory_space=pl.ANY)] * 2
        self.out_specs += [pl.BlockSpec(memory_space=pltpu.VMEM)]
        self.scratch = [
            pltpu.VMEM((8, 8, 128), FULL),
            pltpu.VMEM((8, 128), FULL),
            pltpu.VMEM((2, 128, 2 * STRIP), LOW),
            pltpu.VMEM((8, 8, STRIP), FULL),
            pltpu.VMEM((8, 8, STRIP), FULL),
            pltpu.VMEM((4, 8, STRIP), FULL),
            pltpu.VMEM((2, 2, 6 * D), FULL),
            DMA((3, 8)),
            DMA((3, 8)),
            DMA((6,)),
        ]

    def steps(self, ins, outs, scratch):
        at = Place()
        w, n = at.w, at.n
        images, clips, *shards = ins
        cond, clip, held, terms, arrived, got, made, send, recv, local = scratch

        def across(stage, step, src, dst):
            to = (lax.bitwise_xor(w, step), n)
            return remote(src, dst, send.at[stage, step], recv.at[stage, step], to)

        def first(step):
            return across(0, step, images.at[lax.bitwise_xor(w, step)], cond.at[w])

        def second(step):
            return across(1, step, terms.at[lax.bitwise_xor(w, step)], arrived.at[w])

        def third(step):
            to = (w, lax.bitwise_xor(n, step))
            return remote(got.at[n], got.at[n], send.at[2, step], recv.at[2, step], to)

        def loads():
            return [
                pltpu.make_async_copy(images.at[w], cond.at[w], local.at[0]),
                pltpu.make_async_copy(clips, clip, local.at[1]),
                pltpu.make_async_copy(shards[0], held.at[0], local.at[2]),
                pltpu.make_async_copy(shards[1], held.at[1], local.at[3]),
            ]

        def stores():
            return [
                pltpu.make_async_copy(made.at[b], outs[b], local.at[4 + b]) for b in range(2)
            ]

        def start():
            for copy in loads():
                copy.start()
            for step in range(1, 8):
                first(step).start()

        def project():
            for copy in loads():
                copy.wait()
            for step in range(1, 8):
                first(step).wait_recv()
            flat = jnp.concatenate([cond[:, 0, :], clip[...]], axis=0).astype(LOW)
            outs[2][8:16, :] = cond[:, 0, :]
            for g in range(8):
                outs[2][g : g + 1, :] = clip[g // 4 : g // 4 + 1, :]
            for b in range(2):
                product = nn(flat, held[b])
                for g in range(8):
                    for r, row in enumerate((8 + g // 4, g)):
                        for q in range(2):
                            to = r * 4 + strips(b, q)
                            terms[g, to : to + 1, :] = product[row : row + 1, q * STRIP : (q + 1) * STRIP]
            for step in range(1, 8):
                second(step).start()

        def total():
            value = terms[w]
            for step in range(1, 8):
                second(step).wait_recv()
                value = value + arrived[lax.bitwise_xor(w, step)]
            got[n] = value
            for step in range(1, 4):
                third(step).start()

        def spread():
            for step in range(1, 4):
                third(step).wait_recv()
            for col in range(4):
                for b in range(2):
                    for r in range(2):
                        for q in range(2):
                            here = r * 4 + strips(b, q)
                            to = col * 2 * STRIP + q * STRIP
                            made[b, r : r + 1, to : to + STRIP] = got[col, here : here + 1, :]
            for copy in stores():
                copy.start()

        def settle():
            for copy in stores():
                copy.wait()
            for step in range(1, 8):
                first(step).wait_send()
                second(step).wait_send()
            for step in range(1, 4):
                third(step).wait_send()

        return start, project, total, spread, settle


class ModulationBack:
    takes = 0

    def __init__(self):
        self.out_shape = [shape((128, 2 * STRIP), FULL)] * 2
        self.out_specs = [pl.BlockSpec(memory_space=pltpu.VMEM)] * 2
        self.scratch = [
            pltpu.VMEM((4, 8, STRIP), FULL),
            pltpu.VMEM((4, 8, STRIP), FULL),
            pltpu.VMEM((8, 8, STRIP), FULL),
            pltpu.VMEM((2, 2, 6 * D), FULL),
            pltpu.VMEM((16, 128), FULL),
            DMA((2, 8)),
            DMA((2, 8)),
            DMA((5,)),
        ]

    def steps(self, ins, outs, scratch):
        at = Place()
        w, n = at.w, at.n
        pieces, arrived, every, grads, cond, send, recv, local = scratch

        def along(step):
            to = (w, lax.bitwise_xor(n, step))
            src = pieces.at[lax.bitwise_xor(n, step)]
            return remote(src, arrived.at[n], send.at[0, step], recv.at[0, step], to)

        def across(step):
            to = (lax.bitwise_xor(w, step), n)
            return remote(every.at[w], every.at[w], send.at[1, step], recv.at[1, step], to)

        def begin():
            cond_ref, early, late = self.sources
            copies = [pltpu.make_async_copy(cond_ref, cond, local.at[4])]
            for b in range(2):
                cut = pl.ds(2 * D, 4 * D)
                here = grads.at[b, :, pl.ds(0, 2 * D)]
                copies.append(pltpu.make_async_copy(early[b], here, local.at[2 * b]))
                here = grads.at[b, :, cut]
                copies.append(pltpu.make_async_copy(late[b].at[:, cut], here, local.at[2 * b + 1]))
            for copy in copies:
                copy.start()
            for copy in copies:
                copy.wait()
            for col in range(4):
                for b in range(2):
                    for r in range(2):
                        for q in range(2):
                            to = r * 4 + strips(b, q)
                            here = col * 2 * STRIP + q * STRIP
                            pieces[col, to : to + 1, :] = grads[b, r : r + 1, here : here + STRIP]
            for step in range(1, 4):
                along(step).start()

        def finish():
            value = pieces[n]
            for step in range(1, 4):
                along(step).wait_recv()
                value = value + arrived[lax.bitwise_xor(n, step)]
            every[w] = value
            for step in range(1, 8):
                across(step).start()
            for step in range(1, 8):
                across(step).wait_recv()
            for b in range(2):
                for q in range(2):
                    rows = [every[:, r * 4 + strips(b, q), :] for r in range(2)]
                    outs[b][:, q * STRIP : (q + 1) * STRIP] = lax.dot_general(
                        cond[...],
                        jnp.concatenate(rows, axis=0),
                        (((0,), (0,)), ((), ())),
                        precision=lax.Precision.HIGHEST,
                        preferred_element_type=FULL,
                    )
            for step in range(1, 4):
                along(step).wait_send()
            for step in range(1, 8):
                across(step).wait_send()

        return begin, finish


TILES = 32
JOINT_TILES = 18


def thirds(value):
    high = value.astype(LOW)
    rest = value - high.astype(FULL)
    middle = rest.astype(LOW)
    return high, middle, (rest - middle.astype(FULL)).astype(LOW)


def gathered_by(value, pattern):
    first = half_mask()
    zero = jnp.zeros_like(value)
    both = jnp.concatenate([jnp.where(first, value, zero), jnp.where(first, zero, value)], axis=0)
    parts = [nn(part, pattern) for part in thirds(both)]
    return parts[0] + (parts[1] + parts[2])


class BiasBack:
    takes = 2

    def __init__(self):
        self.out_shape = [shape((TILES, 8, 256), FULL)]
        self.out_specs = [pl.BlockSpec(memory_space=pltpu.VMEM)]
        gaps = HEADS // 2 * (2 * TW - 1)
        self.scratch = [
            pltpu.VMEM((CHUNK, gaps, 128), FULL),
            pltpu.VMEM((2 * SW, 8, 2, SW, 128), FULL),
            pltpu.VMEM((2 * gaps, 256), FULL),
            pltpu.VMEM((2, 8, 2 * SW, 256), FULL),
            pltpu.VMEM((TILES, 8, 256), FULL),
            pltpu.VMEM((8, 4, 8, 256), FULL),
            pltpu.VMEM((4, 4, 8, 256), FULL),
            DMA((CHUNK + 2 * SW,)),
            DMA((3, 8)),
            DMA((3, 8)),
        ]

    def steps(self, ins, outs, scratch):
        at = Place()
        w, n = at.w, at.n
        joint_grad, space_grad = ins
        (result,) = outs
        joint_rows, space_rows, joint_sum, space_sum, tiles, groups, line, local, send, recv = scratch
        query = lax.broadcasted_iota(jnp.int32, (128, 256), 0) % CHUNK
        column = lax.broadcasted_iota(jnp.int32, (128, 256), 1)

        def load(k):
            if k < CHUNK:
                return pltpu.make_async_copy(joint_grad.at[:, k, :], joint_rows.at[k], local.at[k])
            k -= CHUNK
            src = space_grad.at[:, :, k // SW, :, k % SW, :]
            return pltpu.make_async_copy(src, space_rows.at[k], local.at[CHUNK + k])

        def start():
            joint_sum[...] = jnp.zeros_like(joint_sum)
            space_sum[...] = jnp.zeros_like(space_sum)
            tiles[...] = jnp.zeros_like(tiles)
            for k in range(CHUNK + 2 * SW):
                load(k).start()

        def joint_part(part):
            for k in range(part * SW, (part + 1) * SW):
                load(k).wait()

            @pl.loop(0, SW)
            def _(col):
                to = (query // SW - part + SW - 1) * SPAN_T + query % SW - col + SW - 1
                pattern = jnp.where(column == to, 1.0, 0.0).astype(LOW)
                joint_sum[...] += gathered_by(joint_rows[part * SW + col], pattern)

        def space_part(part):
            for k in range(CHUNK + part * 4, CHUNK + part * 4 + 4):
                load(k).wait()

            @pl.loop(0, 4)
            def _(i):
                col = part * 4 + i
                to = query // SW * SPAN_S + lax.rem(n, 2) * SW + query % SW - col + 2 * SW - 1
                pattern = jnp.where(column == to, 1.0, 0.0).astype(LOW)
                value = gathered_by(space_rows[col].reshape(128, 128), pattern)
                space_sum[...] += value.reshape(2, 8, 2 * SW, 256)

        def across(stage, step, src, dst):
            to = (lax.bitwise_xor(w, step), n)
            return remote(src, dst, send.at[stage, step], recv.at[stage, step], to)

        def first(step):
            src = tiles.at[span(lax.bitwise_xor(w, step), 4)]
            return across(0, step, src, groups.at[w])

        def second(step):
            to = (w, lax.bitwise_xor(n, step))
            return remote(line.at[n], line.at[n], send.at[1, step], recv.at[1, step], to)

        def third(step):
            here = result.at[span(w, 4)]
            return across(2, step, here, here)

        def settle():
            for t in range(JOINT_TILES):
                tiles[t] = joint_sum[t * 8 : (t + 1) * 8, :]
            for half in range(2):
                total = jnp.zeros((8, 1024), FULL)
                for row in range(2 * SW):
                    here = space_sum[half, :, row, :]
                    here = jnp.concatenate([here, jnp.zeros((8, 768), FULL)], axis=1)
                    total = total + pltpu.roll(here, (2 * SW - 1 - row) * SPAN_S, 1)
                moved = pltpu.roll(total, SW * SPAN_S, 1)
                total = jnp.where(n >= 2, moved, total)
                for q in range(4):
                    tiles[JOINT_TILES + half * 4 + q] = total[:, q * 256 : (q + 1) * 256]
            for step in range(1, 8):
                first(step).start()

        def sum_groups():
            value = tiles[span(w, 4)]
            for step in range(1, 8):
                first(step).wait_recv()
                value = value + groups[lax.bitwise_xor(w, step)]
            line[n] = value
            for step in range(1, 4):
                second(step).start()

        def sum_line():
            for step in range(1, 4):
                second(step).wait_recv()
            result[span(w, 4)] = (line[0] + line[1]) + (line[2] + line[3])
            for step in range(1, 8):
                third(step).start()

        def done():
            for step in range(1, 8):
                third(step).wait_recv()
            for step in range(1, 8):
                first(step).wait_send()
                third(step).wait_send()
            for step in range(1, 4):
                second(step).wait_send()

        made = [start] + [functools.partial(joint_part, p) for p in range(SW)]
        made += [functools.partial(space_part, p) for p in range(4)]
        return made + [settle, sum_groups, sum_line, done]


def bias_tables(tiles):
    gaps = 2 * TW - 1
    joint = tiles[:JOINT_TILES].reshape(2, HEADS // 2, gaps, 256)[..., : SPAN_T**2]
    space = tiles[JOINT_TILES : JOINT_TILES + 8].reshape(2, 4, 8, 256)
    space = space.transpose(2, 0, 1, 3).reshape(HEADS, 1024)[:, : SPAN_S**2]
    return space, joint.transpose(1, 0, 2, 3).reshape(HEADS, -1)


FORWARD_ENDS = (
    0, 15, 30, 141, 1, 4, 16, 19, 31, 34, 121, 126, 131, 136, 2, 5, 45, 142, 8, 46, 20, 17, 23,
    120, 143, 125, 130, 135, 32, 35, 75, 3, 38, 6, 122, 76, 9, 127, 49, 132, 50, 10, 24, 21, 137,
    60, 25, 36, 47, 90, 39, 79, 91, 40, 18, 144, 7, 12, 80, 33, 145, 77, 53, 92, 54, 48, 64, 11,
    13, 14, -1, 51, 123, -1, 61, -1, 94, 83, -1, -1, -1, -1, 128, 95, -1, 22, 27, 84, -1, -1, 133,
    55, 37, 42, 81, 138, -1, -1, 26, 28, -1, 96, 29, -1, 124, 41, 43, 85, 52, 57, 44, 129, 68, 100,
    65, 134, 56, 58, 98, 59, 139, 140, -1, -1, -1, 62, 99, 105, -1, -1, -1, 69, -1, -1, 106, -1,
    -1, 78, -1, -1, -1, 66, -1, -1, -1, -1, 63, -1, -1, -1, -1, -1, -1, 109, -1, -1, -1, -1, 93,
    -1, -1, 110, 82, 87, 107, 70, -1, -1, -1, 67, 108, 72, -1, 113, -1, -1, 86, 88, -1, 89, 97,
    102, -1, -1, -1, 114, -1, 71, 73, -1, -1, 74, 111, -1, -1, -1, 112, 101, 117, 103, -1, -1, 115,
    -1, -1, -1, 104, 116, 118, -1, -1, -1, -1, 119, -1, -1, -1, -1, -1, -1, -1, -1, -1, -1, -1, -1,
    -1, -1, -1, -1, -1, -1, -1, -1, -1, -1, -1, -1, -1, -1, -1, -1, -1, -1, -1, -1, -1, -1, -1, -1,
)
FORWARD_MIDDLES = (
    0, 15, 30, 141, 1, 2, 4, 45, 142, 16, 17, 19, 31, 32, 34, 143, 3, 121, 5, 75, 126, 131, 136, 6,
    47, 90, 18, 46, 120, 125, 130, 8, 135, 33, 144, 77, 49, 145, 20, 122, 21, 23, 92, 127, 35, 48,
    132, 36, 123, 10, 38, 137, 60, 76, 128, 7, 12, 9, 133, 79, 61, 138, 51, 91, 94, 124, 22, 27,
    25, 129, 50, 37, 42, 134, 81, 139, 140, 53, 40, 24, 62, 105, 78, 96, 63, 11, 13, 39, 14, -1,
    93, -1, 52, 57, -1, 107, 55, -1, 64, -1, 80, -1, 83, -1, 26, 28, -1, 65, 29, -1, -1, -1, 41,
    85, 95, 43, -1, -1, -1, 44, -1, 98, -1, -1, -1, 54, -1, -1, -1, -1, -1, -1, -1, 66, -1, -1,
    100, -1, -1, -1, -1, -1, -1, -1, -1, -1, 109, -1, -1, 82, 87, -1, -1, -1, -1, 67, 72, 106, 56,
    58, 97, 102, 59, -1, 108, 111, -1, -1, 70, 68, 86, 84, 88, -1, 89, -1, -1, 71, 69, 73, -1, -1,
    74, -1, 99, -1, -1, -1, 101, 113, 103, -1, -1, 104, -1, 110, -1, -1, 115, 112, 117, -1, -1,
    114, -1, -1, 116, 118, -1, -1, 119, -1, -1, -1, -1, -1, -1, -1, -1, -1, -1, -1, -1, -1, -1, -1,
    -1, -1, -1, -1, -1, -1, -1, -1, -1, -1, -1, -1, -1, -1, -1, -1, -1, -1, -1, -1, -1, -1, -1, -1,
)
BACK_JOINT_ENDS = (
    -1, -1, -1, -1, -1, -1, -1, -1, -1, -1, -1, -1, -1, -1, -1, -1, -1, -1, -1, -1, -1, -1, -1, -1,
    -1, -1, -1, -1, -1, -1, -1, -1, 0, -1, 1, 2, 3, 4, 5, 17, -1, 18, -1, 19, 6, 20, 7, 21, 22, 34,
    8, 35, 9, 36, 10, 37, 11, 38, 12, 39, -1, -1, -1, -1, -1, -1, -1, 13, 23, 24, -1, -1, -1, -1,
    -1, -1, -1, -1, -1, 14, 25, 26, 27, 28, 29, -1, -1, -1, -1, -1, 40, 41, -1, -1, 15, -1, 42, 43,
    44, 45, 46, -1, -1, 30, -1, 16, -1, -1, -1, 31, -1, -1, -1, 51, 32, 52, 53, 54, 55, -1, 56, 47,
    48, 49, -1, 33, -1, -1, -1, 57, 58, -1, -1, -1, 50, 59, 60, 61, 62, 63, -1, -1, 64, -1, -1, -1,
    65, -1, -1, -1, 66, -1, -1, -1, -1, -1, -1, -1, -1, 67, -1, -1, -1, -1, -1, -1, -1, -1,
)
BACK_JOINT_MIDDLES = (
    -1, -1, -1, -1, -1, -1, -1, -1, -1, -1, -1, -1, -1, -1, -1, -1, -1, -1, -1, -1, -1, -1, -1, -1,
    -1, -1, -1, -1, -1, -1, -1, -1, 0, -1, 1, 2, 3, 4, 5, 17, -1, 18, -1, 19, 6, 20, 7, 21, 22, 34,
    8, 35, 9, 36, 10, 37, 11, 38, 12, 39, -1, -1, -1, -1, -1, -1, -1, 23, 24, -1, -1, -1, -1, -1,
    -1, 13, -1, -1, -1, 25, 26, 27, 28, 29, -1, -1, -1, -1, -1, 40, 14, 41, -1, -1, 15, 42, 43, 44,
    45, 46, -1, -1, -1, -1, 16, -1, -1, -1, -1, 30, -1, -1, 51, 31, 52, 32, 53, 54, 55, 56, -1, -1,
    -1, 33, 47, -1, 48, -1, 57, 49, 58, 50, -1, -1, 59, 60, 61, 62, 63, -1, -1, -1, -1, -1, -1, -1,
    -1, 64, -1, -1, -1, 65, -1, 66, -1, -1, -1, 67, -1, -1, -1, -1, -1, -1, -1, -1, -1, -1,
)
BACK_SPACE_ENDS = (
    0, -1, 1, 2, 3, 4, 5, -1, -1, -1, -1, -1, 6, 7, -1, -1, -1, -1, 8, 9, 10, 11, 17, 12, 18, 13,
    19, 20, 21, -1, 22, -1, -1, 14, -1, -1, -1, -1, -1, 15, -1, -1, -1, -1, -1, -1, -1, 23, 16, 24,
    -1, 68, 69, 70, 71, 25, 26, 27, 28, 34, 29, 35, 30, 36, 37, 38, 39, -1, 31, -1, 72, 73, 74, 75,
    32, -1, -1, 76, 77, 78, 79, 40, 41, 42, 43, 44, 45, 46, -1, 47, 48, 49, -1, 80, 81, -1, -1, -1,
    82, -1, -1, -1, -1, -1, 83, 84, -1, -1, -1, 33, -1, 51, 87, 52, 88, 53, 89, 54, 90, 55, 91, 56,
    92, 57, 93, 58, 94, 59, 95, 60, 96, 61, 97, 62, 98, 63, 99, 64, 100, 65, 101, 66, -1, 50, 102,
    85, 103, 86, 67,
)
BACK_SPACE_MIDDLES = (
    0, -1, 1, 2, 3, 4, 5, -1, -1, -1, -1, -1, 6, 7, -1, -1, -1, -1, 8, 9, 10, 11, 17, 12, 18, -1,
    19, 20, 21, 22, -1, -1, -1, -1, 13, -1, -1, -1, -1, 14, -1, -1, 15, -1, -1, -1, -1, 16, 23, 24,
    -1, 25, 26, 27, 28, 34, 29, 35, 36, 37, 38, 39, -1, 68, -1, -1, -1, 69, -1, 76, 70, -1, 40, 77,
    41, 42, 43, 44, 45, 46, 71, -1, 78, -1, 30, -1, -1, -1, -1, 79, 31, -1, -1, -1, 32, -1, 72, -1,
    -1, 51, 87, 73, 52, 74, 88, 53, 75, 89, 54, 90, 55, 33, 91, 56, 92, 57, 80, 93, 58, 94, 59, 81,
    95, 60, 96, 61, 82, 97, 62, 98, 63, 83, 99, 47, 84, 100, 48, 101, 49, -1, 50, 64, 102, 85, 65,
    103, 66, 86, 67,
)


def exact(left, right, dims):
    return lax.dot_general(
        left, right, (dims, ((), ())), precision=lax.Precision.HIGHEST, preferred_element_type=FULL
    )


def joint_pattern():
    keys, queries = np.meshgrid(np.arange(CHUNK), np.arange(CHUNK), indexing="ij")
    at = (queries // SW - keys // SW + SW - 1) * SPAN_T + queries % SW - keys % SW + SW - 1
    return (jnp.arange(SPAN_T**2)[:, None] == jnp.asarray(at.reshape(-1), jnp.int32)[None, :]).astype(FULL)


def joint_table(lookup):
    flat = lookup.reshape(HEADS * (2 * TW - 1), SPAN_T**2)
    grid = exact(flat, joint_pattern(), ((1,), (0,)))
    grid = grid.reshape(HEADS // 2, 2, 2 * TW - 1, CHUNK, CHUNK)
    return jnp.concatenate([grid[:, 0], grid[:, 1]], axis=-1)


def joint_table_back(grad):
    grad = grad.reshape(HEADS // 2, 2 * TW - 1, CHUNK, 2 * CHUNK)
    pairs = jnp.stack([grad[..., :CHUNK], grad[..., CHUNK:]], axis=1)
    flat = pairs.reshape(HEADS * (2 * TW - 1), CHUNK * CHUNK)
    return exact(flat, joint_pattern(), ((1,), (1,))).reshape(HEADS, -1)


def space_pattern(quarter):
    query = jnp.arange(CHUNK)
    key_col = jnp.arange(2 * SW)
    gap = quarter % 2 * SW + (query % SW)[None, :] - key_col[:, None] + 2 * SW - 1
    row = jnp.broadcast_to((query // SW)[None, :], gap.shape)
    at = (row * SPAN_S + gap).reshape(-1)
    return (jnp.arange(SW * SPAN_S)[:, None] == at[None, :]).astype(FULL)


def space_table(lookup, quarter):
    grid = lookup.reshape(HEADS, SPAN_S, SPAN_S)
    seen = lax.dynamic_slice_in_dim(grid, quarter // 2 * SW, 3 * SW - 1, 1)
    rows = jnp.stack([seen[:, 2 * SW - 1 - k : 3 * SW - 1 - k] for k in range(2 * SW)])
    made = exact(rows.reshape(2 * SW * HEADS, SW * SPAN_S), space_pattern(quarter), ((1,), (0,)))
    made = made.reshape(2, SW, HEADS // 2, 2, 2, SW, CHUNK)
    made = made.transpose(2, 0, 4, 1, 5, 3, 6)
    return made.reshape(HEADS // 2, 4 * CHUNK, 2 * CHUNK)


def space_table_back(grad, quarter):
    made = grad.reshape(HEADS // 2, 2, 2, SW, SW, 2, CHUNK).transpose(1, 3, 0, 5, 2, 4, 6)
    flat = made.reshape(2 * SW * HEADS, 2 * SW * CHUNK)
    rows = exact(flat, space_pattern(quarter), ((1,), (1,))).reshape(2 * SW, HEADS, SW, SPAN_S)
    seen = sum(
        jnp.pad(rows[k], ((0, 0), (2 * SW - 1 - k, k), (0, 0))) for k in range(2 * SW)
    )
    grid = jnp.zeros((HEADS, SPAN_S, SPAN_S), FULL)
    return lax.dynamic_update_slice_in_dim(grid, seen, quarter // 2 * SW, 1).reshape(HEADS, -1)


def modulations(cond, shards):
    groups = cond.shape[0]
    rows = shards[0].shape[0]
    own = lax.dynamic_slice_in_dim(cond, lax.axis_index("wide") * rows, rows, 2)
    flat = own.reshape(groups * 2, rows)
    terms = jnp.stack([nn(flat, s).reshape(groups, 2, -1) for s in shards], axis=1)
    summed = lax.psum_scatter(terms, "wide", scatter_dimension=0, tiled=False)
    gathered = lax.all_gather(summed, "narrow", axis=0, tiled=False)
    return gathered.transpose(1, 2, 0, 3).reshape(2, 2, 6 * D)


def modulation_grads(cond, grads, rows):
    groups = cond.shape[0]
    own = lax.dynamic_slice_in_dim(cond, lax.axis_index("wide") * rows, rows, 2)
    flat = own.reshape(groups * 2, rows).astype(FULL)
    summed = lax.psum_scatter(
        grads.reshape(2, 2, 4, -1), "narrow", scatter_dimension=2, tiled=False
    )
    gathered = lax.all_gather(summed, "wide", axis=0, tiled=False)
    return [exact(flat, gathered[:, b].reshape(groups * 2, -1), ((0,), (0,))) for b in range(2)]


def gather_flat(shards):
    wide, narrow = lax.axis_size("wide"), lax.axis_size("narrow")
    project, output, expand, shrink = shards
    rows = project.shape[0]

    def settle(blocks):
        rows, cols = blocks.shape[-2:]
        blocks = blocks.reshape(wide, narrow, rows, cols).transpose(0, 2, 1, 3)
        return blocks.reshape(wide * rows, narrow * cols)

    first = lax.all_gather(
        jnp.concatenate([project, output, expand], axis=1), ("wide", "narrow"), axis=0, tiled=False
    )
    second = lax.all_gather(shrink, ("wide", "narrow"), axis=0, tiled=False)
    a, b = project.shape[1], project.shape[1] + output.shape[1]
    return settle(first[..., :a]), settle(first[..., a:b]), settle(first[..., b:]), settle(second)


def scatter_plain(partials):
    outs = []
    for g in partials:
        summed = lax.psum_scatter(g, "wide", scatter_dimension=0, tiled=True)
        outs.append(lax.psum_scatter(summed, "narrow", scatter_dimension=1, tiled=True).astype(FULL))
    return outs


def saved(b):
    return b.branch, b.middle, b.normed, b.active, b.slope, b.reduced


def mlp_takes(b):
    return A.live, b.rows, b.attended, b.mods, b.output, b.expand, b.shrink


def back_takes(b, grad):
    early = A.live, grad, b.attended, b.mods, b.branch, b.middle, b.normed, b.reduced
    return early + (b.output, b.active, b.slope, b.expand, b.shrink)


def back_gives(b):
    return b.to_shrink, b.to_expand, b.to_output, b.to_middle, b.to_attended, b.late


def weights_of(b):
    return b.project, b.output, b.expand, b.shrink


def shards_of(b):
    return b.own_project, b.own_output, b.own_expand, b.own_shrink


def partials_of(b):
    return b.to_shrink, b.to_expand, b.to_output, b.to_project


def grads_of(b):
    return b.grad_shrink, b.grad_expand, b.grad_output, b.grad_project


def stages():
    return {
        S.triple: (
            space_triple(),
            (A.all_rows, S.mods, S.project),
            (S.first, S.queries, S.pairs),
        ),
        S.attend: (
            space_attend(),
            (S.queries, S.pairs, S.pairs, S.table),
            (S.attended,),
        ),
        S.mlp: (
            mlp(False),
            mlp_takes(S),
            saved(S) + (J.rows,),
        ),
        J.triple: (
            joint_triple(),
            (J.rows, J.mods, J.project),
            (J.first, J.three),
        ),
        J.attend: (
            joint_attend(),
            (J.three,) * 3 + (J.table,),
            (J.attended,),
        ),
        J.mlp: (
            mlp(True),
            mlp_takes(J),
            saved(J) + (A.output_tokens,),
        ),
        J.mlp_back: (
            mlp_back(True),
            back_takes(J, A.cotangent),
            back_gives(J),
        ),
        J.attend_back: (
            joint_attend_back(),
            (J.three,) * 3 + (J.table, J.to_attended),
            (J.to_three, J.to_table),
        ),
        J.project_back: (
            joint_project_back(),
            (J.rows, J.mods, J.first, J.to_middle, J.project, J.to_three),
            (J.to_project, J.to_rows, J.early),
        ),
        S.mlp_back: (
            mlp_back(False),
            back_takes(S, J.to_rows),
            back_gives(S),
        ),
        S.attend_back: (
            space_attend_back(),
            (S.queries, S.pairs, S.pairs, S.table, S.to_attended),
            (S.to_queries, S.to_pairs, S.to_table),
        ),
        S.project_back: (
            space_project_back(),
            (S.first, S.project, S.to_queries, S.to_pairs),
            (S.to_project, A.to_first),
        ),
        S.weight_back: (
            space_weight_back(),
            (S.first, S.to_queries, S.to_pairs),
            (S.to_project,),
        ),
        A.finish: (
            finish(),
            (S.rows, S.mods, A.own_first, S.to_middle),
            (A.grad_tokens, S.early),
        ),
    }


def apart(values, names):
    for name in names:
        phase, takes, gives = stages()[name]
        values.update(zip(gives, phase(*[values[k] for k in takes])))


def together(values, plan, tables, engine, moved, brought, name, more=(), prepare=None, inline={}, made={}):
    table = stages()
    outs, args = dict(made), {}
    steps = [k for k in plan if k not in inline]
    for phase_name in steps:
        phase, takes, gives = table[phase_name]
        outs.update(zip(gives, phase.out_shape))
    for phase_name in steps:
        for k in table[phase_name][1]:
            if k not in outs and k not in brought:
                args[k] = values[k]
    for k in tuple(moved) + tuple(more):
        if k not in outs:
            args[k] = values[k]

    def script(refs, engine_outs, feed):
        refs.update(zip(brought, engine_outs))
        if prepare is not None:
            prepare(refs)
        feed.follow(tables)
        feed.enter()
        for phase_name in plan:
            if phase_name in inline:
                feed.do(feed.slot)
                inline[phase_name](refs, feed)
                continue
            phase, takes, gives = table[phase_name]
            phase.inside(feed.over(phase), [refs[k] for k in takes], [refs[k] for k in gives])
        feed.rest()

    results, arrived = fused(script, args, outs, engine, moved, name)
    values.update(results)
    values.update(zip(brought, arrived))


def body(
    tokens,
    clip_cond,
    image_cond,
    image_count,
    space_modulate,
    space_project,
    space_output,
    space_expand,
    space_reduce,
    space_bias,
    joint_modulate,
    joint_project,
    joint_output,
    joint_expand,
    joint_reduce,
    joint_bias,
    cotangent,
):
    small = lax.axis_size("wide") == 8
    narrow = lax.axis_index("narrow")
    wide = lax.axis_index("wide")
    rows = space_modulate.shape[0]
    low_clips = jax.nn.silu(clip_cond.astype(FULL)).astype(LOW)
    low_images = jax.nn.silu(image_cond.astype(FULL)).astype(LOW)
    values = {
        A.live: (image_count > 0).astype(FULL),
        S.rows: tokens,
        A.cotangent: cotangent,
        S.table: space_table(space_bias, narrow),
        J.table: joint_table(joint_bias),
    }
    weights = weights_of(S) + weights_of(J)
    space_shards = space_project, space_output, space_expand, space_reduce
    joint_shards = joint_project, joint_output, joint_expand, joint_reduce

    if small:
        moved = shards_of(S) + shards_of(J)
        shapes = [v.shape for v in space_shards + joint_shards]
        values.update(zip(moved, space_shards + joint_shards))
        values[A.images] = jnp.broadcast_to(low_images.astype(FULL).reshape(8, 1, rows), (8, 8, rows))
        own_clips = lax.dynamic_slice_in_dim(low_clips, wide * rows, rows, 1).astype(FULL)
        values[A.clips] = jnp.pad(own_clips, ((0, 6), (0, 0)))
        values[S.own_modulate] = space_modulate
        values[J.own_modulate] = joint_modulate
        gather = Gather(shapes, True, 0)

        def triple(refs, feed):
            takes = refs[S.rows], refs[A.all_rows], refs[S.mods], refs[S.project]
            gives = refs[S.first], refs[S.queries], refs[S.pairs]
            space_triple_parts(feed, 18, Place().order, *takes, *gives)

        whole_triple = stages()[S.triple]
        together(
            values,
            FORWARD,
            (FORWARD_ENDS, FORWARD_MIDDLES),
            Joined(gather, Modulation()),
            moved + (S.rows, A.images, A.clips, S.own_modulate, J.own_modulate),
            weights + (A.all_rows, S.mods, J.mods, A.cond),
            "forward",
            inline={A.triple: triple},
            made=dict(zip(whole_triple[2], whole_triple[0].out_shape)),
        )
        project_shape, output_shape, expand_shape, shrink_shape = shapes[:4]
        shapes = [shrink_shape, expand_shape, output_shape, project_shape]
        engine = Scatter(shapes, False, 1)
        tables = BACK_JOINT_ENDS, BACK_JOINT_MIDDLES
        together(values, BACK_JOINT, tables, engine, partials_of(J), grads_of(J), "back_joint")
        back = ModulationBack()
        engine = Scatter(shapes, True, 2)

        def first_back(refs, feed):
            takes = refs[S.project], refs[S.to_queries], refs[S.to_pairs]
            space_first_back(feed, 8, Place().order, *takes, engine.line_held)

        def prepare(refs):
            early = refs[S.early], refs[J.early]
            back.sources = refs[A.cond], early, (refs[S.late], refs[J.late])

        together(
            values,
            BACK_SPACE,
            (BACK_SPACE_ENDS, BACK_SPACE_MIDDLES),
            Joined(Joined(engine, back), BiasBack()),
            partials_of(S) + (J.to_table, S.to_table),
            grads_of(S) + (A.own_first, S.modulate, J.modulate, A.bias),
            "back_space",
            (A.cond, S.late, J.early, J.late, S.project),
            prepare,
            {A.first_back: first_back},
        )
        modulate = values[S.modulate], values[J.modulate]
        bias = bias_tables(values[A.bias])
    else:
        image_all = lax.all_gather(low_images, "wide", axis=0, tiled=True)
        cond = jnp.stack([jnp.repeat(low_clips, 4, axis=0), image_all], axis=1)
        values[S.mods], values[J.mods] = modulations(
            cond, (space_modulate, joint_modulate)
        )
        values.update(zip(weights[:4], gather_flat(space_shards)))
        values.update(zip(weights[4:], gather_flat(joint_shards)))
        values[A.all_rows] = lax.all_gather(tokens, "narrow", axis=0, tiled=True)
        apart(values, (S.triple,) + FORWARD[1:] + BACK_JOINT + (S.attend_back, S.project_back))
        for b in (J, S):
            values.update(zip(grads_of(b), scatter_plain([values[k] for k in partials_of(b)])))
        values[A.own_first] = lax.psum_scatter(
            values[A.to_first].astype(FULL), "narrow", scatter_dimension=0, tiled=True
        )
        apart(values, [A.finish])
        both = [
            jnp.concatenate([values[b.early], values[b.late][:, 2 * D :]], axis=1) for b in (S, J)
        ]
        modulate = modulation_grads(cond, jnp.stack(both), rows)
        space_grad = space_table_back(values[S.to_table], narrow)
        grads = jnp.concatenate([space_grad, joint_table_back(values[J.to_table])], axis=1)
        bias = lax.psum(grads, ("wide", "narrow"))
        split = space_bias.shape[1]
        bias = bias[:, :split], bias[:, split:]
    outs = [values[A.output_tokens], values[A.grad_tokens]]
    for i, b in enumerate((S, J)):
        outs += [modulate[i]] + [values[k] for k in reversed(grads_of(b))] + [bias[i]]
    return tuple(outs)


FORWARD = A.triple, S.attend, S.mlp, J.triple, J.attend, J.mlp
BACK_JOINT = J.mlp_back, J.attend_back, J.project_back, S.mlp_back
BACK_SPACE = S.attend_back, A.first_back, S.weight_back, A.finish


def solution(mesh):
    rows = P(("wide", "narrow"), None)
    block = P("wide", "narrow")
    in_specs = (
        (rows, P(), P("wide", None), P("wide"))
        + (block,) * 5
        + (P(),)
        + (block,) * 5
        + (P(), rows)
    )
    out_specs = (rows, rows) + ((block,) * 5 + (P(),)) * 2
    return jax.shard_map(body, mesh=mesh, in_specs=in_specs, out_specs=out_specs, check_vma=False)
```

```python
import functools
import math

import jax
import jax.numpy as jnp
import numpy as np
from jax import lax
from jax.experimental import pallas as pl
from jax.experimental.pallas import tpu as pltpu
from jax.sharding import PartitionSpec as P

D = 1024
HEADS = 16
HEAD_DIM = 64
FF = 4096
SW = 8
TW = 5
CHUNK = SW * SW
CLIP_ROWS = TW * CHUNK
ROWS_DEV = CLIP_ROWS + 4 * CHUNK
SPAN_S = 4 * SW - 1
SPAN_T = 2 * SW - 1
MESH = pl.DeviceIdType.MESH


epsilon = 1e-06


def normalise(values):
    centred = values - jnp.mean(values, axis=-1, keepdims=True)
    spread = jnp.mean(centred * centred, axis=-1, keepdims=True)
    scale = lax.rsqrt(spread + epsilon)
    return centred * scale, scale


def norm_back(unit, scale, grad):
    return scale * (
        grad
        - jnp.mean(grad, axis=-1, keepdims=True)
        - unit * jnp.mean(grad * unit, axis=-1, keepdims=True)
    )


def nn(left, right):
    return lax.dot_general(left, right, (((1,), (0,)), ((), ())), preferred_element_type=jnp.float32)


def nt(left, right):
    return lax.dot_general(left, right, (((1,), (1,)), ((), ())), preferred_element_type=jnp.float32)


def tn(left, right):
    return lax.dot_general(left, right, (((0,), (0,)), ((), ())), preferred_element_type=jnp.float32)


def each_chunk(body, count=ROWS_DEV // CHUNK):
    @pl.loop(0, count)
    def _(i):
        inner = lax.rem(i, ROWS_DEV // CHUNK)
        seq = jnp.where(inner >= CLIP_ROWS // CHUNK, 1, 0)
        body(pl.ds(pl.multiple_of(i * CHUNK, CHUNK), CHUNK), pl.ds(seq, 1))


def part(index):
    return slice(index * D, (index + 1) * D)


class Tiled:
    def __init__(self, block, index):
        self.block, self.index = block, index

    def spec(self):
        return pl.BlockSpec(self.block, self.index)


class Whole:
    def __init__(self, block):
        self.block = block

    def spec(self):
        rank = len(self.block)
        return pl.BlockSpec(self.block, lambda *_: (0,) * rank, pipeline_mode=pl.Buffered(1))


class Scalars:
    def spec(self):
        return pl.BlockSpec(memory_space=pltpu.SMEM)


SCALARS = Scalars()
whole, spec = Whole, Tiled


def params(limit=56):
    return pltpu.CompilerParams(vmem_limit_bytes=limit * 2**20)


def shape(dims, kind):
    return jax.ShapeDtypeStruct(dims, kind)


LOW = jnp.bfloat16
FULL = jnp.float32


class Phase:
    def __init__(self, kernel, *, grid, in_specs, out_specs, out_shape, name, ticks=1, scratch_shapes=()):
        self.kernel, self.grid, self.name, self.ticks = kernel, grid, name, ticks
        self.in_specs, self.out_specs, self.out_shape = in_specs, out_specs, out_shape
        self.scratch = list(scratch_shapes)

    def __call__(self, *args):
        return pl.pallas_call(
            functools.partial(self.kernel, lambda t: None),
            grid=self.grid,
            in_specs=[s.spec() for s in self.in_specs],
            out_specs=[s.spec() for s in self.out_specs],
            out_shape=self.out_shape,
            scratch_shapes=self.scratch,
            compiler_params=params(),
            name=self.name,
        )(*args)

    def inside(self, tick, ins, outs):
        specs = list(self.in_specs) + list(self.out_specs)
        refs = list(ins) + list(outs)
        first_out = len(ins)
        held = [i for i, s in enumerate(specs) if isinstance(s, Whole)]
        tiled = [i for i, s in enumerate(specs) if isinstance(s, Tiled)]

        def scoped(buffers, scratch, sems):
            place = dict(zip(held, buffers))
            loads = [
                pltpu.make_async_copy(refs[i], place[i], sems.at[at])
                for at, i in enumerate(held)
                if i < first_out
            ]
            for load in loads:
                load.start()
            for load in loads:
                load.wait()

            def body(*blocks):
                now = dict(zip(tiled, blocks))
                now.update(place)
                operands = [now.get(i, refs[i]) for i in range(len(refs))]
                self.kernel(tick, *operands, *scratch)

            pltpu.emit_pipeline(
                body,
                grid=self.grid,
                in_specs=[specs[i].spec() for i in tiled if i < first_out],
                out_specs=[specs[i].spec() for i in tiled if i >= first_out],
            )(*[refs[i] for i in tiled])
            stores = [
                pltpu.make_async_copy(place[i], refs[i], sems.at[at])
                for at, i in enumerate(held)
                if i >= first_out
            ]
            for store in stores:
                store.start()
            for store in stores:
                store.wait()

        kinds = [refs[i].dtype for i in held]
        pl.run_scoped(
            scoped,
            [pltpu.VMEM(specs[i].block, kind) for i, kind in zip(held, kinds)],
            self.scratch,
            pltpu.SemaphoreType.DMA((len(held),)),
        )


def space_triple_kernel(tick, rows, mods, weight, normed, queries, pairs):
    step = pl.program_id(0)

    @pl.when(step == 0)
    def _():
        def chunk(at, seq):
            unit, _ = normalise(rows[at, :].astype(FULL))
            normed[at, :] = (unit * (1.0 + mods[seq, part(1)]) + mods[seq, part(0)]).astype(LOW)

        each_chunk(chunk, 4 * ROWS_DEV // CHUNK)

    tick(0)

    @pl.when(step < 2)
    def _():
        own = span(lax.axis_index("narrow"), ROWS_DEV)
        queries[...] = nn(normed[own, :], weight[...]).astype(LOW)

    for q in range(4):
        if q:
            tick(q)

        @pl.when(step >= 2)
        def _():
            pairs[q] = nn(normed[q * ROWS_DEV : (q + 1) * ROWS_DEV, :], weight[...]).astype(LOW)


def space_triple():
    tile = 512
    return Phase(
        space_triple_kernel,
        grid=(3 * D // tile,),
        in_specs=[
            whole((4 * ROWS_DEV, D)),
            whole((2, 6 * D)),
            spec((D, tile), lambda t: (0, t)),
        ],
        out_specs=[
            whole((4 * ROWS_DEV, D)),
            spec((ROWS_DEV, tile), lambda t: (0, jnp.minimum(t, 1))),
            spec((4, ROWS_DEV, tile), lambda t: (0, 0, jnp.maximum(t - 2, 0))),
        ],
        out_shape=[
            shape((4 * ROWS_DEV, D), LOW),
            shape((ROWS_DEV, D), LOW),
            shape((4, ROWS_DEV, 2 * D), LOW),
        ],
        name="space_triple",
        ticks=4,
    )


def space_triple_parts(feed, ticks, order, own_rows, all_rows, mods, weight, first, queries, pairs):
    tile = 512
    slot = feed.slot
    feed.slot += ticks

    def scoped(weights, modulation, rows, normed, made, sems):
        loads = [
            pltpu.make_async_copy(weight, weights, sems.at[0]),
            pltpu.make_async_copy(mods, modulation, sems.at[1]),
        ]
        for load in loads:
            load.start()
        stores = []
        at_slot = slot
        for j in range(4):
            side = j % 2
            here = span(order[j], ROWS_DEV)
            if j:
                feed.do(at_slot)
            source = all_rows.at[here] if j else own_rows
            fetch = pltpu.make_async_copy(source, rows.at[side], sems.at[2 + j])
            fetch.start()
            if j == 0:
                for load in loads:
                    load.wait()
            if j >= 2:
                for store in stores[j - 2]:
                    store.wait()
            fetch.wait()

            def chunk(at, seq):
                unit, _ = normalise(rows[side, at, :].astype(FULL))
                value = unit * (1.0 + modulation[seq, part(1)]) + modulation[seq, part(0)]
                normed[side, at, :] = value.astype(LOW)

            each_chunk(chunk)
            stores.append([pltpu.make_async_copy(normed.at[side], first.at[here], sems.at[6 + j])])
            stores[j][0].start()
            for t in range(2 if j else 0, 3 * D // tile):
                if t > (2 if j else 0):
                    feed.do(at_slot)
                at_slot += 1
                columns = slice(t * tile, (t + 1) * tile)
                made[side, :, columns] = nn(normed[side], weights[:, columns]).astype(LOW)
            out = made.at[side, :, pl.ds(D, 2 * D)]
            stores[j].append(pltpu.make_async_copy(out, pairs.at[order[j]], sems.at[10 + j]))
            if j == 0:
                out = made.at[0, :, pl.ds(0, D)]
                stores[j].append(pltpu.make_async_copy(out, queries, sems.at[14]))
            for store in stores[j][1:]:
                store.start()
        for store in stores[2] + stores[3]:
            store.wait()

    pl.run_scoped(
        scoped,
        pltpu.VMEM((D, 3 * D), LOW),
        pltpu.VMEM((2, 6 * D), FULL),
        pltpu.VMEM((2, ROWS_DEV, D), LOW),
        pltpu.VMEM((2, ROWS_DEV, D), LOW),
        pltpu.VMEM((2, ROWS_DEV, 3 * D), LOW),
        pltpu.SemaphoreType.DMA((15,)),
    )


def joint_triple_kernel(tick, rows, mods, weight, normed, triple):
    @pl.when(pl.program_id(0) == 0)
    def _():
        def chunk(at, seq):
            unit, _ = normalise(rows[at, :])
            normed[at, :] = (unit * (1.0 + mods[seq, part(1)]) + mods[seq, part(0)]).astype(LOW)

        each_chunk(chunk)

    tick(0)
    triple[...] = nn(normed[...], weight[...]).astype(LOW)


def joint_triple():
    tile = 512
    return Phase(
        joint_triple_kernel,
        grid=(3 * D // tile,),
        in_specs=[whole((ROWS_DEV, D)), whole((2, 6 * D)), spec((D, tile), lambda t: (0, t))],
        out_specs=[whole((ROWS_DEV, D)), spec((ROWS_DEV, tile), lambda t: (0, t))],
        out_shape=[shape((ROWS_DEV, D), LOW), shape((ROWS_DEV, 3 * D), LOW)],
        name="joint_triple",
        ticks=1,
    )


def half_mask():
    return lax.broadcasted_iota(jnp.int32, (1, 2 * HEAD_DIM), 1) < HEAD_DIM


def split_heads(rows):
    first = half_mask()
    zero = jnp.zeros_like(rows)
    return jnp.concatenate([jnp.where(first, rows, zero), jnp.where(first, zero, rows)], axis=0)


def join_heads(stacked):
    return jnp.where(half_mask(), stacked[:CHUNK], stacked[CHUNK:])


def softmax_keys(keys, queries, bias):
    scores = nt(keys, queries) * HEAD_DIM**-0.5 + bias
    powered = jnp.exp(scores - jnp.max(scores, axis=0, keepdims=True))
    return powered / jnp.sum(powered, axis=0, keepdims=True)


def attend(queries, keys, values, bias):
    probs = softmax_keys(keys, split_heads(queries), bias)
    return join_heads(tn(values, probs.astype(LOW)).T).astype(LOW)


def attend_back(queries, keys, values, bias, grad):
    queries, grad = split_heads(queries), split_heads(grad)
    probs = softmax_keys(keys, queries, bias)
    grad_values = nn(probs.astype(LOW), grad)
    grad_probs = nt(values, grad)
    centre = jnp.sum(probs * grad_probs, axis=0, keepdims=True)
    grad_scores = (probs * (grad_probs - centre)).astype(LOW)
    grad_queries = join_heads(tn(keys, grad_scores).T) * HEAD_DIM**-0.5
    grad_keys = nn(grad_scores, queries) * HEAD_DIM**-0.5
    return grad_queries, grad_keys, grad_values, grad_scores.astype(FULL)


def space_attend_kernel(tick, queries, keys, values, bias, out):
    table = bias[0]
    for i in range(ROWS_DEV // CHUNK):
        if i % 3 == 0:
            tick(i // 3)
        at = slice(i * CHUNK, (i + 1) * CHUNK)
        key_rows = keys[:, at, :].reshape(4 * CHUNK, 2 * HEAD_DIM)
        value_rows = values[:, at, :].reshape(4 * CHUNK, 2 * HEAD_DIM)
        out[at, :] = attend(queries[at, :], key_rows, value_rows, table)


def space_attend():
    wide = 2 * HEAD_DIM
    return Phase(
        space_attend_kernel,
        grid=(HEADS // 2,),
        in_specs=[
            spec((ROWS_DEV, wide), lambda h: (0, h)),
            spec((4, ROWS_DEV, wide), lambda h: (0, 0, h)),
            spec((4, ROWS_DEV, wide), lambda h: (0, 0, h + HEADS // 2)),
            spec((1, 4 * CHUNK, wide), lambda h: (h, 0, 0)),
        ],
        out_specs=[spec((ROWS_DEV, wide), lambda h: (0, h))],
        out_shape=[shape((ROWS_DEV, D), LOW)],
        name="space_attend",
        ticks=3,
    )


def space_attend_back_kernel(tick, queries, keys, values, bias, grad, grad_q, grad_pairs, grad_bias):
    table = bias[0]
    for i in range(ROWS_DEV // CHUNK):
        if i % 3 == 0:
            tick(i // 3)
        at = slice(i * CHUNK, (i + 1) * CHUNK)
        key_rows = keys[:, at, :].reshape(4 * CHUNK, 2 * HEAD_DIM)
        value_rows = values[:, at, :].reshape(4 * CHUNK, 2 * HEAD_DIM)
        to_q, to_k, to_v, to_bias = attend_back(
            queries[at, :], key_rows, value_rows, table, grad[at, :]
        )
        grad_q[at, :] = to_q.astype(LOW)
        grad_pairs[0, :, at, :] = to_k.astype(LOW).reshape(4, CHUNK, 2 * HEAD_DIM)
        grad_pairs[1, :, at, :] = to_v.astype(LOW).reshape(4, CHUNK, 2 * HEAD_DIM)
        to_bias = to_bias.reshape(2, 2, SW, SW, 2 * HEAD_DIM)
        if i == 0:
            grad_bias[0] = to_bias
        else:
            grad_bias[0] += to_bias


def space_attend_back():
    wide = 2 * HEAD_DIM
    head = spec((ROWS_DEV, wide), lambda h: (0, h))
    four = spec((4, ROWS_DEV, wide), lambda h: (0, 0, h))
    table = spec((1, 4 * CHUNK, wide), lambda h: (h, 0, 0))
    return Phase(
        space_attend_back_kernel,
        grid=(HEADS // 2,),
        in_specs=[
            head,
            four,
            spec((4, ROWS_DEV, wide), lambda h: (0, 0, h + HEADS // 2)),
            table,
            head,
        ],
        out_specs=[
            head,
            spec((2, 4, ROWS_DEV, wide), lambda h: (0, 0, 0, h)),
            spec((1, 2, 2, SW, SW, wide), lambda h: (h, 0, 0, 0, 0, 0)),
        ],
        out_shape=[
            shape((ROWS_DEV, D), LOW),
            shape((2, 4, ROWS_DEV, D), LOW),
            shape((HEADS // 2, 2, 2, SW, SW, wide), FULL),
        ],
        name="space_attend_back",
        ticks=3,
    )


def clip_table(bias, frame):
    return jnp.concatenate([bias[0, frame - t + TW - 1] for t in range(TW)], axis=0)


def joint_attend_kernel(tick, queries, keys, values, bias, out):
    for i in range(ROWS_DEV // CHUNK):
        if i % 3 == 0:
            tick(i // 3)
        at = slice(i * CHUNK, (i + 1) * CHUNK)
        seen = slice(0, CLIP_ROWS) if i < TW else at
        table = clip_table(bias, i) if i < TW else bias[0, TW - 1]
        out[at, :] = attend(queries[at, :], keys[seen, :], values[seen, :], table)


def joint_specs():
    wide = 2 * HEAD_DIM
    return [
        spec((ROWS_DEV, wide), lambda h: (0, h)),
        spec((ROWS_DEV, wide), lambda h: (0, h + HEADS // 2)),
        spec((ROWS_DEV, wide), lambda h: (0, h + HEADS)),
        spec((1, 2 * TW - 1, CHUNK, wide), lambda h: (h, 0, 0, 0)),
    ]


def joint_attend():
    return Phase(
        joint_attend_kernel,
        grid=(HEADS // 2,),
        in_specs=joint_specs(),
        out_specs=[spec((ROWS_DEV, 2 * HEAD_DIM), lambda h: (0, h))],
        out_shape=[shape((ROWS_DEV, D), LOW)],
        name="joint_attend",
        ticks=3,
    )


def joint_attend_back_kernel(
    tick, queries, keys, values, bias, grad, grads, grad_bias, sum_k, sum_v
):
    grad_bias[...] = jnp.zeros_like(grad_bias)
    for i in range(ROWS_DEV // CHUNK):
        if i % 3 == 0:
            tick(i // 3)
        at = slice(i * CHUNK, (i + 1) * CHUNK)
        seen = slice(0, CLIP_ROWS) if i < TW else at
        table = clip_table(bias, i) if i < TW else bias[0, TW - 1]
        to_q, to_k, to_v, to_bias = attend_back(
            queries[at, :], keys[seen, :], values[seen, :], table, grad[at, :]
        )
        grads[0, at, :] = to_q.astype(LOW)
        if i >= TW:
            grad_bias[TW - 1] += to_bias
            grads[1, at, :] = to_k.astype(LOW)
            grads[2, at, :] = to_v.astype(LOW)
            continue
        for t in range(TW):
            grad_bias[i - t + TW - 1] += to_bias[t * CHUNK : (t + 1) * CHUNK]
        if i == 0:
            sum_k[...] = to_k
            sum_v[...] = to_v
        elif i < TW - 1:
            sum_k[...] += to_k
            sum_v[...] += to_v
        else:
            grads[1, seen, :] = (sum_k[...] + to_k).astype(LOW)
            grads[2, seen, :] = (sum_v[...] + to_v).astype(LOW)


def joint_attend_back():
    wide = 2 * HEAD_DIM
    head = spec((ROWS_DEV, wide), lambda h: (0, h))
    return Phase(
        joint_attend_back_kernel,
        grid=(HEADS // 2,),
        in_specs=joint_specs() + [head],
        out_specs=[
            spec((3, ROWS_DEV, wide), lambda h: (0, 0, h)),
            spec((2 * TW - 1, CHUNK, wide), lambda h: (h, 0, 0)),
        ],
        out_shape=[
            shape((3, ROWS_DEV, D), LOW),
            shape((HEADS // 2 * (2 * TW - 1), CHUNK, wide), FULL),
        ],
        scratch_shapes=[pltpu.VMEM((CLIP_ROWS, wide), FULL)] * 2,
        name="joint_attend_back",
        ticks=3,
    )


def mlp_kernel(last_block, tick, live, rows, attended, mods, output, expand, shrink, *refs):
    branch, middle, normed, active, slope, reduced, result, total = refs
    step = pl.program_id(0)

    @pl.when(step == 0)
    def _():
        def chunk(at, seq):
            grown = nn(attended[at, :], output[...])
            branch[at, :] = grown.astype(LOW)
            mixed = rows[at, :].astype(FULL) + mods[seq, part(2)] * grown
            middle[at, :] = mixed
            unit, _ = normalise(mixed)
            normed[at, :] = (unit * (1.0 + mods[seq, part(4)]) + mods[seq, part(3)]).astype(LOW)

        each_chunk(chunk)
        total[...] = jnp.zeros_like(total)

    tick(0)
    before = nn(normed[...], expand[...])
    inner = 0.5 * (1.0 + lax.erf(before * 0.5**0.5))
    low_active = (before * inner).astype(LOW)
    tick(1)
    active[...] = low_active
    slope[...] = (inner + before * jnp.exp(-0.5 * before * before) * (2.0 * math.pi) ** -0.5).astype(LOW)
    total[...] += nn(low_active, shrink[...])

    @pl.when(step == pl.num_programs(0) - 1)
    def _():
        def chunk(at, seq):
            reduced[at, :] = total[at, :].astype(LOW)
            value = middle[at, :] + mods[seq, part(5)] * total[at, :]
            if last_block:
                value = value * jnp.where(seq.start > 0, live[0], 1.0)
            result[at, :] = value.astype(result.dtype)

        each_chunk(chunk)


def mlp(last_block):
    tile = 512
    square = whole((ROWS_DEV, D))
    strip = spec((ROWS_DEV, tile), lambda f: (0, f))
    return Phase(
        functools.partial(mlp_kernel, last_block),
        grid=(FF // tile,),
        in_specs=[
            SCALARS,
            square,
            square,
            whole((2, 6 * D)),
            whole((D, D)),
            spec((D, tile), lambda f: (0, f)),
            spec((tile, D), lambda f: (f, 0)),
        ],
        out_specs=[square, square, square, strip, strip, square, square],
        out_shape=[
            shape((ROWS_DEV, D), LOW),
            shape((ROWS_DEV, D), FULL),
            shape((ROWS_DEV, D), LOW),
            shape((ROWS_DEV, FF), LOW),
            shape((ROWS_DEV, FF), LOW),
            shape((ROWS_DEV, D), LOW),
            shape((ROWS_DEV, D), LOW if last_block else FULL),
        ],
        scratch_shapes=[pltpu.VMEM((ROWS_DEV, D), FULL)],
        name="mlp",
        ticks=2,
    )


def mlp_back_kernel(first_block, tick, live, *refs):
    (grad_result, attended, mods, branch, middle, normed, reduced, output, active, slope) = refs[:10]
    expand, shrink = refs[10:12]
    grad_shrink, grad_expand, grad_output, grad_middle, grad_attended, grad_mods = refs[12:18]
    grad_reduced, normed_t, total = refs[18:]
    grad_branch = grad_reduced
    step = pl.program_id(0)

    def incoming(at, seq):
        value = grad_result[at, :].astype(FULL)
        if first_block:
            value = value * jnp.where(seq.start > 0, live[0], 1.0)
        return value

    @pl.when(step == 0)
    def _():
        grad_mods[...] = jnp.zeros_like(grad_mods)

        def chunk(at, seq):
            value = incoming(at, seq)
            grad_reduced[at, :] = (mods[seq, part(5)] * value).astype(LOW)
            grad_mods[seq, part(5)] += jnp.sum(
                reduced[at, :].astype(FULL) * value, axis=0, keepdims=True
            )

        each_chunk(chunk)
        total[...] = jnp.zeros_like(total)
        normed_t[...] = normed[...].T

    tick(0)
    grad_active = nt(grad_reduced[...], shrink[...])
    grad_before = (grad_active * slope[...].astype(FULL)).astype(LOW)
    tick(1)
    grad_shrink[...] = tn(active[...], grad_reduced[...]).astype(LOW)
    tick(2)
    grad_expand[...] = nn(normed_t[...], grad_before).astype(LOW)
    tick(3)
    total[...] += nt(grad_before, expand[...])

    @pl.when(step == pl.num_programs(0) - 1)
    def _():
        def chunk(at, seq):
            grad = total[at, :]
            unit, scale = normalise(middle[at, :])
            grad_mods[seq, part(3)] += jnp.sum(grad, axis=0, keepdims=True)
            grad_mods[seq, part(4)] += jnp.sum(unit * grad, axis=0, keepdims=True)
            value = incoming(at, seq) + norm_back(unit, scale, (1.0 + mods[seq, part(4)]) * grad)
            grad_middle[at, :] = value
            grad_mods[seq, part(2)] += jnp.sum(
                branch[at, :].astype(FULL) * value, axis=0, keepdims=True
            )
            grad_branch[at, :] = (mods[seq, part(2)] * value).astype(LOW)

        each_chunk(chunk)
        grad_attended[...] = nt(grad_branch[...], output[...]).astype(LOW)
        grad_output[...] = tn(attended[...], grad_branch[...]).astype(LOW)


def mlp_back(first_block):
    tile = 512
    square = whole((ROWS_DEV, D))
    strip = spec((ROWS_DEV, tile), lambda f: (0, f))
    across = spec((D, tile), lambda f: (0, f))
    down = spec((tile, D), lambda f: (f, 0))
    return Phase(
        functools.partial(mlp_back_kernel, first_block),
        grid=(FF // tile,),
        in_specs=[
            SCALARS,
            square,
            square,
            whole((2, 6 * D)),
            square,
            square,
            square,
            square,
            whole((D, D)),
            strip,
            strip,
            across,
            down,
        ],
        out_specs=[down, across, whole((D, D)), square, square, whole((2, 6 * D))],
        out_shape=[
            shape((FF, D), LOW),
            shape((D, FF), LOW),
            shape((D, D), LOW),
            shape((ROWS_DEV, D), FULL),
            shape((ROWS_DEV, D), LOW),
            shape((2, 6 * D), FULL),
        ],
        scratch_shapes=[
            pltpu.VMEM((ROWS_DEV, D), LOW),
            pltpu.VMEM((D, ROWS_DEV), LOW),
            pltpu.VMEM((ROWS_DEV, D), FULL),
        ],
        name="mlp_back",
        ticks=4,
    )


def finish_rows(rows, grad_normed, grad_middle, mods, grad_rows, grad_mods):
    grad_mods[...] = jnp.zeros_like(grad_mods)

    def chunk(at, seq):
        grad = grad_normed[at, :].astype(FULL)
        unit, scale = normalise(rows[at, :].astype(FULL))
        grad_mods[seq, part(0)] += jnp.sum(grad, axis=0, keepdims=True)
        grad_mods[seq, part(1)] += jnp.sum(unit * grad, axis=0, keepdims=True)
        grad_rows[at, :] = grad_middle[at, :] + norm_back(
            unit, scale, (1.0 + mods[seq, part(1)]) * grad
        )

    each_chunk(chunk)


def joint_project_back_kernel(
    tick, rows, mods, normed, grad_middle, weight, grad, grad_weight, grad_rows, grad_mods, total, normed_t
):
    step = pl.program_id(0)

    @pl.when(step == 0)
    def _():
        total[...] = jnp.zeros_like(total)
        normed_t[...] = normed[...].T

    tick(0)
    grad_weight[...] = nn(normed_t[...], grad[0]).astype(LOW)
    tick(1)
    total[...] += nt(grad[0], weight[...])

    @pl.when(step == pl.num_programs(0) - 1)
    def _():
        finish_rows(rows, total, grad_middle, mods, grad_rows, grad_mods)


def joint_project_back():
    tile = 512
    square = whole((ROWS_DEV, D))
    across = spec((D, tile), lambda t: (0, t))
    return Phase(
        joint_project_back_kernel,
        grid=(3 * D // tile,),
        in_specs=[square, whole((2, 6 * D)), square, square, across, spec((1, ROWS_DEV, tile), lambda t: (t // 2, 0, t % 2))],
        out_specs=[across, square, whole((2, 2 * D))],
        out_shape=[shape((D, 3 * D), LOW), shape((ROWS_DEV, D), FULL), shape((2, 2 * D), FULL)],
        scratch_shapes=[pltpu.VMEM((ROWS_DEV, D), FULL), pltpu.VMEM((D, ROWS_DEV), LOW)],
        name="joint_project_back",
        ticks=2,
    )


def space_project_back_kernel(tick, normed, weight, grad_q, grad_pairs, grad_weight, grad_normed, total):
    step = pl.program_id(0)
    own = span(lax.axis_index("narrow"), ROWS_DEV)

    @pl.when(step == 0)
    def _():
        total[...] = jnp.zeros_like(total)

    tick(0)

    @pl.when(step < 2)
    def _():
        grad_weight[...] = tn(normed[own, :], grad_q[...]).astype(LOW)
        total[own, :] += nt(grad_q[...], weight[...])

    @pl.when(step >= 2)
    def _():
        flat = grad_pairs[0].reshape(4 * ROWS_DEV, grad_pairs.shape[-1])
        grad_weight[...] = tn(normed[...], flat).astype(LOW)

    for q in range(4):
        tick(q + 1)

        @pl.when(step >= 2)
        def _():
            at = slice(q * ROWS_DEV, (q + 1) * ROWS_DEV)
            total[at, :] += nt(grad_pairs[0, q], weight[...])

    @pl.when(step == pl.num_programs(0) - 1)
    def _():
        grad_normed[...] = total[...].astype(LOW)


def space_project_back():
    tile = 512
    across = spec((D, tile), lambda t: (0, t))

    def pair(t):
        late = jnp.maximum(t - 2, 0)
        return (late // 2, 0, 0, late % 2)

    return Phase(
        space_project_back_kernel,
        grid=(3 * D // tile,),
        in_specs=[
            whole((4 * ROWS_DEV, D)),
            across,
            spec((ROWS_DEV, tile), lambda t: (0, jnp.minimum(t, 1))),
            spec((1, 4, ROWS_DEV, tile), pair),
        ],
        out_specs=[across, whole((4 * ROWS_DEV, D))],
        out_shape=[shape((D, 3 * D), LOW), shape((4 * ROWS_DEV, D), LOW)],
        scratch_shapes=[pltpu.VMEM((4 * ROWS_DEV, D), FULL)],
        name="space_project_back",
        ticks=5,
    )


def space_first_back(feed, ticks, order, weight, grad_q, grad_pairs, out):
    half = ROWS_DEV // 2
    first = feed.slot
    feed.slot += ticks

    def scoped(weights, queries, pairs, sems):
        def pair_load(j):
            return pltpu.make_async_copy(
                grad_pairs.at[:, order[j]], pairs.at[(3 - j) % 2], sems.at[(3 - j) % 2]
            )

        loads = [
            pltpu.make_async_copy(weight, weights, sems.at[2]),
            pltpu.make_async_copy(grad_q, queries, sems.at[3]),
        ]
        for load in loads:
            load.start()
        pair_load(3).start()
        for load in loads:
            load.wait()
        for step in range(4):
            j = 3 - step
            if j:
                pair_load(j - 1).start()
            pair_load(j).wait()
            for side in range(2):
                if step + side:
                    feed.do(first + 2 * step + side)
                rows = slice(side * half, (side + 1) * half)
                value = nt(pairs[step % 2, 0, rows, :], weights[:, part(1)])
                value += nt(pairs[step % 2, 1, rows, :], weights[:, part(2)])
                if j == 0:
                    value += nt(queries[rows, :], weights[:, part(0)])
                for p in range(2):
                    piece = value[p * (half // 2) : (p + 1) * (half // 2)]
                    out[2 * side + p, order[j]] = piece.astype(LOW)

    pl.run_scoped(
        scoped,
        pltpu.VMEM((D, 3 * D), LOW),
        pltpu.VMEM((ROWS_DEV, D), LOW),
        pltpu.VMEM((2, 2, ROWS_DEV, D), LOW),
        pltpu.SemaphoreType.DMA((4,)),
    )


def space_weight_back_kernel(tick, normed, grad_q, grad_pairs, grad_weight):
    step = pl.program_id(0)
    own = span(lax.axis_index("narrow"), ROWS_DEV)
    tick(0)

    @pl.when(step < 2)
    def _():
        grad_weight[...] = tn(normed[own, :], grad_q[...]).astype(LOW)

    for side in range(2):
        if side:
            tick(1)

        @pl.when(step >= 2)
        def _():
            columns = slice(side * 256, (side + 1) * 256)
            flat = grad_pairs[0, :, :, columns].reshape(4 * ROWS_DEV, 256)
            grad_weight[:, columns] = tn(normed[...], flat).astype(LOW)


def space_weight_back():
    tile = 512

    def pair(t):
        late = jnp.maximum(t - 2, 0)
        return (late // 2, 0, 0, late % 2)

    return Phase(
        space_weight_back_kernel,
        grid=(3 * D // tile,),
        in_specs=[
            whole((4 * ROWS_DEV, D)),
            spec((ROWS_DEV, tile), lambda t: (0, jnp.minimum(t, 1))),
            spec((1, 4, ROWS_DEV, tile), pair),
        ],
        out_specs=[spec((D, tile), lambda t: (0, t))],
        out_shape=[shape((D, 3 * D), LOW)],
        name="space_weight_back",
        ticks=2,
    )


def finish_kernel(tick, rows, mods, grad_normed, grad_middle, grad_rows, grad_mods):
    tick(0)
    finish_rows(rows, grad_normed, grad_middle, mods, grad_rows, grad_mods)


def finish():
    square = whole((ROWS_DEV, D))
    return Phase(
        finish_kernel,
        grid=(1,),
        in_specs=[square, whole((2, 6 * D)), square, square],
        out_specs=[square, whole((2, 2 * D))],
        out_shape=[shape((ROWS_DEV, D), FULL), shape((2, 2 * D), FULL)],
        name="finish",
    )


class Place:
    def __init__(self):
        self.w = lax.axis_index("wide")
        self.n = lax.axis_index("narrow")
        self.c = lax.bitwise_xor(self.w, 1)
        self.x = lax.bitwise_xor(self.w, 2)
        self.y = lax.bitwise_xor(self.w, 4)
        self.d = lax.bitwise_xor(self.w, 6)
        self.up = jnp.minimum(self.n + 1, 3)
        self.down = jnp.maximum(self.n - 1, 0)
        self.order = (
            self.n,
            lax.bitwise_xor(self.n, 1),
            jnp.where(self.n < 2, 2, 1),
            jnp.where(self.n < 2, 3, 0),
        )

    def enter(self):
        barrier = pltpu.get_barrier_semaphore()
        for peer in (self.x, self.y, self.c):
            pl.semaphore_signal(barrier, inc=1, device_id=(peer, self.n), device_id_type=MESH)

        @pl.when(self.n > 0)
        def _():
            pl.semaphore_signal(barrier, inc=1, device_id=(self.w, self.n - 1), device_id_type=MESH)

        @pl.when(self.n < 3)
        def _():
            pl.semaphore_signal(barrier, inc=1, device_id=(self.w, self.n + 1), device_id_type=MESH)

        ends = jnp.where(self.n > 0, 1, 0) + jnp.where(self.n < 3, 1, 0)
        pl.semaphore_wait(barrier, 3 + ends)

    def enter_all(self):
        barrier = pltpu.get_barrier_semaphore()
        for step in range(1, 8):
            peer = (lax.bitwise_xor(self.w, step), self.n)
            pl.semaphore_signal(barrier, inc=1, device_id=peer, device_id_type=MESH)
        for step in range(1, 4):
            peer = (self.w, lax.bitwise_xor(self.n, step))
            pl.semaphore_signal(barrier, inc=1, device_id=peer, device_id_type=MESH)
        pl.semaphore_wait(barrier, 10)

    def passes_on(self, col):
        return jnp.logical_or(
            jnp.logical_and(col < self.n, self.n < 3), jnp.logical_and(col > self.n, self.n > 0)
        )

    def carried(self, col):
        return jnp.logical_or(
            jnp.logical_and(col > self.n, self.n > 0), jnp.logical_and(col < self.n, self.n < 3)
        )


def remote(src, dst, send, recv, to):
    return pltpu.make_async_remote_copy(
        src_ref=src, dst_ref=dst, send_sem=send, recv_sem=recv, device_id=to, device_id_type=MESH
    )


def span(index, size):
    return pl.ds(pl.multiple_of(index * size, size), size)


DMA = pltpu.SemaphoreType.DMA
FOLDS = [(3, 1), (3, 3), (3, 0), (3, 2)]
FOLDS += [(2, 3), (1, 3), (2, 2), (1, 2), (1, 1), (2, 1), (1, 0), (2, 0)]
FOLDS += [(0, 3), (0, 2), (0, 1), (0, 0)]
LOADS = 2
PIECES = 4
PIECE = ROWS_DEV // PIECES


class Names:
    def __init__(self, owner):
        self.owner = owner

    def __getattr__(self, name):
        return self.owner, name


A, S, J = Names(0), Names(1), Names(2)


class Feed:
    def __init__(self, enter):
        self.enter, self.steps, self.drains = enter, [], []

    def add(self, function, *args):
        self.steps.append(functools.partial(function, *args))

    def drain(self, function, *args):
        self.drains.append(functools.partial(function, *args))

    def follow(self, tables):
        self.lists = []
        for table in tables:
            parts = [[]]
            for number in table:
                if number < 0:
                    parts.append([])
                else:
                    parts[-1].append(self.steps[number])
            self.lists.append(parts)
        self.slot = 0
        self.at_end = jnp.logical_or(Place().n == 0, Place().n == 3)

    def do(self, slot):
        ends, middles = (parts[slot] for parts in self.lists)

        @pl.when(self.at_end)
        def _():
            for step in ends:
                step()

        @pl.when(jnp.logical_not(self.at_end))
        def _():
            for step in middles:
                step()

    def over(self, phase):
        first, total = self.slot, phase.grid[0]
        self.do(first)
        self.slot += total * phase.ticks

        def tick(t):
            for i in range(total):
                slot = first + i * phase.ticks + t
                if slot > first and any(parts[slot] for parts in self.lists):

                    @pl.when(pl.program_id(0) == i)
                    def _():
                        self.do(slot)

        return tick

    def rest(self):
        self.do(self.slot)
        for step in self.drains:
            step()


class Gather:
    def __init__(self, shapes, line, collective_id):
        self.shapes, self.line, self.collective_id = shapes, line, collective_id
        count, lines = len(shapes), 1 if line else 0
        self.in_specs = [pl.BlockSpec(memory_space=pl.ANY)] * (count + lines)
        self.out_specs = self.in_specs
        self.out_shape = [shape((8 * r, 4 * c), LOW) for r, c in shapes]
        self.out_shape += [shape((4 * ROWS_DEV, D), LOW)] * lines
        self.scratch = [
            DMA((count, 5)),
            DMA((count, 4)),
            DMA((count, 2, 4)),
            DMA((count, 2, 4)),
            DMA((count, 2, 4)),
            DMA((count, 2, 4)),
            DMA((count, 4)),
            DMA((count, 4)),
            DMA((count,)),
        ]
        self.scratch += [DMA((PIECES, 5)), DMA((PIECES, 4)), DMA((PIECES,))] * lines

    def steps(self, ins, outs, scratch):
        at = Place()
        shapes, count = self.shapes, len(self.shapes)
        w, n = at.w, at.n
        shards, fulls = ins[:count], outs[:count]
        z_send, z_recv, x_send, x_recv, y_send, y_recv, c_send, c_recv, own_sem = scratch[:9]

        def block(k, row, col):
            rows, cols = shapes[k]
            return fulls[k].at[span(row, rows), span(col, cols)]

        def z_copy(k, src, col, slot, to):
            return remote(src, block(k, w, col), z_send.at[k, slot], z_recv.at[k, col], (w, to))

        def x_copy(k, src, row, far, col):
            sems = x_send.at[k, far, col], x_recv.at[k, far, col]
            return remote(src, block(k, row, col), *sems, (at.x, n))

        def y_copy(k, src, row, far, col):
            sems = y_send.at[k, far, col], y_recv.at[k, far, col]
            return remote(src, block(k, row, col), *sems, (at.y, n))

        def c_copy(k, chip):
            row = (w, at.x, at.y, at.d)[chip]
            here = fulls[k].at[span(row, shapes[k][0])]
            return remote(here, here, c_send.at[k, chip], c_recv.at[k, chip], (at.c, n))

        def own_copy(k):
            return pltpu.make_async_copy(shards[k], block(k, w, n), own_sem.at[k])

        def own(k):
            @pl.when(n < 3)
            def _():
                z_copy(k, shards[k], n, n, at.up).start()

            @pl.when(n > 0)
            def _():
                z_copy(k, shards[k], n, 4, at.down).start()

            x_copy(k, shards[k], w, 0, n).start()
            y_copy(k, shards[k], w, 0, n).start()
            own_copy(k).start()

        def z_stage(k, j):
            col = at.order[j]
            here = block(k, w, col)
            z_copy(k, here, col, col, at.up).wait_recv()

            @pl.when(at.passes_on(col))
            def _():
                z_copy(k, here, col, col, jnp.where(col < n, at.up, at.down)).start()

            x_copy(k, here, w, 0, col).start()
            y_copy(k, here, w, 0, col).start()

        def near_stage(k, j):
            col = at.order[j]
            from_x = block(k, at.x, col)
            from_y = block(k, at.y, col)
            x_copy(k, from_x, at.x, 0, col).wait_recv()
            if j < 2:
                y_copy(k, from_x, at.x, 1, col).start()
            y_copy(k, from_y, at.y, 0, col).wait_recv()
            if j >= 2:
                x_copy(k, from_y, at.y, 1, col).start()

        def far_stage(k, j):
            col = at.order[j]
            far = block(k, at.d, col)
            (y_copy if j < 2 else x_copy)(k, far, at.d, 1, col).wait_recv()

        def rows_on(k):
            own_copy(k).wait()
            for chip in range(3):
                c_copy(k, chip).start()

        def far_on(k):
            c_copy(k, 3).start()

        def ready(k):
            for chip in range(4):
                c_copy(k, chip).wait_recv()

        def drain(k):
            for j in range(4):
                col = at.order[j]
                here = block(k, w, col)

                @pl.when(at.passes_on(col) if j else n < 3)
                def _():
                    z_copy(k, here, col, col, at.up).wait_send()

                x_copy(k, here, w, 0, col).wait_send()
                y_copy(k, here, w, 0, col).wait_send()
                (y_copy if j < 2 else x_copy)(k, here, w, 1, col).wait_send()
            for chip in range(4):
                c_copy(k, chip).wait_send()

            @pl.when(n > 0)
            def _():
                z_copy(k, shards[k], n, 4, at.down).wait_send()

        if self.line:
            rows, all_rows = ins[count], outs[count]
            t_send, t_recv, t_own = scratch[9:]

            def piece(p, col):
                return all_rows.at[pl.ds(pl.multiple_of(col * ROWS_DEV + p * PIECE, 16), PIECE)]

            def t_copy(p, src, col, slot, to):
                dst = piece(p, col)
                return remote(src, dst, t_send.at[p, slot], t_recv.at[p, col], (w, to))

            def t_own_copy(p):
                here = pl.ds(p * PIECE, PIECE)
                return pltpu.make_async_copy(rows.at[here], piece(p, n), t_own.at[p])

            def t_start(p, late):
                src = rows.at[pl.ds(p * PIECE, PIECE)]
                if not late:
                    t_own_copy(p).start()

                @pl.when(n == 2 if late else n < 2)
                def _():
                    t_copy(p, src, n, n, at.up).start()

                @pl.when(n == 1 if late else n >= 2)
                def _():
                    t_copy(p, src, n, 4, at.down).start()

            def t_stage(p, j):
                col = at.order[j]
                here = piece(p, col)
                t_copy(p, here, col, col, at.up).wait_recv()

                @pl.when(at.passes_on(col))
                def _():
                    t_copy(p, here, col, col, jnp.where(col < n, at.up, at.down)).start()

            def t_drain(p):
                for j in range(4):
                    col = at.order[j]
                    here = piece(p, col)

                    @pl.when(at.passes_on(col) if j else n < 3)
                    def _():
                        t_copy(p, here, col, col, at.up).wait_send()

                @pl.when(n > 0)
                def _():
                    t_copy(p, piece(p, n), n, 4, at.down).wait_send()

            def t_ready():
                for p in range(PIECES):
                    t_own_copy(p).wait()

        items = Feed(at.enter)
        for k in range(count):
            items.add(own, k)
            for j in range(1, 4):
                items.add(z_stage, k, j)
            for j in range(4):
                items.add(near_stage, k, j)
            for j in range(4):
                items.add(far_stage, k, j)
            items.add(rows_on, k)
            items.add(far_on, k)
            items.add(ready, k)
            items.drain(drain, k)
        if self.line:
            for p in range(PIECES):
                items.add(t_start, p, False)
                items.add(t_start, p, True)
                for j in range(1, 4):
                    items.add(t_stage, p, j)
                items.drain(t_drain, p)
            items.add(t_ready)
        return items


class Scatter:
    def __init__(self, shapes, line, collective_id):
        self.shapes, self.line, self.collective_id = shapes, line, collective_id
        count, lines = len(shapes), 1 if line else 0
        self.out_shape = [shape(s, FULL) for s in shapes] + [shape((ROWS_DEV, D), FULL)] * lines
        self.out_specs = [pl.BlockSpec(memory_space=pltpu.VMEM)] * len(self.out_shape)
        self.scratch = []
        for s in shapes:
            self.scratch += [
                pltpu.VMEM((4, 4) + s, LOW),
                pltpu.VMEM((4,) + s, LOW),
                pltpu.VMEM((2, 4) + s, LOW),
                pltpu.VMEM((5,) + s, LOW),
                pltpu.VMEM((LOADS,) + s, LOW),
            ]
        self.scratch += [
            DMA((count, 4, 4)),
            DMA((count, 4, 4)),
            DMA((count, 4, 4)),
            DMA((count, 4)),
            DMA((count, 4)),
            DMA((count, 2, 4)),
            DMA((count, 2, 4)),
            DMA((count, 4)),
            DMA((count, 5)),
        ]
        self.scratch += [
            pltpu.VMEM((PIECES, 4, PIECE, D), LOW),
            pltpu.VMEM((PIECES, 5, PIECE, D), LOW),
            DMA((PIECES, 4)),
            DMA((PIECES, 5)),
        ] * lines

    def steps(self, ins, outs, scratch):
        at = Place()
        shapes, count = self.shapes, len(self.shapes)
        w, n, order = at.w, at.n, at.order
        chips = (w, at.x, at.y, at.d)
        held, far_in, near_in, z_in, staged = (scratch[i : 5 * count : 5] for i in range(5))
        load, c_send, c_recv, d_send, d_recv, n_send, n_recv, z_send, z_recv = scratch[
            5 * count : 5 * count + 9
        ]

        def source(k, row, col):
            rows, cols = shapes[k]
            return ins[k].at[span(row, rows), span(col, cols)]

        def load_copy(k, chip, j):
            slot = FOLDS.index((chip, j)) % LOADS
            return pltpu.make_async_copy(
                source(k, chips[chip], order[j]), staged[k].at[slot], load.at[k, chip, j]
            )

        def c_copy(k, chip, col):
            src = source(k, lax.bitwise_xor(chips[chip], 1), col)
            sems = c_send.at[k, chip, col], c_recv.at[k, chip, col]
            return remote(src, held[k].at[chip, col], *sems, (at.c, n))

        def d_copy(k, j):
            sems = d_send.at[k, j], d_recv.at[k, j]
            to = (at.x if j < 2 else at.y, n)
            return remote(held[k].at[3, order[j]], far_in[k].at[j], *sems, to)

        def n_copy(k, chip, col):
            sems = n_send.at[k, chip - 1, col], n_recv.at[k, chip - 1, col]
            dst = near_in[k].at[chip - 1, col]
            return remote(held[k].at[chip, col], dst, *sems, (chips[chip], n))

        def z_copy(k, col, slot, to):
            sems = z_send.at[k, col], z_recv.at[k, slot]
            return remote(held[k].at[0, col], z_in[k].at[slot], *sems, (w, to))

        def add(target, rows, *others):
            step = 64 if rows % 64 == 0 else 48

            @pl.loop(0, rows // step)
            def _(i):
                here = span(i, step)
                total = target[here, :]
                for other in others:
                    total = total + other[here, :]
                target[here, :] = total

        def fold(k, chip, j, *others):
            number = FOLDS.index((chip, j))
            load_copy(k, chip, j).wait()
            c_copy(k, chip, order[j]).wait_recv()
            add(held[k].at[chip, order[j]], shapes[k][0], staged[k].at[number % LOADS], *others)
            if number + LOADS < len(FOLDS):
                load_copy(k, *FOLDS[number + LOADS]).start()

        def begin(k):
            for chip, j in FOLDS:
                c_copy(k, chip, order[j]).start()
            for chip, j in FOLDS[:LOADS]:
                load_copy(k, chip, j).start()

        def far(k, j):
            fold(k, 3, j)
            d_copy(k, j).start()

        def near(k, j):
            chip = 2 if j >= 2 else 1
            fold(k, chip, j)
            n_copy(k, chip, order[j]).start()

        def near_far(k, j):
            chip = 1 if j >= 2 else 2
            d_copy(k, j).wait_recv()
            fold(k, chip, j, far_in[k].at[j])
            n_copy(k, chip, order[j]).start()

        def line_slot(col):
            to = jnp.where(col > n, at.up, at.down)
            return jnp.where(jnp.logical_and(col < n, to == col), 4, col), to

        def fold_near(k, j):
            col = order[j]
            n_copy(k, 1, col).wait_recv()
            n_copy(k, 2, col).wait_recv()
            fold(k, 0, j, near_in[k].at[0, col], near_in[k].at[1, col])

        def along(k, j):
            col = order[j]
            fold_near(k, j)

            @pl.when(at.carried(col))
            def _():
                z_copy(k, col, col, at.up).wait_recv()
                add(held[k].at[0, col], shapes[k][0], z_in[k].at[col])

            slot, to = line_slot(col)
            z_copy(k, col, slot, to).start()

        def last(k):
            fold_near(k, 0)
            outs[k][...] = held[k][0, n].astype(FULL)

            @pl.when(n > 0)
            def _():
                z_copy(k, n, n, at.up).wait_recv()
                outs[k][...] += z_in[k][n].astype(FULL)

            @pl.when(n < 3)
            def _():
                z_copy(k, n, 4, at.up).wait_recv()
                outs[k][...] += z_in[k][4].astype(FULL)

        def drain(k):
            for chip in range(4):
                for col in range(4):
                    c_copy(k, chip, col).wait_send()
            for j in range(4):
                d_copy(k, j).wait_send()
                n_copy(k, 1, j).wait_send()
                n_copy(k, 2, j).wait_send()
            for j in range(1, 4):
                z_copy(k, order[j], order[j], at.up).wait_send()

        if self.line:
            line_held, line_in, line_send, line_recv = scratch[5 * count + 9 :]
            self.line_held = line_held

            def line_copy(p, col, slot, to):
                sems = line_send.at[p, col], line_recv.at[p, slot]
                return remote(line_held.at[p, col], line_in.at[p, slot], *sems, (w, to))

            def line_stage(j, p):
                col = order[j]

                @pl.when(at.carried(col))
                def _():
                    line_copy(p, col, col, at.up).wait_recv()
                    add(line_held.at[p, col], PIECE, line_in.at[p, col])

                slot, to = line_slot(col)
                line_copy(p, col, slot, to).start()

            def line_last(p):
                here = pl.ds(p * PIECE, PIECE)
                outs[count][here, :] = line_held[p, n].astype(FULL)

                @pl.when(n > 0)
                def _():
                    line_copy(p, n, n, at.up).wait_recv()
                    outs[count][here, :] += line_in[p, n].astype(FULL)

                @pl.when(n < 3)
                def _():
                    line_copy(p, n, 4, at.up).wait_recv()
                    outs[count][here, :] += line_in[p, 4].astype(FULL)

            def line_drain():
                for p in range(PIECES):
                    for j in range(1, 4):
                        line_copy(p, order[j], order[j], at.up).wait_send()

        items = Feed(at.enter)
        for k in range(count):
            items.add(begin, k)
            for j in (1, 3, 0, 2):
                items.add(far, k, j)
            for j in (3, 2, 1, 0):
                items.add(near, k, j)
                items.add(near_far, k, j)
            for j in (3, 2, 1):
                items.add(along, k, j)
            items.add(last, k)
            items.drain(drain, k)
        if self.line:
            for j in (3, 2, 1):
                for p in range(PIECES):
                    items.add(line_stage, j, p)
            for p in range(PIECES):
                items.add(line_last, p)
            items.add(lambda: None)
            items.drain(line_drain)
        return items


def fused(script, args, outs, engine, moved, name):
    in_specs = [SCALARS.spec() if k == A.live else pl.BlockSpec(memory_space=pl.ANY) for k in args]
    counts = [len(args), len(outs), len(engine.out_specs)]

    def kernel(*refs):
        groups = []
        for count in counts:
            groups.append(refs[:count])
            refs = refs[count:]
        named = dict(zip(list(args) + list(outs), groups[0] + groups[1]))
        feed = engine.steps([named[k] for k in moved], groups[2], refs)
        script(named, groups[2], feed)

    results = pl.pallas_call(
        kernel,
        in_specs=in_specs,
        out_specs=[pl.BlockSpec(memory_space=pl.ANY)] * len(outs) + engine.out_specs,
        out_shape=list(outs.values()) + engine.out_shape,
        scratch_shapes=engine.scratch,
        compiler_params=pltpu.CompilerParams(
            collective_id=engine.collective_id, has_side_effects=True, vmem_limit_bytes=62 * 2**20
        ),
        cost_estimate=pl.CostEstimate(flops=100_000_000_000, bytes_accessed=0, transcendentals=0),
        name=name,
    )(*args.values())
    return dict(zip(outs, results)), list(results[len(outs) :])


class Joined:
    def __init__(self, engine, other):
        self.engine, self.other = engine, other
        self.collective_id = engine.collective_id
        self.out_specs = engine.out_specs + other.out_specs
        self.out_shape = engine.out_shape + other.out_shape
        self.scratch = engine.scratch + other.scratch

    def steps(self, ins, outs, scratch):
        cuts = len(ins) - self.other.takes, len(self.engine.out_specs), len(self.engine.scratch)
        feed = self.engine.steps(ins[: cuts[0]], outs[: cuts[1]], scratch[: cuts[2]])
        for step in self.other.steps(ins[cuts[0] :], outs[cuts[1] :], scratch[cuts[2] :]):
            feed.add(step)
        feed.enter = Place().enter_all
        return feed


STRIP = 768


def strips(b, q):
    return b * 2 + q


class Modulation:
    takes = 4

    def __init__(self):
        self.out_shape = [shape((2, 6 * D), FULL)] * 2 + [shape((16, 128), FULL)]
        self.out_specs = [pl.BlockSpec(memory_space=pl.ANY)] * 2
        self.out_specs += [pl.BlockSpec(memory_space=pltpu.VMEM)]
        self.scratch = [
            pltpu.VMEM((8, 8, 128), FULL),
            pltpu.VMEM((8, 128), FULL),
            pltpu.VMEM((2, 128, 2 * STRIP), LOW),
            pltpu.VMEM((8, 8, STRIP), FULL),
            pltpu.VMEM((8, 8, STRIP), FULL),
            pltpu.VMEM((4, 8, STRIP), FULL),
            pltpu.VMEM((2, 2, 6 * D), FULL),
            DMA((3, 8)),
            DMA((3, 8)),
            DMA((6,)),
        ]

    def steps(self, ins, outs, scratch):
        at = Place()
        w, n = at.w, at.n
        images, clips, *shards = ins
        cond, clip, held, terms, arrived, got, made, send, recv, local = scratch

        def across(stage, step, src, dst):
            to = (lax.bitwise_xor(w, step), n)
            return remote(src, dst, send.at[stage, step], recv.at[stage, step], to)

        def first(step):
            return across(0, step, images.at[lax.bitwise_xor(w, step)], cond.at[w])

        def second(step):
            return across(1, step, terms.at[lax.bitwise_xor(w, step)], arrived.at[w])

        def third(step):
            to = (w, lax.bitwise_xor(n, step))
            return remote(got.at[n], got.at[n], send.at[2, step], recv.at[2, step], to)

        def loads():
            return [
                pltpu.make_async_copy(images.at[w], cond.at[w], local.at[0]),
                pltpu.make_async_copy(clips, clip, local.at[1]),
                pltpu.make_async_copy(shards[0], held.at[0], local.at[2]),
                pltpu.make_async_copy(shards[1], held.at[1], local.at[3]),
            ]

        def stores():
            return [
                pltpu.make_async_copy(made.at[b], outs[b], local.at[4 + b]) for b in range(2)
            ]

        def start():
            for copy in loads():
                copy.start()
            for step in range(1, 8):
                first(step).start()

        def project():
            for copy in loads():
                copy.wait()
            for step in range(1, 8):
                first(step).wait_recv()
            flat = jnp.concatenate([cond[:, 0, :], clip[...]], axis=0).astype(LOW)
            outs[2][8:16, :] = cond[:, 0, :]
            for g in range(8):
                outs[2][g : g + 1, :] = clip[g // 4 : g // 4 + 1, :]
            for b in range(2):
                product = nn(flat, held[b])
                for g in range(8):
                    for r, row in enumerate((8 + g // 4, g)):
                        for q in range(2):
                            to = r * 4 + strips(b, q)
                            terms[g, to : to + 1, :] = product[row : row + 1, q * STRIP : (q + 1) * STRIP]
            for step in range(1, 8):
                second(step).start()

        def total():
            value = terms[w]
            for step in range(1, 8):
                second(step).wait_recv()
                value = value + arrived[lax.bitwise_xor(w, step)]
            got[n] = value
            for step in range(1, 4):
                third(step).start()

        def spread():
            for step in range(1, 4):
                third(step).wait_recv()
            for col in range(4):
                for b in range(2):
                    for r in range(2):
                        for q in range(2):
                            here = r * 4 + strips(b, q)
                            to = col * 2 * STRIP + q * STRIP
                            made[b, r : r + 1, to : to + STRIP] = got[col, here : here + 1, :]
            for copy in stores():
                copy.start()

        def settle():
            for copy in stores():
                copy.wait()
            for step in range(1, 8):
                first(step).wait_send()
                second(step).wait_send()
            for step in range(1, 4):
                third(step).wait_send()

        return start, project, total, spread, settle


class ModulationBack:
    takes = 0

    def __init__(self):
        self.out_shape = [shape((128, 2 * STRIP), FULL)] * 2
        self.out_specs = [pl.BlockSpec(memory_space=pltpu.VMEM)] * 2
        self.scratch = [
            pltpu.VMEM((4, 8, STRIP), FULL),
            pltpu.VMEM((4, 8, STRIP), FULL),
            pltpu.VMEM((8, 8, STRIP), FULL),
            pltpu.VMEM((2, 2, 6 * D), FULL),
            pltpu.VMEM((16, 128), FULL),
            DMA((2, 8)),
            DMA((2, 8)),
            DMA((5,)),
        ]

    def steps(self, ins, outs, scratch):
        at = Place()
        w, n = at.w, at.n
        pieces, arrived, every, grads, cond, send, recv, local = scratch

        def along(step):
            to = (w, lax.bitwise_xor(n, step))
            src = pieces.at[lax.bitwise_xor(n, step)]
            return remote(src, arrived.at[n], send.at[0, step], recv.at[0, step], to)

        def across(step):
            to = (lax.bitwise_xor(w, step), n)
            return remote(every.at[w], every.at[w], send.at[1, step], recv.at[1, step], to)

        def begin():
            cond_ref, early, late = self.sources
            copies = [pltpu.make_async_copy(cond_ref, cond, local.at[4])]
            for b in range(2):
                cut = pl.ds(2 * D, 4 * D)
                here = grads.at[b, :, pl.ds(0, 2 * D)]
                copies.append(pltpu.make_async_copy(early[b], here, local.at[2 * b]))
                here = grads.at[b, :, cut]
                copies.append(pltpu.make_async_copy(late[b].at[:, cut], here, local.at[2 * b + 1]))
            for copy in copies:
                copy.start()
            for copy in copies:
                copy.wait()
            for col in range(4):
                for b in range(2):
                    for r in range(2):
                        for q in range(2):
                            to = r * 4 + strips(b, q)
                            here = col * 2 * STRIP + q * STRIP
                            pieces[col, to : to + 1, :] = grads[b, r : r + 1, here : here + STRIP]
            for step in range(1, 4):
                along(step).start()

        def finish():
            value = pieces[n]
            for step in range(1, 4):
                along(step).wait_recv()
                value = value + arrived[lax.bitwise_xor(n, step)]
            every[w] = value
            for step in range(1, 8):
                across(step).start()
            for step in range(1, 8):
                across(step).wait_recv()
            for b in range(2):
                for q in range(2):
                    rows = [every[:, r * 4 + strips(b, q), :] for r in range(2)]
                    outs[b][:, q * STRIP : (q + 1) * STRIP] = lax.dot_general(
                        cond[...],
                        jnp.concatenate(rows, axis=0),
                        (((0,), (0,)), ((), ())),
                        precision=lax.Precision.HIGHEST,
                        preferred_element_type=FULL,
                    )
            for step in range(1, 4):
                along(step).wait_send()
            for step in range(1, 8):
                across(step).wait_send()

        return begin, finish


TILES = 32
JOINT_TILES = 18


def thirds(value):
    high = value.astype(LOW)
    rest = value - high.astype(FULL)
    middle = rest.astype(LOW)
    return high, middle, (rest - middle.astype(FULL)).astype(LOW)


def gathered_by(value, pattern):
    first = half_mask()
    zero = jnp.zeros_like(value)
    both = jnp.concatenate([jnp.where(first, value, zero), jnp.where(first, zero, value)], axis=0)
    parts = [nn(part, pattern) for part in thirds(both)]
    return parts[0] + (parts[1] + parts[2])


class BiasBack:
    takes = 2

    def __init__(self):
        self.out_shape = [shape((TILES, 8, 256), FULL)]
        self.out_specs = [pl.BlockSpec(memory_space=pltpu.VMEM)]
        gaps = HEADS // 2 * (2 * TW - 1)
        self.scratch = [
            pltpu.VMEM((CHUNK, gaps, 128), FULL),
            pltpu.VMEM((2 * SW, 8, 2, SW, 128), FULL),
            pltpu.VMEM((2 * gaps, 256), FULL),
            pltpu.VMEM((2, 8, 2 * SW, 256), FULL),
            pltpu.VMEM((TILES, 8, 256), FULL),
            pltpu.VMEM((8, 4, 8, 256), FULL),
            pltpu.VMEM((4, 4, 8, 256), FULL),
            DMA((CHUNK + 2 * SW,)),
            DMA((3, 8)),
            DMA((3, 8)),
        ]

    def steps(self, ins, outs, scratch):
        at = Place()
        w, n = at.w, at.n
        joint_grad, space_grad = ins
        (result,) = outs
        joint_rows, space_rows, joint_sum, space_sum, tiles, groups, line, local, send, recv = scratch
        query = lax.broadcasted_iota(jnp.int32, (128, 256), 0) % CHUNK
        column = lax.broadcasted_iota(jnp.int32, (128, 256), 1)

        def load(k):
            if k < CHUNK:
                return pltpu.make_async_copy(joint_grad.at[:, k, :], joint_rows.at[k], local.at[k])
            k -= CHUNK
            src = space_grad.at[:, :, k // SW, :, k % SW, :]
            return pltpu.make_async_copy(src, space_rows.at[k], local.at[CHUNK + k])

        def start():
            joint_sum[...] = jnp.zeros_like(joint_sum)
            space_sum[...] = jnp.zeros_like(space_sum)
            tiles[...] = jnp.zeros_like(tiles)
            for k in range(CHUNK + 2 * SW):
                load(k).start()

        def joint_part(part):
            for k in range(part * SW, (part + 1) * SW):
                load(k).wait()

            @pl.loop(0, SW)
            def _(col):
                to = (query // SW - part + SW - 1) * SPAN_T + query % SW - col + SW - 1
                pattern = jnp.where(column == to, 1.0, 0.0).astype(LOW)
                joint_sum[...] += gathered_by(joint_rows[part * SW + col], pattern)

        def space_part(part):
            for k in range(CHUNK + part * 4, CHUNK + part * 4 + 4):
                load(k).wait()

            @pl.loop(0, 4)
            def _(i):
                col = part * 4 + i
                to = query // SW * SPAN_S + lax.rem(n, 2) * SW + query % SW - col + 2 * SW - 1
                pattern = jnp.where(column == to, 1.0, 0.0).astype(LOW)
                value = gathered_by(space_rows[col].reshape(128, 128), pattern)
                space_sum[...] += value.reshape(2, 8, 2 * SW, 256)

        def across(stage, step, src, dst):
            to = (lax.bitwise_xor(w, step), n)
            return remote(src, dst, send.at[stage, step], recv.at[stage, step], to)

        def first(step):
            src = tiles.at[span(lax.bitwise_xor(w, step), 4)]
            return across(0, step, src, groups.at[w])

        def second(step):
            to = (w, lax.bitwise_xor(n, step))
            return remote(line.at[n], line.at[n], send.at[1, step], recv.at[1, step], to)

        def third(step):
            here = result.at[span(w, 4)]
            return across(2, step, here, here)

        def settle():
            for t in range(JOINT_TILES):
                tiles[t] = joint_sum[t * 8 : (t + 1) * 8, :]
            for half in range(2):
                total = jnp.zeros((8, 1024), FULL)
                for row in range(2 * SW):
                    here = space_sum[half, :, row, :]
                    here = jnp.concatenate([here, jnp.zeros((8, 768), FULL)], axis=1)
                    total = total + pltpu.roll(here, (2 * SW - 1 - row) * SPAN_S, 1)
                moved = pltpu.roll(total, SW * SPAN_S, 1)
                total = jnp.where(n >= 2, moved, total)
                for q in range(4):
                    tiles[JOINT_TILES + half * 4 + q] = total[:, q * 256 : (q + 1) * 256]
            for step in range(1, 8):
                first(step).start()

        def sum_groups():
            value = tiles[span(w, 4)]
            for step in range(1, 8):
                first(step).wait_recv()
                value = value + groups[lax.bitwise_xor(w, step)]
            line[n] = value
            for step in range(1, 4):
                second(step).start()

        def sum_line():
            for step in range(1, 4):
                second(step).wait_recv()
            result[span(w, 4)] = (line[0] + line[1]) + (line[2] + line[3])
            for step in range(1, 8):
                third(step).start()

        def done():
            for step in range(1, 8):
                third(step).wait_recv()
            for step in range(1, 8):
                first(step).wait_send()
                third(step).wait_send()
            for step in range(1, 4):
                second(step).wait_send()

        made = [start] + [functools.partial(joint_part, p) for p in range(SW)]
        made += [functools.partial(space_part, p) for p in range(4)]
        return made + [settle, sum_groups, sum_line, done]


def bias_tables(tiles):
    gaps = 2 * TW - 1
    joint = tiles[:JOINT_TILES].reshape(2, HEADS // 2, gaps, 256)[..., : SPAN_T**2]
    space = tiles[JOINT_TILES : JOINT_TILES + 8].reshape(2, 4, 8, 256)
    space = space.transpose(2, 0, 1, 3).reshape(HEADS, 1024)[:, : SPAN_S**2]
    return space, joint.transpose(1, 0, 2, 3).reshape(HEADS, -1)


FORWARD_ENDS = (
    0, 15, 30, 141, 1, 4, 16, 19, 31, 34, 121, 126, 131, 136, 2, 5, 45, 142, 8, 46, 20, 17, 23,
    120, 143, 125, 130, 135, 32, 35, 75, 3, 38, 6, 122, 76, 9, 127, 49, 132, 50, 10, 24, 21, 137,
    60, 25, 36, 47, 90, 39, 79, 91, 40, 18, 144, 7, 12, 80, 33, 145, 77, 53, 92, 54, 48, 64, 11,
    13, 14, -1, 51, 123, -1, 61, -1, 94, 83, -1, -1, -1, -1, 128, 95, -1, 22, 27, 84, -1, -1, 133,
    55, 37, 42, 81, 138, -1, -1, 26, 28, -1, 96, 29, -1, 124, 41, 43, 85, 52, 57, 44, 129, 68, 100,
    65, 134, 56, 58, 98, 59, 139, 140, -1, -1, -1, 62, 99, 105, -1, -1, -1, 69, -1, -1, 106, -1,
    -1, 78, -1, -1, -1, 66, -1, -1, -1, -1, 63, -1, -1, -1, -1, -1, -1, 109, -1, -1, -1, -1, 93,
    -1, -1, 110, 82, 87, 107, 70, -1, -1, -1, 67, 108, 72, -1, 113, -1, -1, 86, 88, -1, 89, 97,
    102, -1, -1, -1, 114, -1, 71, 73, -1, -1, 74, 111, -1, -1, -1, 112, 101, 117, 103, -1, -1, 115,
    -1, -1, -1, 104, 116, 118, -1, -1, -1, -1, 119, -1, -1, -1, -1, -1, -1, -1, -1, -1, -1, -1, -1,
    -1, -1, -1, -1, -1, -1, -1, -1, -1, -1, -1, -1, -1, -1, -1, -1, -1, -1, -1, -1, -1, -1, -1, -1,
)
FORWARD_MIDDLES = (
    0, 15, 30, 141, 1, 2, 4, 45, 142, 16, 17, 19, 31, 32, 34, 143, 3, 121, 5, 75, 126, 131, 136, 6,
    47, 90, 18, 46, 120, 125, 130, 8, 135, 33, 144, 77, 49, 145, 20, 122, 21, 23, 92, 127, 35, 48,
    132, 36, 123, 10, 38, 137, 60, 76, 128, 7, 12, 9, 133, 79, 61, 138, 51, 91, 94, 124, 22, 27,
    25, 129, 50, 37, 42, 134, 81, 139, 140, 53, 40, 24, 62, 105, 78, 96, 63, 11, 13, 39, 14, -1,
    93, -1, 52, 57, -1, 107, 55, -1, 64, -1, 80, -1, 83, -1, 26, 28, -1, 65, 29, -1, -1, -1, 41,
    85, 95, 43, -1, -1, -1, 44, -1, 98, -1, -1, -1, 54, -1, -1, -1, -1, -1, -1, -1, 66, -1, -1,
    100, -1, -1, -1, -1, -1, -1, -1, -1, -1, 109, -1, -1, 82, 87, -1, -1, -1, -1, 67, 72, 106, 56,
    58, 97, 102, 59, -1, 108, 111, -1, -1, 70, 68, 86, 84, 88, -1, 89, -1, -1, 71, 69, 73, -1, -1,
    74, -1, 99, -1, -1, -1, 101, 113, 103, -1, -1, 104, -1, 110, -1, -1, 115, 112, 117, -1, -1,
    114, -1, -1, 116, 118, -1, -1, 119, -1, -1, -1, -1, -1, -1, -1, -1, -1, -1, -1, -1, -1, -1, -1,
    -1, -1, -1, -1, -1, -1, -1, -1, -1, -1, -1, -1, -1, -1, -1, -1, -1, -1, -1, -1, -1, -1, -1, -1,
)
BACK_JOINT_ENDS = (
    -1, -1, -1, -1, -1, -1, -1, -1, -1, -1, -1, -1, -1, -1, -1, -1, -1, -1, -1, -1, -1, -1, -1, -1,
    -1, -1, -1, -1, -1, -1, -1, -1, 0, -1, 1, -1, 2, 3, 4, 17, 5, -1, -1, -1, 18, 19, 6, 20, 7, 21,
    34, 22, -1, -1, 35, 8, 36, 9, 37, 10, 38, 11, 39, 12, -1, -1, -1, -1, -1, -1, -1, 13, -1, 23,
    24, -1, -1, -1, -1, -1, -1, -1, -1, -1, -1, 25, 14, 26, 27, 28, 29, -1, -1, 40, 41, -1, -1, -1,
    15, -1, 42, 43, 44, 45, 46, -1, -1, 30, -1, -1, 16, -1, 51, -1, 31, 52, 53, 54, 55, 56, -1, -1,
    32, -1, -1, -1, 47, -1, -1, 48, -1, 49, -1, -1, 33, -1, -1, 57, 58, -1, -1, -1, 50, 59, 60, 61,
    62, 63, -1, -1, 64, -1, -1, -1, 65, -1, -1, -1, 66, -1, -1, -1, -1, -1, -1, -1, -1, 67,
)
BACK_JOINT_MIDDLES = (
    -1, -1, -1, -1, -1, -1, -1, -1, -1, -1, -1, -1, -1, -1, -1, -1, -1, -1, -1, -1, -1, -1, -1, -1,
    -1, -1, -1, -1, -1, -1, -1, -1, 0, -1, 1, -1, 2, 3, 4, 17, 5, -1, -1, -1, 18, 19, 6, 20, 7, 21,
    34, 22, -1, -1, 35, 8, 36, 9, 37, 10, 38, 11, 39, 12, -1, -1, -1, -1, -1, -1, -1, -1, 23, 24,
    -1, -1, -1, -1, -1, 13, -1, -1, -1, -1, -1, 25, 26, 27, 28, 29, -1, -1, 40, 41, -1, -1, 14, -1,
    15, -1, 42, 43, 44, 45, 46, -1, -1, -1, -1, 16, -1, 51, 30, -1, 52, 53, 54, 55, 56, -1, -1, -1,
    -1, -1, 31, 32, -1, -1, -1, -1, -1, 47, 33, -1, 48, -1, 57, 49, 58, -1, 50, -1, 59, 60, 61, 62,
    63, -1, -1, -1, -1, -1, -1, -1, -1, 64, -1, -1, -1, 65, -1, 66, -1, -1, -1, -1, 67, -1,
)
BACK_SPACE_ENDS = (
    0, -1, 1, -1, 2, 3, 4, -1, 5, -1, -1, -1, -1, 6, 7, -1, -1, -1, -1, -1, 8, 9, 10, 11, 17, 12,
    -1, 18, 13, 19, 20, 21, -1, 22, -1, -1, -1, 14, -1, -1, -1, -1, 15, -1, -1, -1, -1, -1, 68, 69,
    70, 71, 23, 24, -1, 16, 25, 26, 27, 28, 34, 29, -1, 35, 30, 72, 73, 74, 75, 36, 37, 38, 39, -1,
    31, -1, 76, 77, 78, 79, -1, 32, -1, 80, -1, 40, 41, 42, 43, 81, 44, 45, 46, -1, 47, -1, 48, 49,
    -1, -1, 82, -1, -1, -1, -1, 83, 84, -1, -1, -1, 51, 87, 52, 88, 53, 89, 54, 90, 55, 91, 56, 92,
    57, 93, 58, 33, 94, 59, 95, 60, 96, 61, 97, 62, 98, 63, 99, 64, 100, 65, 101, 66, -1, 102, 85,
    103, 50, 86, 67,
)
BACK_SPACE_MIDDLES = (
    0, -1, 1, -1, 2, 3, 4, -1, 5, -1, -1, -1, -1, 6, 7, -1, -1, -1, -1, -1, 8, 9, 10, 11, 17, 12,
    -1, 18, -1, 19, 20, 21, -1, 22, -1, -1, -1, -1, 13, -1, -1, -1, -1, 14, -1, -1, 15, -1, 16, 23,
    24, -1, -1, -1, 25, 26, 68, 27, 28, 34, 29, -1, 35, 36, 69, 37, 38, 39, -1, 76, -1, 70, 77, -1,
    -1, 71, -1, -1, 40, 78, 41, 42, 43, 44, 45, 30, 46, -1, -1, -1, 79, -1, 72, -1, -1, -1, -1, 51,
    87, 73, 52, 74, 88, 53, 75, 89, 54, 90, 55, 31, 91, 56, 32, 92, 57, 80, 93, 58, 94, 59, 81, 95,
    60, 96, 61, 82, 97, 62, 98, 63, 83, 99, 84, 100, 33, 101, 47, -1, 48, 102, 64, 85, 49, 103, 65,
    50, 66, 86, 67,
)


def exact(left, right, dims):
    return lax.dot_general(
        left, right, (dims, ((), ())), precision=lax.Precision.HIGHEST, preferred_element_type=FULL
    )


def joint_pattern():
    keys, queries = np.meshgrid(np.arange(CHUNK), np.arange(CHUNK), indexing="ij")
    at = (queries // SW - keys // SW + SW - 1) * SPAN_T + queries % SW - keys % SW + SW - 1
    return (jnp.arange(SPAN_T**2)[:, None] == jnp.asarray(at.reshape(-1), jnp.int32)[None, :]).astype(FULL)


def joint_table(lookup):
    flat = lookup.reshape(HEADS * (2 * TW - 1), SPAN_T**2)
    grid = exact(flat, joint_pattern(), ((1,), (0,)))
    grid = grid.reshape(HEADS // 2, 2, 2 * TW - 1, CHUNK, CHUNK)
    return jnp.concatenate([grid[:, 0], grid[:, 1]], axis=-1)


def joint_table_back(grad):
    grad = grad.reshape(HEADS // 2, 2 * TW - 1, CHUNK, 2 * CHUNK)
    pairs = jnp.stack([grad[..., :CHUNK], grad[..., CHUNK:]], axis=1)
    flat = pairs.reshape(HEADS * (2 * TW - 1), CHUNK * CHUNK)
    return exact(flat, joint_pattern(), ((1,), (1,))).reshape(HEADS, -1)


def space_pattern(quarter):
    query = jnp.arange(CHUNK)
    key_col = jnp.arange(2 * SW)
    gap = quarter % 2 * SW + (query % SW)[None, :] - key_col[:, None] + 2 * SW - 1
    row = jnp.broadcast_to((query // SW)[None, :], gap.shape)
    at = (row * SPAN_S + gap).reshape(-1)
    return (jnp.arange(SW * SPAN_S)[:, None] == at[None, :]).astype(FULL)


def space_table(lookup, quarter):
    grid = lookup.reshape(HEADS, SPAN_S, SPAN_S)
    seen = lax.dynamic_slice_in_dim(grid, quarter // 2 * SW, 3 * SW - 1, 1)
    rows = jnp.stack([seen[:, 2 * SW - 1 - k : 3 * SW - 1 - k] for k in range(2 * SW)])
    made = exact(rows.reshape(2 * SW * HEADS, SW * SPAN_S), space_pattern(quarter), ((1,), (0,)))
    made = made.reshape(2, SW, HEADS // 2, 2, 2, SW, CHUNK)
    made = made.transpose(2, 0, 4, 1, 5, 3, 6)
    return made.reshape(HEADS // 2, 4 * CHUNK, 2 * CHUNK)


def space_table_back(grad, quarter):
    made = grad.reshape(HEADS // 2, 2, 2, SW, SW, 2, CHUNK).transpose(1, 3, 0, 5, 2, 4, 6)
    flat = made.reshape(2 * SW * HEADS, 2 * SW * CHUNK)
    rows = exact(flat, space_pattern(quarter), ((1,), (1,))).reshape(2 * SW, HEADS, SW, SPAN_S)
    seen = sum(
        jnp.pad(rows[k], ((0, 0), (2 * SW - 1 - k, k), (0, 0))) for k in range(2 * SW)
    )
    grid = jnp.zeros((HEADS, SPAN_S, SPAN_S), FULL)
    return lax.dynamic_update_slice_in_dim(grid, seen, quarter // 2 * SW, 1).reshape(HEADS, -1)


def modulations(cond, shards):
    groups = cond.shape[0]
    rows = shards[0].shape[0]
    own = lax.dynamic_slice_in_dim(cond, lax.axis_index("wide") * rows, rows, 2)
    flat = own.reshape(groups * 2, rows)
    terms = jnp.stack([nn(flat, s).reshape(groups, 2, -1) for s in shards], axis=1)
    summed = lax.psum_scatter(terms, "wide", scatter_dimension=0, tiled=False)
    gathered = lax.all_gather(summed, "narrow", axis=0, tiled=False)
    return gathered.transpose(1, 2, 0, 3).reshape(2, 2, 6 * D)


def modulation_grads(cond, grads, rows):
    groups = cond.shape[0]
    own = lax.dynamic_slice_in_dim(cond, lax.axis_index("wide") * rows, rows, 2)
    flat = own.reshape(groups * 2, rows).astype(FULL)
    summed = lax.psum_scatter(
        grads.reshape(2, 2, 4, -1), "narrow", scatter_dimension=2, tiled=False
    )
    gathered = lax.all_gather(summed, "wide", axis=0, tiled=False)
    return [exact(flat, gathered[:, b].reshape(groups * 2, -1), ((0,), (0,))) for b in range(2)]


def gather_flat(shards):
    wide, narrow = lax.axis_size("wide"), lax.axis_size("narrow")
    project, output, expand, shrink = shards
    rows = project.shape[0]

    def settle(blocks):
        rows, cols = blocks.shape[-2:]
        blocks = blocks.reshape(wide, narrow, rows, cols).transpose(0, 2, 1, 3)
        return blocks.reshape(wide * rows, narrow * cols)

    first = lax.all_gather(
        jnp.concatenate([project, output, expand], axis=1), ("wide", "narrow"), axis=0, tiled=False
    )
    second = lax.all_gather(shrink, ("wide", "narrow"), axis=0, tiled=False)
    a, b = project.shape[1], project.shape[1] + output.shape[1]
    return settle(first[..., :a]), settle(first[..., a:b]), settle(first[..., b:]), settle(second)


def scatter_plain(partials):
    outs = []
    for g in partials:
        summed = lax.psum_scatter(g, "wide", scatter_dimension=0, tiled=True)
        outs.append(lax.psum_scatter(summed, "narrow", scatter_dimension=1, tiled=True).astype(FULL))
    return outs


def saved(b):
    return b.branch, b.middle, b.normed, b.active, b.slope, b.reduced


def mlp_takes(b):
    return A.live, b.rows, b.attended, b.mods, b.output, b.expand, b.shrink


def back_takes(b, grad):
    early = A.live, grad, b.attended, b.mods, b.branch, b.middle, b.normed, b.reduced
    return early + (b.output, b.active, b.slope, b.expand, b.shrink)


def back_gives(b):
    return b.to_shrink, b.to_expand, b.to_output, b.to_middle, b.to_attended, b.late


def weights_of(b):
    return b.project, b.output, b.expand, b.shrink


def shards_of(b):
    return b.own_project, b.own_output, b.own_expand, b.own_shrink


def partials_of(b):
    return b.to_shrink, b.to_expand, b.to_output, b.to_project


def grads_of(b):
    return b.grad_shrink, b.grad_expand, b.grad_output, b.grad_project


def stages():
    return {
        S.triple: (
            space_triple(),
            (A.all_rows, S.mods, S.project),
            (S.first, S.queries, S.pairs),
        ),
        S.attend: (
            space_attend(),
            (S.queries, S.pairs, S.pairs, S.table),
            (S.attended,),
        ),
        S.mlp: (
            mlp(False),
            mlp_takes(S),
            saved(S) + (J.rows,),
        ),
        J.triple: (
            joint_triple(),
            (J.rows, J.mods, J.project),
            (J.first, J.three),
        ),
        J.attend: (
            joint_attend(),
            (J.three,) * 3 + (J.table,),
            (J.attended,),
        ),
        J.mlp: (
            mlp(True),
            mlp_takes(J),
            saved(J) + (A.output_tokens,),
        ),
        J.mlp_back: (
            mlp_back(True),
            back_takes(J, A.cotangent),
            back_gives(J),
        ),
        J.attend_back: (
            joint_attend_back(),
            (J.three,) * 3 + (J.table, J.to_attended),
            (J.to_three, J.to_table),
        ),
        J.project_back: (
            joint_project_back(),
            (J.rows, J.mods, J.first, J.to_middle, J.project, J.to_three),
            (J.to_project, J.to_rows, J.early),
        ),
        S.mlp_back: (
            mlp_back(False),
            back_takes(S, J.to_rows),
            back_gives(S),
        ),
        S.attend_back: (
            space_attend_back(),
            (S.queries, S.pairs, S.pairs, S.table, S.to_attended),
            (S.to_queries, S.to_pairs, S.to_table),
        ),
        S.project_back: (
            space_project_back(),
            (S.first, S.project, S.to_queries, S.to_pairs),
            (S.to_project, A.to_first),
        ),
        S.weight_back: (
            space_weight_back(),
            (S.first, S.to_queries, S.to_pairs),
            (S.to_project,),
        ),
        A.finish: (
            finish(),
            (S.rows, S.mods, A.own_first, S.to_middle),
            (A.grad_tokens, S.early),
        ),
    }


def apart(values, names):
    for name in names:
        phase, takes, gives = stages()[name]
        values.update(zip(gives, phase(*[values[k] for k in takes])))


def together(values, plan, tables, engine, moved, brought, name, more=(), prepare=None, inline={}, made={}):
    table = stages()
    outs, args = dict(made), {}
    steps = [k for k in plan if k not in inline]
    for phase_name in steps:
        phase, takes, gives = table[phase_name]
        outs.update(zip(gives, phase.out_shape))
    for phase_name in steps:
        for k in table[phase_name][1]:
            if k not in outs and k not in brought:
                args[k] = values[k]
    for k in tuple(moved) + tuple(more):
        if k not in outs:
            args[k] = values[k]

    def script(refs, engine_outs, feed):
        refs.update(zip(brought, engine_outs))
        if prepare is not None:
            prepare(refs)
        feed.follow(tables)
        feed.enter()
        for phase_name in plan:
            if phase_name in inline:
                feed.do(feed.slot)
                inline[phase_name](refs, feed)
                continue
            phase, takes, gives = table[phase_name]
            phase.inside(feed.over(phase), [refs[k] for k in takes], [refs[k] for k in gives])
        feed.rest()

    results, arrived = fused(script, args, outs, engine, moved, name)
    values.update(results)
    values.update(zip(brought, arrived))


def body(
    tokens,
    clip_cond,
    image_cond,
    image_count,
    space_modulate,
    space_project,
    space_output,
    space_expand,
    space_reduce,
    space_bias,
    joint_modulate,
    joint_project,
    joint_output,
    joint_expand,
    joint_reduce,
    joint_bias,
    cotangent,
):
    small = lax.axis_size("wide") == 8
    narrow = lax.axis_index("narrow")
    wide = lax.axis_index("wide")
    rows = space_modulate.shape[0]
    low_clips = jax.nn.silu(clip_cond.astype(FULL)).astype(LOW)
    low_images = jax.nn.silu(image_cond.astype(FULL)).astype(LOW)
    values = {
        A.live: (image_count > 0).astype(FULL),
        S.rows: tokens,
        A.cotangent: cotangent,
        S.table: space_table(space_bias, narrow),
        J.table: joint_table(joint_bias),
    }
    weights = weights_of(S) + weights_of(J)
    space_shards = space_project, space_output, space_expand, space_reduce
    joint_shards = joint_project, joint_output, joint_expand, joint_reduce

    if small:
        moved = shards_of(S) + shards_of(J)
        shapes = [v.shape for v in space_shards + joint_shards]
        values.update(zip(moved, space_shards + joint_shards))
        values[A.images] = jnp.broadcast_to(low_images.astype(FULL).reshape(8, 1, rows), (8, 8, rows))
        own_clips = lax.dynamic_slice_in_dim(low_clips, wide * rows, rows, 1).astype(FULL)
        values[A.clips] = jnp.pad(own_clips, ((0, 6), (0, 0)))
        values[S.own_modulate] = space_modulate
        values[J.own_modulate] = joint_modulate
        gather = Gather(shapes, True, 0)

        def triple(refs, feed):
            takes = refs[S.rows], refs[A.all_rows], refs[S.mods], refs[S.project]
            gives = refs[S.first], refs[S.queries], refs[S.pairs]
            space_triple_parts(feed, 18, Place().order, *takes, *gives)

        whole_triple = stages()[S.triple]
        together(
            values,
            FORWARD,
            (FORWARD_ENDS, FORWARD_MIDDLES),
            Joined(gather, Modulation()),
            moved + (S.rows, A.images, A.clips, S.own_modulate, J.own_modulate),
            weights + (A.all_rows, S.mods, J.mods, A.cond),
            "forward",
            inline={A.triple: triple},
            made=dict(zip(whole_triple[2], whole_triple[0].out_shape)),
        )
        project_shape, output_shape, expand_shape, shrink_shape = shapes[:4]
        shapes = [shrink_shape, expand_shape, output_shape, project_shape]
        engine = Scatter(shapes, False, 1)
        tables = BACK_JOINT_ENDS, BACK_JOINT_MIDDLES
        together(values, BACK_JOINT, tables, engine, partials_of(J), grads_of(J), "back_joint")
        back = ModulationBack()
        engine = Scatter(shapes, True, 2)

        def first_back(refs, feed):
            takes = refs[S.project], refs[S.to_queries], refs[S.to_pairs]
            space_first_back(feed, 8, Place().order, *takes, engine.line_held)

        def prepare(refs):
            early = refs[S.early], refs[J.early]
            back.sources = refs[A.cond], early, (refs[S.late], refs[J.late])

        together(
            values,
            BACK_SPACE,
            (BACK_SPACE_ENDS, BACK_SPACE_MIDDLES),
            Joined(Joined(engine, back), BiasBack()),
            partials_of(S) + (J.to_table, S.to_table),
            grads_of(S) + (A.own_first, S.modulate, J.modulate, A.bias),
            "back_space",
            (A.cond, S.late, J.early, J.late, S.project),
            prepare,
            {A.first_back: first_back},
        )
        modulate = values[S.modulate], values[J.modulate]
        bias = bias_tables(values[A.bias])
    else:
        image_all = lax.all_gather(low_images, "wide", axis=0, tiled=True)
        cond = jnp.stack([jnp.repeat(low_clips, 4, axis=0), image_all], axis=1)
        values[S.mods], values[J.mods] = modulations(
            cond, (space_modulate, joint_modulate)
        )
        values.update(zip(weights[:4], gather_flat(space_shards)))
        values.update(zip(weights[4:], gather_flat(joint_shards)))
        values[A.all_rows] = lax.all_gather(tokens, "narrow", axis=0, tiled=True)
        apart(values, (S.triple,) + FORWARD[1:] + BACK_JOINT + (S.attend_back, S.project_back))
        for b in (J, S):
            values.update(zip(grads_of(b), scatter_plain([values[k] for k in partials_of(b)])))
        values[A.own_first] = lax.psum_scatter(
            values[A.to_first].astype(FULL), "narrow", scatter_dimension=0, tiled=True
        )
        apart(values, [A.finish])
        both = [
            jnp.concatenate([values[b.early], values[b.late][:, 2 * D :]], axis=1) for b in (S, J)
        ]
        modulate = modulation_grads(cond, jnp.stack(both), rows)
        space_grad = space_table_back(values[S.to_table], narrow)
        grads = jnp.concatenate([space_grad, joint_table_back(values[J.to_table])], axis=1)
        bias = lax.psum(grads, ("wide", "narrow"))
        split = space_bias.shape[1]
        bias = bias[:, :split], bias[:, split:]
    outs = [values[A.output_tokens], values[A.grad_tokens]]
    for i, b in enumerate((S, J)):
        outs += [modulate[i]] + [values[k] for k in reversed(grads_of(b))] + [bias[i]]
    return tuple(outs)


FORWARD = A.triple, S.attend, S.mlp, J.triple, J.attend, J.mlp
BACK_JOINT = J.mlp_back, J.attend_back, J.project_back, S.mlp_back
BACK_SPACE = S.attend_back, A.first_back, S.weight_back, A.finish


def solution(mesh):
    rows = P(("wide", "narrow"), None)
    block = P("wide", "narrow")
    in_specs = (
        (rows, P(), P("wide", None), P("wide"))
        + (block,) * 5
        + (P(),)
        + (block,) * 5
        + (P(), rows)
    )
    out_specs = (rows, rows) + ((block,) * 5 + (P(),)) * 2
    return jax.shard_map(body, mesh=mesh, in_specs=in_specs, out_specs=out_specs, check_vma=False)
```
